32 devices in a mesh: group: 4 (over x, core), resp: 8 (over z, y).
Axes of the slice: x: 2, y: 2, z: 4, core: 2. Of those that a mesh axis runs over, the one named last changes fastest.
Arguments:
- prompt_in: bfloat16 [4, 1024, 10240], P('group', 'resp'), may hold values from -6 to 6
- prompt_dt: bfloat16 [4, 1024, 128], P('group', 'resp'), may hold values from -3 to 9
- doc_starts: int32 [4, 4], P('group'), may hold values from 0 to 127, as said below
- resp_in: bfloat16 [4, 8, 256, 10240], P('group', 'resp'), may hold values from -6 to 6
- resp_dt: bfloat16 [4, 8, 256, 128], P('group', 'resp'), may hold values from -3 to 9
- resp_len: int32 [4, 8], P('group', 'resp'), may hold values from 64 to 256, as said below
- upstream: bfloat16 [4, 8, 256, 8192], P('group', 'resp'), may hold values from -6 to 6
- reward: float32 [4, 8], P('group', 'resp'), may hold values from -4 to 4
- conv_w: float32 [4, 10240], replicated, may hold values from -3 to 3
- conv_b: float32 [10240], replicated, may hold values from -0.5 to 0.5
- head_params: float32 [3, 128], replicated, may hold values from -5.5 to 1.5
Outputs:
- grad_conv_w: float32 [4, 10240], replicated
- grad_conv_b: float32 [10240], replicated
- grad_heads: float32 [3, 128], replicated
The draws below stay inside these ranges and needn't reach their ends.
Inputs may be any that keep to these rules, and one draw needn't show every extreme that they name: doc_starts begins with 0 and rises strictly; all documents but the last start within the first 128 positions. `resp_len`: each group has a response of 256 tokens.
All inputs are finite; a program needn't handle non-finite values.
Results may differ from the reference program's by a relative error of at most 0.01.
Values may be sent and summed in bfloat16 or wider, within the bound.
No kernel may reach another device: no remote copies, remote signals or barrier semaphores. Data moves between devices by JAX's collectives and lax.ppermute only.
A program may use at most 448 MiB of HBM per device.

```python
import jax
import jax.numpy as jnp
from jax import lax

H = 128
P_SIZE = 64
N = 256
G = 4
K = 4
DOCS = 4
PTOK_DEV = 128
RTOK = 256
GROUPS = 4
RESP = 8
PROMPT = 1024
CONV = 10240
N_RESP = 8


def step_inputs(key, array_dims):
    key_baseline, key_spike, key_height = jax.random.split(key, 3)
    ambient_level = jnp.clip(0.5 * jax.random.normal(key_baseline, array_dims, jnp.float32), -3.0, 3.0)
    spike_events = jax.random.uniform(key_spike, array_dims, jnp.float32) < 1.0 / (4.0 * PTOK_DEV)
    spike_level = 7.5 + 1.5 * jax.random.uniform(key_height, array_dims, jnp.float32)
    return jnp.where(spike_events, spike_level, ambient_level)


def draw_prompt_dt(key, part):
    key = jax.random.fold_in(key, 11)
    return step_inputs(key, (GROUPS, PROMPT, H)).astype(jnp.bfloat16)


def draw_resp_dt(key, part):
    key = jax.random.fold_in(key, 12)
    return step_inputs(key, (GROUPS, RESP, RTOK, H)).astype(jnp.bfloat16)


def draw_head_params(key, part):
    key = jax.random.fold_in(key, 13)
    key_intensity, key_bias, key_skip = jax.random.split(key, 3)
    rates = jax.random.uniform(key_intensity, (H,), jnp.float32, -3.9, 1.1)
    biases = jax.random.uniform(key_bias, (H,), jnp.float32, -5.0, -3.0)
    skips = jax.random.uniform(key_skip, (H,), jnp.float32, 0.5, 1.5)
    return jnp.stack([rates, biases, skips], axis=0)


def draw_doc_starts(key, part):
    key = jax.random.fold_in(key, 14)
    key_last, key_first, key_second, key_pick = jax.random.split(key, 4)
    last_start = jax.random.randint(key_last, (GROUPS,), DOCS - 1, max(DOCS, PTOK_DEV // 2))
    chosen = jax.random.randint(key_pick, (), 0, GROUPS)
    last_start = jnp.where(jnp.arange(GROUPS) == chosen, PTOK_DEV - 1, last_start)
    first_start = 1 + jax.random.randint(key_first, (GROUPS,), 0, 2 ** 20) % (last_start - 2)
    second_start = first_start + 1 + jax.random.randint(key_second, (GROUPS,), 0, 2 ** 20) % (last_start - first_start - 1)
    zero_start = jnp.zeros((GROUPS,), jnp.int32)
    return jnp.stack([zero_start, first_start, second_start, last_start], axis=1).astype(jnp.int32)


def draw_resp_len(key, part):
    key = jax.random.fold_in(key, 15)
    key_len, key_pick = jax.random.split(key)
    lengths = jax.random.randint(key_len, (GROUPS, RESP), RTOK // 4, RTOK + 1)
    chosen = jax.random.randint(key_pick, (GROUPS,), 0, RESP)
    lengths = jnp.where(jnp.arange(RESP)[None, :] == chosen[:, None], RTOK, lengths)
    return lengths.astype(jnp.int32)


def block_scale(rng, dims, cuts, least, largest):
    factor_of, own = 1.0, jax.random.fold_in(rng, 6)
    for position, blocks in cuts:
        draws = jnp.exp(jax.random.uniform(jax.random.fold_in(own, position), (blocks,), jnp.float32, least / len(cuts), largest / len(cuts)))
        factor_of = factor_of * jnp.repeat(draws, dims[position] // blocks).reshape([-1 if axis == position else 1 for axis in range(len(dims))])
    return factor_of


def bell_draw(own_key, extent, spread, reach, cuts=(), held_as=jnp.bfloat16):
    level = block_scale(own_key, extent, cuts, -0.22, 0.18) if cuts else 1.0
    entries = jax.random.normal(own_key, extent, jnp.float32) * spread * level
    return jnp.minimum(jnp.maximum(entries, -reach), reach).astype(held_as)


def setup_inputs(seed: int = 0) -> dict:
    arg_keys = jax.random.split(jax.random.key(seed), 12)
    return {
        "prompt_in": bell_draw(arg_keys[0], (GROUPS, PROMPT, CONV), 1.0, 6.0, ((0, 4), (1, 8))),
        "prompt_dt": draw_prompt_dt(jax.random.fold_in(arg_keys[11], 71), 0),
        "doc_starts": draw_doc_starts(jax.random.fold_in(arg_keys[11], 71), 0),
        "resp_in": bell_draw(arg_keys[3], (GROUPS, RESP, RTOK, CONV), 1.0, 6.0, ((0, 4), (1, 8))),
        "resp_dt": draw_resp_dt(jax.random.fold_in(arg_keys[11], 71), 0),
        "resp_len": draw_resp_len(jax.random.fold_in(arg_keys[11], 71), 0),
        "upstream": bell_draw(arg_keys[6], (GROUPS, RESP, RTOK, H * P_SIZE), 1.0, 6.0, ((0, 4), (1, 8))),
        "reward": bell_draw(arg_keys[7], (GROUPS, RESP), 1.0, 4.0, ((0, 4), (1, 8)), jnp.float32),
        "conv_w": bell_draw(arg_keys[8], (K, CONV), K ** -0.5, 3.0, (), jnp.float32),
        "conv_b": jnp.clip(jax.random.uniform(arg_keys[9], (CONV,), jnp.float32, -0.5, 0.5), -0.5, 0.5),
        "head_params": draw_head_params(jax.random.fold_in(arg_keys[11], 71), 0),
    }


def doc_number(starts, positions):
    return lax.optimization_barrier(jnp.sum((starts[None, :] <= positions[:, None]).astype(jnp.int32), axis=1))

def conv_silu(inputs_rows, conv_tail, tap_mask, conv_w, conv_b):
    n_rows = inputs_rows.shape[0]
    taps_back = conv_w.shape[0] - 1
    extended = jnp.concatenate([conv_tail, inputs_rows], axis=0).astype(jnp.float32)
    total = conv_b[None, :] + conv_w[taps_back][None, :] * extended[taps_back:]
    for offset in range(1, taps_back + 1):
        total = total + conv_w[taps_back - offset][None, :] * extended[taps_back - offset:taps_back - offset + n_rows] * tap_mask[:, offset - 1:offset]
    return jax.nn.silu(total).astype(jnp.bfloat16)

def prompt_state(params, inputs_rows, step_unbounded, conv_tail, tap_mask, in_last, carry_on):
    conv_w, conv_b, head_params = params
    n_rows = inputs_rows.shape[0]
    activated = conv_silu(inputs_rows, conv_tail, tap_mask, conv_w, conv_b)
    x_part = activated[:, :H * P_SIZE].reshape(n_rows, G, H // G, P_SIZE)
    b_part = activated[:, H * P_SIZE:H * P_SIZE + G * N].reshape(n_rows, G, N)
    step_size = jax.nn.softplus(step_unbounded.astype(jnp.float32) + head_params[1][None, :])
    log_decay = -jnp.exp(head_params[0])[None, :] * step_size
    whole_log = lax.optimization_barrier(jnp.sum(log_decay, axis=0))
    after_log = whole_log[None, :] - jnp.cumsum(log_decay, axis=0)
    weighting = in_last[:, None] * jnp.exp(after_log) * step_size
    scaled = (x_part * weighting.reshape(n_rows, G, H // G, 1)).astype(jnp.bfloat16)
    ssm_state = jnp.einsum('tgjp,tgn->gjpn', scaled.astype(jnp.float32), b_part.astype(jnp.float32)).reshape(H, P_SIZE, N)
    return (ssm_state, carry_on * jnp.exp(whole_log))

def group_mix(inputs):
    c_part, b_part, x_part, step_size, cum_decay, begin = inputs
    n_rows = c_part.shape[0]
    scores = jnp.dot(c_part, b_part.T, preferred_element_type=jnp.float32)
    log_gap = cum_decay.T[:, :, None] - cum_decay.T[:, None, :]
    causal = jnp.arange(n_rows)[:, None] >= jnp.arange(n_rows)[None, :]
    decays = jnp.exp(jnp.where(causal[None], log_gap, -1e+30))
    weights_mix = (scores[None] * decays * step_size.T[:, None, :]).astype(jnp.bfloat16)
    within = jnp.einsum('jts,sjp->tjp', weights_mix.astype(jnp.float32), x_part.astype(jnp.float32))
    carried = jnp.einsum('tn,jpn->tjp', c_part.astype(jnp.float32), begin.astype(jnp.float32)) * jnp.exp(cum_decay)[:, :, None]
    return within + carried

def response_out(params, begin, inputs_rows, step_unbounded, conv_tail):
    conv_w, conv_b, head_params = params
    n_rows = inputs_rows.shape[0]
    per_group = H // G
    activated = conv_silu(inputs_rows, conv_tail, jnp.ones((n_rows, K - 1), jnp.float32), conv_w, conv_b)
    x_part = activated[:, :H * P_SIZE].reshape(n_rows, G, per_group, P_SIZE)
    b_part = activated[:, H * P_SIZE:H * P_SIZE + G * N].reshape(n_rows, G, N)
    c_part = activated[:, H * P_SIZE + G * N:].reshape(n_rows, G, N)
    step_size = jax.nn.softplus(step_unbounded.astype(jnp.float32) + head_params[1][None, :])
    cum_decay = jnp.cumsum(-jnp.exp(head_params[0])[None, :] * step_size, axis=0)
    mixed = lax.map(jax.checkpoint(group_mix), (c_part.transpose(1, 0, 2), b_part.transpose(1, 0, 2), x_part.transpose(1, 0, 2, 3), step_size.reshape(n_rows, G, per_group).transpose(1, 0, 2), cum_decay.reshape(n_rows, G, per_group).transpose(1, 0, 2), begin.reshape(G, per_group, P_SIZE, N)))
    flat = mixed.transpose(1, 0, 2, 3).reshape(n_rows, H * P_SIZE)
    return flat + x_part.reshape(n_rows, H * P_SIZE).astype(jnp.float32) * jnp.repeat(head_params[2], P_SIZE)[None, :]

def reference(prompt_in, prompt_dt, doc_starts, resp_in, resp_dt, resp_len, upstream, reward, conv_w, conv_b, head_params):
    params = (conv_w, conv_b, head_params)
    taps_back = K - 1

    def one_group(inputs):
        p_rows, p_step, starts, r_rows, r_step, lengths, grad_out, rewards = inputs
        positions = jnp.arange(PROMPT, dtype=jnp.int32)
        doc_ids = doc_number(starts, positions)
        tap_mask = jnp.stack([(doc_number(starts, positions - offset) == doc_ids).astype(jnp.float32) for offset in range(1, taps_back + 1)], axis=1)
        blocks_in = p_rows.reshape(N_RESP, PTOK_DEV, CONV)
        prev_tail = jnp.concatenate([jnp.zeros((1, taps_back, CONV), p_rows.dtype), blocks_in[:-1, PTOK_DEV - taps_back:]], axis=0)
        block_docs = doc_ids.reshape(N_RESP, PTOK_DEV)
        last_docs = block_docs[:, -1]
        in_last = (block_docs == last_docs[:, None]).astype(jnp.float32)
        first_prev = doc_number(starts, positions.reshape(N_RESP, PTOK_DEV)[:, 0] - 1)
        carry_on = (first_prev == last_docs).astype(jnp.float32)
        block_inputs = (blocks_in, p_step.reshape(N_RESP, PTOK_DEV, H), prev_tail, tap_mask.reshape(N_RESP, PTOK_DEV, taps_back), in_last, carry_on)

        def block_state(blk):
            return prompt_state(params, blk[0], blk[1], blk[2], blk[3], blk[4], blk[5])
        states, carries = lax.map(block_state, block_inputs)

        def advance(held, inputs_pair):
            return (inputs_pair[0][:, None, None] * held + inputs_pair[1], held)
        final_state, befores = lax.scan(advance, jnp.zeros((H, P_SIZE, N), jnp.float32), (carries, states))

        def backward_product(running, decay_total):
            return (running * decay_total, running)
        _, suffixes = lax.scan(backward_product, jnp.ones((H,), jnp.float32), carries, reverse=True)
        start = final_state.astype(jnp.bfloat16)
        conv_tail = p_rows[PROMPT - taps_back:]
        advantage = rewards - jnp.sum(rewards) / N_RESP

        def one_response(inputs_resp):
            rows_one, step_one, length, grad_one, adv_one = inputs_resp
            in_length = (jnp.arange(RTOK) < length).astype(jnp.float32)
            cotangent = grad_one.astype(jnp.float32) * (adv_one / RTOK * in_length)[:, None]

            def respond(prm, begin):
                return response_out(prm, begin, rows_one, step_one, conv_tail)
            _, pullback = jax.vjp(respond, params, start)
            return pullback(cotangent)
        resp_grads, begin_grads = lax.map(one_response, (r_rows, r_step, lengths, grad_out, advantage))
        grad_state = lax.optimization_barrier(jnp.sum(begin_grads.astype(jnp.float32), axis=0))

        def block_grads(blk):
            inner_sum = lax.optimization_barrier(jnp.sum(grad_state * blk[7], axis=(1, 2)))

            def local(prm):
                return prompt_state(prm, blk[0], blk[1], blk[2], blk[3], blk[4], blk[5])
            _, pullback = jax.vjp(local, params)
            return pullback((blk[6][:, None, None] * grad_state, blk[6] * inner_sum))[0]
        prompt_grads = lax.map(block_grads, block_inputs + (suffixes, befores))
        return tuple((lax.optimization_barrier(jnp.sum(a, axis=0)) + lax.optimization_barrier(jnp.sum(b, axis=0)) for a, b in zip(resp_grads, prompt_grads)))
    per_group = lax.map(one_group, (prompt_in, prompt_dt, doc_starts, resp_in, resp_dt, resp_len, upstream, reward))
    return (lax.optimization_barrier(jnp.sum(per_group[0], axis=0)), lax.optimization_barrier(jnp.sum(per_group[1], axis=0)), lax.optimization_barrier(jnp.sum(per_group[2], axis=0)))
```

```python
import functools

import jax
import jax.numpy as jnp
from jax import lax
from jax.experimental import pallas as pl
from jax.experimental.pallas import tpu as pltpu
from jax.sharding import PartitionSpec as P

H = 128
PS = 64
N = 256
G = 4
K = 4
HG = H // G
XC = H * PS
GX = HG * PS
LANES = 128
PAD = 8
VMEM_LIMIT = 50 * 2**20

f32 = jnp.float32
bf16 = jnp.bfloat16

NN = (((1,), (0,)), ((), ()))
NT = (((1,), (1,)), ((), ()))


def dot(a, b, dims=NN, precision=None):
    return lax.dot_general(a, b, dims, precision=precision, preferred_element_type=f32)


def halves(v):
    hi = v.astype(bf16)
    return hi, (v - hi.astype(f32)).astype(bf16)


def indicator(first, width):
    row = lax.broadcasted_iota(jnp.int32, (LANES, width), 0)
    head = lax.shift_right_logical(lax.broadcasted_iota(jnp.int32, (LANES, width), 1), 6)
    return jnp.where(row - first == head, 1.0, 0.0).astype(bf16)


def expand(v, ind):
    hi, lo = halves(v)
    return dot(hi, ind) + dot(lo, ind)


def head_sums(z_hi, z_lo, ind):
    return dot(z_hi, ind, NT) + dot(z_lo, ind, NT)


def triangle(n, keep):
    i = lax.broadcasted_iota(jnp.int32, (n, n), 0)
    j = lax.broadcasted_iota(jnp.int32, (n, n), 1)
    return jnp.where(keep(i, j), 1.0, 0.0).astype(f32)


def tri_sum(tri, v):
    return dot(tri, v, precision=lax.Precision.HIGHEST)


def softplus(z):
    return jnp.maximum(z, 0.0) + jnp.log1p(jnp.exp(-jnp.abs(z)))


def sigmoid(z):
    return 0.5 * jnp.tanh(0.5 * z) + 0.5


def taps_of(ext, lanes, row, rows):
    return [ext[pl.ds(PAD - K + 1 + k + row, rows), lanes] for k in range(K)]


def conv_pre(taps, wb, masks=None):
    total = wb[K : K + 1] + wb[K - 1 : K] * taps[K - 1]
    for k in range(K - 1):
        term = wb[k : k + 1] * taps[k]
        if masks is not None:
            term = term * masks[k]
        total = total + term
    return total


def act_and_slope(pre):
    sig = sigmoid(pre)
    act = pre * sig
    return act, sig + act * (1.0 - sig)


def fold8(v):
    return jnp.sum(v.reshape(v.shape[0] // 8, 8, v.shape[1]), axis=0)


def lane_loop(width, body, step=LANES):
    def one(i, _):
        body(pl.ds(pl.multiple_of(i * step, step), step))
        return 0

    lax.fori_loop(0, width // step, one, 0)


RC = 64


def conv_forward(u, tail, wb, ext, act, slope, rows, width):
    def body(lanes):
        ext[0:PAD, lanes] = tail[:, lanes]
        ext[PAD : PAD + rows, lanes] = u[:, lanes].astype(f32)
        w = wb[:, lanes]
        for r in range(0, rows, RC):
            a, s = act_and_slope(conv_pre(taps_of(ext, lanes, r, RC), w))
            act[r : r + RC, lanes] = a.astype(bf16)
            if slope is not None:
                slope[r : r + RC, lanes] = s

    lane_loop(width, body)


def conv_backward(ext, slope, lanes, cotangent, grad, rows):
    sums = [jnp.zeros((8, LANES), f32) for _ in range(K + 1)]
    for r in range(0, rows, RC):
        d = cotangent(r) * slope[r : r + RC, lanes]
        taps = taps_of(ext, lanes, r, RC)
        for k in range(K):
            sums[k] = sums[k] + fold8(d * taps[k])
        sums[K] = sums[K] + fold8(d)
    for k in range(K + 1):
        grad[k : k + 1, lanes] = jnp.sum(sums[k], axis=0, keepdims=True)


def steps_kernel(len_ref, dt, hp, step, cum, cum_t, decay_in):
    rows = dt.shape[0]
    s = softplus(dt[...].astype(f32) + hp[1:2])
    logd = -jnp.exp(hp[0:1]) * s
    c = tri_sum(triangle(rows, lambda i, j: i >= j), logd)
    step[...] = s
    cum[...] = c
    cum_t[...] = c.T
    t = lax.broadcasted_iota(jnp.int32, c.shape, 0)
    decay_in[...] = jnp.where(t < len_ref[0, 0], jnp.exp(c), 0.0)


def resp_state_kernel(per, adv, u_c, tail_c, wb_c, dy, decay_in, state, weighted, c_out, ext, c_t):
    slab = pl.program_id(0)
    rows, width = dy.shape

    @pl.when(slab % per == 0)
    def _():
        conv_forward(u_c, tail_c, wb_c, ext, c_out, None, rows, N)
        c_t[...] = c_out[...].astype(f32).T.astype(bf16)

    ind = indicator(slab * (width // PS), width)
    a = (dy[...].astype(f32) * expand(decay_in[...], ind)).astype(bf16)
    weighted[...] = a
    state[0] = (dot(c_t[...], a) * adv[0, 0]).astype(bf16)


def resp_mid_kernel(
    len_ref, u_x, u_b, tail_x, tail_b, wb_x, wb_b, c_act, dy, step, cum, cum4, cum_t4, skip,
    grad_x, grad_b, dc, row_out, col_out,
    ext, ext_b, x_s, xs_s, b_s, dym, slope, slope_b, step_e, y_s, t_s,
    a1, bm, sw_e, u_off, y_off, z_hi, z_lo,
):
    g = pl.program_id(0)
    rows = u_x.shape[0]
    half = rows // 2
    conv_forward(u_x, tail_x, wb_x, ext, x_s, slope, rows, GX)
    conv_forward(u_b, tail_b, wb_b, ext_b, b_s, slope_b, rows, N)
    ind = indicator(g * HG, GX)
    step_e[...] = expand(step[...], ind)
    cum_v = cum[...]
    mid = cum_v[half - 1 : half]
    sw_e[...] = expand(jnp.exp(mid - cum_v[:half]) * step[:half], ind)
    y_off[...] = expand(jnp.exp(cum_v[half:] - mid), ind)
    live = jnp.where(lax.broadcasted_iota(jnp.int32, (rows, LANES), 0) < len_ref[0, 0], 1.0, 0.0)

    def prepare(lanes):
        d = dy[:, lanes].astype(f32) * live
        dym[:, lanes] = d.astype(bf16)
        x = x_s[:, lanes].astype(f32)
        xs_s[:, lanes] = (x * step_e[:, lanes]).astype(bf16)
        bm[:, lanes] = (x[:half] * sw_e[:, lanes]).astype(bf16)
        a1[:, lanes] = (d[half:] * y_off[:, lanes]).astype(bf16)

    lane_loop(GX, prepare)

    c_v, b_v = c_act[...], b_s[...]
    c0, c1, b0, b1 = c_v[:half], c_v[half:], b_v[:half], b_v[half:]
    i = lax.broadcasted_iota(jnp.int32, (half, half), 0)
    j = lax.broadcasted_iota(jnp.int32, (half, half), 1)
    lane = lax.broadcasted_iota(jnp.int32, (half, LANES), 1)
    first = jnp.where(lane < PS, 1.0, 0.0).astype(bf16)
    second = jnp.where(lane >= PS, 1.0, 0.0).astype(bf16)

    y_off[...] = dot(dot(c1, b0, NT).astype(bf16), bm[...])
    u_off[...] = dot(dot(b0, c1, NT).astype(bf16), a1[...])
    d10 = dot(a1[...], bm[...], NT)

    d_diag = []
    for q, (c_q, b_q) in enumerate(((c0, b0), (c1, b1))):
        r = slice(q * half, (q + 1) * half)
        lower = jnp.where(i >= j, dot(c_q, b_q, NT), 0.0)
        upper = jnp.where(j >= i, dot(b_q, c_q, NT), 0.0)
        d_sc = jnp.zeros((half, half), f32)
        for p in range(HG // 2):
            lanes = slice(p * LANES, (p + 1) * LANES)
            xs_p, dy_p = xs_s[r, lanes], dym[r, lanes]
            xb = jnp.concatenate([xs_p * first, xs_p * second], axis=0)
            dyb = jnp.concatenate([dy_p * first, dy_p * second], axis=0)
            d_m = dot(dy_p, xb, NT)
            mats, mats_t = [], []
            for a in range(2):
                h = 2 * p + a
                gap = jnp.exp(-jnp.abs(cum4[0, r, h : h + 1] - cum_t4[0, h : h + 1, r]))
                d_sc = d_sc + d_m[:, a * half : (a + 1) * half] * gap
                mats.append((gap * lower).astype(bf16))
                mats_t.append((gap * upper).astype(bf16))
            y_s[r, lanes] = dot(jnp.concatenate(mats, axis=1), xb)
            t_s[r, lanes] = dot(jnp.concatenate(mats_t, axis=1), dyb)
        d_diag.append(jnp.where(i >= j, d_sc, 0.0))

    d00, d11 = d_diag
    dc[:half] = dot(d00.astype(bf16), b0)
    dc[half:] = dot(d11.astype(bf16), b1) + dot(d10.astype(bf16), b0)
    db0 = dot(d00.T.astype(bf16), c0) + dot(d10.T.astype(bf16), c1)
    db1 = dot(d11.T.astype(bf16), c1)
    db = jnp.concatenate([db0, db1], axis=0)
    for k in range(N // LANES):
        lanes = slice(k * LANES, (k + 1) * LANES)
        conv_backward(ext_b, slope_b, lanes, lambda r: db[r : r + RC, lanes], grad_b, rows)

    def put(z, r, lanes):
        hi, lo = halves(z)
        z_hi[r : r + RC, lanes] = hi
        z_lo[r : r + RC, lanes] = lo

    def row_products(lanes):
        for r in range(0, rows, RC):
            z = dym[r : r + RC, lanes].astype(f32) * y_s[r : r + RC, lanes]
            if r >= half:
                o = r - half
                z = z + a1[o : o + RC, lanes].astype(f32) * y_off[o : o + RC, lanes]
            put(z, r, lanes)

    lane_loop(GX, row_products)
    row_sum = head_sums(z_hi[...], z_lo[...], ind)

    def finish(lanes):
        d_skip = jnp.zeros((8, LANES), f32)
        for r in range(0, rows, RC):
            t = t_s[r : r + RC, lanes]
            z = xs_s[r : r + RC, lanes].astype(f32) * t
            if r < half:
                z = z + bm[r : r + RC, lanes].astype(f32) * u_off[r : r + RC, lanes]
            put(z, r, lanes)
            d_skip = d_skip + fold8(
                dym[r : r + RC, lanes].astype(f32) * x_s[r : r + RC, lanes].astype(f32)
            )

        def cotangent(r):
            d = step_e[r : r + RC, lanes] * t_s[r : r + RC, lanes]
            d = d + skip[:, lanes] * dym[r : r + RC, lanes].astype(f32)
            if r < half:
                d = d + sw_e[r : r + RC, lanes] * u_off[r : r + RC, lanes]
            return d

        conv_backward(ext, slope, lanes, cotangent, grad_x, rows)
        grad_x[K + 1 : K + 2, lanes] = jnp.sum(d_skip, axis=0, keepdims=True)

    lane_loop(GX, finish)
    col_sum = head_sums(z_hi[...], z_lo[...], ind)

    @pl.when(g == 0)
    def _():
        row_out[...] = row_sum
        col_out[...] = col_sum

    @pl.when(g > 0)
    def _():
        row_out[...] += row_sum
        col_out[...] += col_sum


def resp_end_kernel(
    u_c, tail_c, wb_c, c_act, weighted, start, dc, row_in, col_in, step, dt, hp,
    grad_c, grad_h, ext, c_s, slope, total,
):
    g = pl.program_id(0)
    rows = u_c.shape[0]
    per, _, width = start.shape
    conv_forward(u_c, tail_c, wb_c, ext, c_s, slope, rows, N)
    d = dc[...]

    @pl.when(g == 0)
    def _():
        total[...] = row_in[...] - col_in[...]

    for s in range(per):
        a = weighted[:, s * width : (s + 1) * width]
        st = start[s]
        z_hi, z_lo = halves(a.astype(f32) * dot(c_act[...], st))
        total[...] += head_sums(z_hi, z_lo, indicator(g * HG + s * (width // PS), width))
        d = d + dot(a, st, NT)
    for k in range(N // LANES):
        lanes = slice(k * LANES, (k + 1) * LANES)
        conv_backward(ext, slope, lanes, lambda r: d[r : r + RC, lanes], grad_c, rows)

    @pl.when(g == pl.num_programs(0) - 1)
    def _():
        d_log = tri_sum(triangle(rows, lambda i, j: j >= i), total[...])
        rate = -jnp.exp(hp[0:1])
        s = step[...]
        d_step = col_in[...] / s + rate * d_log
        grad_h[...] = jnp.zeros_like(grad_h)
        grad_h[0:1] = jnp.sum(d_log * rate * s, axis=0, keepdims=True)
        grad_h[1:2] = jnp.sum(
            d_step * sigmoid(dt[...].astype(f32) + hp[1:2]), axis=0, keepdims=True
        )


RB = 256


def prompt_conv(v, masks, wb, ext, act, slope, row, width):
    def body(lanes):
        ext[PAD : PAD + RB, lanes] = v[pl.ds(row, RB), lanes].astype(f32)
        w = wb[:, lanes]
        for r in range(0, RB, RC):
            m = [masks[pl.ds(row + r, RC), k : k + 1] for k in range(K - 1)]
            a, s = act_and_slope(conv_pre(taps_of(ext, lanes, r, RC), w, m))
            act[r : r + RC, lanes] = a.astype(bf16)
            if slope is not None:
                slope[r : r + RC, lanes] = s

    lane_loop(width, body)


def prompt_state_kernel(v, masks, wb, hp, start, weight, step, ext, act, acc):
    rows = v.shape[0]
    width = start.shape[1]
    ind = indicator(0, width)
    later = triangle(RB, lambda i, j: j > i)
    ahead = jnp.zeros((1, LANES), f32)
    acc[...] = jnp.zeros_like(acc)
    for row in range(rows - RB, -1, -RB):
        s = softplus(v[row : row + RB, width + N :].astype(f32) + hp[1:2])
        logd = -jnp.exp(hp[0:1]) * s
        after = tri_sum(later, logd) + ahead
        ahead = ahead + jnp.sum(logd, axis=0, keepdims=True)
        w = masks[row : row + RB, K - 1 : K] * jnp.exp(after) * s
        step[row : row + RB] = s
        weight[row : row + RB] = w
        if row:
            ext[0:PAD] = v[row - 16 : row, : width + N].astype(f32)[16 - PAD :]
        else:
            ext[0:PAD] = jnp.zeros((PAD, width + N), f32)
        prompt_conv(v, masks, wb, ext, act, None, row, width + N)
        wx = (act[:, :width].astype(f32) * expand(w, ind)).astype(bf16)
        acc[...] += dot(act[:, width:].astype(f32).T.astype(bf16), wx)
    start[...] = acc[...].astype(bf16)


def prompt_grad_kernel(
    v, masks, wb, hp, weight, step, states,
    grad, grad_h, ext, act, slope, g_s, d_s, sums,
):
    rows = v.shape[0]
    width = states.shape[2]
    ind = indicator(0, width)
    earlier = triangle(RB, lambda i, j: j < i)
    total = states[0].astype(f32)
    for k in range(1, states.shape[0]):
        total = total + states[k].astype(f32)
    g_s[...] = total.astype(bf16)
    behind = jnp.zeros((1, LANES), f32)
    rate = -jnp.exp(hp[0:1])
    d_rate = jnp.zeros((1, LANES), f32)
    d_bias = jnp.zeros((1, LANES), f32)
    sums[...] = jnp.zeros_like(sums)
    for row in range(0, rows, RB):
        if row:
            ext[0:PAD] = v[row - 16 : row, : width + N].astype(f32)[16 - PAD :]
        else:
            ext[0:PAD] = jnp.zeros((PAD, width + N), f32)
        prompt_conv(v, masks, wb, ext, act, slope, row, width + N)
        w_e = expand(weight[row : row + RB], ind)
        t = dot(act[:, width:], g_s[...])
        wx = (act[:, :width].astype(f32) * w_e).astype(bf16)
        d_s[:, :width] = t * w_e
        d_s[:, width:] = dot(wx, g_s[...], NT)
        z_hi, z_lo = halves(wx.astype(f32) * t)
        q = head_sums(z_hi, z_lo, ind)
        d_log = tri_sum(earlier, q) + behind
        behind = behind + jnp.sum(q, axis=0, keepdims=True)
        s = step[row : row + RB]
        d_step = q / s + rate * d_log
        z = v[row : row + RB, width + N :].astype(f32) + hp[1:2]
        d_rate = d_rate + jnp.sum(d_log * rate * s, axis=0, keepdims=True)
        d_bias = d_bias + jnp.sum(d_step * sigmoid(z), axis=0, keepdims=True)

        def back(lanes):
            acc = [jnp.zeros((8, LANES), f32) for _ in range(K + 1)]
            for r in range(0, RB, RC):
                d = d_s[r : r + RC, lanes] * slope[r : r + RC, lanes]
                taps = taps_of(ext, lanes, r, RC)
                for k in range(K):
                    part = d * taps[k]
                    if k < K - 1:
                        part = part * masks[pl.ds(row + r, RC), k : k + 1]
                    acc[k] = acc[k] + fold8(part)
                acc[K] = acc[K] + fold8(d)
            for k in range(K + 1):
                sums[k : k + 1, lanes] += jnp.sum(acc[k], axis=0, keepdims=True)

        lane_loop(width + N, back)
    grad[...] = sums[...]
    grad_h[...] = jnp.zeros_like(grad_h)
    grad_h[0:1] = d_rate
    grad_h[1:2] = d_bias


def params(*semantics):
    return pltpu.CompilerParams(vmem_limit_bytes=VMEM_LIMIT, dimension_semantics=semantics or None)


SMEM = pl.BlockSpec(memory_space=pltpu.SMEM)


def whole(shape):
    return pl.BlockSpec(shape, lambda *_: (0,) * len(shape))


def sds(shape, dtype):
    return jax.ShapeDtypeStruct(shape, dtype)


def response_steps(length, dt, hp):
    rows = dt.shape[0]
    square = sds((rows, H), f32)
    return pl.pallas_call(
        steps_kernel,
        out_shape=(square, square, sds((H, rows), f32), square),
        in_specs=[SMEM, pl.BlockSpec(), pl.BlockSpec()],
        compiler_params=params(),
        name="resp_steps",
    )(length, dt, hp)


def response_state(n, scale, u, tail, wb, dy, decay_in):
    rows = u.shape[0]
    per = n // G
    width = XC // n
    c_at = lambda i: (0, XC // N + G + i // per)
    return pl.pallas_call(
        functools.partial(resp_state_kernel, per),
        grid=(n,),
        in_specs=[
            SMEM,
            pl.BlockSpec((rows, N), c_at),
            pl.BlockSpec((PAD, N), c_at),
            pl.BlockSpec((PAD, N), c_at),
            pl.BlockSpec((rows, width), lambda i: (0, i)),
            whole((rows, H)),
        ],
        out_specs=[
            pl.BlockSpec((1, N, width), lambda i: (i, 0, 0)),
            pl.BlockSpec((rows, width), lambda i: (0, i)),
            pl.BlockSpec((rows, N), lambda i: (0, i // per)),
        ],
        out_shape=(sds((n, N, width), bf16), sds((rows, XC), bf16), sds((rows, G * N), bf16)),
        scratch_shapes=[pltpu.VMEM((PAD + rows, N), f32), pltpu.VMEM((N, rows), bf16)],
        compiler_params=params("arbitrary"),
        cost_estimate=pl.CostEstimate(
            flops=2 * rows * N * XC, bytes_accessed=14 * 2**20, transcendentals=rows * G * N
        ),
        name="resp_state",
    )(scale, u, tail, wb, dy, decay_in)


def response_mid(length, u, tail, wb, c_act, dy, step, cum, cum4, cum_t4, skip):
    rows = u.shape[0]
    half = rows // 2
    x_at = lambda g: (0, g)
    b_at = lambda g: (0, XC // N + g)
    v = pltpu.VMEM
    return pl.pallas_call(
        resp_mid_kernel,
        grid=(G,),
        in_specs=[
            SMEM,
            pl.BlockSpec((rows, GX), x_at),
            pl.BlockSpec((rows, N), b_at),
            pl.BlockSpec((PAD, GX), x_at),
            pl.BlockSpec((PAD, N), b_at),
            pl.BlockSpec((PAD, GX), x_at),
            pl.BlockSpec((PAD, N), b_at),
            pl.BlockSpec((rows, N), x_at),
            pl.BlockSpec((rows, GX), x_at),
            whole((rows, H)),
            whole((rows, H)),
            pl.BlockSpec((1, rows, HG), lambda g: (g, 0, 0)),
            pl.BlockSpec((1, HG, rows), lambda g: (g, 0, 0)),
            pl.BlockSpec((1, GX), x_at),
        ],
        out_specs=[
            pl.BlockSpec((PAD, GX), x_at),
            pl.BlockSpec((PAD, N), x_at),
            pl.BlockSpec((rows, N), x_at),
            whole((rows, H)),
            whole((rows, H)),
        ],
        out_shape=(
            sds((PAD, XC), f32),
            sds((PAD, G * N), f32),
            sds((rows, G * N), f32),
            sds((rows, H), f32),
            sds((rows, H), f32),
        ),
        scratch_shapes=[
            v((PAD + rows, GX), f32),
            v((PAD + rows, N), f32),
            v((rows, GX), bf16),
            v((rows, GX), bf16),
            v((rows, N), bf16),
            v((rows, GX), bf16),
            v((rows, GX), f32),
            v((rows, N), f32),
            v((rows, GX), f32),
            v((rows, GX), f32),
            v((rows, GX), f32),
            v((half, GX), bf16),
            v((half, GX), bf16),
            v((half, GX), f32),
            v((half, GX), f32),
            v((half, GX), f32),
            v((rows, GX), bf16),
            v((rows, GX), bf16),
        ],
        compiler_params=params("arbitrary"),
        cost_estimate=pl.CostEstimate(
            flops=12 * 2**30, bytes_accessed=12 * 2**20, transcendentals=rows * half * H
        ),
        name="resp_mid",
    )(length, u, u, tail, tail, wb, wb, c_act, dy, step, cum, cum4, cum_t4, skip)


def response_end(u, tail, wb, c_act, weighted, start, dc, row_in, col_in, step, dt, hp):
    rows = u.shape[0]
    n, _, width = start.shape
    per = n // G
    c_at = lambda g: (0, XC // N + G + g)
    g_at = lambda g: (0, g)
    v = pltpu.VMEM
    return pl.pallas_call(
        resp_end_kernel,
        grid=(G,),
        in_specs=[
            pl.BlockSpec((rows, N), c_at),
            pl.BlockSpec((PAD, N), c_at),
            pl.BlockSpec((PAD, N), c_at),
            pl.BlockSpec((rows, N), g_at),
            pl.BlockSpec((rows, GX), g_at),
            pl.BlockSpec((per, N, width), lambda g: (g, 0, 0)),
            pl.BlockSpec((rows, N), g_at),
            whole((rows, H)),
            whole((rows, H)),
            whole((rows, H)),
            whole((rows, H)),
            whole((PAD, H)),
        ],
        out_specs=[pl.BlockSpec((PAD, N), g_at), whole((PAD, H))],
        out_shape=(sds((PAD, G * N), f32), sds((PAD, H), f32)),
        scratch_shapes=[
            v((PAD + rows, N), f32),
            v((rows, N), bf16),
            v((rows, N), f32),
            v((rows, H), f32),
        ],
        compiler_params=params("arbitrary"),
        cost_estimate=pl.CostEstimate(
            flops=4 * rows * N * XC, bytes_accessed=12 * 2**20, transcendentals=rows * G * N
        ),
        name="resp_end",
    )(u, tail, wb, c_act, weighted, start, dc, row_in, col_in, step, dt, hp)


def prompt_state(v, masks, wb, hp, width):
    rows = v.shape[0]
    s = pltpu.VMEM
    return pl.pallas_call(
        prompt_state_kernel,
        out_shape=(sds((N, width), bf16), sds((rows, LANES), f32), sds((rows, LANES), f32)),
        scratch_shapes=[
            s((PAD + RB, width + N), f32),
            s((RB, width + N), bf16),
            s((N, width), f32),
        ],
        compiler_params=params(),
        cost_estimate=pl.CostEstimate(
            flops=2 * rows * N * width, bytes_accessed=4 * 2**20, transcendentals=rows * width
        ),
        name="prompt_state",
    )(v, masks, wb, hp)


def prompt_grad(v, masks, wb, hp, weight, step, states):
    rows = v.shape[0]
    width = states.shape[2]
    s = pltpu.VMEM
    return pl.pallas_call(
        prompt_grad_kernel,
        out_shape=(sds((PAD, width + N), f32), sds((PAD, LANES), f32)),
        scratch_shapes=[
            s((PAD + RB, width + N), f32),
            s((RB, width + N), bf16),
            s((RB, width + N), f32),
            s((N, width), bf16),
            s((RB, width + N), f32),
            s((PAD, width + N), f32),
        ],
        compiler_params=params(),
        cost_estimate=pl.CostEstimate(
            flops=4 * rows * N * width, bytes_accessed=8 * 2**20, transcendentals=rows * width
        ),
        name="prompt_grad",
    )(v, masks, wb, hp, weight, step, states)


def doc_number(starts, positions):
    return jnp.sum((starts[None, :] <= positions[:, None]).astype(jnp.int32), axis=1)


def prompt_masks(starts, rows):
    positions = jnp.arange(rows, dtype=jnp.int32)
    docs = doc_number(starts, positions)
    same = [doc_number(starts, positions - (K - 1 - k)) == docs for k in range(K - 1)]
    columns = jnp.stack(same + [docs == docs[rows - 1]], axis=1).astype(f32)
    return jnp.pad(columns, ((0, 0), (0, PAD - K)))


def pad_rows(a):
    return jnp.pad(a, ((0, PAD - a.shape[0]), (0, 0)))


def shards(
    prompt_in, prompt_dt, doc_starts, resp_in, resp_dt, resp_len, upstream, reward,
    conv_w, conv_b, head_params,
):
    n = lax.axis_size("resp")
    me = lax.axis_index("resp")
    hs = H // n
    width = XC // n
    per = n // G
    block = prompt_in.shape[1]
    slots = resp_in.shape[2]
    rows_in, dt_in = prompt_in[0], prompt_dt[0]
    u, dt, dy = resp_in[0, 0], resp_dt[0, 0], upstream[0, 0]

    r = reward[0, 0]
    r_hi = r.astype(bf16)
    r_mid = (r - r_hi.astype(f32)).astype(bf16)
    r_lo = (r - r_hi.astype(f32) - r_mid.astype(f32)).astype(bf16)
    tail_size = (K - 1) * rows_in.shape[1] // LANES
    small = jnp.concatenate(
        [
            rows_in[block - K + 1 :].reshape(tail_size, LANES),
            jnp.broadcast_to(jnp.stack([r_hi, r_mid, r_lo, jnp.zeros_like(r_lo)])[:, None], (4, LANES)),
            jnp.zeros((12, LANES), bf16),
        ]
    )
    small = lax.all_gather(small, "resp")
    tail_rows = small[n - 1, :tail_size].reshape(K - 1, -1).astype(f32)
    tail = jnp.pad(tail_rows, ((PAD - K + 1, 0), (0, 0)))
    rewards = jnp.sum(small[:, tail_size : tail_size + 3, 0].astype(f32), axis=1)
    scale = (r - jnp.sum(rewards) / n) / slots
    wb = pad_rows(jnp.concatenate([conv_w, conv_b[None]], axis=0))
    hp = pad_rows(head_params)

    x_parts = rows_in[:, :XC].reshape(block, n, width).transpose(1, 0, 2)
    b_parts = jnp.repeat(
        rows_in[:, XC : XC + G * N].reshape(block, G, N).transpose(1, 0, 2), per, axis=0
    )
    dt_parts = jnp.pad(
        dt_in.reshape(block, n, hs).transpose(1, 0, 2), ((0, 0), (0, 0), (0, LANES - hs))
    )
    v = lax.all_to_all(
        jnp.concatenate([x_parts, b_parts, dt_parts], axis=2), "resp", 0, 0
    ).reshape(n * block, width + N + LANES)
    masks = prompt_masks(doc_starts[0], n * block)
    my_group = me // per
    wb_mine = jnp.concatenate(
        [
            lax.dynamic_slice(wb, (0, me * width), (PAD, width)),
            lax.dynamic_slice(wb, (0, XC + my_group * N), (PAD, N)),
        ],
        axis=1,
    )
    hp_mine = jnp.pad(lax.dynamic_slice(hp, (0, me * hs), (PAD, hs)), ((0, 0), (0, LANES - hs)))

    length = resp_len.astype(jnp.int32)
    step, cum, cum_t, decay_in = response_steps(length, dt, hp)
    d_states, weighted, c_act = response_state(
        n, scale.reshape(1, 1), u, tail, wb, dy, decay_in
    )
    start_mine, weight, p_step = prompt_state(v, masks, wb_mine, hp_mine, width)
    start = lax.all_gather(start_mine, "resp")
    d_states = lax.all_to_all(d_states, "resp", 0, 0)

    cum4 = cum.reshape(slots, G, HG).transpose(1, 0, 2)
    skip = jnp.repeat(head_params[2], PS)[None, :]
    grad_x, grad_b, dc, row_in, col_in = response_mid(
        length, u, tail, wb, c_act, dy, step, cum, cum4, cum_t.reshape(G, HG, slots), skip
    )
    p_grad, p_heads = prompt_grad(v, masks, wb_mine, hp_mine, weight, p_step, d_states)
    grad_c, r_heads = response_end(
        u, tail, wb, c_act, weighted, start, dc, row_in, col_in, step, dt, hp
    )

    conv = jnp.concatenate([grad_x, grad_b, grad_c], axis=1)[: K + 1] * scale
    mine = lax.dynamic_slice(conv, (0, me * width), (K + 1, width)) + p_grad[: K + 1, :width]
    conv = lax.dynamic_update_slice(conv, mine, (0, me * width))
    at_b = XC + my_group * N
    mine = lax.dynamic_slice(conv, (0, at_b), (K + 1, N)) + p_grad[: K + 1, width:]
    conv = lax.dynamic_update_slice(conv, mine, (0, at_b))
    d_skip = jnp.sum(grad_x[K + 1].reshape(H, PS), axis=1)
    heads = jnp.concatenate([r_heads[:2], d_skip[None]], axis=0) * scale
    mine = lax.dynamic_slice(heads, (0, me * hs), (2, hs)) + p_heads[:2, :hs]
    heads = lax.dynamic_update_slice(heads, mine, (0, me * hs))
    conv, heads = lax.psum((conv, heads), ("group", "resp"))
    return conv[:K], conv[K], heads


def solution(mesh):
    in_specs = (
        P("group", "resp", None),
        P("group", "resp", None),
        P("group", None),
        P("group", "resp", None, None),
        P("group", "resp", None, None),
        P("group", "resp"),
        P("group", "resp", None, None),
        P("group", "resp"),
        P(),
        P(),
        P(),
    )
    out_specs = (P(), P(), P())
    return jax.shard_map(shards, mesh=mesh, in_specs=in_specs, out_specs=out_specs, check_vma=False)
```

```python
import functools

import jax
import jax.numpy as jnp
from jax import lax
from jax.experimental import pallas as pl
from jax.experimental.pallas import tpu as pltpu
from jax.sharding import PartitionSpec as P

H = 128
PS = 64
N = 256
G = 4
K = 4
HG = H // G
XC = H * PS
GX = HG * PS
LANES = 128
PAD = 8
VMEM_LIMIT = 50 * 2**20

f32 = jnp.float32
bf16 = jnp.bfloat16

NN = (((1,), (0,)), ((), ()))
NT = (((1,), (1,)), ((), ()))


def dot(a, b, dims=NN, precision=None):
    return lax.dot_general(a, b, dims, precision=precision, preferred_element_type=f32)


def halves(v):
    hi = v.astype(bf16)
    return hi, (v - hi.astype(f32)).astype(bf16)


def indicator(first, width):
    row = lax.broadcasted_iota(jnp.int32, (LANES, width), 0)
    head = lax.shift_right_logical(lax.broadcasted_iota(jnp.int32, (LANES, width), 1), 6)
    return jnp.where(row - first == head, 1.0, 0.0).astype(bf16)


def expand(v, ind):
    hi, lo = halves(v)
    return dot(hi, ind) + dot(lo, ind)


def head_sums(z_hi, z_lo, ind):
    return dot(z_hi, ind, NT) + dot(z_lo, ind, NT)


def triangle(n, keep):
    i = lax.broadcasted_iota(jnp.int32, (n, n), 0)
    j = lax.broadcasted_iota(jnp.int32, (n, n), 1)
    return jnp.where(keep(i, j), 1.0, 0.0).astype(f32)


def tri_sum(tri, v):
    return dot(tri, v, precision=lax.Precision.HIGHEST)


def softplus(z):
    return jnp.maximum(z, 0.0) + jnp.log1p(jnp.exp(-jnp.abs(z)))


def sigmoid(z):
    return 0.5 * jnp.tanh(0.5 * z) + 0.5


def taps_of(ext, lanes, row, rows):
    return [ext[pl.ds(PAD - K + 1 + k + row, rows), lanes] for k in range(K)]


def conv_pre(taps, wb, masks=None):
    total = wb[K : K + 1] + wb[K - 1 : K] * taps[K - 1]
    for k in range(K - 1):
        term = wb[k : k + 1] * taps[k]
        if masks is not None:
            term = term * masks[k]
        total = total + term
    return total


def act_and_slope(pre):
    sig = sigmoid(pre)
    act = pre * sig
    return act, sig + act * (1.0 - sig)


def fold8(v):
    return jnp.sum(v.reshape(v.shape[0] // 8, 8, v.shape[1]), axis=0)


def lane_loop(width, body, step=LANES):
    def one(i, _):
        body(pl.ds(pl.multiple_of(i * step, step), step))
        return 0

    lax.fori_loop(0, width // step, one, 0)


RC = 64


def conv_forward(u, tail, wb, ext, act, slope, rows, width):
    def body(lanes):
        ext[0:PAD, lanes] = tail[:, lanes]
        ext[PAD : PAD + rows, lanes] = u[:, lanes].astype(f32)
        w = wb[:, lanes]
        for r in range(0, rows, RC):
            a, s = act_and_slope(conv_pre(taps_of(ext, lanes, r, RC), w))
            act[r : r + RC, lanes] = a.astype(bf16)
            if slope is not None:
                slope[r : r + RC, lanes] = s

    lane_loop(width, body)


def conv_backward(ext, slope, lanes, cotangent, grad, rows):
    sums = [jnp.zeros((8, LANES), f32) for _ in range(K + 1)]
    for r in range(0, rows, RC):
        d = cotangent(r) * slope[r : r + RC, lanes]
        taps = taps_of(ext, lanes, r, RC)
        for k in range(K):
            sums[k] = sums[k] + fold8(d * taps[k])
        sums[K] = sums[K] + fold8(d)
    for k in range(K + 1):
        grad[k : k + 1, lanes] = jnp.sum(sums[k], axis=0, keepdims=True)


def steps_kernel(len_ref, dt, hp, step, cum, cum_t, decay_in):
    rows = dt.shape[0]
    s = softplus(dt[...].astype(f32) + hp[1:2])
    logd = -jnp.exp(hp[0:1]) * s
    c = tri_sum(triangle(rows, lambda i, j: i >= j), logd)
    step[...] = s
    cum[...] = c
    cum_t[...] = c.T
    t = lax.broadcasted_iota(jnp.int32, c.shape, 0)
    decay_in[...] = jnp.where(t < len_ref[0, 0], jnp.exp(c), 0.0)


def resp_state_kernel(per, adv, u_c, tail_c, wb_c, dy, decay_in, state, weighted, c_out, ext, c_t):
    slab = pl.program_id(0)
    rows, width = dy.shape

    @pl.when(slab % per == 0)
    def _():
        conv_forward(u_c, tail_c, wb_c, ext, c_out, None, rows, N)
        c_t[...] = c_out[...].astype(f32).T.astype(bf16)

    ind = indicator(slab * (width // PS), width)
    a = (dy[...].astype(f32) * expand(decay_in[...], ind)).astype(bf16)
    weighted[...] = a
    state[0] = (dot(c_t[...], a) * adv[0, 0]).astype(bf16)


def resp_mid_kernel(
    base, len_ref, u_x, u_b, tail_x, tail_b, wb_x, wb_b, c_act, dy, step, cum, cum4, cum_t4, skip,
    grad_x, grad_b, dc, row_out, col_out,
    ext, ext_b, x_s, xs_s, b_s, dym, slope, slope_b, step_e, y_s, t_s,
    a1, bm, sw_e, u_off, y_off, z_hi, z_lo,
):
    step_no = pl.program_id(0)
    g = step_no + base
    rows = u_x.shape[0]
    half = rows // 2
    conv_forward(u_x, tail_x, wb_x, ext, x_s, slope, rows, GX)
    conv_forward(u_b, tail_b, wb_b, ext_b, b_s, slope_b, rows, N)
    ind = indicator(g * HG, GX)
    step_e[...] = expand(step[...], ind)
    cum_v = cum[...]
    mid = cum_v[half - 1 : half]
    sw_e[...] = expand(jnp.exp(mid - cum_v[:half]) * step[:half], ind)
    y_off[...] = expand(jnp.exp(cum_v[half:] - mid), ind)
    live = jnp.where(lax.broadcasted_iota(jnp.int32, (rows, LANES), 0) < len_ref[0, 0], 1.0, 0.0)

    def prepare(lanes):
        d = dy[:, lanes].astype(f32) * live
        dym[:, lanes] = d.astype(bf16)
        x = x_s[:, lanes].astype(f32)
        xs_s[:, lanes] = (x * step_e[:, lanes]).astype(bf16)
        bm[:, lanes] = (x[:half] * sw_e[:, lanes]).astype(bf16)
        a1[:, lanes] = (d[half:] * y_off[:, lanes]).astype(bf16)

    lane_loop(GX, prepare)

    c_v, b_v = c_act[...], b_s[...]
    c0, c1, b0, b1 = c_v[:half], c_v[half:], b_v[:half], b_v[half:]
    i = lax.broadcasted_iota(jnp.int32, (half, half), 0)
    j = lax.broadcasted_iota(jnp.int32, (half, half), 1)
    lane = lax.broadcasted_iota(jnp.int32, (half, LANES), 1)
    first = jnp.where(lane < PS, 1.0, 0.0).astype(bf16)
    second = jnp.where(lane >= PS, 1.0, 0.0).astype(bf16)

    y_off[...] = dot(dot(c1, b0, NT).astype(bf16), bm[...])
    u_off[...] = dot(dot(b0, c1, NT).astype(bf16), a1[...])
    d10 = dot(a1[...], bm[...], NT)

    d_diag = []
    for q, (c_q, b_q) in enumerate(((c0, b0), (c1, b1))):
        r = slice(q * half, (q + 1) * half)
        lower = jnp.where(i >= j, dot(c_q, b_q, NT), 0.0)
        upper = jnp.where(j >= i, dot(b_q, c_q, NT), 0.0)
        d_sc = jnp.zeros((half, half), f32)
        for p in range(HG // 2):
            lanes = slice(p * LANES, (p + 1) * LANES)
            xs_p, dy_p = xs_s[r, lanes], dym[r, lanes]
            xb = jnp.concatenate([xs_p * first, xs_p * second], axis=0)
            dyb = jnp.concatenate([dy_p * first, dy_p * second], axis=0)
            d_m = dot(dy_p, xb, NT)
            mats, mats_t = [], []
            for a in range(2):
                h = 2 * p + a
                gap = jnp.exp(-jnp.abs(cum4[0, r, h : h + 1] - cum_t4[0, h : h + 1, r]))
                d_sc = d_sc + d_m[:, a * half : (a + 1) * half] * gap
                mats.append((gap * lower).astype(bf16))
                mats_t.append((gap * upper).astype(bf16))
            y_s[r, lanes] = dot(jnp.concatenate(mats, axis=1), xb)
            t_s[r, lanes] = dot(jnp.concatenate(mats_t, axis=1), dyb)
        d_diag.append(jnp.where(i >= j, d_sc, 0.0))

    d00, d11 = d_diag
    dc[:half] = dot(d00.astype(bf16), b0)
    dc[half:] = dot(d11.astype(bf16), b1) + dot(d10.astype(bf16), b0)
    db0 = dot(d00.T.astype(bf16), c0) + dot(d10.T.astype(bf16), c1)
    db1 = dot(d11.T.astype(bf16), c1)
    db = jnp.concatenate([db0, db1], axis=0)
    for k in range(N // LANES):
        lanes = slice(k * LANES, (k + 1) * LANES)
        conv_backward(ext_b, slope_b, lanes, lambda r: db[r : r + RC, lanes], grad_b, rows)

    def put(z, r, lanes):
        hi, lo = halves(z)
        z_hi[r : r + RC, lanes] = hi
        z_lo[r : r + RC, lanes] = lo

    def row_products(lanes):
        for r in range(0, rows, RC):
            z = dym[r : r + RC, lanes].astype(f32) * y_s[r : r + RC, lanes]
            if r >= half:
                o = r - half
                z = z + a1[o : o + RC, lanes].astype(f32) * y_off[o : o + RC, lanes]
            put(z, r, lanes)

    lane_loop(GX, row_products)
    row_sum = head_sums(z_hi[...], z_lo[...], ind)

    def finish(lanes):
        d_skip = jnp.zeros((8, LANES), f32)
        for r in range(0, rows, RC):
            t = t_s[r : r + RC, lanes]
            z = xs_s[r : r + RC, lanes].astype(f32) * t
            if r < half:
                z = z + bm[r : r + RC, lanes].astype(f32) * u_off[r : r + RC, lanes]
            put(z, r, lanes)
            d_skip = d_skip + fold8(
                dym[r : r + RC, lanes].astype(f32) * x_s[r : r + RC, lanes].astype(f32)
            )

        def cotangent(r):
            d = step_e[r : r + RC, lanes] * t_s[r : r + RC, lanes]
            d = d + skip[:, lanes] * dym[r : r + RC, lanes].astype(f32)
            if r < half:
                d = d + sw_e[r : r + RC, lanes] * u_off[r : r + RC, lanes]
            return d

        conv_backward(ext, slope, lanes, cotangent, grad_x, rows)
        grad_x[K + 1 : K + 2, lanes] = jnp.sum(d_skip, axis=0, keepdims=True)

    lane_loop(GX, finish)
    col_sum = head_sums(z_hi[...], z_lo[...], ind)

    @pl.when(step_no == 0)
    def _():
        row_out[...] = row_sum
        col_out[...] = col_sum

    @pl.when(step_no > 0)
    def _():
        row_out[...] += row_sum
        col_out[...] += col_sum


def resp_end_kernel(
    u_c, tail_c, wb_c, c_act, weighted, start, dc, row_a, row_b, col_a, col_b, step, dt, hp,
    grad_c, grad_h, ext, c_s, slope, total,
):
    g = pl.program_id(0)
    rows = u_c.shape[0]
    per, _, width = start.shape
    conv_forward(u_c, tail_c, wb_c, ext, c_s, slope, rows, N)
    d = dc[...]

    @pl.when(g == 0)
    def _():
        total[...] = (row_a[...] + row_b[...]) - (col_a[...] + col_b[...])

    for s in range(per):
        a = weighted[:, s * width : (s + 1) * width]
        st = start[s]
        z_hi, z_lo = halves(a.astype(f32) * dot(c_act[...], st))
        total[...] += head_sums(z_hi, z_lo, indicator(g * HG + s * (width // PS), width))
        d = d + dot(a, st, NT)
    for k in range(N // LANES):
        lanes = slice(k * LANES, (k + 1) * LANES)
        conv_backward(ext, slope, lanes, lambda r: d[r : r + RC, lanes], grad_c, rows)

    @pl.when(g == pl.num_programs(0) - 1)
    def _():
        d_log = tri_sum(triangle(rows, lambda i, j: j >= i), total[...])
        rate = -jnp.exp(hp[0:1])
        s = step[...]
        d_step = (col_a[...] + col_b[...]) / s + rate * d_log
        grad_h[...] = jnp.zeros_like(grad_h)
        grad_h[0:1] = jnp.sum(d_log * rate * s, axis=0, keepdims=True)
        grad_h[1:2] = jnp.sum(
            d_step * sigmoid(dt[...].astype(f32) + hp[1:2]), axis=0, keepdims=True
        )


RB = 256


def prompt_conv(v, masks, wb, ext, act, slope, row, width):
    def body(lanes):
        ext[PAD : PAD + RB, lanes] = v[pl.ds(row, RB), lanes].astype(f32)
        w = wb[:, lanes]
        for r in range(0, RB, RC):
            m = [masks[pl.ds(row + r, RC), k : k + 1] for k in range(K - 1)]
            a, s = act_and_slope(conv_pre(taps_of(ext, lanes, r, RC), w, m))
            act[r : r + RC, lanes] = a.astype(bf16)
            if slope is not None:
                slope[r : r + RC, lanes] = s

    lane_loop(width, body)


def prompt_state_kernel(v, masks, wb, hp, earlier_out, start, weight, step, ext, act, acc):
    rows = v.shape[0]
    width = start.shape[1]
    ind = indicator(0, width)
    later = triangle(RB, lambda i, j: j > i)
    ahead = jnp.zeros((1, LANES), f32)
    acc[...] = jnp.zeros_like(acc)
    for row in range(rows - RB, -1, -RB):
        s = softplus(v[row : row + RB, width + N :].astype(f32) + hp[1:2])
        logd = -jnp.exp(hp[0:1]) * s
        after = tri_sum(later, logd) + ahead
        ahead = ahead + jnp.sum(logd, axis=0, keepdims=True)
        w = masks[row : row + RB, K - 1 : K] * jnp.exp(after) * s
        step[row : row + RB] = s
        weight[row : row + RB] = w
        if row:
            ext[0:PAD] = v[row - 16 : row, : width + N].astype(f32)[16 - PAD :]
        else:
            ext[0:PAD] = jnp.zeros((PAD, width + N), f32)
        prompt_conv(v, masks, wb, ext, act, None, row, width + N)
        wx = (act[:, :width].astype(f32) * expand(w, ind)).astype(bf16)
        acc[...] += dot(act[:, width:].astype(f32).T.astype(bf16), wx)
    start[...] = acc[...].astype(bf16)


def prompt_grad_kernel(
    v, masks, wb, hp, weight, step, states,
    grad, grad_h, ext, act, slope, g_s, d_s, sums,
):
    rows = v.shape[0]
    width = states.shape[2]
    ind = indicator(0, width)
    earlier = triangle(RB, lambda i, j: j < i)
    total = states[0].astype(f32)
    for k in range(1, states.shape[0]):
        total = total + states[k].astype(f32)
    g_s[...] = total.astype(bf16)
    behind = jnp.zeros((1, LANES), f32)
    rate = -jnp.exp(hp[0:1])
    d_rate = jnp.zeros((1, LANES), f32)
    d_bias = jnp.zeros((1, LANES), f32)
    sums[...] = jnp.zeros_like(sums)
    for row in range(0, rows, RB):
        if row:
            ext[0:PAD] = v[row - 16 : row, : width + N].astype(f32)[16 - PAD :]
        else:
            ext[0:PAD] = jnp.zeros((PAD, width + N), f32)
        prompt_conv(v, masks, wb, ext, act, slope, row, width + N)
        w_e = expand(weight[row : row + RB], ind)
        t = dot(act[:, width:], g_s[...])
        wx = (act[:, :width].astype(f32) * w_e).astype(bf16)
        d_s[:, :width] = t * w_e
        d_s[:, width:] = dot(wx, g_s[...], NT)
        z_hi, z_lo = halves(wx.astype(f32) * t)
        q = head_sums(z_hi, z_lo, ind)
        d_log = tri_sum(earlier, q) + behind
        behind = behind + jnp.sum(q, axis=0, keepdims=True)
        s = step[row : row + RB]
        d_step = q / s + rate * d_log
        z = v[row : row + RB, width + N :].astype(f32) + hp[1:2]
        d_rate = d_rate + jnp.sum(d_log * rate * s, axis=0, keepdims=True)
        d_bias = d_bias + jnp.sum(d_step * sigmoid(z), axis=0, keepdims=True)

        def back(lanes):
            acc = [jnp.zeros((8, LANES), f32) for _ in range(K + 1)]
            for r in range(0, RB, RC):
                d = d_s[r : r + RC, lanes] * slope[r : r + RC, lanes]
                taps = taps_of(ext, lanes, r, RC)
                for k in range(K):
                    part = d * taps[k]
                    if k < K - 1:
                        part = part * masks[pl.ds(row + r, RC), k : k + 1]
                    acc[k] = acc[k] + fold8(part)
                acc[K] = acc[K] + fold8(d)
            for k in range(K + 1):
                sums[k : k + 1, lanes] += jnp.sum(acc[k], axis=0, keepdims=True)

        lane_loop(width + N, back)
    grad[...] = sums[...]
    grad_h[...] = jnp.zeros_like(grad_h)
    grad_h[0:1] = d_rate
    grad_h[1:2] = d_bias


def params(*semantics):
    return pltpu.CompilerParams(vmem_limit_bytes=VMEM_LIMIT, dimension_semantics=semantics or None)


SMEM = pl.BlockSpec(memory_space=pltpu.SMEM)


def whole(shape):
    return pl.BlockSpec(shape, lambda *_: (0,) * len(shape))


def sds(shape, dtype):
    return jax.ShapeDtypeStruct(shape, dtype)


def response_steps(length, dt, hp):
    rows = dt.shape[0]
    square = sds((rows, H), f32)
    return pl.pallas_call(
        steps_kernel,
        out_shape=(square, square, sds((H, rows), f32), square),
        in_specs=[SMEM, pl.BlockSpec(), pl.BlockSpec()],
        compiler_params=params(),
        name="resp_steps",
    )(length, dt, hp)


def response_state(n, scale, u, tail, wb, dy, decay_in):
    rows = u.shape[0]
    per = n // G
    width = XC // n
    c_at = lambda i: (0, XC // N + G + i // per)
    return pl.pallas_call(
        functools.partial(resp_state_kernel, per),
        grid=(n,),
        in_specs=[
            SMEM,
            pl.BlockSpec((rows, N), c_at),
            pl.BlockSpec((PAD, N), c_at),
            pl.BlockSpec((PAD, N), c_at),
            pl.BlockSpec((rows, width), lambda i: (0, i)),
            whole((rows, H)),
        ],
        out_specs=[
            pl.BlockSpec((1, N, width), lambda i: (i, 0, 0)),
            pl.BlockSpec((rows, width), lambda i: (0, i)),
            pl.BlockSpec((rows, N), lambda i: (0, i // per)),
        ],
        out_shape=(sds((n, N, width), bf16), sds((rows, XC), bf16), sds((rows, G * N), bf16)),
        scratch_shapes=[pltpu.VMEM((PAD + rows, N), f32), pltpu.VMEM((N, rows), bf16)],
        compiler_params=params("arbitrary"),
        cost_estimate=pl.CostEstimate(
            flops=2 * rows * N * XC, bytes_accessed=14 * 2**20, transcendentals=rows * G * N
        ),
        name="resp_state",
    )(scale, u, tail, wb, dy, decay_in)


def response_mid(base, count, length, u, tail, wb, c_act, dy, step, cum, cum4, cum_t4, skip):
    rows = u.shape[0]
    half = rows // 2
    x_at = lambda g: (0, base + g)
    b_at = lambda g: (0, XC // N + base + g)
    out_at = lambda g: (0, g)
    v = pltpu.VMEM
    return pl.pallas_call(
        functools.partial(resp_mid_kernel, base),
        grid=(count,),
        in_specs=[
            SMEM,
            pl.BlockSpec((rows, GX), x_at),
            pl.BlockSpec((rows, N), b_at),
            pl.BlockSpec((PAD, GX), x_at),
            pl.BlockSpec((PAD, N), b_at),
            pl.BlockSpec((PAD, GX), x_at),
            pl.BlockSpec((PAD, N), b_at),
            pl.BlockSpec((rows, N), x_at),
            pl.BlockSpec((rows, GX), x_at),
            whole((rows, H)),
            whole((rows, H)),
            pl.BlockSpec((1, rows, HG), lambda g: (base + g, 0, 0)),
            pl.BlockSpec((1, HG, rows), lambda g: (base + g, 0, 0)),
            pl.BlockSpec((1, GX), x_at),
        ],
        out_specs=[
            pl.BlockSpec((PAD, GX), out_at),
            pl.BlockSpec((PAD, N), out_at),
            pl.BlockSpec((rows, N), out_at),
            whole((rows, H)),
            whole((rows, H)),
        ],
        out_shape=(
            sds((PAD, count * GX), f32),
            sds((PAD, count * N), f32),
            sds((rows, count * N), f32),
            sds((rows, H), f32),
            sds((rows, H), f32),
        ),
        scratch_shapes=[
            v((PAD + rows, GX), f32),
            v((PAD + rows, N), f32),
            v((rows, GX), bf16),
            v((rows, GX), bf16),
            v((rows, N), bf16),
            v((rows, GX), bf16),
            v((rows, GX), f32),
            v((rows, N), f32),
            v((rows, GX), f32),
            v((rows, GX), f32),
            v((rows, GX), f32),
            v((half, GX), bf16),
            v((half, GX), bf16),
            v((half, GX), f32),
            v((half, GX), f32),
            v((half, GX), f32),
            v((rows, GX), bf16),
            v((rows, GX), bf16),
        ],
        compiler_params=params("arbitrary"),
        cost_estimate=pl.CostEstimate(
            flops=count * 8 * 2**30, bytes_accessed=count * 3 * 2**20, transcendentals=rows * half * H
        ),
        name="resp_mid",
    )(length, u, u, tail, tail, wb, wb, c_act, dy, step, cum, cum4, cum_t4, skip)


def response_end(u, tail, wb, c_act, weighted, start, dc, rows_in, cols_in, step, dt, hp):
    rows = u.shape[0]
    n, _, width = start.shape
    per = n // G
    c_at = lambda g: (0, XC // N + G + g)
    g_at = lambda g: (0, g)
    v = pltpu.VMEM
    return pl.pallas_call(
        resp_end_kernel,
        grid=(G,),
        in_specs=[
            pl.BlockSpec((rows, N), c_at),
            pl.BlockSpec((PAD, N), c_at),
            pl.BlockSpec((PAD, N), c_at),
            pl.BlockSpec((rows, N), g_at),
            pl.BlockSpec((rows, GX), g_at),
            pl.BlockSpec((per, N, width), lambda g: (g, 0, 0)),
            pl.BlockSpec((rows, N), g_at),
            whole((rows, H)),
            whole((rows, H)),
            whole((rows, H)),
            whole((rows, H)),
            whole((rows, H)),
            whole((rows, H)),
            whole((PAD, H)),
        ],
        out_specs=[pl.BlockSpec((PAD, N), g_at), whole((PAD, H))],
        out_shape=(sds((PAD, G * N), f32), sds((PAD, H), f32)),
        scratch_shapes=[
            v((PAD + rows, N), f32),
            v((rows, N), bf16),
            v((rows, N), f32),
            v((rows, H), f32),
        ],
        compiler_params=params("arbitrary"),
        cost_estimate=pl.CostEstimate(
            flops=4 * rows * N * XC, bytes_accessed=12 * 2**20, transcendentals=rows * G * N
        ),
        name="resp_end",
    )(u, tail, wb, c_act, weighted, start, dc, *rows_in, *cols_in, step, dt, hp)


def prompt_state(v, masks, wb, hp, earlier_out, width):
    rows = v.shape[0]
    s = pltpu.VMEM
    return pl.pallas_call(
        prompt_state_kernel,
        in_specs=[pl.BlockSpec()] * 4 + [pl.BlockSpec(memory_space=pl.ANY)],
        out_shape=(sds((N, width), bf16), sds((rows, LANES), f32), sds((rows, LANES), f32)),
        scratch_shapes=[
            s((PAD + RB, width + N), f32),
            s((RB, width + N), bf16),
            s((N, width), f32),
        ],
        compiler_params=params(),
        cost_estimate=pl.CostEstimate(
            flops=2 * rows * N * width, bytes_accessed=4 * 2**20, transcendentals=rows * width
        ),
        name="prompt_state",
    )(v, masks, wb, hp, earlier_out)


def prompt_grad(v, masks, wb, hp, weight, step, states):
    rows = v.shape[0]
    width = states.shape[2]
    s = pltpu.VMEM
    return pl.pallas_call(
        prompt_grad_kernel,
        out_shape=(sds((PAD, width + N), f32), sds((PAD, LANES), f32)),
        scratch_shapes=[
            s((PAD + RB, width + N), f32),
            s((RB, width + N), bf16),
            s((RB, width + N), f32),
            s((N, width), bf16),
            s((RB, width + N), f32),
            s((PAD, width + N), f32),
        ],
        compiler_params=params(),
        cost_estimate=pl.CostEstimate(
            flops=4 * rows * N * width, bytes_accessed=8 * 2**20, transcendentals=rows * width
        ),
        name="prompt_grad",
    )(v, masks, wb, hp, weight, step, states)


def doc_number(starts, positions):
    return jnp.sum((starts[None, :] <= positions[:, None]).astype(jnp.int32), axis=1)


def prompt_masks(starts, rows):
    positions = jnp.arange(rows, dtype=jnp.int32)
    docs = doc_number(starts, positions)
    same = [doc_number(starts, positions - (K - 1 - k)) == docs for k in range(K - 1)]
    columns = jnp.stack(same + [docs == docs[rows - 1]], axis=1).astype(f32)
    return jnp.pad(columns, ((0, 0), (0, PAD - K)))


def pad_rows(a):
    return jnp.pad(a, ((0, PAD - a.shape[0]), (0, 0)))


def sum_over_all(flat):
    axes = ("group", "resp")
    devices = lax.axis_size(axes)
    rows = -(-flat.size // (devices * LANES))
    flat = jnp.pad(flat, (0, devices * rows * LANES - flat.size)).reshape(devices, rows, LANES)
    mine = jnp.sum(lax.all_to_all(flat, axes, 0, 0), axis=0)
    return lax.all_gather(mine, axes).reshape(-1)


def shards(
    prompt_in, prompt_dt, doc_starts, resp_in, resp_dt, resp_len, upstream, reward,
    conv_w, conv_b, head_params,
):
    n = lax.axis_size("resp")
    me = lax.axis_index("resp")
    hs = H // n
    width = XC // n
    per = n // G
    block = prompt_in.shape[1]
    slots = resp_in.shape[2]
    rows_in, dt_in = prompt_in[0], prompt_dt[0]
    u, dt, dy = resp_in[0, 0], resp_dt[0, 0], upstream[0, 0]

    r = reward[0, 0]
    r_hi = r.astype(bf16)
    r_mid = (r - r_hi.astype(f32)).astype(bf16)
    r_lo = (r - r_hi.astype(f32) - r_mid.astype(f32)).astype(bf16)
    tail_size = (K - 1) * rows_in.shape[1] // LANES
    small = jnp.concatenate(
        [
            rows_in[block - K + 1 :].reshape(tail_size, LANES),
            jnp.broadcast_to(jnp.stack([r_hi, r_mid, r_lo, jnp.zeros_like(r_lo)])[:, None], (4, LANES)),
            jnp.zeros((12, LANES), bf16),
        ]
    )
    small = lax.all_gather(small, "resp")
    wb = pad_rows(jnp.concatenate([conv_w, conv_b[None]], axis=0))
    hp = pad_rows(head_params)

    x_parts = rows_in[:, :XC].reshape(block, n, width).transpose(1, 0, 2)
    b_parts = jnp.repeat(
        rows_in[:, XC : XC + G * N].reshape(block, G, N).transpose(1, 0, 2), per, axis=0
    )
    dt_parts = jnp.pad(
        dt_in.reshape(block, n, hs).transpose(1, 0, 2), ((0, 0), (0, 0), (0, LANES - hs))
    )
    parts = jnp.concatenate([x_parts, b_parts, dt_parts], axis=2)
    parts, small = lax.optimization_barrier((parts, small))
    v = lax.all_to_all(parts, "resp", 0, 0).reshape(n * block, width + N + LANES)
    tail_rows = small[n - 1, :tail_size].reshape(K - 1, -1).astype(f32)
    tail = jnp.pad(tail_rows, ((PAD - K + 1, 0), (0, 0)))
    rewards = jnp.sum(small[:, tail_size : tail_size + 3, 0].astype(f32), axis=1)
    scale = (r - jnp.sum(rewards) / n) / slots
    masks = prompt_masks(doc_starts[0], n * block)
    my_group = me // per
    wb_mine = jnp.concatenate(
        [
            lax.dynamic_slice(wb, (0, me * width), (PAD, width)),
            lax.dynamic_slice(wb, (0, XC + my_group * N), (PAD, N)),
        ],
        axis=1,
    )
    hp_mine = jnp.pad(lax.dynamic_slice(hp, (0, me * hs), (PAD, hs)), ((0, 0), (0, LANES - hs)))

    length = resp_len.astype(jnp.int32)
    step, cum, cum_t, decay_in = response_steps(length, dt, hp)
    d_states, weighted, c_act = response_state(
        n, scale.reshape(1, 1), u, tail, wb, dy, decay_in
    )
    d_states = lax.all_to_all(d_states, "resp", 0, 0)

    cum4 = cum.reshape(slots, G, HG).transpose(1, 0, 2)
    skip = jnp.repeat(head_params[2], PS)[None, :]

    def mid(base, count):
        return response_mid(
            base, count, length, u, tail, wb, c_act, dy, step, cum, cum4,
            cum_t.reshape(G, HG, slots), skip,
        )

    first = mid(0, G // 2)
    start_mine, weight, p_step = prompt_state(v, masks, wb_mine, hp_mine, first[1], width)
    start = lax.all_gather(start_mine, "resp")
    second = mid(G // 2, G - G // 2)
    grad_x, grad_b, dc = (jnp.concatenate(ab, axis=1) for ab in zip(first[:3], second[:3]))
    rows_in, cols_in = zip(first[3:], second[3:])
    p_grad, p_heads = prompt_grad(v, masks, wb_mine, hp_mine, weight, p_step, d_states)
    grad_c, r_heads = response_end(
        u, tail, wb, c_act, weighted, start, dc, rows_in, cols_in, step, dt, hp
    )

    conv = jnp.concatenate([grad_x, grad_b, grad_c], axis=1)[: K + 1] * scale
    mine = lax.dynamic_slice(conv, (0, me * width), (K + 1, width)) + p_grad[: K + 1, :width]
    conv = lax.dynamic_update_slice(conv, mine, (0, me * width))
    at_b = XC + my_group * N
    mine = lax.dynamic_slice(conv, (0, at_b), (K + 1, N)) + p_grad[: K + 1, width:]
    conv = lax.dynamic_update_slice(conv, mine, (0, at_b))
    d_skip = jnp.sum(grad_x[K + 1].reshape(H, PS), axis=1)
    heads = jnp.concatenate([r_heads[:2], d_skip[None]], axis=0) * scale
    mine = lax.dynamic_slice(heads, (0, me * hs), (2, hs)) + p_heads[:2, :hs]
    heads = lax.dynamic_update_slice(heads, mine, (0, me * hs))
    flat = sum_over_all(jnp.concatenate([conv.reshape(-1), heads.reshape(-1)]))
    at_heads = conv.size
    conv = flat[:at_heads].reshape(conv.shape)
    return conv[:K], conv[K], flat[at_heads : at_heads + heads.size].reshape(heads.shape)


def solution(mesh):
    in_specs = (
        P("group", "resp", None),
        P("group", "resp", None),
        P("group", None),
        P("group", "resp", None, None),
        P("group", "resp", None, None),
        P("group", "resp"),
        P("group", "resp", None, None),
        P("group", "resp"),
        P(),
        P(),
        P(),
    )
    out_specs = (P(), P(), P())
    return jax.shard_map(shards, mesh=mesh, in_specs=in_specs, out_specs=out_specs, check_vma=False)
```

```python
import functools

import jax
import jax.numpy as jnp
from jax import lax
from jax.experimental import pallas as pl
from jax.experimental.pallas import tpu as pltpu
from jax.sharding import PartitionSpec as P

H = 128
PS = 64
N = 256
G = 4
K = 4
HG = H // G
XC = H * PS
GX = HG * PS
LANES = 128
PAD = 8
VMEM_LIMIT = 50 * 2**20

f32 = jnp.float32
bf16 = jnp.bfloat16

NN = (((1,), (0,)), ((), ()))
NT = (((1,), (1,)), ((), ()))


def dot(a, b, dims=NN, precision=None):
    return lax.dot_general(a, b, dims, precision=precision, preferred_element_type=f32)


def halves(v):
    hi = v.astype(bf16)
    return hi, (v - hi.astype(f32)).astype(bf16)


def indicator(first, width):
    row = lax.broadcasted_iota(jnp.int32, (LANES, width), 0)
    head = lax.shift_right_logical(lax.broadcasted_iota(jnp.int32, (LANES, width), 1), 6)
    return jnp.where(row - first == head, 1.0, 0.0).astype(bf16)


def expand(v, ind):
    hi, lo = halves(v)
    return dot(hi, ind) + dot(lo, ind)


def head_sums(z_hi, z_lo, ind):
    return dot(z_hi, ind, NT) + dot(z_lo, ind, NT)


def triangle(n, keep):
    i = lax.broadcasted_iota(jnp.int32, (n, n), 0)
    j = lax.broadcasted_iota(jnp.int32, (n, n), 1)
    return jnp.where(keep(i, j), 1.0, 0.0).astype(f32)


def tri_sum(tri, v):
    return dot(tri, v, precision=lax.Precision.HIGHEST)


def softplus(z):
    return jnp.maximum(z, 0.0) + jnp.log1p(jnp.exp(-jnp.abs(z)))


def sigmoid(z):
    return 0.5 * jnp.tanh(0.5 * z) + 0.5


def taps_of(ext, lanes, row, rows):
    return [ext[pl.ds(PAD - K + 1 + k + row, rows), lanes] for k in range(K)]


def conv_pre(taps, wb, masks=None):
    total = wb[K : K + 1] + wb[K - 1 : K] * taps[K - 1]
    for k in range(K - 1):
        term = wb[k : k + 1] * taps[k]
        if masks is not None:
            term = term * masks[k]
        total = total + term
    return total


def act_and_slope(pre):
    sig = sigmoid(pre)
    act = pre * sig
    return act, sig + act * (1.0 - sig)


def fold8(v):
    return jnp.sum(v.reshape(v.shape[0] // 8, 8, v.shape[1]), axis=0)


def lane_loop(width, body, step=LANES):
    def one(i, _):
        body(pl.ds(pl.multiple_of(i * step, step), step))
        return 0

    lax.fori_loop(0, width // step, one, 0)


RC = 64


def conv_forward(u, tail, wb, ext, act, slope, rows, width):
    def body(lanes):
        ext[0:PAD, lanes] = tail[:, lanes]
        ext[PAD : PAD + rows, lanes] = u[:, lanes].astype(f32)
        w = wb[:, lanes]
        for r in range(0, rows, RC):
            a, s = act_and_slope(conv_pre(taps_of(ext, lanes, r, RC), w))
            act[r : r + RC, lanes] = a.astype(bf16)
            if slope is not None:
                slope[r : r + RC, lanes] = s

    lane_loop(width, body)


def conv_backward(ext, slope, lanes, cotangent, grad, rows):
    sums = [jnp.zeros((8, LANES), f32) for _ in range(K + 1)]
    for r in range(0, rows, RC):
        d = cotangent(r) * slope[r : r + RC, lanes]
        taps = taps_of(ext, lanes, r, RC)
        for k in range(K):
            sums[k] = sums[k] + fold8(d * taps[k])
        sums[K] = sums[K] + fold8(d)
    for k in range(K + 1):
        grad[k : k + 1, lanes] = jnp.sum(sums[k], axis=0, keepdims=True)


def steps_kernel(len_ref, dt, hp, step, cum, cum_t, decay_in):
    rows = dt.shape[0]
    s = softplus(dt[...].astype(f32) + hp[1:2])
    logd = -jnp.exp(hp[0:1]) * s
    c = tri_sum(triangle(rows, lambda i, j: i >= j), logd)
    step[...] = s
    cum[...] = c
    cum_t[...] = c.T
    t = lax.broadcasted_iota(jnp.int32, c.shape, 0)
    decay_in[...] = jnp.where(t < len_ref[0, 0], jnp.exp(c), 0.0)


def resp_state_kernel(
    per, side, adv, u_c, tail_c, wb_c, dy, decay_in, kept, sent, weighted, c_out, ext, c_t
):
    slab = pl.program_id(0)
    rows, width = dy.shape

    @pl.when(slab % per == 0)
    def _():
        conv_forward(u_c, tail_c, wb_c, ext, c_out, None, rows, N)
        c_t[...] = c_out[...].astype(f32).T.astype(bf16)

    ind = indicator(slab * (width // PS), width)
    a = (dy[...].astype(f32) * expand(decay_in[...], ind)).astype(bf16)
    weighted[...] = a
    state = (dot(c_t[...], a) * adv[0, 0]).astype(bf16)

    @pl.when(slab % 2 == side[0, 0])
    def _():
        kept[0] = state

    @pl.when(slab % 2 != side[0, 0])
    def _():
        sent[0] = state


def resp_mid_kernel(
    base, len_ref, u_x, u_b, tail_x, tail_b, wb_x, wb_b, c_act, dy, step, cum, cum4, cum_t4, skip,
    grad_x, grad_b, dc, row_out, col_out,
    ext, ext_b, x_s, xs_s, b_s, dym, slope, slope_b, step_e, y_s, t_s,
    a1, bm, sw_e, u_off, y_off, z_hi, z_lo,
):
    step_no = pl.program_id(0)
    g = step_no + base
    rows = u_x.shape[0]
    half = rows // 2
    conv_forward(u_x, tail_x, wb_x, ext, x_s, slope, rows, GX)
    conv_forward(u_b, tail_b, wb_b, ext_b, b_s, slope_b, rows, N)
    ind = indicator(g * HG, GX)
    step_e[...] = expand(step[...], ind)
    cum_v = cum[...]
    mid = cum_v[half - 1 : half]
    sw_e[...] = expand(jnp.exp(mid - cum_v[:half]) * step[:half], ind)
    y_off[...] = expand(jnp.exp(cum_v[half:] - mid), ind)
    live = jnp.where(lax.broadcasted_iota(jnp.int32, (rows, LANES), 0) < len_ref[0, 0], 1.0, 0.0)

    def prepare(lanes):
        d = dy[:, lanes].astype(f32) * live
        dym[:, lanes] = d.astype(bf16)
        x = x_s[:, lanes].astype(f32)
        xs_s[:, lanes] = (x * step_e[:, lanes]).astype(bf16)
        bm[:, lanes] = (x[:half] * sw_e[:, lanes]).astype(bf16)
        a1[:, lanes] = (d[half:] * y_off[:, lanes]).astype(bf16)

    lane_loop(GX, prepare)

    c_v, b_v = c_act[...], b_s[...]
    c0, c1, b0, b1 = c_v[:half], c_v[half:], b_v[:half], b_v[half:]
    i = lax.broadcasted_iota(jnp.int32, (half, half), 0)
    j = lax.broadcasted_iota(jnp.int32, (half, half), 1)
    lane = lax.broadcasted_iota(jnp.int32, (half, LANES), 1)
    first = jnp.where(lane < PS, 1.0, 0.0).astype(bf16)
    second = jnp.where(lane >= PS, 1.0, 0.0).astype(bf16)

    y_off[...] = dot(dot(c1, b0, NT).astype(bf16), bm[...])
    u_off[...] = dot(dot(b0, c1, NT).astype(bf16), a1[...])
    d10 = dot(a1[...], bm[...], NT)

    d_diag = []
    for q, (c_q, b_q) in enumerate(((c0, b0), (c1, b1))):
        r = slice(q * half, (q + 1) * half)
        lower = jnp.where(i >= j, dot(c_q, b_q, NT), 0.0)
        upper = jnp.where(j >= i, dot(b_q, c_q, NT), 0.0)
        d_sc = jnp.zeros((half, half), f32)
        for p in range(HG // 2):
            lanes = slice(p * LANES, (p + 1) * LANES)
            xs_p, dy_p = xs_s[r, lanes], dym[r, lanes]
            xb = jnp.concatenate([xs_p * first, xs_p * second], axis=0)
            dyb = jnp.concatenate([dy_p * first, dy_p * second], axis=0)
            d_m = dot(dy_p, xb, NT)
            mats, mats_t = [], []
            for a in range(2):
                h = 2 * p + a
                gap = jnp.exp(-jnp.abs(cum4[0, r, h : h + 1] - cum_t4[0, h : h + 1, r]))
                d_sc = d_sc + d_m[:, a * half : (a + 1) * half] * gap
                mats.append((gap * lower).astype(bf16))
                mats_t.append((gap * upper).astype(bf16))
            y_s[r, lanes] = dot(jnp.concatenate(mats, axis=1), xb)
            t_s[r, lanes] = dot(jnp.concatenate(mats_t, axis=1), dyb)
        d_diag.append(jnp.where(i >= j, d_sc, 0.0))

    d00, d11 = d_diag
    dc[:half] = dot(d00.astype(bf16), b0)
    dc[half:] = dot(d11.astype(bf16), b1) + dot(d10.astype(bf16), b0)
    db0 = dot(d00.T.astype(bf16), c0) + dot(d10.T.astype(bf16), c1)
    db1 = dot(d11.T.astype(bf16), c1)
    db = jnp.concatenate([db0, db1], axis=0)
    for k in range(N // LANES):
        lanes = slice(k * LANES, (k + 1) * LANES)
        conv_backward(ext_b, slope_b, lanes, lambda r: db[r : r + RC, lanes], grad_b, rows)

    def put(z, r, lanes):
        hi, lo = halves(z)
        z_hi[r : r + RC, lanes] = hi
        z_lo[r : r + RC, lanes] = lo

    def row_products(lanes):
        for r in range(0, rows, RC):
            z = dym[r : r + RC, lanes].astype(f32) * y_s[r : r + RC, lanes]
            if r >= half:
                o = r - half
                z = z + a1[o : o + RC, lanes].astype(f32) * y_off[o : o + RC, lanes]
            put(z, r, lanes)

    lane_loop(GX, row_products)
    row_sum = head_sums(z_hi[...], z_lo[...], ind)

    def finish(lanes):
        d_skip = jnp.zeros((8, LANES), f32)
        for r in range(0, rows, RC):
            t = t_s[r : r + RC, lanes]
            z = xs_s[r : r + RC, lanes].astype(f32) * t
            if r < half:
                z = z + bm[r : r + RC, lanes].astype(f32) * u_off[r : r + RC, lanes]
            put(z, r, lanes)
            d_skip = d_skip + fold8(
                dym[r : r + RC, lanes].astype(f32) * x_s[r : r + RC, lanes].astype(f32)
            )

        def cotangent(r):
            d = step_e[r : r + RC, lanes] * t_s[r : r + RC, lanes]
            d = d + skip[:, lanes] * dym[r : r + RC, lanes].astype(f32)
            if r < half:
                d = d + sw_e[r : r + RC, lanes] * u_off[r : r + RC, lanes]
            return d

        conv_backward(ext, slope, lanes, cotangent, grad_x, rows)
        grad_x[K + 1 : K + 2, lanes] = jnp.sum(d_skip, axis=0, keepdims=True)

    lane_loop(GX, finish)
    col_sum = head_sums(z_hi[...], z_lo[...], ind)

    @pl.when(step_no == 0)
    def _():
        row_out[...] = row_sum
        col_out[...] = col_sum

    @pl.when(step_no > 0)
    def _():
        row_out[...] += row_sum
        col_out[...] += col_sum


def resp_end_kernel(
    u_c, tail_c, wb_c, c_act, weighted, start, dc, row_a, row_b, col_a, col_b, step, dt, hp,
    grad_c, grad_h, ext, c_s, slope, total,
):
    g = pl.program_id(0)
    rows = u_c.shape[0]
    per, _, width = start.shape
    conv_forward(u_c, tail_c, wb_c, ext, c_s, slope, rows, N)
    d = dc[...]

    @pl.when(g == 0)
    def _():
        total[...] = (row_a[...] + row_b[...]) - (col_a[...] + col_b[...])

    for s in range(per):
        a = weighted[:, s * width : (s + 1) * width]
        st = start[s]
        z_hi, z_lo = halves(a.astype(f32) * dot(c_act[...], st))
        total[...] += head_sums(z_hi, z_lo, indicator(g * HG + s * (width // PS), width))
        d = d + dot(a, st, NT)
    for k in range(N // LANES):
        lanes = slice(k * LANES, (k + 1) * LANES)
        conv_backward(ext, slope, lanes, lambda r: d[r : r + RC, lanes], grad_c, rows)

    @pl.when(g == pl.num_programs(0) - 1)
    def _():
        d_log = tri_sum(triangle(rows, lambda i, j: j >= i), total[...])
        rate = -jnp.exp(hp[0:1])
        s = step[...]
        d_step = (col_a[...] + col_b[...]) / s + rate * d_log
        grad_h[...] = jnp.zeros_like(grad_h)
        grad_h[0:1] = jnp.sum(d_log * rate * s, axis=0, keepdims=True)
        grad_h[1:2] = jnp.sum(
            d_step * sigmoid(dt[...].astype(f32) + hp[1:2]), axis=0, keepdims=True
        )


RB = 256


def prompt_conv(v, masks, wb, ext, act, slope, row, width):
    def body(lanes):
        ext[PAD : PAD + RB, lanes] = v[pl.ds(row, RB), lanes].astype(f32)
        w = wb[:, lanes]
        for r in range(0, RB, RC):
            m = [masks[pl.ds(row + r, RC), k : k + 1] for k in range(K - 1)]
            a, s = act_and_slope(conv_pre(taps_of(ext, lanes, r, RC), w, m))
            act[r : r + RC, lanes] = a.astype(bf16)
            if slope is not None:
                slope[r : r + RC, lanes] = s

    lane_loop(width, body)


def prompt_state_kernel(v, masks, wb, hp, earlier_out, start, weight, step, ext, act, acc):
    rows = v.shape[0]
    width = start.shape[1]
    ind = indicator(0, width)
    later = triangle(RB, lambda i, j: j > i)
    ahead = jnp.zeros((1, LANES), f32)
    acc[...] = jnp.zeros_like(acc)
    for row in range(rows - RB, -1, -RB):
        s = softplus(v[row : row + RB, width + N :].astype(f32) + hp[1:2])
        logd = -jnp.exp(hp[0:1]) * s
        after = tri_sum(later, logd) + ahead
        ahead = ahead + jnp.sum(logd, axis=0, keepdims=True)
        w = masks[row : row + RB, K - 1 : K] * jnp.exp(after) * s
        step[row : row + RB] = s
        weight[row : row + RB] = w
        if row:
            ext[0:PAD] = v[row - 16 : row, : width + N].astype(f32)[16 - PAD :]
        else:
            ext[0:PAD] = jnp.zeros((PAD, width + N), f32)
        prompt_conv(v, masks, wb, ext, act, None, row, width + N)
        wx = (act[:, :width].astype(f32) * expand(w, ind)).astype(bf16)
        acc[...] += dot(act[:, width:].astype(f32).T.astype(bf16), wx)
    start[...] = acc[...].astype(bf16)


def prompt_grad_kernel(
    v, masks, wb, hp, weight, step, states,
    grad, grad_h, ext, act, slope, g_s, d_s, sums,
):
    rows = v.shape[0]
    width = states.shape[2]
    ind = indicator(0, width)
    earlier = triangle(RB, lambda i, j: j < i)
    total = states[0].astype(f32)
    for k in range(1, states.shape[0]):
        total = total + states[k].astype(f32)
    g_s[...] = total.astype(bf16)
    behind = jnp.zeros((1, LANES), f32)
    rate = -jnp.exp(hp[0:1])
    d_rate = jnp.zeros((1, LANES), f32)
    d_bias = jnp.zeros((1, LANES), f32)
    sums[...] = jnp.zeros_like(sums)
    for row in range(0, rows, RB):
        if row:
            ext[0:PAD] = v[row - 16 : row, : width + N].astype(f32)[16 - PAD :]
        else:
            ext[0:PAD] = jnp.zeros((PAD, width + N), f32)
        prompt_conv(v, masks, wb, ext, act, slope, row, width + N)
        w_e = expand(weight[row : row + RB], ind)
        t = dot(act[:, width:], g_s[...])
        wx = (act[:, :width].astype(f32) * w_e).astype(bf16)
        d_s[:, :width] = t * w_e
        d_s[:, width:] = dot(wx, g_s[...], NT)
        z_hi, z_lo = halves(wx.astype(f32) * t)
        q = head_sums(z_hi, z_lo, ind)
        d_log = tri_sum(earlier, q) + behind
        behind = behind + jnp.sum(q, axis=0, keepdims=True)
        s = step[row : row + RB]
        d_step = q / s + rate * d_log
        z = v[row : row + RB, width + N :].astype(f32) + hp[1:2]
        d_rate = d_rate + jnp.sum(d_log * rate * s, axis=0, keepdims=True)
        d_bias = d_bias + jnp.sum(d_step * sigmoid(z), axis=0, keepdims=True)

        def back(lanes):
            acc = [jnp.zeros((8, LANES), f32) for _ in range(K + 1)]
            for r in range(0, RB, RC):
                d = d_s[r : r + RC, lanes] * slope[r : r + RC, lanes]
                taps = taps_of(ext, lanes, r, RC)
                for k in range(K):
                    part = d * taps[k]
                    if k < K - 1:
                        part = part * masks[pl.ds(row + r, RC), k : k + 1]
                    acc[k] = acc[k] + fold8(part)
                acc[K] = acc[K] + fold8(d)
            for k in range(K + 1):
                sums[k : k + 1, lanes] += jnp.sum(acc[k], axis=0, keepdims=True)

        lane_loop(width + N, back)
    grad[...] = sums[...]
    grad_h[...] = jnp.zeros_like(grad_h)
    grad_h[0:1] = d_rate
    grad_h[1:2] = d_bias


def add_kernel(a, b, earlier_out, out):
    out[...] = (a[...].astype(f32) + b[...].astype(f32)).astype(bf16)


def params(*semantics):
    return pltpu.CompilerParams(vmem_limit_bytes=VMEM_LIMIT, dimension_semantics=semantics or None)


SMEM = pl.BlockSpec(memory_space=pltpu.SMEM)


def whole(shape):
    return pl.BlockSpec(shape, lambda *_: (0,) * len(shape))


def sds(shape, dtype):
    return jax.ShapeDtypeStruct(shape, dtype)


def response_steps(length, dt, hp):
    rows = dt.shape[0]
    square = sds((rows, H), f32)
    return pl.pallas_call(
        steps_kernel,
        out_shape=(square, square, sds((H, rows), f32), square),
        in_specs=[SMEM, pl.BlockSpec(), pl.BlockSpec()],
        compiler_params=params(),
        name="resp_steps",
    )(length, dt, hp)


def response_state(n, side, scale, u, tail, wb, dy, decay_in):
    rows = u.shape[0]
    per = n // G
    width = XC // n
    c_at = lambda i: (0, XC // N + G + i // per)
    return pl.pallas_call(
        functools.partial(resp_state_kernel, per),
        grid=(n,),
        in_specs=[
            SMEM,
            SMEM,
            pl.BlockSpec((rows, N), c_at),
            pl.BlockSpec((PAD, N), c_at),
            pl.BlockSpec((PAD, N), c_at),
            pl.BlockSpec((rows, width), lambda i: (0, i)),
            whole((rows, H)),
        ],
        out_specs=[
            pl.BlockSpec((1, N, width), lambda i: (i // 2, 0, 0)),
            pl.BlockSpec((1, N, width), lambda i: (i // 2, 0, 0)),
            pl.BlockSpec((rows, width), lambda i: (0, i)),
            pl.BlockSpec((rows, N), lambda i: (0, i // per)),
        ],
        out_shape=(
            sds((n // 2, N, width), bf16),
            sds((n // 2, N, width), bf16),
            sds((rows, XC), bf16),
            sds((rows, G * N), bf16),
        ),
        scratch_shapes=[pltpu.VMEM((PAD + rows, N), f32), pltpu.VMEM((N, rows), bf16)],
        compiler_params=params("arbitrary"),
        cost_estimate=pl.CostEstimate(
            flops=2 * rows * N * XC, bytes_accessed=14 * 2**20, transcendentals=rows * G * N
        ),
        name="resp_state",
    )(side, scale, u, tail, wb, dy, decay_in)


def response_mid(base, count, length, u, tail, wb, c_act, dy, step, cum, cum4, cum_t4, skip):
    rows = u.shape[0]
    half = rows // 2
    x_at = lambda g: (0, base + g)
    b_at = lambda g: (0, XC // N + base + g)
    out_at = lambda g: (0, g)
    v = pltpu.VMEM
    return pl.pallas_call(
        functools.partial(resp_mid_kernel, base),
        grid=(count,),
        in_specs=[
            SMEM,
            pl.BlockSpec((rows, GX), x_at),
            pl.BlockSpec((rows, N), b_at),
            pl.BlockSpec((PAD, GX), x_at),
            pl.BlockSpec((PAD, N), b_at),
            pl.BlockSpec((PAD, GX), x_at),
            pl.BlockSpec((PAD, N), b_at),
            pl.BlockSpec((rows, N), x_at),
            pl.BlockSpec((rows, GX), x_at),
            whole((rows, H)),
            whole((rows, H)),
            pl.BlockSpec((1, rows, HG), lambda g: (base + g, 0, 0)),
            pl.BlockSpec((1, HG, rows), lambda g: (base + g, 0, 0)),
            pl.BlockSpec((1, GX), x_at),
        ],
        out_specs=[
            pl.BlockSpec((PAD, GX), out_at),
            pl.BlockSpec((PAD, N), out_at),
            pl.BlockSpec((rows, N), out_at),
            whole((rows, H)),
            whole((rows, H)),
        ],
        out_shape=(
            sds((PAD, count * GX), f32),
            sds((PAD, count * N), f32),
            sds((rows, count * N), f32),
            sds((rows, H), f32),
            sds((rows, H), f32),
        ),
        scratch_shapes=[
            v((PAD + rows, GX), f32),
            v((PAD + rows, N), f32),
            v((rows, GX), bf16),
            v((rows, GX), bf16),
            v((rows, N), bf16),
            v((rows, GX), bf16),
            v((rows, GX), f32),
            v((rows, N), f32),
            v((rows, GX), f32),
            v((rows, GX), f32),
            v((rows, GX), f32),
            v((half, GX), bf16),
            v((half, GX), bf16),
            v((half, GX), f32),
            v((half, GX), f32),
            v((half, GX), f32),
            v((rows, GX), bf16),
            v((rows, GX), bf16),
        ],
        compiler_params=params("arbitrary"),
        cost_estimate=pl.CostEstimate(
            flops=count * 8 * 2**30, bytes_accessed=count * 3 * 2**20, transcendentals=rows * half * H
        ),
        name="resp_mid",
    )(length, u, u, tail, tail, wb, wb, c_act, dy, step, cum, cum4, cum_t4, skip)


def response_end(u, tail, wb, c_act, weighted, start, dc, rows_in, cols_in, step, dt, hp):
    rows = u.shape[0]
    n, _, width = start.shape
    per = n // G
    c_at = lambda g: (0, XC // N + G + g)
    g_at = lambda g: (0, g)
    v = pltpu.VMEM
    return pl.pallas_call(
        resp_end_kernel,
        grid=(G,),
        in_specs=[
            pl.BlockSpec((rows, N), c_at),
            pl.BlockSpec((PAD, N), c_at),
            pl.BlockSpec((PAD, N), c_at),
            pl.BlockSpec((rows, N), g_at),
            pl.BlockSpec((rows, GX), g_at),
            pl.BlockSpec((per, N, width), lambda g: (g, 0, 0)),
            pl.BlockSpec((rows, N), g_at),
            whole((rows, H)),
            whole((rows, H)),
            whole((rows, H)),
            whole((rows, H)),
            whole((rows, H)),
            whole((rows, H)),
            whole((PAD, H)),
        ],
        out_specs=[pl.BlockSpec((PAD, N), g_at), whole((PAD, H))],
        out_shape=(sds((PAD, G * N), f32), sds((PAD, H), f32)),
        scratch_shapes=[
            v((PAD + rows, N), f32),
            v((rows, N), bf16),
            v((rows, N), f32),
            v((rows, H), f32),
        ],
        compiler_params=params("arbitrary"),
        cost_estimate=pl.CostEstimate(
            flops=4 * rows * N * XC, bytes_accessed=12 * 2**20, transcendentals=rows * G * N
        ),
        name="resp_end",
    )(u, tail, wb, c_act, weighted, start, dc, *rows_in, *cols_in, step, dt, hp)


def add_pairs(a, b, earlier_out):
    block = pl.BlockSpec((1,) + a.shape[1:], lambda i: (i, 0, 0))
    return pl.pallas_call(
        add_kernel,
        grid=(a.shape[0],),
        in_specs=[block, block, pl.BlockSpec(memory_space=pl.ANY)],
        out_specs=block,
        out_shape=sds(a.shape, bf16),
        compiler_params=params("arbitrary"),
        cost_estimate=pl.CostEstimate(flops=a.size, bytes_accessed=6 * a.size, transcendentals=0),
        name="add_pairs",
    )(a, b, earlier_out)


def prompt_state(v, masks, wb, hp, earlier_out, width):
    rows = v.shape[0]
    s = pltpu.VMEM
    return pl.pallas_call(
        prompt_state_kernel,
        in_specs=[pl.BlockSpec()] * 4 + [pl.BlockSpec(memory_space=pl.ANY)],
        out_shape=(sds((N, width), bf16), sds((rows, LANES), f32), sds((rows, LANES), f32)),
        scratch_shapes=[
            s((PAD + RB, width + N), f32),
            s((RB, width + N), bf16),
            s((N, width), f32),
        ],
        compiler_params=params(),
        cost_estimate=pl.CostEstimate(
            flops=2 * rows * N * width, bytes_accessed=4 * 2**20, transcendentals=rows * width
        ),
        name="prompt_state",
    )(v, masks, wb, hp, earlier_out)


def prompt_grad(v, masks, wb, hp, weight, step, states):
    rows = v.shape[0]
    width = states.shape[2]
    s = pltpu.VMEM
    return pl.pallas_call(
        prompt_grad_kernel,
        out_shape=(sds((PAD, width + N), f32), sds((PAD, LANES), f32)),
        scratch_shapes=[
            s((PAD + RB, width + N), f32),
            s((RB, width + N), bf16),
            s((RB, width + N), f32),
            s((N, width), bf16),
            s((RB, width + N), f32),
            s((PAD, width + N), f32),
        ],
        compiler_params=params(),
        cost_estimate=pl.CostEstimate(
            flops=4 * rows * N * width, bytes_accessed=8 * 2**20, transcendentals=rows * width
        ),
        name="prompt_grad",
    )(v, masks, wb, hp, weight, step, states)


def doc_number(starts, positions):
    return jnp.sum((starts[None, :] <= positions[:, None]).astype(jnp.int32), axis=1)


def prompt_masks(starts, rows):
    positions = jnp.arange(rows, dtype=jnp.int32)
    docs = doc_number(starts, positions)
    same = [doc_number(starts, positions - (K - 1 - k)) == docs for k in range(K - 1)]
    columns = jnp.stack(same + [docs == docs[rows - 1]], axis=1).astype(f32)
    return jnp.pad(columns, ((0, 0), (0, PAD - K)))


def pad_rows(a):
    return jnp.pad(a, ((0, PAD - a.shape[0]), (0, 0)))


def to_all(block, axes, devices):
    return lax.all_to_all(jnp.broadcast_to(block[None], (devices,) + block.shape), axes, 0, 0)


def sum_over_all(flat):
    axes = ("group", "resp")
    devices = lax.axis_size(axes)
    rows = -(-flat.size // (devices * LANES))
    flat = jnp.pad(flat, (0, devices * rows * LANES - flat.size)).reshape(devices, rows, LANES)
    mine = jnp.sum(lax.all_to_all(flat, axes, 0, 0), axis=0)
    return to_all(mine, axes, devices).reshape(-1)


def shards(
    prompt_in, prompt_dt, doc_starts, resp_in, resp_dt, resp_len, upstream, reward,
    conv_w, conv_b, head_params,
):
    n = lax.axis_size("resp")
    me = lax.axis_index("resp")
    hs = H // n
    width = XC // n
    per = n // G
    block = prompt_in.shape[1]
    slots = resp_in.shape[2]
    rows_in, dt_in = prompt_in[0], prompt_dt[0]
    u, dt, dy = resp_in[0, 0], resp_dt[0, 0], upstream[0, 0]

    r = reward[0, 0]
    r_hi = r.astype(bf16)
    r_mid = (r - r_hi.astype(f32)).astype(bf16)
    r_lo = (r - r_hi.astype(f32) - r_mid.astype(f32)).astype(bf16)
    tail_size = (K - 1) * rows_in.shape[1] // LANES
    small = jnp.concatenate(
        [
            rows_in[block - K + 1 :].reshape(tail_size, LANES),
            jnp.broadcast_to(jnp.stack([r_hi, r_mid, r_lo, jnp.zeros_like(r_lo)])[:, None], (4, LANES)),
            jnp.zeros((12, LANES), bf16),
        ]
    )
    small = to_all(small, "resp", n)
    wb = pad_rows(jnp.concatenate([conv_w, conv_b[None]], axis=0))
    hp = pad_rows(head_params)

    x_parts = rows_in[:, :XC].reshape(block, n, width).transpose(1, 0, 2)
    b_parts = jnp.repeat(
        rows_in[:, XC : XC + G * N].reshape(block, G, N).transpose(1, 0, 2), per, axis=0
    )
    dt_parts = jnp.pad(
        dt_in.reshape(block, n, hs).transpose(1, 0, 2), ((0, 0), (0, 0), (0, LANES - hs))
    )
    parts = jnp.concatenate([x_parts, b_parts, dt_parts], axis=2)
    parts, small = lax.optimization_barrier((parts, small))
    v = lax.all_to_all(parts, "resp", 0, 0).reshape(n * block, width + N + LANES)
    tail_rows = small[n - 1, :tail_size].reshape(K - 1, -1).astype(f32)
    tail = jnp.pad(tail_rows, ((PAD - K + 1, 0), (0, 0)))
    rewards = jnp.sum(small[:, tail_size : tail_size + 3, 0].astype(f32), axis=1)
    scale = (r - jnp.sum(rewards) / n) / slots
    masks = prompt_masks(doc_starts[0], n * block)
    my_group = me // per
    wb_mine = jnp.concatenate(
        [
            lax.dynamic_slice(wb, (0, me * width), (PAD, width)),
            lax.dynamic_slice(wb, (0, XC + my_group * N), (PAD, N)),
        ],
        axis=1,
    )
    hp_mine = jnp.pad(lax.dynamic_slice(hp, (0, me * hs), (PAD, hs)), ((0, 0), (0, LANES - hs)))

    length = resp_len.astype(jnp.int32)
    step, cum, cum_t, decay_in = response_steps(length, dt, hp)
    kept, sent, weighted, c_act = response_state(
        n, (me % 2).reshape(1, 1), scale.reshape(1, 1), u, tail, wb, dy, decay_in
    )
    met = lax.ppermute(sent, "resp", [(i, i ^ 1) for i in range(n)])

    cum4 = cum.reshape(slots, G, HG).transpose(1, 0, 2)
    skip = jnp.repeat(head_params[2], PS)[None, :]

    def mid(base, count):
        return response_mid(
            base, count, length, u, tail, wb, c_act, dy, step, cum, cum4,
            cum_t.reshape(G, HG, slots), skip,
        )

    first = mid(0, G // 2)
    pair_sums = add_pairs(kept, met, first[1])
    d_states = lax.all_to_all(
        pair_sums, "resp", 0, 0,
        axis_index_groups=[list(range(0, n, 2)), list(range(1, n, 2))],
    )
    start_mine, weight, p_step = prompt_state(v, masks, wb_mine, hp_mine, pair_sums, width)
    start = lax.all_gather(start_mine, "resp")
    second = mid(G // 2, G - G // 2)
    grad_x, grad_b, dc = (jnp.concatenate(ab, axis=1) for ab in zip(first[:3], second[:3]))
    rows_in, cols_in = zip(first[3:], second[3:])
    p_grad, p_heads = prompt_grad(v, masks, wb_mine, hp_mine, weight, p_step, d_states)
    grad_c, r_heads = response_end(
        u, tail, wb, c_act, weighted, start, dc, rows_in, cols_in, step, dt, hp
    )

    conv = jnp.concatenate([grad_x, grad_b, grad_c], axis=1)[: K + 1] * scale
    mine = lax.dynamic_slice(conv, (0, me * width), (K + 1, width)) + p_grad[: K + 1, :width]
    conv = lax.dynamic_update_slice(conv, mine, (0, me * width))
    at_b = XC + my_group * N
    mine = lax.dynamic_slice(conv, (0, at_b), (K + 1, N)) + p_grad[: K + 1, width:]
    conv = lax.dynamic_update_slice(conv, mine, (0, at_b))
    d_skip = jnp.sum(grad_x[K + 1].reshape(H, PS), axis=1)
    heads = jnp.concatenate([r_heads[:2], d_skip[None]], axis=0) * scale
    mine = lax.dynamic_slice(heads, (0, me * hs), (2, hs)) + p_heads[:2, :hs]
    heads = lax.dynamic_update_slice(heads, mine, (0, me * hs))
    flat = sum_over_all(jnp.concatenate([conv.reshape(-1), heads.reshape(-1)]))
    at_heads = conv.size
    conv = flat[:at_heads].reshape(conv.shape)
    return conv[:K], conv[K], flat[at_heads : at_heads + heads.size].reshape(heads.shape)


def solution(mesh):
    in_specs = (
        P("group", "resp", None),
        P("group", "resp", None),
        P("group", None),
        P("group", "resp", None, None),
        P("group", "resp", None, None),
        P("group", "resp"),
        P("group", "resp", None, None),
        P("group", "resp"),
        P(),
        P(),
        P(),
    )
    out_specs = (P(), P(), P())
    return jax.shard_map(shards, mesh=mesh, in_specs=in_specs, out_specs=out_specs, check_vma=False)
```

```python
import functools

import jax
import jax.numpy as jnp
from jax import lax
from jax.experimental import pallas as pl
from jax.experimental.pallas import tpu as pltpu
from jax.sharding import PartitionSpec as P

H = 128
PS = 64
N = 256
G = 4
K = 4
HG = H // G
XC = H * PS
GX = HG * PS
LANES = 128
PAD = 8

f32 = jnp.float32
bf16 = jnp.bfloat16

NN = (((1,), (0,)), ((), ()))
NT = (((1,), (1,)), ((), ()))


def dot(a, b, dims=NN, precision=None):
    return lax.dot_general(a, b, dims, precision=precision, preferred_element_type=f32)


def halves(v):
    hi = v.astype(bf16)
    return hi, (v - hi.astype(f32)).astype(bf16)


def indicator(first, width):
    row = lax.broadcasted_iota(jnp.int32, (LANES, width), 0)
    head = lax.shift_right_logical(lax.broadcasted_iota(jnp.int32, (LANES, width), 1), 6)
    return jnp.where(row - first == head, 1.0, 0.0).astype(bf16)


def expand(v, ind):
    hi, lo = halves(v)
    return dot(hi, ind) + dot(lo, ind)


def head_sums(z_hi, z_lo, ind):
    return dot(z_hi, ind, NT) + dot(z_lo, ind, NT)


def triangle(n, keep):
    i = lax.broadcasted_iota(jnp.int32, (n, n), 0)
    j = lax.broadcasted_iota(jnp.int32, (n, n), 1)
    return jnp.where(keep(i, j), 1.0, 0.0).astype(f32)


def tri_sum(tri, v):
    return dot(tri, v, precision=lax.Precision.HIGHEST)


def softplus(z):
    return jnp.maximum(z, 0.0) + jnp.log1p(jnp.exp(-jnp.abs(z)))


def sigmoid(z):
    return 0.5 * jnp.tanh(0.5 * z) + 0.5


def taps_of(ext, lanes, row, rows):
    return [ext[pl.ds(PAD - K + 1 + k + row, rows), lanes] for k in range(K)]


def conv_pre(taps, wb, masks=None):
    total = wb[K : K + 1] + wb[K - 1 : K] * taps[K - 1]
    for k in range(K - 1):
        term = wb[k : k + 1] * taps[k]
        if masks is not None:
            term = term * masks[k]
        total = total + term
    return total


def act_and_slope(pre):
    sig = sigmoid(pre)
    act = pre * sig
    return act, sig + act * (1.0 - sig)


def fold8(v):
    return jnp.sum(v.reshape(v.shape[0] // 8, 8, v.shape[1]), axis=0)


def lane_loop(width, body, step=LANES):
    def one(i, _):
        body(pl.ds(pl.multiple_of(i * step, step), step))
        return 0

    lax.fori_loop(0, width // step, one, 0)


RC = 64


def conv_forward(u, tail, wb, ext, act, slope, rows, width):
    def body(lanes):
        ext[0:PAD, lanes] = tail[:, lanes]
        ext[PAD : PAD + rows, lanes] = u[:, lanes].astype(f32)
        w = wb[:, lanes]
        for r in range(0, rows, RC):
            a, s = act_and_slope(conv_pre(taps_of(ext, lanes, r, RC), w))
            act[r : r + RC, lanes] = a.astype(bf16)
            if slope is not None:
                slope[r : r + RC, lanes] = s

    lane_loop(width, body)


def conv_backward(ext, slope, lanes, cotangent, grad, rows):
    sums = [jnp.zeros((8, LANES), f32) for _ in range(K + 1)]
    for r in range(0, rows, RC):
        d = cotangent(r) * slope[r : r + RC, lanes]
        taps = taps_of(ext, lanes, r, RC)
        for k in range(K):
            sums[k] = sums[k] + fold8(d * taps[k])
        sums[K] = sums[K] + fold8(d)
    for k in range(K + 1):
        grad[k : k + 1, lanes] = jnp.sum(sums[k], axis=0, keepdims=True)


def steps_kernel(len_ref, dt, hp, step, cum, cum_t, decay_in):
    rows = dt.shape[0]
    s = softplus(dt[...].astype(f32) + hp[1:2])
    logd = -jnp.exp(hp[0:1]) * s
    c = tri_sum(triangle(rows, lambda i, j: i >= j), logd)
    step[...] = s
    cum[...] = c
    cum_t[...] = c.T
    t = lax.broadcasted_iota(jnp.int32, c.shape, 0)
    decay_in[...] = jnp.where(t < len_ref[0, 0], jnp.exp(c), 0.0)


def resp_state_kernel(adv, u_c, tail_c, wb_c, dy, decay_in, state, weighted, c_out, ext):
    g = pl.program_id(0)
    rows, width = dy.shape
    conv_forward(u_c, tail_c, wb_c, ext, c_out, None, rows, N)
    c_t = c_out[...].astype(f32).T.astype(bf16)
    a = (dy[...].astype(f32) * expand(decay_in[...], indicator(g * HG, width))).astype(bf16)
    weighted[...] = a
    state[0] = (dot(c_t, a) * adv[0, 0]).astype(bf16)


def resp_mid_kernel(
    base, len_ref, u_x, u_b, tail_x, tail_b, wb_x, wb_b, c_act, dy, step, cum, cum4, cum_t4, skip,
    earlier_out,
    grad_x, grad_b, dc, row_out, col_out,
    ext, ext_b, x_s, xs_s, b_s, dym, slope, slope_b, step_e, y_s, t_s,
    a1, bm, sw_e, u_off, y_off, z_hi, z_lo,
):
    step_no = pl.program_id(0)
    g = step_no + base
    rows = u_x.shape[0]
    half = rows // 2
    conv_forward(u_x, tail_x, wb_x, ext, x_s, slope, rows, GX)
    conv_forward(u_b, tail_b, wb_b, ext_b, b_s, slope_b, rows, N)
    ind = indicator(g * HG, GX)
    step_e[...] = expand(step[...], ind)
    cum_v = cum[...]
    mid = cum_v[half - 1 : half]
    sw_e[...] = expand(jnp.exp(mid - cum_v[:half]) * step[:half], ind)
    y_off[...] = expand(jnp.exp(cum_v[half:] - mid), ind)
    live = jnp.where(lax.broadcasted_iota(jnp.int32, (rows, LANES), 0) < len_ref[0, 0], 1.0, 0.0)

    def prepare(lanes):
        d = dy[:, lanes].astype(f32) * live
        dym[:, lanes] = d.astype(bf16)
        x = x_s[:, lanes].astype(f32)
        xs_s[:, lanes] = (x * step_e[:, lanes]).astype(bf16)
        bm[:, lanes] = (x[:half] * sw_e[:, lanes]).astype(bf16)
        a1[:, lanes] = (d[half:] * y_off[:, lanes]).astype(bf16)

    lane_loop(GX, prepare)

    c_v, b_v = c_act[...], b_s[...]
    c0, c1, b0, b1 = c_v[:half], c_v[half:], b_v[:half], b_v[half:]
    i = lax.broadcasted_iota(jnp.int32, (half, half), 0)
    j = lax.broadcasted_iota(jnp.int32, (half, half), 1)
    lane = lax.broadcasted_iota(jnp.int32, (half, LANES), 1)
    first = jnp.where(lane < PS, 1.0, 0.0).astype(bf16)
    second = jnp.where(lane >= PS, 1.0, 0.0).astype(bf16)

    y_off[...] = dot(dot(c1, b0, NT).astype(bf16), bm[...])
    u_off[...] = dot(dot(b0, c1, NT).astype(bf16), a1[...])
    d10 = dot(a1[...], bm[...], NT)

    d_diag = []
    for q, (c_q, b_q) in enumerate(((c0, b0), (c1, b1))):
        r = slice(q * half, (q + 1) * half)
        lower = jnp.where(i >= j, dot(c_q, b_q, NT), 0.0)
        upper = jnp.where(j >= i, dot(b_q, c_q, NT), 0.0)
        d_sc = jnp.zeros((half, half), f32)
        for p in range(HG // 2):
            lanes = slice(p * LANES, (p + 1) * LANES)
            xs_p, dy_p = xs_s[r, lanes], dym[r, lanes]
            xb = jnp.concatenate([xs_p * first, xs_p * second], axis=0)
            dyb = jnp.concatenate([dy_p * first, dy_p * second], axis=0)
            d_m = dot(dy_p, xb, NT)
            mats, mats_t = [], []
            for a in range(2):
                h = 2 * p + a
                gap = jnp.exp(-jnp.abs(cum4[0, r, h : h + 1] - cum_t4[0, h : h + 1, r]))
                d_sc = d_sc + d_m[:, a * half : (a + 1) * half] * gap
                mats.append((gap * lower).astype(bf16))
                mats_t.append((gap * upper).astype(bf16))
            y_s[r, lanes] = dot(jnp.concatenate(mats, axis=1), xb)
            t_s[r, lanes] = dot(jnp.concatenate(mats_t, axis=1), dyb)
        d_diag.append(jnp.where(i >= j, d_sc, 0.0))

    d00, d11 = d_diag
    dc[:half] = dot(d00.astype(bf16), b0)
    dc[half:] = dot(d11.astype(bf16), b1) + dot(d10.astype(bf16), b0)
    db0 = dot(d00.T.astype(bf16), c0) + dot(d10.T.astype(bf16), c1)
    db1 = dot(d11.T.astype(bf16), c1)
    db = jnp.concatenate([db0, db1], axis=0)
    for k in range(N // LANES):
        lanes = slice(k * LANES, (k + 1) * LANES)
        conv_backward(ext_b, slope_b, lanes, lambda r: db[r : r + RC, lanes], grad_b, rows)

    def put(z, r, lanes):
        hi, lo = halves(z)
        z_hi[r : r + RC, lanes] = hi
        z_lo[r : r + RC, lanes] = lo

    def row_products(lanes):
        for r in range(0, rows, RC):
            z = dym[r : r + RC, lanes].astype(f32) * y_s[r : r + RC, lanes]
            if r >= half:
                o = r - half
                z = z + a1[o : o + RC, lanes].astype(f32) * y_off[o : o + RC, lanes]
            put(z, r, lanes)

    lane_loop(GX, row_products)
    row_sum = head_sums(z_hi[...], z_lo[...], ind)

    def finish(lanes):
        d_skip = jnp.zeros((8, LANES), f32)
        for r in range(0, rows, RC):
            t = t_s[r : r + RC, lanes]
            z = xs_s[r : r + RC, lanes].astype(f32) * t
            if r < half:
                z = z + bm[r : r + RC, lanes].astype(f32) * u_off[r : r + RC, lanes]
            put(z, r, lanes)
            d_skip = d_skip + fold8(
                dym[r : r + RC, lanes].astype(f32) * x_s[r : r + RC, lanes].astype(f32)
            )

        def cotangent(r):
            d = step_e[r : r + RC, lanes] * t_s[r : r + RC, lanes]
            d = d + skip[:, lanes] * dym[r : r + RC, lanes].astype(f32)
            if r < half:
                d = d + sw_e[r : r + RC, lanes] * u_off[r : r + RC, lanes]
            return d

        conv_backward(ext, slope, lanes, cotangent, grad_x, rows)
        grad_x[K + 1 : K + 2, lanes] = jnp.sum(d_skip, axis=0, keepdims=True)

    lane_loop(GX, finish)
    col_sum = head_sums(z_hi[...], z_lo[...], ind)

    @pl.when(step_no == 0)
    def _():
        row_out[...] = row_sum
        col_out[...] = col_sum

    @pl.when(step_no > 0)
    def _():
        row_out[...] += row_sum
        col_out[...] += col_sum


def resp_end_kernel(
    u_c, tail_c, wb_c, c_act, weighted, start, dc, row_in, col_in, step, dt, hp, earlier_out,
    grad_c, grad_h, ext, c_s, slope, total,
):
    g = pl.program_id(0)
    rows = u_c.shape[0]
    per, _, width = start.shape
    conv_forward(u_c, tail_c, wb_c, ext, c_s, slope, rows, N)
    d = dc[...]

    @pl.when(g == 0)
    def _():
        total[...] = row_in[...] - col_in[...]

    for s in range(per):
        a = weighted[:, s * width : (s + 1) * width]
        st = start[s]
        z_hi, z_lo = halves(a.astype(f32) * dot(c_act[...], st))
        total[...] += head_sums(z_hi, z_lo, indicator(g * HG + s * (width // PS), width))
        d = d + dot(a, st, NT)
    for k in range(N // LANES):
        lanes = slice(k * LANES, (k + 1) * LANES)
        conv_backward(ext, slope, lanes, lambda r: d[r : r + RC, lanes], grad_c, rows)

    @pl.when(g == pl.num_programs(0) - 1)
    def _():
        d_log = tri_sum(triangle(rows, lambda i, j: j >= i), total[...])
        rate = -jnp.exp(hp[0:1])
        s = step[...]
        d_step = col_in[...] / s + rate * d_log
        grad_h[...] = jnp.zeros_like(grad_h)
        grad_h[0:1] = jnp.sum(d_log * rate * s, axis=0, keepdims=True)
        grad_h[1:2] = jnp.sum(
            d_step * sigmoid(dt[...].astype(f32) + hp[1:2]), axis=0, keepdims=True
        )


RB = 256


def prompt_conv(v, masks, wb, ext, act, slope, row, width):
    def body(lanes):
        ext[PAD : PAD + RB, lanes] = v[pl.ds(row, RB), lanes].astype(f32)
        w = wb[:, lanes]
        for r in range(0, RB, RC):
            m = [masks[pl.ds(row + r, RC), k : k + 1] for k in range(K - 1)]
            a, s = act_and_slope(conv_pre(taps_of(ext, lanes, r, RC), w, m))
            act[r : r + RC, lanes] = a.astype(bf16)
            if slope is not None:
                slope[r : r + RC, lanes] = s

    lane_loop(width, body)


def rows_before(v, halo, row, width):
    if row:
        return v[row - 16 : row, :width].astype(f32)[16 - PAD :]
    return halo[...]


def prompt_state_kernel(
    place, v, halo, dt_all, masks, wb, hp, start, weight, step, beyond, ext, act, acc
):
    rows = v.shape[0]
    width = start.shape[1]
    first = place[0, 1]
    ind = indicator(place[0, 0] * HG, width)
    later = triangle(RB, lambda i, j: j > i)
    rate = -jnp.exp(hp[0:1])
    ahead = jnp.zeros((1, LANES), f32)
    slopes = jnp.zeros((1, LANES), f32)
    for row in range(0, dt_all.shape[0], RB):
        s = softplus(dt_all[row : row + RB].astype(f32) + hp[1:2])
        position = row + lax.broadcasted_iota(jnp.int32, s.shape, 0)
        past = position >= first + rows
        sig = sigmoid(dt_all[row : row + RB].astype(f32) + hp[1:2])
        ahead = ahead + rate * jnp.sum(jnp.where(past, s, 0.0), axis=0, keepdims=True)
        slopes = slopes + rate * jnp.sum(jnp.where(past, sig, 0.0), axis=0, keepdims=True)
    beyond[...] = jnp.zeros_like(beyond)
    beyond[0:1] = ahead
    beyond[1:2] = slopes
    acc[...] = jnp.zeros_like(acc)
    for row in range(rows - RB, -1, -RB):
        at = pl.ds(pl.multiple_of(first + row, RB), RB)
        s = softplus(dt_all[at, :].astype(f32) + hp[1:2])
        logd = rate * s
        after = tri_sum(later, logd) + ahead
        ahead = ahead + jnp.sum(logd, axis=0, keepdims=True)
        w = masks[row : row + RB, K - 1 : K] * jnp.exp(after) * s
        step[row : row + RB] = s
        weight[row : row + RB] = w
        ext[0:PAD] = rows_before(v, halo, row, width + N)
        prompt_conv(v, masks, wb, ext, act, None, row, width + N)
        wx = (act[:, :width].astype(f32) * expand(w, ind)).astype(bf16)
        acc[...] += dot(act[:, width:].astype(f32).T.astype(bf16), wx)
    start[...] = acc[...].astype(bf16)


def prompt_grad_kernel(
    count, place, v, halo, dt_mine, masks, wb, hp, weight, step, beyond, *refs
):
    states = refs[:count]
    grad, grad_h, ext, act, slope, g_s, d_s, sums = refs[count:]
    rows = v.shape[0]
    width = g_s.shape[1]
    ind = indicator(place[0, 0] * HG, width)
    earlier = triangle(RB, lambda i, j: j < i)
    total = states[0][...].astype(f32)
    for k in range(1, count):
        total = total + states[k][...].astype(f32)
    g_s[...] = total.astype(bf16)
    behind = jnp.zeros((1, LANES), f32)
    rate = -jnp.exp(hp[0:1])
    d_rate = jnp.zeros((1, LANES), f32)
    d_bias = jnp.zeros((1, LANES), f32)
    sums[...] = jnp.zeros_like(sums)
    for row in range(0, rows, RB):
        ext[0:PAD] = rows_before(v, halo, row, width + N)
        prompt_conv(v, masks, wb, ext, act, slope, row, width + N)
        w_e = expand(weight[row : row + RB], ind)
        t = dot(act[:, width:], g_s[...])
        wx = (act[:, :width].astype(f32) * w_e).astype(bf16)
        d_s[:, :width] = t * w_e
        d_s[:, width:] = dot(wx, g_s[...], NT)
        z_hi, z_lo = halves(wx.astype(f32) * t)
        q = head_sums(z_hi, z_lo, ind)
        d_log = tri_sum(earlier, q) + behind
        behind = behind + jnp.sum(q, axis=0, keepdims=True)
        s = step[row : row + RB]
        d_step = q / s + rate * d_log
        sig = sigmoid(dt_mine[row : row + RB].astype(f32) + hp[1:2])
        d_rate = d_rate + jnp.sum(d_log * rate * s, axis=0, keepdims=True)
        d_bias = d_bias + jnp.sum(d_step * sig, axis=0, keepdims=True)

        def back(lanes):
            acc = [jnp.zeros((8, LANES), f32) for _ in range(K + 1)]
            for r in range(0, RB, RC):
                d = d_s[r : r + RC, lanes] * slope[r : r + RC, lanes]
                taps = taps_of(ext, lanes, r, RC)
                for k in range(K):
                    part = d * taps[k]
                    if k < K - 1:
                        part = part * masks[pl.ds(row + r, RC), k : k + 1]
                    acc[k] = acc[k] + fold8(part)
                acc[K] = acc[K] + fold8(d)
            for k in range(K + 1):
                sums[k : k + 1, lanes] += jnp.sum(acc[k], axis=0, keepdims=True)

        lane_loop(width + N, back)
    grad[...] = sums[...]
    grad_h[...] = jnp.zeros_like(grad_h)
    grad_h[0:1] = d_rate + behind * beyond[0:1]
    grad_h[1:2] = d_bias + behind * beyond[1:2]


def add_kernel(count, *refs):
    total = refs[0][...].astype(f32)
    for k in range(1, count):
        total = total + refs[k][...].astype(f32)
    refs[-1][...] = total.astype(bf16)


def params(mib, *semantics):
    return pltpu.CompilerParams(
        vmem_limit_bytes=mib * 2**20, dimension_semantics=semantics or None
    )


SMEM = pl.BlockSpec(memory_space=pltpu.SMEM)


def whole(shape):
    return pl.BlockSpec(shape, lambda *_: (0,) * len(shape))


def sds(shape, dtype):
    return jax.ShapeDtypeStruct(shape, dtype)


def response_steps(length, dt, hp):
    rows = dt.shape[0]
    square = sds((rows, H), f32)
    return pl.pallas_call(
        steps_kernel,
        out_shape=(square, square, sds((H, rows), f32), square),
        in_specs=[SMEM, pl.BlockSpec(), pl.BlockSpec()],
        compiler_params=params(8),
        name="resp_steps",
    )(length, dt, hp)


def response_state(scale, u, tail, wb, dy, decay_in):
    rows = u.shape[0]
    c_at = lambda g: (0, XC // N + G + g)
    g_at = lambda g: (0, g)
    return pl.pallas_call(
        resp_state_kernel,
        grid=(G,),
        in_specs=[
            SMEM,
            pl.BlockSpec((rows, N), c_at),
            pl.BlockSpec((PAD, N), c_at),
            pl.BlockSpec((PAD, N), c_at),
            pl.BlockSpec((rows, GX), g_at),
            whole((rows, H)),
        ],
        out_specs=[
            pl.BlockSpec((1, N, GX), lambda g: (g, 0, 0)),
            pl.BlockSpec((rows, GX), g_at),
            pl.BlockSpec((rows, N), g_at),
        ],
        out_shape=(sds((G, N, GX), bf16), sds((rows, XC), bf16), sds((rows, G * N), bf16)),
        scratch_shapes=[pltpu.VMEM((PAD + rows, N), f32)],
        compiler_params=params(24, "arbitrary"),
        cost_estimate=pl.CostEstimate(
            flops=2 * rows * N * XC, bytes_accessed=14 * 2**20, transcendentals=rows * G * N
        ),
        name="resp_state",
    )(scale, u, tail, wb, dy, decay_in)


def response_mid(
    base, count, length, u, tail, wb, c_act, dy, step, cum, cum4, cum_t4, skip, earlier_out
):
    rows = u.shape[0]
    half = rows // 2
    x_at = lambda g: (0, base + g)
    b_at = lambda g: (0, XC // N + base + g)
    out_at = lambda g: (0, g)
    v = pltpu.VMEM
    return pl.pallas_call(
        functools.partial(resp_mid_kernel, base),
        grid=(count,),
        in_specs=[
            SMEM,
            pl.BlockSpec((rows, GX), x_at),
            pl.BlockSpec((rows, N), b_at),
            pl.BlockSpec((PAD, GX), x_at),
            pl.BlockSpec((PAD, N), b_at),
            pl.BlockSpec((PAD, GX), x_at),
            pl.BlockSpec((PAD, N), b_at),
            pl.BlockSpec((rows, N), x_at),
            pl.BlockSpec((rows, GX), x_at),
            whole((rows, H)),
            whole((rows, H)),
            pl.BlockSpec((1, rows, HG), lambda g: (base + g, 0, 0)),
            pl.BlockSpec((1, HG, rows), lambda g: (base + g, 0, 0)),
            pl.BlockSpec((1, GX), x_at),
            pl.BlockSpec(memory_space=pl.ANY),
        ],
        out_specs=[
            pl.BlockSpec((PAD, GX), out_at),
            pl.BlockSpec((PAD, N), out_at),
            pl.BlockSpec((rows, N), out_at),
            whole((rows, H)),
            whole((rows, H)),
        ],
        out_shape=(
            sds((PAD, count * GX), f32),
            sds((PAD, count * N), f32),
            sds((rows, count * N), f32),
            sds((rows, H), f32),
            sds((rows, H), f32),
        ),
        scratch_shapes=[
            v((PAD + rows, GX), f32),
            v((PAD + rows, N), f32),
            v((rows, GX), bf16),
            v((rows, GX), bf16),
            v((rows, N), bf16),
            v((rows, GX), bf16),
            v((rows, GX), f32),
            v((rows, N), f32),
            v((rows, GX), f32),
            v((rows, GX), f32),
            v((rows, GX), f32),
            v((half, GX), bf16),
            v((half, GX), bf16),
            v((half, GX), f32),
            v((half, GX), f32),
            v((half, GX), f32),
            v((rows, GX), bf16),
            v((rows, GX), bf16),
        ],
        compiler_params=params(40, "arbitrary"),
        cost_estimate=pl.CostEstimate(
            flops=count * 8 * 2**30, bytes_accessed=count * 3 * 2**20, transcendentals=rows * half * H
        ),
        name="resp_mid",
    )(
        length, u, u, tail, tail, wb, wb, c_act, dy, step, cum, cum4, cum_t4, skip, earlier_out
    )


def response_end(
    u, tail, wb, c_act, weighted, start, dc, row_in, col_in, step, dt, hp, earlier_out
):
    rows = u.shape[0]
    n, _, width = start.shape
    per = n // G
    c_at = lambda g: (0, XC // N + G + g)
    g_at = lambda g: (0, g)
    v = pltpu.VMEM
    return pl.pallas_call(
        resp_end_kernel,
        grid=(G,),
        in_specs=[
            pl.BlockSpec((rows, N), c_at),
            pl.BlockSpec((PAD, N), c_at),
            pl.BlockSpec((PAD, N), c_at),
            pl.BlockSpec((rows, N), g_at),
            pl.BlockSpec((rows, GX), g_at),
            pl.BlockSpec((per, N, width), lambda g: (g, 0, 0)),
            pl.BlockSpec((rows, N), g_at),
            whole((rows, H)),
            whole((rows, H)),
            whole((rows, H)),
            whole((rows, H)),
            whole((PAD, H)),
            pl.BlockSpec(memory_space=pl.ANY),
        ],
        out_specs=[pl.BlockSpec((PAD, N), g_at), whole((PAD, H))],
        out_shape=(sds((PAD, G * N), f32), sds((PAD, H), f32)),
        scratch_shapes=[
            v((PAD + rows, N), f32),
            v((rows, N), bf16),
            v((rows, N), f32),
            v((rows, H), f32),
        ],
        compiler_params=params(24, "arbitrary"),
        cost_estimate=pl.CostEstimate(
            flops=4 * rows * N * XC, bytes_accessed=12 * 2**20, transcendentals=rows * G * N
        ),
        name="resp_end",
    )(u, tail, wb, c_act, weighted, start, dc, row_in, col_in, step, dt, hp, earlier_out)


def add_states(terms, earlier_out, copies=None):
    rows, width = terms[0].shape
    part = rows // 4
    block = pl.BlockSpec((part, width), lambda i, *_: (i, 0))
    if copies is None:
        grid, out, out_shape = (4,), block, (rows, width)
    else:
        grid = (4, copies)
        out = pl.BlockSpec((None, part, width), lambda i, j: (j, i, 0))
        out_shape = (copies, rows, width)
    size = rows * width
    return pl.pallas_call(
        functools.partial(add_kernel, len(terms)),
        grid=grid,
        in_specs=[block] * len(terms) + [pl.BlockSpec(memory_space=pl.ANY)],
        out_specs=out,
        out_shape=sds(out_shape, bf16),
        compiler_params=params(8, *["arbitrary"] * len(grid)),
        cost_estimate=pl.CostEstimate(
            flops=size * len(terms), bytes_accessed=2 * size * (len(terms) + 1), transcendentals=0
        ),
        name="add_states",
    )(*terms, earlier_out)


def prompt_state(place, v, halo, dt_all, masks, wb, hp):
    rows = v.shape[0]
    width = v.shape[1] - N
    s = pltpu.VMEM
    return pl.pallas_call(
        prompt_state_kernel,
        in_specs=[SMEM] + [pl.BlockSpec()] * 6,
        out_shape=(
            sds((N, width), bf16),
            sds((rows, LANES), f32),
            sds((rows, LANES), f32),
            sds((PAD, LANES), f32),
        ),
        scratch_shapes=[
            s((PAD + RB, width + N), f32),
            s((RB, width + N), bf16),
            s((N, width), f32),
        ],
        compiler_params=params(28),
        cost_estimate=pl.CostEstimate(
            flops=2 * rows * N * width, bytes_accessed=4 * 2**20, transcendentals=rows * width
        ),
        name="prompt_state",
    )(place, v, halo, dt_all, masks, wb, hp)


def prompt_grad(place, v, halo, dt_mine, masks, wb, hp, weight, step, beyond, states):
    rows = v.shape[0]
    width = v.shape[1] - N
    s = pltpu.VMEM
    return pl.pallas_call(
        functools.partial(prompt_grad_kernel, len(states)),
        in_specs=[SMEM] + [pl.BlockSpec()] * (9 + len(states)),
        out_shape=(sds((PAD, width + N), f32), sds((PAD, LANES), f32)),
        scratch_shapes=[
            s((PAD + RB, width + N), f32),
            s((RB, width + N), bf16),
            s((RB, width + N), f32),
            s((N, width), bf16),
            s((RB, width + N), f32),
            s((PAD, width + N), f32),
        ],
        compiler_params=params(36),
        cost_estimate=pl.CostEstimate(
            flops=4 * rows * N * width, bytes_accessed=8 * 2**20, transcendentals=rows * width
        ),
        name="prompt_grad",
    )(place, v, halo, dt_mine, masks, wb, hp, weight, step, beyond, *states)


def doc_number(starts, positions):
    return jnp.sum((starts[None, :] <= positions[:, None]).astype(jnp.int32), axis=1)


def prompt_masks(starts, rows):
    positions = jnp.arange(rows, dtype=jnp.int32)
    docs = doc_number(starts, positions)
    same = [doc_number(starts, positions - (K - 1 - k)) == docs for k in range(K - 1)]
    columns = jnp.stack(same + [docs == docs[rows - 1]], axis=1).astype(f32)
    return jnp.pad(columns, ((0, 0), (0, PAD - K)))


def pad_rows(a):
    return jnp.pad(a, ((0, PAD - a.shape[0]), (0, 0)))


def to_all(block, axes, devices, groups=None):
    copies = jnp.broadcast_to(block[None], (devices,) + block.shape)
    return lax.all_to_all(copies, axes, 0, 0, axis_index_groups=groups)


def sum_over_all(flat):
    axes = ("group", "resp")
    devices = lax.axis_size(axes)
    rows = -(-flat.size // (devices * LANES))
    flat = jnp.pad(flat, (0, devices * rows * LANES - flat.size)).reshape(devices, rows, LANES)
    mine = jnp.sum(lax.all_to_all(flat, axes, 0, 0), axis=0)
    return to_all(mine, axes, devices).reshape(-1)


def shards(
    prompt_in, prompt_dt, doc_starts, resp_in, resp_dt, resp_len, upstream, reward,
    conv_w, conv_b, head_params,
):
    n = lax.axis_size("resp")
    me = lax.axis_index("resp")
    clusters = n // G
    mine = me % G
    cluster = me // G
    inside = [list(range(c * G, c * G + G)) for c in range(clusters)]
    block = prompt_in.shape[1]
    slots = resp_in.shape[2]
    rows_in, dt_in = prompt_in[0], prompt_dt[0]
    u, dt, dy = resp_in[0, 0], resp_dt[0, 0], upstream[0, 0]

    r = reward[0, 0]
    r_hi = r.astype(bf16)
    r_mid = (r - r_hi.astype(f32)).astype(bf16)
    r_lo = (r - r_hi.astype(f32) - r_mid.astype(f32)).astype(bf16)
    tail_size = (K - 1) * rows_in.shape[1] // LANES
    small = jnp.concatenate(
        [
            rows_in[block - K + 1 :].reshape(tail_size, LANES),
            dt_in,
            jnp.broadcast_to(
                jnp.stack([r_hi, r_mid, r_lo, jnp.zeros_like(r_lo)])[:, None], (4, LANES)
            ),
            jnp.zeros((12, LANES), bf16),
        ]
    )
    small = to_all(small, "resp", n)
    wb = pad_rows(jnp.concatenate([conv_w, conv_b[None]], axis=0))
    hp = pad_rows(head_params)

    x_parts = rows_in[:, :XC].reshape(block, G, GX).transpose(1, 0, 2)
    b_parts = rows_in[:, XC : XC + G * N].reshape(block, G, N).transpose(1, 0, 2)
    parts = jnp.concatenate([x_parts, b_parts], axis=2)
    parts, small = lax.optimization_barrier((parts, small))
    v = lax.all_to_all(parts, "resp", 0, 0, axis_index_groups=inside)
    v = v.reshape(G * block, GX + N)

    def own_channels(a):
        return jnp.concatenate(
            [
                lax.dynamic_slice(a, (0, mine * GX), (PAD, GX)),
                lax.dynamic_slice(a, (0, XC + mine * N), (PAD, N)),
            ],
            axis=1,
        )

    def last_rows(device):
        rows = lax.dynamic_index_in_dim(small, device, 0, False)[:tail_size]
        return jnp.pad(rows.reshape(K - 1, -1).astype(f32), ((PAD - K + 1, 0), (0, 0)))

    tail = last_rows(n - 1)
    halo = own_channels(last_rows(jnp.maximum(cluster * G - 1, 0)))
    dt_all = small[:, tail_size : tail_size + block].reshape(n * block, H)
    dt_mine = lax.dynamic_slice(dt_all, (cluster * G * block, 0), (G * block, H))
    at_reward = tail_size + block
    rewards = jnp.sum(small[:, at_reward : at_reward + 3, 0].astype(f32), axis=1)
    scale = (r - jnp.sum(rewards) / n) / slots
    masks = lax.dynamic_slice(
        prompt_masks(doc_starts[0], n * block), (cluster * G * block, 0), (G * block, PAD)
    )
    wb_mine = own_channels(wb)
    place = jnp.stack([mine, cluster * G * block]).astype(jnp.int32).reshape(1, 2)

    length = resp_len.astype(jnp.int32)
    step, cum, cum_t, decay_in = response_steps(length, dt, hp)
    d_states, weighted, c_act = response_state(scale.reshape(1, 1), u, tail, wb, dy, decay_in)
    d_states = lax.all_to_all(d_states, "resp", 0, 0, axis_index_groups=inside)

    cum4 = cum.reshape(slots, G, HG).transpose(1, 0, 2)
    skip = jnp.repeat(head_params[2], PS)[None, :]

    def mid(g, earlier_out):
        return response_mid(
            g, 1, length, u, tail, wb, c_act, dy, step, cum, cum4,
            cum_t.reshape(G, HG, slots), skip, earlier_out,
        )

    def across(part):
        routes = [[(i, (i + c * G) % n) for i in range(n)] for c in range(1, clusters)]
        return [part] + [lax.ppermute(part, "resp", route) for route in routes]

    part, weight, p_step, beyond = prompt_state(place, v, halo, dt_all, masks, wb_mine, hp)
    parts_of_start = across(part)
    mids = [mid(0, weight)]
    mids.append(mid(1, mids[0][1]))
    part = add_states([d_states[k] for k in range(G)], mids[1][1])
    parts_of_grad = across(part)
    start = add_states(parts_of_start, part, copies=G)
    mids.append(mid(2, start))
    start = lax.all_to_all(start, "resp", 0, 0, axis_index_groups=inside)
    mids.append(mid(3, mids[2][1]))
    p_grad, p_heads = prompt_grad(
        place, v, halo, dt_mine, masks, wb_mine, hp, weight, p_step, beyond, parts_of_grad
    )
    grad_x, grad_b, dc = (jnp.concatenate([m[k] for m in mids], axis=1) for k in range(3))
    row_in, col_in = (mids[0][k] + mids[1][k] + mids[2][k] + mids[3][k] for k in (3, 4))
    grad_c, r_heads = response_end(
        u, tail, wb, c_act, weighted, start, dc, row_in, col_in, step, dt, hp, p_heads
    )

    conv = jnp.concatenate([grad_x, grad_b, grad_c], axis=1)[: K + 1] * scale
    for at, size, first in ((mine * GX, GX, 0), (XC + mine * N, N, GX)):
        own = lax.dynamic_slice(conv, (0, at), (K + 1, size))
        own = own + p_grad[: K + 1, first : first + size]
        conv = lax.dynamic_update_slice(conv, own, (0, at))
    d_skip = jnp.sum(grad_x[K + 1].reshape(H, PS), axis=1)
    heads = jnp.concatenate([r_heads[:2], d_skip[None]], axis=0) * scale
    heads = heads + jnp.pad(p_heads[:2], ((0, 1), (0, 0)))
    flat = sum_over_all(jnp.concatenate([conv.reshape(-1), heads.reshape(-1)]))
    at_heads = conv.size
    conv = flat[:at_heads].reshape(conv.shape)
    return conv[:K], conv[K], flat[at_heads : at_heads + heads.size].reshape(heads.shape)


def solution(mesh):
    in_specs = (
        P("group", "resp", None),
        P("group", "resp", None),
        P("group", None),
        P("group", "resp", None, None),
        P("group", "resp", None, None),
        P("group", "resp"),
        P("group", "resp", None, None),
        P("group", "resp"),
        P(),
        P(),
        P(),
    )
    out_specs = (P(), P(), P())
    return jax.shard_map(shards, mesh=mesh, in_specs=in_specs, out_specs=out_specs, check_vma=False)
```

```python
import functools

import jax
import jax.numpy as jnp
from jax import lax
from jax.experimental import pallas as pl
from jax.experimental.pallas import tpu as pltpu
from jax.sharding import PartitionSpec as P

H = 128
PS = 64
N = 256
G = 4
K = 4
HG = H // G
XC = H * PS
GX = HG * PS
LANES = 128
PAD = 8
VMEM_MIB = 63

f32 = jnp.float32
bf16 = jnp.bfloat16

NN = (((1,), (0,)), ((), ()))
NT = (((1,), (1,)), ((), ()))


def dot(a, b, dims=NN, precision=None):
    return lax.dot_general(a, b, dims, precision=precision, preferred_element_type=f32)


def halves(v):
    hi = v.astype(bf16)
    return hi, (v - hi.astype(f32)).astype(bf16)


def indicator(first, width):
    row = lax.broadcasted_iota(jnp.int32, (LANES, width), 0)
    head = lax.shift_right_logical(lax.broadcasted_iota(jnp.int32, (LANES, width), 1), 6)
    return jnp.where(row - first == head, 1.0, 0.0).astype(bf16)


def expand(v, ind):
    hi, lo = halves(v)
    return dot(hi, ind) + dot(lo, ind)


def head_sums(z_hi, z_lo, ind):
    return dot(z_hi, ind, NT) + dot(z_lo, ind, NT)


def triangle(n, keep):
    i = lax.broadcasted_iota(jnp.int32, (n, n), 0)
    j = lax.broadcasted_iota(jnp.int32, (n, n), 1)
    return jnp.where(keep(i, j), 1.0, 0.0).astype(f32)


def tri_sum(tri, v):
    return dot(tri, v, precision=lax.Precision.HIGHEST)


def softplus(z):
    return jnp.maximum(z, 0.0) + jnp.log1p(jnp.exp(-jnp.abs(z)))


def sigmoid(z):
    return 0.5 * jnp.tanh(0.5 * z) + 0.5


def taps_of(ext, lanes, row, rows):
    return [ext[pl.ds(PAD - K + 1 + k + row, rows), lanes] for k in range(K)]


def conv_pre(taps, wb, masks=None):
    total = wb[K : K + 1] + wb[K - 1 : K] * taps[K - 1]
    for k in range(K - 1):
        term = wb[k : k + 1] * taps[k]
        if masks is not None:
            term = term * masks[k]
        total = total + term
    return total


def act_and_slope(pre):
    sig = sigmoid(pre)
    act = pre * sig
    return act, sig + act * (1.0 - sig)


def fold8(v):
    return jnp.sum(v.reshape(v.shape[0] // 8, 8, v.shape[1]), axis=0)


def as_rows(parts):
    row = lax.broadcasted_iota(jnp.int32, (PAD, LANES), 0)
    total = jnp.zeros((PAD, LANES), f32)
    for k, part in enumerate(parts):
        total = total + jnp.where(row == k, jnp.sum(part, axis=0, keepdims=True), 0.0)
    return total


def lane_loop(width, body, step=LANES):
    def one(i, _):
        body(pl.ds(pl.multiple_of(i * step, step), step))
        return 0

    lax.fori_loop(0, width // step, one, 0)


RC = 64


def conv_forward(u, tail, wb, ext, act, slope, rows, width):
    def body(lanes):
        ext[0:PAD, lanes] = tail[:, lanes]
        ext[PAD : PAD + rows, lanes] = u[:, lanes].astype(f32)
        w = wb[:, lanes]
        for r in range(0, rows, RC):
            a, s = act_and_slope(conv_pre(taps_of(ext, lanes, r, RC), w))
            act[r : r + RC, lanes] = a.astype(bf16)
            if slope is not None:
                slope[r : r + RC, lanes] = s

    lane_loop(width, body)


def conv_backward(ext, slope, lanes, cotangent, grad, rows):
    sums = [jnp.zeros((8, LANES), f32) for _ in range(K + 1)]
    for r in range(0, rows, RC):
        d = cotangent(r) * slope[r : r + RC, lanes]
        taps = taps_of(ext, lanes, r, RC)
        for k in range(K):
            sums[k] = sums[k] + fold8(d * taps[k])
        sums[K] = sums[K] + fold8(d)
    grad[:, lanes] = as_rows(sums)


def steps_kernel(len_ref, dt, hp, step, cum, cum_t, decay_in):
    rows = dt.shape[0]
    s = softplus(dt[...].astype(f32) + hp[1:2])
    logd = -jnp.exp(hp[0:1]) * s
    c = tri_sum(triangle(rows, lambda i, j: i >= j), logd)
    step[...] = s
    cum[...] = c
    cum_t[...] = c.T
    t = lax.broadcasted_iota(jnp.int32, c.shape, 0)
    decay_in[...] = jnp.where(t < len_ref[0, 0], jnp.exp(c), 0.0)


def resp_state_kernel(adv, u_c, tail_c, wb_c, dy, decay_in, state, weighted, c_out, ext):
    g = pl.program_id(0)
    rows, width = dy.shape
    conv_forward(u_c, tail_c, wb_c, ext, c_out, None, rows, N)
    c_t = c_out[...].astype(f32).T.astype(bf16)
    a = (dy[...].astype(f32) * expand(decay_in[...], indicator(g * HG, width))).astype(bf16)
    weighted[...] = a
    state[0] = (dot(c_t, a) * adv[0, 0]).astype(bf16)


def resp_mid_kernel(
    g, len_ref, u_x, u_b, tail_x, tail_b, wb_x, wb_b, c_act, dy, step, cum, cum4, cum_t4, skip,
    earlier_out, *refs,
):
    if g:
        sums_in, refs = refs[3], refs[4:]
    (
    grad_x, grad_b, dc, sums_out,
    ext, ext_b, x_s, xs_s, b_s, dym, slope, slope_b, step_e, y_s, t_s,
    a1, bm, sw_e, u_off, y_off, z_hi, z_lo, d_skip,
    ) = refs
    rows = u_x.shape[0]
    half = rows // 2
    conv_forward(u_x, tail_x, wb_x, ext, x_s, slope, rows, GX)
    conv_forward(u_b, tail_b, wb_b, ext_b, b_s, slope_b, rows, N)
    ind = indicator(g * HG, GX)
    step_e[...] = expand(step[...], ind)
    cum_v = cum[...]
    mid = cum_v[half - 1 : half]
    sw_e[...] = expand(jnp.exp(mid - cum_v[:half]) * step[:half], ind)
    y_off[...] = expand(jnp.exp(cum_v[half:] - mid), ind)
    live = jnp.where(lax.broadcasted_iota(jnp.int32, (rows, LANES), 0) < len_ref[0, 0], 1.0, 0.0)

    def prepare(lanes):
        d = dy[:, lanes].astype(f32) * live
        dym[:, lanes] = d.astype(bf16)
        x = x_s[:, lanes].astype(f32)
        xs_s[:, lanes] = (x * step_e[:, lanes]).astype(bf16)
        bm[:, lanes] = (x[:half] * sw_e[:, lanes]).astype(bf16)
        a1[:, lanes] = (d[half:] * y_off[:, lanes]).astype(bf16)

    lane_loop(GX, prepare)

    c_v, b_v = c_act[...], b_s[...]
    c0, c1, b0, b1 = c_v[:half], c_v[half:], b_v[:half], b_v[half:]
    i = lax.broadcasted_iota(jnp.int32, (half, half), 0)
    j = lax.broadcasted_iota(jnp.int32, (half, half), 1)
    lane = lax.broadcasted_iota(jnp.int32, (half, LANES), 1)
    first = jnp.where(lane < PS, 1.0, 0.0).astype(bf16)
    second = jnp.where(lane >= PS, 1.0, 0.0).astype(bf16)

    y_off[...] = dot(dot(c1, b0, NT).astype(bf16), bm[...])
    u_off[...] = dot(dot(b0, c1, NT).astype(bf16), a1[...])
    d10 = dot(a1[...], bm[...], NT)

    d_diag = []
    for q, (c_q, b_q) in enumerate(((c0, b0), (c1, b1))):
        r = slice(q * half, (q + 1) * half)
        lower = jnp.where(i >= j, dot(c_q, b_q, NT), 0.0)
        upper = jnp.where(j >= i, dot(b_q, c_q, NT), 0.0)
        d_sc = jnp.zeros((half, half), f32)
        for p in range(HG // 2):
            lanes = slice(p * LANES, (p + 1) * LANES)
            xs_p, dy_p = xs_s[r, lanes], dym[r, lanes]
            xb = jnp.concatenate([xs_p * first, xs_p * second], axis=0)
            dyb = jnp.concatenate([dy_p * first, dy_p * second], axis=0)
            d_m = dot(dy_p, xb, NT)
            mats, mats_t = [], []
            for a in range(2):
                h = 2 * p + a
                gap = jnp.exp(-jnp.abs(cum4[0, r, h : h + 1] - cum_t4[0, h : h + 1, r]))
                d_sc = d_sc + d_m[:, a * half : (a + 1) * half] * gap
                mats.append((gap * lower).astype(bf16))
                mats_t.append((gap * upper).astype(bf16))
            y_s[r, lanes] = dot(jnp.concatenate(mats, axis=1), xb)
            t_s[r, lanes] = dot(jnp.concatenate(mats_t, axis=1), dyb)
        d_diag.append(jnp.where(i >= j, d_sc, 0.0))

    d00, d11 = d_diag
    dc[:half] = dot(d00.astype(bf16), b0)
    dc[half:] = dot(d11.astype(bf16), b1) + dot(d10.astype(bf16), b0)
    db0 = dot(d00.T.astype(bf16), c0) + dot(d10.T.astype(bf16), c1)
    db1 = dot(d11.T.astype(bf16), c1)
    db = jnp.concatenate([db0, db1], axis=0)
    for k in range(N // LANES):
        lanes = slice(k * LANES, (k + 1) * LANES)
        conv_backward(ext_b, slope_b, lanes, lambda r: db[r : r + RC, lanes], grad_b, rows)

    def put(z, r, lanes):
        hi, lo = halves(z)
        z_hi[r : r + RC, lanes] = hi
        z_lo[r : r + RC, lanes] = lo

    def row_products(lanes):
        for r in range(0, rows, RC):
            z = dym[r : r + RC, lanes].astype(f32) * y_s[r : r + RC, lanes]
            if r >= half:
                o = r - half
                z = z + a1[o : o + RC, lanes].astype(f32) * y_off[o : o + RC, lanes]
            put(z, r, lanes)

    lane_loop(GX, row_products)
    row_sum = head_sums(z_hi[...], z_lo[...], ind)

    def finish(lanes):
        d_skips = jnp.zeros((8, LANES), f32)
        for r in range(0, rows, RC):
            t = t_s[r : r + RC, lanes]
            z = xs_s[r : r + RC, lanes].astype(f32) * t
            if r < half:
                z = z + bm[r : r + RC, lanes].astype(f32) * u_off[r : r + RC, lanes]
            put(z, r, lanes)
            d_skips = d_skips + fold8(
                dym[r : r + RC, lanes].astype(f32) * x_s[r : r + RC, lanes].astype(f32)
            )

        def cotangent(r):
            d = step_e[r : r + RC, lanes] * t_s[r : r + RC, lanes]
            d = d + skip[:, lanes] * dym[r : r + RC, lanes].astype(f32)
            if r < half:
                d = d + sw_e[r : r + RC, lanes] * u_off[r : r + RC, lanes]
            return d

        conv_backward(ext, slope, lanes, cotangent, grad_x, rows)
        d_skip[:, lanes] = d_skips

    lane_loop(GX, finish)
    col_sum = head_sums(z_hi[...], z_lo[...], ind)

    skip_sum = head_sums(*halves(d_skip[...]), ind)
    for at, part in ((0, row_sum), (rows, col_sum), (2 * rows, skip_sum)):
        span = slice(at, at + part.shape[0])
        sums_out[span] = sums_in[span] + part if g else part


X_TILES = XC // LANES
B_TILES = G * N // LANES
HEAD_TILE = X_TILES + 2 * B_TILES


def tile(k):
    return slice(k * LANES, (k + 1) * LANES)


def resp_end_kernel(
    place, scale, u_c, tail_c, wb_c, c_act, weighted, start, dc, sums, step, dt, hp,
    grad_x, grad_b, p_grad, p_heads,
    packed, ext, c_s, slope, total, grad_c,
):
    g = pl.program_id(0)
    rows, width = weighted.shape
    conv_forward(u_c, tail_c, wb_c, ext, c_s, slope, rows, N)

    @pl.when(g == 0)
    def _():
        total[...] = sums[0:rows] - sums[rows : 2 * rows]

    a = weighted[...]
    z_hi, z_lo = halves(a.astype(f32) * dot(c_act[...], start[0]))
    total[...] += head_sums(z_hi, z_lo, indicator(g * HG, width))
    d = dc[...] + dot(a, start[0], NT)
    for k in range(N // LANES):
        conv_backward(ext, slope, tile(k), lambda r: d[r : r + RC, tile(k)], grad_c, rows)
        packed[X_TILES + B_TILES + g * (N // LANES) + k] = grad_c[:, tile(k)] * scale[0, 0]

    @pl.when(g == pl.num_programs(0) - 1)
    def _():
        d_log = tri_sum(triangle(rows, lambda i, j: j >= i), total[...])
        rate = -jnp.exp(hp[0:1])
        s = step[...]
        d_step = sums[rows : 2 * rows] / s + rate * d_log
        sig = sigmoid(dt[...].astype(f32) + hp[1:2])
        heads = as_rows([d_log * rate * s, d_step * sig, sums[2 * rows :]])
        for k in range(X_TILES):
            packed[k] = grad_x[:, tile(k)] * scale[0, 0]
        for k in range(B_TILES):
            packed[X_TILES + k] = grad_b[:, tile(k)] * scale[0, 0]
        for k in range(width // LANES):
            packed[place[0, 0] * (width // LANES) + k] += p_grad[:, tile(k)]
        for k in range(N // LANES):
            packed[X_TILES + place[0, 0] * (N // LANES) + k] += p_grad[:, tile(width // LANES + k)]
        packed[HEAD_TILE] = heads * scale[0, 0] + p_heads[...]
        for k in range(HEAD_TILE + 1, packed.shape[0]):
            packed[k] = jnp.zeros((PAD, LANES), f32)


def unpack_kernel(packed, conv_w, conv_b, heads):
    for k in range(HEAD_TILE):
        conv_w[:, tile(k)] = packed[k, 0:K]
        conv_b[:, tile(k)] = packed[k, K : K + 1]
    heads[...] = packed[HEAD_TILE, 0:3]


RB = 256


def prompt_conv(v, masks, wb, ext, act, slope, row, width):
    def body(lanes):
        ext[PAD : PAD + RB, lanes] = v[pl.ds(row, RB), lanes].astype(f32)
        w = wb[:, lanes]
        for r in range(0, RB, RC):
            m = [masks[pl.ds(row + r, RC), k : k + 1] for k in range(K - 1)]
            a, s = act_and_slope(conv_pre(taps_of(ext, lanes, r, RC), w, m))
            act[r : r + RC, lanes] = a.astype(bf16)
            if slope is not None:
                slope[r : r + RC, lanes] = s

    lane_loop(width, body)


def rows_before(v, halo, row, width):
    if row:
        return v[row - 16 : row, :width].astype(f32)[16 - PAD :]
    return halo[...]


def prompt_state_kernel(
    place, v, halo, dt_all, masks, wb, hp, start, weight, step, beyond, ext, act, acc
):
    rows = v.shape[0]
    width = start.shape[1]
    first = place[0, 1]
    ind = indicator(place[0, 0] * HG, width)
    later = triangle(RB, lambda i, j: j > i)
    rate = -jnp.exp(hp[0:1])
    ahead = jnp.zeros((1, LANES), f32)
    slopes = jnp.zeros((1, LANES), f32)
    for row in range(0, dt_all.shape[0], RB):
        s = softplus(dt_all[row : row + RB].astype(f32) + hp[1:2])
        position = row + lax.broadcasted_iota(jnp.int32, s.shape, 0)
        past = position >= first + rows
        sig = sigmoid(dt_all[row : row + RB].astype(f32) + hp[1:2])
        ahead = ahead + rate * jnp.sum(jnp.where(past, s, 0.0), axis=0, keepdims=True)
        slopes = slopes + rate * jnp.sum(jnp.where(past, sig, 0.0), axis=0, keepdims=True)
    beyond[...] = jnp.zeros_like(beyond)
    beyond[0:1] = ahead
    beyond[1:2] = slopes
    acc[...] = jnp.zeros_like(acc)
    for row in range(rows - RB, -1, -RB):
        at = pl.ds(pl.multiple_of(first + row, RB), RB)
        s = softplus(dt_all[at, :].astype(f32) + hp[1:2])
        logd = rate * s
        after = tri_sum(later, logd) + ahead
        ahead = ahead + jnp.sum(logd, axis=0, keepdims=True)
        w = masks[row : row + RB, K - 1 : K] * jnp.exp(after) * s
        step[row : row + RB] = s
        weight[row : row + RB] = w
        ext[0:PAD] = rows_before(v, halo, row, width + N)
        prompt_conv(v, masks, wb, ext, act, None, row, width + N)
        wx = (act[:, :width].astype(f32) * expand(w, ind)).astype(bf16)
        acc[...] += dot(act[:, width:].astype(f32).T.astype(bf16), wx)
    start[...] = acc[...].astype(bf16)


def prompt_grad_kernel(
    count, place, v, halo, dt_mine, masks, wb, hp, weight, step, beyond, *refs
):
    states = refs[:count]
    grad, grad_h, ext, act, slope, g_s, d_s, sums = refs[count:]
    rows = v.shape[0]
    width = g_s.shape[1]
    ind = indicator(place[0, 0] * HG, width)
    earlier = triangle(RB, lambda i, j: j < i)
    total = states[0][...].astype(f32)
    for k in range(1, count):
        total = total + states[k][...].astype(f32)
    g_s[...] = total.astype(bf16)
    behind = jnp.zeros((1, LANES), f32)
    rate = -jnp.exp(hp[0:1])
    d_rate = jnp.zeros((1, LANES), f32)
    d_bias = jnp.zeros((1, LANES), f32)
    sums[...] = jnp.zeros_like(sums)
    for row in range(0, rows, RB):
        ext[0:PAD] = rows_before(v, halo, row, width + N)
        prompt_conv(v, masks, wb, ext, act, slope, row, width + N)
        w_e = expand(weight[row : row + RB], ind)
        t = dot(act[:, width:], g_s[...])
        wx = (act[:, :width].astype(f32) * w_e).astype(bf16)
        d_s[:, :width] = t * w_e
        d_s[:, width:] = dot(wx, g_s[...], NT)
        z_hi, z_lo = halves(wx.astype(f32) * t)
        q = head_sums(z_hi, z_lo, ind)
        d_log = tri_sum(earlier, q) + behind
        behind = behind + jnp.sum(q, axis=0, keepdims=True)
        s = step[row : row + RB]
        d_step = q / s + rate * d_log
        sig = sigmoid(dt_mine[row : row + RB].astype(f32) + hp[1:2])
        d_rate = d_rate + jnp.sum(d_log * rate * s, axis=0, keepdims=True)
        d_bias = d_bias + jnp.sum(d_step * sig, axis=0, keepdims=True)

        def back(lanes):
            acc = [jnp.zeros((8, LANES), f32) for _ in range(K + 1)]
            for r in range(0, RB, RC):
                d = d_s[r : r + RC, lanes] * slope[r : r + RC, lanes]
                taps = taps_of(ext, lanes, r, RC)
                for k in range(K):
                    part = d * taps[k]
                    if k < K - 1:
                        part = part * masks[pl.ds(row + r, RC), k : k + 1]
                    acc[k] = acc[k] + fold8(part)
                acc[K] = acc[K] + fold8(d)
            for k in range(K + 1):
                sums[k : k + 1, lanes] += jnp.sum(acc[k], axis=0, keepdims=True)

        lane_loop(width + N, back)
    grad[...] = sums[...]
    grad_h[...] = jnp.zeros_like(grad_h)
    grad_h[0:1] = d_rate + behind * beyond[0:1]
    grad_h[1:2] = d_bias + behind * beyond[1:2]


def add_kernel(count, *refs):
    total = refs[0][...].astype(f32)
    for k in range(1, count):
        total = total + refs[k][...].astype(f32)
    refs[-1][...] = total.astype(bf16)


def params(*semantics):
    return pltpu.CompilerParams(
        vmem_limit_bytes=VMEM_MIB * 2**20, dimension_semantics=semantics or None
    )


SMEM = pl.BlockSpec(memory_space=pltpu.SMEM)


def whole(shape):
    return pl.BlockSpec(shape, lambda *_: (0,) * len(shape))


def sds(shape, dtype):
    return jax.ShapeDtypeStruct(shape, dtype)


def response_steps(length, dt, hp):
    rows = dt.shape[0]
    square = sds((rows, H), f32)
    return pl.pallas_call(
        steps_kernel,
        out_shape=(square, square, sds((H, rows), f32), square),
        in_specs=[SMEM, pl.BlockSpec(), pl.BlockSpec()],
        compiler_params=params(),
        name="resp_steps",
    )(length, dt, hp)


def response_state(scale, u, tail, wb, dy, decay_in):
    rows = u.shape[0]
    c_at = lambda g: (0, XC // N + G + g)
    g_at = lambda g: (0, g)
    return pl.pallas_call(
        resp_state_kernel,
        grid=(G,),
        in_specs=[
            SMEM,
            pl.BlockSpec((rows, N), c_at),
            pl.BlockSpec((PAD, N), c_at),
            pl.BlockSpec((PAD, N), c_at),
            pl.BlockSpec((rows, GX), g_at),
            whole((rows, H)),
        ],
        out_specs=[
            pl.BlockSpec((1, N, GX), lambda g: (g, 0, 0)),
            pl.BlockSpec((rows, GX), g_at),
            pl.BlockSpec((rows, N), g_at),
        ],
        out_shape=(sds((G, N, GX), bf16), sds((rows, XC), bf16), sds((rows, G * N), bf16)),
        scratch_shapes=[pltpu.VMEM((PAD + rows, N), f32)],
        compiler_params=params("arbitrary"),
        cost_estimate=pl.CostEstimate(
            flops=2 * rows * N * XC, bytes_accessed=14 * 2**20, transcendentals=rows * G * N
        ),
        name="resp_state",
    )(scale, u, tail, wb, dy, decay_in)


def response_mid(
    g, length, u, tail, wb, c_act, dy, step, cum, cum4, cum_t4, skip, earlier_out, so_far
):
    rows = u.shape[0]
    half = rows // 2
    x_at = lambda i: (0, g)
    b_at = lambda i: (0, XC // N + g)
    sums = (2 * rows + PAD, H)
    v = pltpu.VMEM
    anywhere = pl.BlockSpec(memory_space=pl.ANY)
    return pl.pallas_call(
        functools.partial(resp_mid_kernel, g),
        grid=(1,),
        in_specs=[
            SMEM,
            pl.BlockSpec((rows, GX), x_at),
            pl.BlockSpec((rows, N), b_at),
            pl.BlockSpec((PAD, GX), x_at),
            pl.BlockSpec((PAD, N), b_at),
            pl.BlockSpec((PAD, GX), x_at),
            pl.BlockSpec((PAD, N), b_at),
            pl.BlockSpec((rows, N), x_at),
            pl.BlockSpec((rows, GX), x_at),
            whole((rows, H)),
            whole((rows, H)),
            pl.BlockSpec((1, rows, HG), lambda i: (g, 0, 0)),
            pl.BlockSpec((1, HG, rows), lambda i: (g, 0, 0)),
            pl.BlockSpec((1, GX), x_at),
            anywhere,
        ]
        + ([anywhere] * 3 + [whole(sums)] if so_far else []),
        out_specs=[
            pl.BlockSpec((PAD, GX), x_at),
            pl.BlockSpec((PAD, N), x_at),
            pl.BlockSpec((rows, N), x_at),
            whole(sums),
        ],
        out_shape=(
            sds((PAD, XC), f32),
            sds((PAD, G * N), f32),
            sds((rows, G * N), f32),
            sds(sums, f32),
        ),
        input_output_aliases={15 + k: k for k in range(3)} if so_far else {},
        scratch_shapes=[
            v((PAD + rows, GX), f32),
            v((PAD + rows, N), f32),
            v((rows, GX), bf16),
            v((rows, GX), bf16),
            v((rows, N), bf16),
            v((rows, GX), bf16),
            v((rows, GX), f32),
            v((rows, N), f32),
            v((rows, GX), f32),
            v((rows, GX), f32),
            v((rows, GX), f32),
            v((half, GX), bf16),
            v((half, GX), bf16),
            v((half, GX), f32),
            v((half, GX), f32),
            v((half, GX), f32),
            v((rows, GX), bf16),
            v((rows, GX), bf16),
            v((PAD, GX), f32),
        ],
        compiler_params=params("arbitrary"),
        cost_estimate=pl.CostEstimate(
            flops=8 * 2**30, bytes_accessed=3 * 2**20, transcendentals=rows * half * HG
        ),
        name="resp_mid",
    )(
        length, u, u, tail, tail, wb, wb, c_act, dy, step, cum, cum4, cum_t4, skip, earlier_out,
        *so_far,
    )


def response_end(
    tiles, place, scale, u, tail, wb, c_act, weighted, start, dc, sums, step, dt, hp, grads
):
    rows = u.shape[0]
    c_at = lambda g: (0, XC // N + G + g)
    g_at = lambda g: (0, g)
    v = pltpu.VMEM
    return pl.pallas_call(
        resp_end_kernel,
        grid=(G,),
        in_specs=[
            SMEM,
            SMEM,
            pl.BlockSpec((rows, N), c_at),
            pl.BlockSpec((PAD, N), c_at),
            pl.BlockSpec((PAD, N), c_at),
            pl.BlockSpec((rows, N), g_at),
            pl.BlockSpec((rows, GX), g_at),
            pl.BlockSpec((1, N, GX), lambda g: (g, 0, 0)),
            pl.BlockSpec((rows, N), g_at),
        ]
        + [whole(a.shape) for a in (sums, step, dt, hp, *grads)],
        out_specs=whole((tiles, PAD, LANES)),
        out_shape=sds((tiles, PAD, LANES), f32),
        scratch_shapes=[
            v((PAD + rows, N), f32),
            v((rows, N), bf16),
            v((rows, N), f32),
            v((rows, H), f32),
            v((PAD, N), f32),
        ],
        compiler_params=params("arbitrary"),
        cost_estimate=pl.CostEstimate(
            flops=4 * rows * N * XC, bytes_accessed=12 * 2**20, transcendentals=rows * G * N
        ),
        name="resp_end",
    )(place, scale, u, tail, wb, c_act, weighted, start, dc, sums, step, dt, hp, *grads)


def unpack(packed):
    width = HEAD_TILE * LANES
    return pl.pallas_call(
        unpack_kernel,
        out_shape=(sds((K, width), f32), sds((1, width), f32), sds((3, H), f32)),
        compiler_params=params(),
        name="unpack",
    )(packed)


def add_states(terms, earlier_out, copies=None):
    if not isinstance(terms, list):
        blocks = [
            pl.BlockSpec((None, terms.shape[1] // 4, terms.shape[2]), lambda i, *_, k=k: (k, i, 0))
            for k in range(terms.shape[0])
        ]
        terms = [terms] * terms.shape[0]
    else:
        blocks = None
    rows, width = terms[0].shape[-2:]
    part = rows // 4
    block = pl.BlockSpec((part, width), lambda i, *_: (i, 0))
    blocks = blocks or [block] * len(terms)
    if copies is None:
        grid, out, out_shape = (4,), block, (rows, width)
    else:
        grid = (4, copies)
        out = pl.BlockSpec((None, part, width), lambda i, j: (j, i, 0))
        out_shape = (copies, rows, width)
    size = rows * width
    return pl.pallas_call(
        functools.partial(add_kernel, len(terms)),
        grid=grid,
        in_specs=blocks + [pl.BlockSpec(memory_space=pl.ANY)],
        out_specs=out,
        out_shape=sds(out_shape, bf16),
        compiler_params=params(*["arbitrary"] * len(grid)),
        cost_estimate=pl.CostEstimate(
            flops=size * len(terms), bytes_accessed=2 * size * (len(terms) + 1), transcendentals=0
        ),
        name="add_states",
    )(*terms, earlier_out)


def prompt_state(place, v, halo, dt_all, masks, wb, hp):
    rows = v.shape[0]
    width = v.shape[1] - N
    s = pltpu.VMEM
    return pl.pallas_call(
        prompt_state_kernel,
        in_specs=[SMEM] + [pl.BlockSpec()] * 6,
        out_shape=(
            sds((N, width), bf16),
            sds((rows, LANES), f32),
            sds((rows, LANES), f32),
            sds((PAD, LANES), f32),
        ),
        scratch_shapes=[
            s((PAD + RB, width + N), f32),
            s((RB, width + N), bf16),
            s((N, width), f32),
        ],
        compiler_params=params(),
        cost_estimate=pl.CostEstimate(
            flops=2 * rows * N * width, bytes_accessed=4 * 2**20, transcendentals=rows * width
        ),
        name="prompt_state",
    )(place, v, halo, dt_all, masks, wb, hp)


def prompt_grad(place, v, halo, dt_mine, masks, wb, hp, weight, step, beyond, states):
    rows = v.shape[0]
    width = v.shape[1] - N
    s = pltpu.VMEM
    return pl.pallas_call(
        functools.partial(prompt_grad_kernel, len(states)),
        in_specs=[SMEM] + [pl.BlockSpec()] * (9 + len(states)),
        out_shape=(sds((PAD, width + N), f32), sds((PAD, LANES), f32)),
        scratch_shapes=[
            s((PAD + RB, width + N), f32),
            s((RB, width + N), bf16),
            s((RB, width + N), f32),
            s((N, width), bf16),
            s((RB, width + N), f32),
            s((PAD, width + N), f32),
        ],
        compiler_params=params(),
        cost_estimate=pl.CostEstimate(
            flops=4 * rows * N * width, bytes_accessed=8 * 2**20, transcendentals=rows * width
        ),
        name="prompt_grad",
    )(place, v, halo, dt_mine, masks, wb, hp, weight, step, beyond, *states)


def doc_number(starts, positions):
    return jnp.sum((starts[None, :] <= positions[:, None]).astype(jnp.int32), axis=1)


def prompt_masks(starts, rows):
    positions = jnp.arange(rows, dtype=jnp.int32)
    docs = doc_number(starts, positions)
    same = [doc_number(starts, positions - (K - 1 - k)) == docs for k in range(K - 1)]
    columns = jnp.stack(same + [docs == docs[rows - 1]], axis=1).astype(f32)
    return jnp.pad(columns, ((0, 0), (0, PAD - K)))


def pad_rows(a):
    return jnp.pad(a, ((0, PAD - a.shape[0]), (0, 0)))


def to_all(block, axes, devices, groups=None):
    copies = jnp.broadcast_to(block[None], (devices,) + block.shape)
    return lax.all_to_all(copies, axes, 0, 0, axis_index_groups=groups)


def sum_over_all(packed, axes, devices):
    slices = packed.reshape((devices, packed.shape[0] // devices) + packed.shape[1:])
    mine = jnp.sum(lax.all_to_all(slices, axes, 0, 0), axis=0)
    return to_all(mine, axes, devices).reshape(packed.shape)


def shards(
    prompt_in, prompt_dt, doc_starts, resp_in, resp_dt, resp_len, upstream, reward,
    conv_w, conv_b, head_params,
):
    n = lax.axis_size("resp")
    me = lax.axis_index("resp")
    clusters = n // G
    mine = me % G
    cluster = me // G
    inside = [list(range(c * G, c * G + G)) for c in range(clusters)]
    block = prompt_in.shape[1]
    slots = resp_in.shape[2]
    rows_in, dt_in = prompt_in[0], prompt_dt[0]
    u, dt, dy = resp_in[0, 0], resp_dt[0, 0], upstream[0, 0]

    r = reward[0, 0]
    r_hi = r.astype(bf16)
    r_mid = (r - r_hi.astype(f32)).astype(bf16)
    r_lo = (r - r_hi.astype(f32) - r_mid.astype(f32)).astype(bf16)
    tail_size = (K - 1) * rows_in.shape[1] // LANES
    small = jnp.concatenate(
        [
            rows_in[block - K + 1 :].reshape(tail_size, LANES),
            dt_in,
            jnp.broadcast_to(
                jnp.stack([r_hi, r_mid, r_lo, jnp.zeros_like(r_lo)])[:, None], (4, LANES)
            ),
            jnp.zeros((12, LANES), bf16),
        ]
    )
    small = to_all(small, "resp", n)
    wb = pad_rows(jnp.concatenate([conv_w, conv_b[None]], axis=0))
    hp = pad_rows(head_params)

    x_parts = rows_in[:, :XC].reshape(block, G, GX).transpose(1, 0, 2)
    b_parts = rows_in[:, XC : XC + G * N].reshape(block, G, N).transpose(1, 0, 2)
    parts = jnp.concatenate([x_parts, b_parts], axis=2)
    parts, small = lax.optimization_barrier((parts, small))
    v = lax.all_to_all(parts, "resp", 0, 0, axis_index_groups=inside)
    v = v.reshape(G * block, GX + N)

    def own_channels(a):
        return jnp.concatenate(
            [
                lax.dynamic_slice(a, (0, mine * GX), (PAD, GX)),
                lax.dynamic_slice(a, (0, XC + mine * N), (PAD, N)),
            ],
            axis=1,
        )

    def last_rows(device):
        rows = lax.dynamic_index_in_dim(small, device, 0, False)[:tail_size]
        return jnp.pad(rows.reshape(K - 1, -1).astype(f32), ((PAD - K + 1, 0), (0, 0)))

    tail = last_rows(n - 1)
    halo = own_channels(last_rows(jnp.maximum(cluster * G - 1, 0)))
    dt_all = small[:, tail_size : tail_size + block].reshape(n * block, H)
    dt_mine = lax.dynamic_slice(dt_all, (cluster * G * block, 0), (G * block, H))
    at_reward = tail_size + block
    rewards = jnp.sum(small[:, at_reward : at_reward + 3, 0].astype(f32), axis=1)
    scale = ((r - jnp.sum(rewards) / n) / slots).reshape(1, 1)
    masks = lax.dynamic_slice(
        prompt_masks(doc_starts[0], n * block), (cluster * G * block, 0), (G * block, PAD)
    )
    wb_mine = own_channels(wb)
    place = jnp.stack([mine, cluster * G * block]).astype(jnp.int32).reshape(1, 2)

    length = resp_len.astype(jnp.int32)
    step, cum, cum_t, decay_in = response_steps(length, dt, hp)
    d_states, weighted, c_act = response_state(scale, u, tail, wb, dy, decay_in)
    d_states = lax.all_to_all(d_states, "resp", 0, 0, axis_index_groups=inside)

    cum4 = cum.reshape(slots, G, HG).transpose(1, 0, 2)
    skip = jnp.repeat(head_params[2], PS)[None, :]

    def mid(g, earlier_out, so_far=()):
        return response_mid(
            g, length, u, tail, wb, c_act, dy, step, cum, cum4,
            cum_t.reshape(G, HG, slots), skip, earlier_out, so_far,
        )

    def across(part):
        routes = [[(i, (i + c * G) % n) for i in range(n)] for c in range(1, clusters)]
        return [part] + [lax.ppermute(part, "resp", route) for route in routes]

    part, weight, p_step, beyond = prompt_state(place, v, halo, dt_all, masks, wb_mine, hp)
    parts_of_start = across(part)
    grads = mid(0, weight)
    grads = mid(1, weight, grads)
    part = add_states(d_states, grads[3])
    parts_of_grad = across(part)
    start = add_states(parts_of_start, part, copies=G)
    grads = mid(2, start, grads)
    start = lax.all_to_all(start, "resp", 0, 0, axis_index_groups=inside)
    grad_x, grad_b, dc, sums = mid(3, weight, grads)
    p_grad, p_heads = prompt_grad(
        place, v, halo, dt_mine, masks, wb_mine, hp, weight, p_step, beyond, parts_of_grad
    )

    axes = ("group", "resp")
    devices = lax.axis_size(axes)
    tiles = devices * -(-(HEAD_TILE + 1) // devices)
    packed = response_end(
        tiles, place, scale, u, tail, wb, c_act, weighted, start, dc, sums, step, dt, hp,
        (grad_x, grad_b, p_grad, p_heads),
    )
    grad_w, grad_bias, heads = unpack(sum_over_all(packed, axes, devices))
    return grad_w, grad_bias.reshape(-1), heads


def solution(mesh):
    in_specs = (
        P("group", "resp", None),
        P("group", "resp", None),
        P("group", None),
        P("group", "resp", None, None),
        P("group", "resp", None, None),
        P("group", "resp"),
        P("group", "resp", None, None),
        P("group", "resp"),
        P(),
        P(),
        P(),
    )
    out_specs = (P(), P(), P())
    return jax.shard_map(shards, mesh=mesh, in_specs=in_specs, out_specs=out_specs, check_vma=False)
```

```python
import functools

import jax
import jax.numpy as jnp
from jax import lax
from jax.experimental import pallas as pl
from jax.experimental.pallas import tpu as pltpu
from jax.sharding import PartitionSpec as P

H = 128
PS = 64
N = 256
G = 4
K = 4
HG = H // G
XC = H * PS
GX = HG * PS
LANES = 128
PAD = 8
VMEM_MIB = 63

f32 = jnp.float32
bf16 = jnp.bfloat16

NN = (((1,), (0,)), ((), ()))
NT = (((1,), (1,)), ((), ()))


def dot(a, b, dims=NN, precision=None):
    return lax.dot_general(a, b, dims, precision=precision, preferred_element_type=f32)


def halves(v):
    hi = v.astype(bf16)
    return hi, (v - hi.astype(f32)).astype(bf16)


def indicator(first, width):
    row = lax.broadcasted_iota(jnp.int32, (LANES, width), 0)
    head = lax.shift_right_logical(lax.broadcasted_iota(jnp.int32, (LANES, width), 1), 6)
    return jnp.where(row - first == head, 1.0, 0.0).astype(bf16)


def expand(v, ind):
    hi, lo = halves(v)
    return dot(hi, ind) + dot(lo, ind)


def head_sums(z_hi, z_lo, ind):
    return dot(z_hi, ind, NT) + dot(z_lo, ind, NT)


def triangle(n, keep):
    i = lax.broadcasted_iota(jnp.int32, (n, n), 0)
    j = lax.broadcasted_iota(jnp.int32, (n, n), 1)
    return jnp.where(keep(i, j), 1.0, 0.0).astype(f32)


def tri_sum(tri, v):
    return dot(tri, v, precision=lax.Precision.HIGHEST)


def softplus(z):
    return jnp.maximum(z, 0.0) + jnp.log1p(jnp.exp(-jnp.abs(z)))


def sigmoid(z):
    return 0.5 * jnp.tanh(0.5 * z) + 0.5


def taps_of(ext, lanes, row, rows):
    return [ext[pl.ds(PAD - K + 1 + k + row, rows), lanes] for k in range(K)]


def conv_pre(taps, wb, masks=None):
    total = wb[K : K + 1] + wb[K - 1 : K] * taps[K - 1]
    for k in range(K - 1):
        term = wb[k : k + 1] * taps[k]
        if masks is not None:
            term = term * masks[k]
        total = total + term
    return total


def act_and_slope(pre):
    sig = sigmoid(pre)
    act = pre * sig
    return act, sig + act * (1.0 - sig)


def fold8(v):
    return jnp.sum(v.reshape(v.shape[0] // 8, 8, v.shape[1]), axis=0)


def as_rows(parts):
    row = lax.broadcasted_iota(jnp.int32, (PAD, LANES), 0)
    total = jnp.zeros((PAD, LANES), f32)
    for k, part in enumerate(parts):
        total = total + jnp.where(row == k, jnp.sum(part, axis=0, keepdims=True), 0.0)
    return total


def lane_loop(width, body, step=LANES):
    def one(i, _):
        body(pl.ds(pl.multiple_of(i * step, step), step))
        return 0

    lax.fori_loop(0, width // step, one, 0)


RC = 64


def conv_forward(u, tail, wb, ext, act, slope, rows, width):
    def body(lanes):
        ext[0:PAD, lanes] = tail[:, lanes]
        ext[PAD : PAD + rows, lanes] = u[:, lanes].astype(f32)
        w = wb[:, lanes]
        for r in range(0, rows, RC):
            a, s = act_and_slope(conv_pre(taps_of(ext, lanes, r, RC), w))
            act[r : r + RC, lanes] = a.astype(bf16)
            if slope is not None:
                slope[r : r + RC, lanes] = s

    lane_loop(width, body)


def conv_backward(ext, slope, lanes, cotangent, grad, rows):
    sums = [jnp.zeros((8, LANES), f32) for _ in range(K + 1)]
    for r in range(0, rows, RC):
        d = cotangent(r) * slope[r : r + RC, lanes]
        taps = taps_of(ext, lanes, r, RC)
        for k in range(K):
            sums[k] = sums[k] + fold8(d * taps[k])
        sums[K] = sums[K] + fold8(d)
    grad[:, lanes] = as_rows(sums)


def steps_kernel(len_ref, dt, hp, step, cum, cum_t, decay_in):
    rows = dt.shape[0]
    s = softplus(dt[...].astype(f32) + hp[1:2])
    logd = -jnp.exp(hp[0:1]) * s
    c = tri_sum(triangle(rows, lambda i, j: i >= j), logd)
    step[...] = s
    cum[...] = c
    cum_t[...] = c.T
    t = lax.broadcasted_iota(jnp.int32, c.shape, 0)
    decay_in[...] = jnp.where(t < len_ref[0, 0], jnp.exp(c), 0.0)


def resp_state_kernel(adv, u_c, tail_c, wb_c, dy, decay_in, state, weighted, c_out, ext):
    g = pl.program_id(0)
    rows, width = dy.shape
    conv_forward(u_c, tail_c, wb_c, ext, c_out, None, rows, N)
    c_t = c_out[...].astype(f32).T.astype(bf16)
    a = (dy[...].astype(f32) * expand(decay_in[...], indicator(g * HG, width))).astype(bf16)
    weighted[...] = a
    state[0] = (dot(c_t, a) * adv[0, 0]).astype(bf16)


def resp_mid_kernel(
    g, len_ref, u_x, u_b, tail_x, tail_b, wb_x, wb_b, c_act, dy, step, cum, cum4, cum_t4, skip,
    earlier_out, *refs,
):
    if g:
        sums_in, refs = refs[3], refs[4:]
    (
    grad_x, grad_b, dc, sums_out,
    ext, ext_b, x_s, xs_s, b_s, dym, slope, slope_b, step_e, y_s, t_s,
    a1, bm, sw_e, u_off, y_off, z_hi, z_lo, d_skip,
    ) = refs
    rows = u_x.shape[0]
    half = rows // 2
    conv_forward(u_x, tail_x, wb_x, ext, x_s, slope, rows, GX)
    conv_forward(u_b, tail_b, wb_b, ext_b, b_s, slope_b, rows, N)
    ind = indicator(g * HG, GX)
    step_e[...] = expand(step[...], ind)
    cum_v = cum[...]
    mid = cum_v[half - 1 : half]
    sw_e[...] = expand(jnp.exp(mid - cum_v[:half]) * step[:half], ind)
    y_off[...] = expand(jnp.exp(cum_v[half:] - mid), ind)
    live = jnp.where(lax.broadcasted_iota(jnp.int32, (rows, LANES), 0) < len_ref[0, 0], 1.0, 0.0)

    def prepare(lanes):
        d = dy[:, lanes].astype(f32) * live
        dym[:, lanes] = d.astype(bf16)
        x = x_s[:, lanes].astype(f32)
        xs_s[:, lanes] = (x * step_e[:, lanes]).astype(bf16)
        bm[:, lanes] = (x[:half] * sw_e[:, lanes]).astype(bf16)
        a1[:, lanes] = (d[half:] * y_off[:, lanes]).astype(bf16)

    lane_loop(GX, prepare)

    c_v, b_v = c_act[...], b_s[...]
    c0, c1, b0, b1 = c_v[:half], c_v[half:], b_v[:half], b_v[half:]
    i = lax.broadcasted_iota(jnp.int32, (half, half), 0)
    j = lax.broadcasted_iota(jnp.int32, (half, half), 1)
    lane = lax.broadcasted_iota(jnp.int32, (half, LANES), 1)
    first = jnp.where(lane < PS, 1.0, 0.0).astype(bf16)
    second = jnp.where(lane >= PS, 1.0, 0.0).astype(bf16)

    y_off[...] = dot(dot(c1, b0, NT).astype(bf16), bm[...])
    u_off[...] = dot(dot(b0, c1, NT).astype(bf16), a1[...])
    d10 = dot(a1[...], bm[...], NT)

    d_diag = []
    for q, (c_q, b_q) in enumerate(((c0, b0), (c1, b1))):
        r = slice(q * half, (q + 1) * half)
        lower = jnp.where(i >= j, dot(c_q, b_q, NT), 0.0)
        upper = jnp.where(j >= i, dot(b_q, c_q, NT), 0.0)
        d_sc = jnp.zeros((half, half), f32)
        for p in range(HG // 2):
            lanes = slice(p * LANES, (p + 1) * LANES)
            xs_p, dy_p = xs_s[r, lanes], dym[r, lanes]
            xb = jnp.concatenate([xs_p * first, xs_p * second], axis=0)
            dyb = jnp.concatenate([dy_p * first, dy_p * second], axis=0)
            d_m = dot(dy_p, xb, NT)
            mats, mats_t = [], []
            for a in range(2):
                h = 2 * p + a
                gap = jnp.exp(-jnp.abs(cum4[0, r, h : h + 1] - cum_t4[0, h : h + 1, r]))
                d_sc = d_sc + d_m[:, a * half : (a + 1) * half] * gap
                mats.append((gap * lower).astype(bf16))
                mats_t.append((gap * upper).astype(bf16))
            y_s[r, lanes] = dot(jnp.concatenate(mats, axis=1), xb)
            t_s[r, lanes] = dot(jnp.concatenate(mats_t, axis=1), dyb)
        d_diag.append(jnp.where(i >= j, d_sc, 0.0))

    d00, d11 = d_diag
    dc[:half] = dot(d00.astype(bf16), b0)
    dc[half:] = dot(d11.astype(bf16), b1) + dot(d10.astype(bf16), b0)
    db0 = dot(d00.T.astype(bf16), c0) + dot(d10.T.astype(bf16), c1)
    db1 = dot(d11.T.astype(bf16), c1)
    db = jnp.concatenate([db0, db1], axis=0)
    for k in range(N // LANES):
        lanes = slice(k * LANES, (k + 1) * LANES)
        conv_backward(ext_b, slope_b, lanes, lambda r: db[r : r + RC, lanes], grad_b, rows)

    def put(z, r, lanes):
        hi, lo = halves(z)
        z_hi[r : r + RC, lanes] = hi
        z_lo[r : r + RC, lanes] = lo

    def row_products(lanes):
        for r in range(0, rows, RC):
            z = dym[r : r + RC, lanes].astype(f32) * y_s[r : r + RC, lanes]
            if r >= half:
                o = r - half
                z = z + a1[o : o + RC, lanes].astype(f32) * y_off[o : o + RC, lanes]
            put(z, r, lanes)

    lane_loop(GX, row_products)
    row_sum = head_sums(z_hi[...], z_lo[...], ind)

    def finish(lanes):
        d_skips = jnp.zeros((8, LANES), f32)
        for r in range(0, rows, RC):
            t = t_s[r : r + RC, lanes]
            z = xs_s[r : r + RC, lanes].astype(f32) * t
            if r < half:
                z = z + bm[r : r + RC, lanes].astype(f32) * u_off[r : r + RC, lanes]
            put(z, r, lanes)
            d_skips = d_skips + fold8(
                dym[r : r + RC, lanes].astype(f32) * x_s[r : r + RC, lanes].astype(f32)
            )

        def cotangent(r):
            d = step_e[r : r + RC, lanes] * t_s[r : r + RC, lanes]
            d = d + skip[:, lanes] * dym[r : r + RC, lanes].astype(f32)
            if r < half:
                d = d + sw_e[r : r + RC, lanes] * u_off[r : r + RC, lanes]
            return d

        conv_backward(ext, slope, lanes, cotangent, grad_x, rows)
        d_skip[:, lanes] = d_skips

    lane_loop(GX, finish)
    col_sum = head_sums(z_hi[...], z_lo[...], ind)

    skip_sum = head_sums(*halves(d_skip[...]), ind)
    for at, part in ((0, row_sum), (rows, col_sum), (2 * rows, skip_sum)):
        span = slice(at, at + part.shape[0])
        sums_out[span] = sums_in[span] + part if g else part


X_TILES = XC // LANES
B_TILES = G * N // LANES
C_TILES = X_TILES + 2 * B_TILES
HEAD_TILE = (K + 1) * C_TILES // PAD


def tile(k):
    return slice(k * LANES, (k + 1) * LANES)


def resp_end_kernel(
    place, scale, u_c, tail_c, wb_c, c_act, weighted, start, dc, sums, step, dt, hp,
    grad_x, grad_b, p_grad, p_heads,
    packed, ext, c_s, slope, total, grad_c, tiles,
):
    g = pl.program_id(0)
    rows, width = weighted.shape
    conv_forward(u_c, tail_c, wb_c, ext, c_s, slope, rows, N)

    @pl.when(g == 0)
    def _():
        total[...] = sums[0:rows] - sums[rows : 2 * rows]

    a = weighted[...]
    z_hi, z_lo = halves(a.astype(f32) * dot(c_act[...], start[0]))
    total[...] += head_sums(z_hi, z_lo, indicator(g * HG, width))
    d = dc[...] + dot(a, start[0], NT)
    for k in range(N // LANES):
        conv_backward(ext, slope, tile(k), lambda r: d[r : r + RC, tile(k)], grad_c, rows)
        tiles[X_TILES + B_TILES + g * (N // LANES) + k] = grad_c[:, tile(k)] * scale[0, 0]

    @pl.when(g == pl.num_programs(0) - 1)
    def _():
        d_log = tri_sum(triangle(rows, lambda i, j: j >= i), total[...])
        rate = -jnp.exp(hp[0:1])
        s = step[...]
        d_step = sums[rows : 2 * rows] / s + rate * d_log
        sig = sigmoid(dt[...].astype(f32) + hp[1:2])
        heads = as_rows([d_log * rate * s, d_step * sig, sums[2 * rows :]])
        for k in range(X_TILES):
            tiles[k] = grad_x[:, tile(k)] * scale[0, 0]
        for k in range(B_TILES):
            tiles[X_TILES + k] = grad_b[:, tile(k)] * scale[0, 0]
        for k in range(width // LANES):
            tiles[place[0, 0] * (width // LANES) + k] += p_grad[:, tile(k)]
        for k in range(N // LANES):
            tiles[X_TILES + place[0, 0] * (N // LANES) + k] += p_grad[:, tile(width // LANES + k)]
        for k in range(K + 1):
            for at in range(C_TILES):
                row = k * C_TILES + at
                packed[row // PAD, row % PAD : row % PAD + 1] = tiles[at, k : k + 1]
        packed[HEAD_TILE] = heads * scale[0, 0] + p_heads[...]
        for k in range(HEAD_TILE + 1, packed.shape[0]):
            packed[k] = jnp.zeros((PAD, LANES), f32)


def unpack_kernel(packed, conv_w, conv_b, heads):
    for k in range(K + 1):
        for at in range(C_TILES):
            row = k * C_TILES + at
            part = packed[row // PAD, row % PAD : row % PAD + 1]
            if k < K:
                conv_w[k : k + 1, tile(at)] = part
            else:
                conv_b[:, tile(at)] = part
    heads[...] = packed[HEAD_TILE, 0:3]


RB = 256


def prompt_conv(v, masks, wb, ext, act, slope, row, width):
    def body(lanes):
        ext[PAD : PAD + RB, lanes] = v[pl.ds(row, RB), lanes].astype(f32)
        w = wb[:, lanes]
        for r in range(0, RB, RC):
            m = [masks[pl.ds(row + r, RC), k : k + 1] for k in range(K - 1)]
            a, s = act_and_slope(conv_pre(taps_of(ext, lanes, r, RC), w, m))
            act[r : r + RC, lanes] = a.astype(bf16)
            if slope is not None:
                slope[r : r + RC, lanes] = s

    lane_loop(width, body)


def rows_before(v, halo, row, width):
    if row:
        return v[row - 16 : row, :width].astype(f32)[16 - PAD :]
    return halo[...]


def prompt_state_kernel(
    place, v, halo, dt_all, masks, wb, hp, start, weight, step, beyond, ext, act, acc
):
    rows = v.shape[0]
    width = start.shape[1]
    first = place[0, 1]
    ind = indicator(place[0, 0] * HG, width)
    later = triangle(RB, lambda i, j: j > i)
    rate = -jnp.exp(hp[0:1])
    ahead = jnp.zeros((1, LANES), f32)
    slopes = jnp.zeros((1, LANES), f32)
    for row in range(0, dt_all.shape[0], RB):
        s = softplus(dt_all[row : row + RB].astype(f32) + hp[1:2])
        position = row + lax.broadcasted_iota(jnp.int32, s.shape, 0)
        past = position >= first + rows
        sig = sigmoid(dt_all[row : row + RB].astype(f32) + hp[1:2])
        ahead = ahead + rate * jnp.sum(jnp.where(past, s, 0.0), axis=0, keepdims=True)
        slopes = slopes + rate * jnp.sum(jnp.where(past, sig, 0.0), axis=0, keepdims=True)
    beyond[...] = jnp.zeros_like(beyond)
    beyond[0:1] = ahead
    beyond[1:2] = slopes
    acc[...] = jnp.zeros_like(acc)
    for row in range(rows - RB, -1, -RB):
        at = pl.ds(pl.multiple_of(first + row, RB), RB)
        s = softplus(dt_all[at, :].astype(f32) + hp[1:2])
        logd = rate * s
        after = tri_sum(later, logd) + ahead
        ahead = ahead + jnp.sum(logd, axis=0, keepdims=True)
        w = masks[row : row + RB, K - 1 : K] * jnp.exp(after) * s
        step[row : row + RB] = s
        weight[row : row + RB] = w
        ext[0:PAD] = rows_before(v, halo, row, width + N)
        prompt_conv(v, masks, wb, ext, act, None, row, width + N)
        wx = (act[:, :width].astype(f32) * expand(w, ind)).astype(bf16)
        acc[...] += dot(act[:, width:].astype(f32).T.astype(bf16), wx)
    start[...] = acc[...].astype(bf16)


def prompt_grad_kernel(
    count, place, v, halo, dt_mine, masks, wb, hp, weight, step, beyond, *refs
):
    states = refs[:count]
    grad, grad_h, ext, act, slope, g_s, d_s, sums = refs[count:]
    rows = v.shape[0]
    width = g_s.shape[1]
    ind = indicator(place[0, 0] * HG, width)
    earlier = triangle(RB, lambda i, j: j < i)
    total = states[0][...].astype(f32)
    for k in range(1, count):
        total = total + states[k][...].astype(f32)
    g_s[...] = total.astype(bf16)
    behind = jnp.zeros((1, LANES), f32)
    rate = -jnp.exp(hp[0:1])
    d_rate = jnp.zeros((1, LANES), f32)
    d_bias = jnp.zeros((1, LANES), f32)
    sums[...] = jnp.zeros_like(sums)
    for row in range(0, rows, RB):
        ext[0:PAD] = rows_before(v, halo, row, width + N)
        prompt_conv(v, masks, wb, ext, act, slope, row, width + N)
        w_e = expand(weight[row : row + RB], ind)
        t = dot(act[:, width:], g_s[...])
        wx = (act[:, :width].astype(f32) * w_e).astype(bf16)
        d_s[:, :width] = t * w_e
        d_s[:, width:] = dot(wx, g_s[...], NT)
        z_hi, z_lo = halves(wx.astype(f32) * t)
        q = head_sums(z_hi, z_lo, ind)
        d_log = tri_sum(earlier, q) + behind
        behind = behind + jnp.sum(q, axis=0, keepdims=True)
        s = step[row : row + RB]
        d_step = q / s + rate * d_log
        sig = sigmoid(dt_mine[row : row + RB].astype(f32) + hp[1:2])
        d_rate = d_rate + jnp.sum(d_log * rate * s, axis=0, keepdims=True)
        d_bias = d_bias + jnp.sum(d_step * sig, axis=0, keepdims=True)

        def back(lanes):
            acc = [jnp.zeros((8, LANES), f32) for _ in range(K + 1)]
            for r in range(0, RB, RC):
                d = d_s[r : r + RC, lanes] * slope[r : r + RC, lanes]
                taps = taps_of(ext, lanes, r, RC)
                for k in range(K):
                    part = d * taps[k]
                    if k < K - 1:
                        part = part * masks[pl.ds(row + r, RC), k : k + 1]
                    acc[k] = acc[k] + fold8(part)
                acc[K] = acc[K] + fold8(d)
            for k in range(K + 1):
                sums[k : k + 1, lanes] += jnp.sum(acc[k], axis=0, keepdims=True)

        lane_loop(width + N, back)
    grad[...] = sums[...]
    grad_h[...] = jnp.zeros_like(grad_h)
    grad_h[0:1] = d_rate + behind * beyond[0:1]
    grad_h[1:2] = d_bias + behind * beyond[1:2]


def add_kernel(count, grads, *refs):
    starts, (grad_sum, start) = refs[:count], refs[count + 1 :]
    grad_sum[...] = jnp.sum(grads[...].astype(f32), axis=0).astype(bf16)
    total = starts[0][...].astype(f32)
    for k in range(1, count):
        total = total + starts[k][...].astype(f32)
    total = total.astype(bf16)
    for k in range(start.shape[0]):
        start[k] = total


def params(*semantics):
    return pltpu.CompilerParams(
        vmem_limit_bytes=VMEM_MIB * 2**20, dimension_semantics=semantics or None
    )


SMEM = pl.BlockSpec(memory_space=pltpu.SMEM)


def whole(shape):
    return pl.BlockSpec(shape, lambda *_: (0,) * len(shape))


def sds(shape, dtype):
    return jax.ShapeDtypeStruct(shape, dtype)


def response_steps(length, dt, hp):
    rows = dt.shape[0]
    square = sds((rows, H), f32)
    return pl.pallas_call(
        steps_kernel,
        out_shape=(square, square, sds((H, rows), f32), square),
        in_specs=[SMEM, pl.BlockSpec(), pl.BlockSpec()],
        compiler_params=params(),
        name="resp_steps",
    )(length, dt, hp)


def response_state(scale, u, tail, wb, dy, decay_in):
    rows = u.shape[0]
    c_at = lambda g: (0, XC // N + G + g)
    g_at = lambda g: (0, g)
    return pl.pallas_call(
        resp_state_kernel,
        grid=(G,),
        in_specs=[
            SMEM,
            pl.BlockSpec((rows, N), c_at),
            pl.BlockSpec((PAD, N), c_at),
            pl.BlockSpec((PAD, N), c_at),
            pl.BlockSpec((rows, GX), g_at),
            whole((rows, H)),
        ],
        out_specs=[
            pl.BlockSpec((1, N, GX), lambda g: (g, 0, 0)),
            pl.BlockSpec((rows, GX), g_at),
            pl.BlockSpec((rows, N), g_at),
        ],
        out_shape=(sds((G, N, GX), bf16), sds((rows, XC), bf16), sds((rows, G * N), bf16)),
        scratch_shapes=[pltpu.VMEM((PAD + rows, N), f32)],
        compiler_params=params("arbitrary"),
        cost_estimate=pl.CostEstimate(
            flops=2 * rows * N * XC, bytes_accessed=14 * 2**20, transcendentals=rows * G * N
        ),
        name="resp_state",
    )(scale, u, tail, wb, dy, decay_in)


def response_mid(
    g, length, u, tail, wb, c_act, dy, step, cum, cum4, cum_t4, skip, earlier_out, so_far
):
    rows = u.shape[0]
    half = rows // 2
    x_at = lambda i: (0, g)
    b_at = lambda i: (0, XC // N + g)
    sums = (2 * rows + PAD, H)
    v = pltpu.VMEM
    anywhere = pl.BlockSpec(memory_space=pl.ANY)
    return pl.pallas_call(
        functools.partial(resp_mid_kernel, g),
        grid=(1,),
        in_specs=[
            SMEM,
            pl.BlockSpec((rows, GX), x_at),
            pl.BlockSpec((rows, N), b_at),
            pl.BlockSpec((PAD, GX), x_at),
            pl.BlockSpec((PAD, N), b_at),
            pl.BlockSpec((PAD, GX), x_at),
            pl.BlockSpec((PAD, N), b_at),
            pl.BlockSpec((rows, N), x_at),
            pl.BlockSpec((rows, GX), x_at),
            whole((rows, H)),
            whole((rows, H)),
            pl.BlockSpec((1, rows, HG), lambda i: (g, 0, 0)),
            pl.BlockSpec((1, HG, rows), lambda i: (g, 0, 0)),
            pl.BlockSpec((1, GX), x_at),
            anywhere,
        ]
        + ([anywhere] * 3 + [whole(sums)] if so_far else []),
        out_specs=[
            pl.BlockSpec((PAD, GX), x_at),
            pl.BlockSpec((PAD, N), x_at),
            pl.BlockSpec((rows, N), x_at),
            whole(sums),
        ],
        out_shape=(
            sds((PAD, XC), f32),
            sds((PAD, G * N), f32),
            sds((rows, G * N), f32),
            sds(sums, f32),
        ),
        input_output_aliases={15 + k: k for k in range(3)} if so_far else {},
        scratch_shapes=[
            v((PAD + rows, GX), f32),
            v((PAD + rows, N), f32),
            v((rows, GX), bf16),
            v((rows, GX), bf16),
            v((rows, N), bf16),
            v((rows, GX), bf16),
            v((rows, GX), f32),
            v((rows, N), f32),
            v((rows, GX), f32),
            v((rows, GX), f32),
            v((rows, GX), f32),
            v((half, GX), bf16),
            v((half, GX), bf16),
            v((half, GX), f32),
            v((half, GX), f32),
            v((half, GX), f32),
            v((rows, GX), bf16),
            v((rows, GX), bf16),
            v((PAD, GX), f32),
        ],
        compiler_params=params("arbitrary"),
        cost_estimate=pl.CostEstimate(
            flops=8 * 2**30, bytes_accessed=3 * 2**20, transcendentals=rows * half * HG
        ),
        name="resp_mid",
    )(
        length, u, u, tail, tail, wb, wb, c_act, dy, step, cum, cum4, cum_t4, skip, earlier_out,
        *so_far,
    )


def response_end(
    tiles, place, scale, u, tail, wb, c_act, weighted, start, dc, sums, step, dt, hp, grads
):
    rows = u.shape[0]
    c_at = lambda g: (0, XC // N + G + g)
    g_at = lambda g: (0, g)
    v = pltpu.VMEM
    return pl.pallas_call(
        resp_end_kernel,
        grid=(G,),
        in_specs=[
            SMEM,
            SMEM,
            pl.BlockSpec((rows, N), c_at),
            pl.BlockSpec((PAD, N), c_at),
            pl.BlockSpec((PAD, N), c_at),
            pl.BlockSpec((rows, N), g_at),
            pl.BlockSpec((rows, GX), g_at),
            pl.BlockSpec((1, N, GX), lambda g: (g, 0, 0)),
            pl.BlockSpec((rows, N), g_at),
        ]
        + [whole(a.shape) for a in (sums, step, dt, hp, *grads)],
        out_specs=whole((tiles, PAD, LANES)),
        out_shape=sds((tiles, PAD, LANES), f32),
        scratch_shapes=[
            v((PAD + rows, N), f32),
            v((rows, N), bf16),
            v((rows, N), f32),
            v((rows, H), f32),
            v((PAD, N), f32),
            v((C_TILES, PAD, LANES), f32),
        ],
        compiler_params=params("arbitrary"),
        cost_estimate=pl.CostEstimate(
            flops=4 * rows * N * XC, bytes_accessed=12 * 2**20, transcendentals=rows * G * N
        ),
        name="resp_end",
    )(place, scale, u, tail, wb, c_act, weighted, start, dc, sums, step, dt, hp, *grads)


def unpack(packed):
    width = C_TILES * LANES
    return pl.pallas_call(
        unpack_kernel,
        out_shape=(sds((K, width), f32), sds((1, width), f32), sds((3, H), f32)),
        compiler_params=params(),
        name="unpack",
    )(packed)


def add_states(grads, starts, earlier_out):
    copies, rows, width = grads.shape
    part = rows // 4
    one = pl.BlockSpec((part, width), lambda i: (i, 0))
    many = pl.BlockSpec((copies, part, width), lambda i: (0, i, 0))
    return pl.pallas_call(
        functools.partial(add_kernel, len(starts)),
        grid=(4,),
        in_specs=[many] + [one] * len(starts) + [pl.BlockSpec(memory_space=pl.ANY)],
        out_specs=[one, many],
        out_shape=(sds((rows, width), bf16), sds(grads.shape, bf16)),
        compiler_params=params("arbitrary"),
        cost_estimate=pl.CostEstimate(
            flops=8 * rows * width, bytes_accessed=22 * rows * width, transcendentals=0
        ),
        name="add_states",
    )(grads, *starts, earlier_out)


def prompt_state(place, v, halo, dt_all, masks, wb, hp):
    rows = v.shape[0]
    width = v.shape[1] - N
    s = pltpu.VMEM
    return pl.pallas_call(
        prompt_state_kernel,
        in_specs=[SMEM] + [pl.BlockSpec()] * 6,
        out_shape=(
            sds((N, width), bf16),
            sds((rows, LANES), f32),
            sds((rows, LANES), f32),
            sds((PAD, LANES), f32),
        ),
        scratch_shapes=[
            s((PAD + RB, width + N), f32),
            s((RB, width + N), bf16),
            s((N, width), f32),
        ],
        compiler_params=params(),
        cost_estimate=pl.CostEstimate(
            flops=2 * rows * N * width, bytes_accessed=4 * 2**20, transcendentals=rows * width
        ),
        name="prompt_state",
    )(place, v, halo, dt_all, masks, wb, hp)


def prompt_grad(place, v, halo, dt_mine, masks, wb, hp, weight, step, beyond, states):
    rows = v.shape[0]
    width = v.shape[1] - N
    s = pltpu.VMEM
    return pl.pallas_call(
        functools.partial(prompt_grad_kernel, len(states)),
        in_specs=[SMEM] + [pl.BlockSpec()] * (9 + len(states)),
        out_shape=(sds((PAD, width + N), f32), sds((PAD, LANES), f32)),
        scratch_shapes=[
            s((PAD + RB, width + N), f32),
            s((RB, width + N), bf16),
            s((RB, width + N), f32),
            s((N, width), bf16),
            s((RB, width + N), f32),
            s((PAD, width + N), f32),
        ],
        compiler_params=params(),
        cost_estimate=pl.CostEstimate(
            flops=4 * rows * N * width, bytes_accessed=8 * 2**20, transcendentals=rows * width
        ),
        name="prompt_grad",
    )(place, v, halo, dt_mine, masks, wb, hp, weight, step, beyond, *states)


def doc_number(starts, positions):
    return jnp.sum((starts[None, :] <= positions[:, None]).astype(jnp.int32), axis=1)


def prompt_masks(starts, rows):
    positions = jnp.arange(rows, dtype=jnp.int32)
    docs = doc_number(starts, positions)
    same = [doc_number(starts, positions - (K - 1 - k)) == docs for k in range(K - 1)]
    columns = jnp.stack(same + [docs == docs[rows - 1]], axis=1).astype(f32)
    return jnp.pad(columns, ((0, 0), (0, PAD - K)))


def pad_rows(a):
    return jnp.pad(a, ((0, PAD - a.shape[0]), (0, 0)))


def to_all(block, axes, devices, groups=None):
    copies = jnp.broadcast_to(block[None], (devices,) + block.shape)
    return lax.all_to_all(copies, axes, 0, 0, axis_index_groups=groups)


def sum_over_all(packed, axes, devices):
    slices = packed.reshape((devices, packed.shape[0] // devices) + packed.shape[1:])
    mine = jnp.sum(lax.all_to_all(slices, axes, 0, 0), axis=0)
    return to_all(mine, axes, devices).reshape(packed.shape)


def shards(
    prompt_in, prompt_dt, doc_starts, resp_in, resp_dt, resp_len, upstream, reward,
    conv_w, conv_b, head_params,
):
    n = lax.axis_size("resp")
    me = lax.axis_index("resp")
    clusters = n // G
    mine = me % G
    cluster = me // G
    inside = [list(range(c * G, c * G + G)) for c in range(clusters)]
    block = prompt_in.shape[1]
    slots = resp_in.shape[2]
    rows_in, dt_in = prompt_in[0], prompt_dt[0]
    u, dt, dy = resp_in[0, 0], resp_dt[0, 0], upstream[0, 0]

    r = reward[0, 0]
    r_hi = r.astype(bf16)
    r_mid = (r - r_hi.astype(f32)).astype(bf16)
    r_lo = (r - r_hi.astype(f32) - r_mid.astype(f32)).astype(bf16)
    tail_size = (K - 1) * rows_in.shape[1] // LANES
    small = jnp.concatenate(
        [
            rows_in[block - K + 1 :].reshape(tail_size, LANES),
            dt_in,
            jnp.broadcast_to(
                jnp.stack([r_hi, r_mid, r_lo, jnp.zeros_like(r_lo)])[:, None], (4, LANES)
            ),
            jnp.zeros((12, LANES), bf16),
        ]
    )
    small = to_all(small, "resp", n)
    wb = pad_rows(jnp.concatenate([conv_w, conv_b[None]], axis=0))
    hp = pad_rows(head_params)

    x_parts = rows_in[:, :XC].reshape(block, G, GX).transpose(1, 0, 2)
    b_parts = rows_in[:, XC : XC + G * N].reshape(block, G, N).transpose(1, 0, 2)
    parts = jnp.concatenate([x_parts, b_parts], axis=2)
    v = parts
    for k in range(1, G):
        route = [(c * G + q, c * G + (q + k) % G) for c in range(clusters) for q in range(G)]
        sent = lax.dynamic_index_in_dim(parts, (mine + k) % G, 0, False)
        came = lax.ppermute(sent, "resp", route)
        v = lax.dynamic_update_index_in_dim(v, came, (mine - k) % G, 0)
    v = v.reshape(G * block, GX + N)

    def own_channels(a):
        return jnp.concatenate(
            [
                lax.dynamic_slice(a, (0, mine * GX), (PAD, GX)),
                lax.dynamic_slice(a, (0, XC + mine * N), (PAD, N)),
            ],
            axis=1,
        )

    def last_rows(device):
        rows = lax.dynamic_index_in_dim(small, device, 0, False)[:tail_size]
        return jnp.pad(rows.reshape(K - 1, -1).astype(f32), ((PAD - K + 1, 0), (0, 0)))

    tail = last_rows(n - 1)
    halo = own_channels(last_rows(jnp.maximum(cluster * G - 1, 0)))
    dt_all = small[:, tail_size : tail_size + block].reshape(n * block, H)
    dt_mine = lax.dynamic_slice(dt_all, (cluster * G * block, 0), (G * block, H))
    at_reward = tail_size + block
    rewards = jnp.sum(small[:, at_reward : at_reward + 3, 0].astype(f32), axis=1)
    scale = ((r - jnp.sum(rewards) / n) / slots).reshape(1, 1)
    masks = lax.dynamic_slice(
        prompt_masks(doc_starts[0], n * block), (cluster * G * block, 0), (G * block, PAD)
    )
    wb_mine = own_channels(wb)
    place = jnp.stack([mine, cluster * G * block]).astype(jnp.int32).reshape(1, 2)

    length = resp_len.astype(jnp.int32)
    step, cum, cum_t, decay_in = response_steps(length, dt, hp)
    d_states, weighted, c_act = response_state(scale, u, tail, wb, dy, decay_in)
    d_states = lax.all_to_all(d_states, "resp", 0, 0, axis_index_groups=inside)

    cum4 = cum.reshape(slots, G, HG).transpose(1, 0, 2)
    skip = jnp.repeat(head_params[2], PS)[None, :]

    def mid(g, earlier_out, so_far=()):
        return response_mid(
            g, length, u, tail, wb, c_act, dy, step, cum, cum4,
            cum_t.reshape(G, HG, slots), skip, earlier_out, so_far,
        )

    def across(part):
        routes = [[(i, (i + c * G) % n) for i in range(n)] for c in range(1, clusters)]
        return [part] + [lax.ppermute(part, "resp", route) for route in routes]

    part, weight, p_step, beyond = prompt_state(place, v, halo, dt_all, masks, wb_mine, hp)
    parts_of_start = across(part)
    grads = mid(0, weight)
    grads = mid(1, weight, grads)
    part, start = add_states(d_states, parts_of_start, grads[3])
    parts_of_grad = across(part)
    grads = mid(2, part, grads)
    start = lax.all_to_all(start, "resp", 0, 0, axis_index_groups=inside)
    grad_x, grad_b, dc, sums = mid(3, weight, grads)
    p_grad, p_heads = prompt_grad(
        place, v, halo, dt_mine, masks, wb_mine, hp, weight, p_step, beyond, parts_of_grad
    )

    axes = ("group", "resp")
    devices = lax.axis_size(axes)
    tiles = devices * -(-(HEAD_TILE + 1) // devices)
    packed = response_end(
        tiles, place, scale, u, tail, wb, c_act, weighted, start, dc, sums, step, dt, hp,
        (grad_x, grad_b, p_grad, p_heads),
    )
    grad_w, grad_bias, heads = unpack(sum_over_all(packed, axes, devices))
    return grad_w, grad_bias.reshape(-1), heads


def solution(mesh):
    in_specs = (
        P("group", "resp", None),
        P("group", "resp", None),
        P("group", None),
        P("group", "resp", None, None),
        P("group", "resp", None, None),
        P("group", "resp"),
        P("group", "resp", None, None),
        P("group", "resp"),
        P(),
        P(),
        P(),
    )
    out_specs = (P(), P(), P())
    return jax.shard_map(shards, mesh=mesh, in_specs=in_specs, out_specs=out_specs, check_vma=False)
```

```python
import functools

import jax
import jax.numpy as jnp
from jax import lax
from jax.experimental import pallas as pl
from jax.experimental.pallas import tpu as pltpu
from jax.sharding import PartitionSpec as P

H = 128
PS = 64
N = 256
G = 4
K = 4
HG = H // G
XC = H * PS
GX = HG * PS
LANES = 128
PAD = 8
VMEM_MIB = 63

f32 = jnp.float32
bf16 = jnp.bfloat16

NN = (((1,), (0,)), ((), ()))
NT = (((1,), (1,)), ((), ()))


def dot(a, b, dims=NN, precision=None):
    return lax.dot_general(a, b, dims, precision=precision, preferred_element_type=f32)


def halves(v):
    hi = v.astype(bf16)
    return hi, (v - hi.astype(f32)).astype(bf16)


def indicator(first, width):
    row = lax.broadcasted_iota(jnp.int32, (LANES, width), 0)
    head = lax.shift_right_logical(lax.broadcasted_iota(jnp.int32, (LANES, width), 1), 6)
    return jnp.where(row - first == head, 1.0, 0.0).astype(bf16)


def expand(v, ind):
    hi, lo = halves(v)
    return dot(hi, ind) + dot(lo, ind)


def head_sums(z_hi, z_lo, ind):
    return dot(z_hi, ind, NT) + dot(z_lo, ind, NT)


def triangle(n, keep):
    i = lax.broadcasted_iota(jnp.int32, (n, n), 0)
    j = lax.broadcasted_iota(jnp.int32, (n, n), 1)
    return jnp.where(keep(i, j), 1.0, 0.0).astype(f32)


def tri_sum(tri, v):
    return dot(tri, v, precision=lax.Precision.HIGHEST)


def softplus(z):
    return jnp.maximum(z, 0.0) + jnp.log1p(jnp.exp(-jnp.abs(z)))


def sigmoid(z):
    return 0.5 * jnp.tanh(0.5 * z) + 0.5


def taps_of(ext, lanes, row, rows):
    return [ext[pl.ds(PAD - K + 1 + k + row, rows), lanes] for k in range(K)]


def conv_pre(taps, wb, masks=None):
    total = wb[K : K + 1] + wb[K - 1 : K] * taps[K - 1]
    for k in range(K - 1):
        term = wb[k : k + 1] * taps[k]
        if masks is not None:
            term = term * masks[k]
        total = total + term
    return total


def act_and_slope(pre):
    sig = sigmoid(pre)
    act = pre * sig
    return act, sig + act * (1.0 - sig)


def fold8(v):
    return jnp.sum(v.reshape(v.shape[0] // 8, 8, v.shape[1]), axis=0)


def as_rows(parts):
    row = lax.broadcasted_iota(jnp.int32, (PAD, LANES), 0)
    total = jnp.zeros((PAD, LANES), f32)
    for k, part in enumerate(parts):
        total = total + jnp.where(row == k, jnp.sum(part, axis=0, keepdims=True), 0.0)
    return total


def lane_loop(width, body, step=LANES):
    def one(i, _):
        body(pl.ds(pl.multiple_of(i * step, step), step))
        return 0

    lax.fori_loop(0, width // step, one, 0)


RC = 64


def conv_forward(u, tail, wb, ext, act, slope, rows, width):
    def body(lanes):
        ext[0:PAD, lanes] = tail[:, lanes]
        ext[PAD : PAD + rows, lanes] = u[:, lanes].astype(f32)
        w = wb[:, lanes]
        for r in range(0, rows, RC):
            a, s = act_and_slope(conv_pre(taps_of(ext, lanes, r, RC), w))
            act[r : r + RC, lanes] = a.astype(bf16)
            if slope is not None:
                slope[r : r + RC, lanes] = s

    lane_loop(width, body)


def conv_backward(ext, slope, lanes, cotangent, grad, rows):
    sums = [jnp.zeros((8, LANES), f32) for _ in range(K + 1)]
    for r in range(0, rows, RC):
        d = cotangent(r) * slope[r : r + RC, lanes]
        taps = taps_of(ext, lanes, r, RC)
        for k in range(K):
            sums[k] = sums[k] + fold8(d * taps[k])
        sums[K] = sums[K] + fold8(d)
    grad[:, lanes] = as_rows(sums)


def steps_kernel(len_ref, dt, hp, step, cum, cum_t, decay_in):
    rows = dt.shape[0]
    s = softplus(dt[...].astype(f32) + hp[1:2])
    logd = -jnp.exp(hp[0:1]) * s
    c = tri_sum(triangle(rows, lambda i, j: i >= j), logd)
    step[...] = s
    cum[...] = c
    cum_t[...] = c.T
    t = lax.broadcasted_iota(jnp.int32, c.shape, 0)
    decay_in[...] = jnp.where(t < len_ref[0, 0], jnp.exp(c), 0.0)


def resp_state_kernel(adv, u_c, tail_c, wb_c, dy, decay_in, state, weighted, c_out, ext):
    g = pl.program_id(0)
    rows, width = dy.shape
    conv_forward(u_c, tail_c, wb_c, ext, c_out, None, rows, N)
    c_t = c_out[...].astype(f32).T.astype(bf16)
    a = (dy[...].astype(f32) * expand(decay_in[...], indicator(g * HG, width))).astype(bf16)
    weighted[...] = a
    state[0] = (dot(c_t, a) * adv[0, 0]).astype(bf16)


def resp_mid_kernel(
    g, len_ref, u_x, u_b, tail_x, tail_b, wb_x, wb_b, c_act, dy, step, cum, cum4, cum_t4, skip,
    earlier_out, *refs,
):
    if g:
        sums_in, refs = refs[3], refs[4:]
    else:
        refs = refs[:4] + refs[5:]
    (
    grad_x, grad_b, dc, sums_out,
    ext, ext_b, x_s, xs_s, b_s, dym, slope, slope_b, step_e, y_s, t_s,
    a1, bm, sw_e, u_off, y_off, z_hi, z_lo, d_skip,
    ) = refs
    rows = u_x.shape[0]
    half = rows // 2
    conv_forward(u_x, tail_x, wb_x, ext, x_s, slope, rows, GX)
    conv_forward(u_b, tail_b, wb_b, ext_b, b_s, slope_b, rows, N)
    ind = indicator(g * HG, GX)
    step_e[...] = expand(step[...], ind)
    cum_v = cum[...]
    mid = cum_v[half - 1 : half]
    sw_e[...] = expand(jnp.exp(mid - cum_v[:half]) * step[:half], ind)
    y_off[...] = expand(jnp.exp(cum_v[half:] - mid), ind)
    live = jnp.where(lax.broadcasted_iota(jnp.int32, (rows, LANES), 0) < len_ref[0, 0], 1.0, 0.0)

    def prepare(lanes):
        d = dy[:, lanes].astype(f32) * live
        dym[:, lanes] = d.astype(bf16)
        x = x_s[:, lanes].astype(f32)
        xs_s[:, lanes] = (x * step_e[:, lanes]).astype(bf16)
        bm[:, lanes] = (x[:half] * sw_e[:, lanes]).astype(bf16)
        a1[:, lanes] = (d[half:] * y_off[:, lanes]).astype(bf16)

    lane_loop(GX, prepare)

    c_v, b_v = c_act[...], b_s[...]
    c0, c1, b0, b1 = c_v[:half], c_v[half:], b_v[:half], b_v[half:]
    i = lax.broadcasted_iota(jnp.int32, (half, half), 0)
    j = lax.broadcasted_iota(jnp.int32, (half, half), 1)
    lane = lax.broadcasted_iota(jnp.int32, (half, LANES), 1)
    first = jnp.where(lane < PS, 1.0, 0.0).astype(bf16)
    second = jnp.where(lane >= PS, 1.0, 0.0).astype(bf16)

    y_off[...] = dot(dot(c1, b0, NT).astype(bf16), bm[...])
    u_off[...] = dot(dot(b0, c1, NT).astype(bf16), a1[...])
    d10 = dot(a1[...], bm[...], NT)

    d_diag = []
    for q, (c_q, b_q) in enumerate(((c0, b0), (c1, b1))):
        r = slice(q * half, (q + 1) * half)
        lower = jnp.where(i >= j, dot(c_q, b_q, NT), 0.0)
        upper = jnp.where(j >= i, dot(b_q, c_q, NT), 0.0)
        d_sc = jnp.zeros((half, half), f32)
        for p in range(HG // 2):
            lanes = slice(p * LANES, (p + 1) * LANES)
            xs_p, dy_p = xs_s[r, lanes], dym[r, lanes]
            xb = jnp.concatenate([xs_p * first, xs_p * second], axis=0)
            dyb = jnp.concatenate([dy_p * first, dy_p * second], axis=0)
            d_m = dot(dy_p, xb, NT)
            mats, mats_t = [], []
            for a in range(2):
                h = 2 * p + a
                gap = jnp.exp(-jnp.abs(cum4[0, r, h : h + 1] - cum_t4[0, h : h + 1, r]))
                d_sc = d_sc + d_m[:, a * half : (a + 1) * half] * gap
                mats.append((gap * lower).astype(bf16))
                mats_t.append((gap * upper).astype(bf16))
            y_s[r, lanes] = dot(jnp.concatenate(mats, axis=1), xb)
            t_s[r, lanes] = dot(jnp.concatenate(mats_t, axis=1), dyb)
        d_diag.append(jnp.where(i >= j, d_sc, 0.0))

    d00, d11 = d_diag
    dc[:half] = dot(d00.astype(bf16), b0)
    dc[half:] = dot(d11.astype(bf16), b1) + dot(d10.astype(bf16), b0)
    db0 = dot(d00.T.astype(bf16), c0) + dot(d10.T.astype(bf16), c1)
    db1 = dot(d11.T.astype(bf16), c1)
    db = jnp.concatenate([db0, db1], axis=0)
    for k in range(N // LANES):
        lanes = slice(k * LANES, (k + 1) * LANES)
        conv_backward(ext_b, slope_b, lanes, lambda r: db[r : r + RC, lanes], grad_b, rows)

    def put(z, r, lanes):
        hi, lo = halves(z)
        z_hi[r : r + RC, lanes] = hi
        z_lo[r : r + RC, lanes] = lo

    def row_products(lanes):
        for r in range(0, rows, RC):
            z = dym[r : r + RC, lanes].astype(f32) * y_s[r : r + RC, lanes]
            if r >= half:
                o = r - half
                z = z + a1[o : o + RC, lanes].astype(f32) * y_off[o : o + RC, lanes]
            put(z, r, lanes)

    lane_loop(GX, row_products)
    row_sum = head_sums(z_hi[...], z_lo[...], ind)

    def finish(lanes):
        d_skips = jnp.zeros((8, LANES), f32)
        for r in range(0, rows, RC):
            t = t_s[r : r + RC, lanes]
            z = xs_s[r : r + RC, lanes].astype(f32) * t
            if r < half:
                z = z + bm[r : r + RC, lanes].astype(f32) * u_off[r : r + RC, lanes]
            put(z, r, lanes)
            d_skips = d_skips + fold8(
                dym[r : r + RC, lanes].astype(f32) * x_s[r : r + RC, lanes].astype(f32)
            )

        def cotangent(r):
            d = step_e[r : r + RC, lanes] * t_s[r : r + RC, lanes]
            d = d + skip[:, lanes] * dym[r : r + RC, lanes].astype(f32)
            if r < half:
                d = d + sw_e[r : r + RC, lanes] * u_off[r : r + RC, lanes]
            return d

        conv_backward(ext, slope, lanes, cotangent, grad_x, rows)
        d_skip[:, lanes] = d_skips

    lane_loop(GX, finish)
    col_sum = head_sums(z_hi[...], z_lo[...], ind)

    skip_sum = head_sums(*halves(d_skip[...]), ind)
    for at, part in ((0, row_sum), (rows, col_sum), (2 * rows, skip_sum)):
        span = slice(at, at + part.shape[0])
        sums_out[span] = sums_in[span] + part if g else part


X_TILES = XC // LANES
B_TILES = G * N // LANES
C_TILES = X_TILES + 2 * B_TILES
HEAD_TILE = (K + 1) * C_TILES // PAD


def tile(k):
    return slice(k * LANES, (k + 1) * LANES)


def resp_end_kernel(
    place, scale, u_c, tail_c, wb_c, c_act, weighted, start, dc, sums, step, dt, hp,
    grad_x, grad_b, p_grad, p_heads,
    packed, ext, c_s, slope, total, grad_c, tiles,
):
    g = pl.program_id(0)
    rows, width = weighted.shape
    conv_forward(u_c, tail_c, wb_c, ext, c_s, slope, rows, N)

    @pl.when(g == 0)
    def _():
        total[...] = sums[0:rows] - sums[rows : 2 * rows]

    d = dc[...]
    piece = start.shape[3]
    for c in range(start.shape[1]):
        a = weighted[:, c * piece : (c + 1) * piece]
        z_hi, z_lo = halves(a.astype(f32) * dot(c_act[...], start[0, c]))
        total[...] += head_sums(z_hi, z_lo, indicator(g * HG + c * (piece // PS), piece))
        d = d + dot(a, start[0, c], NT)
    for k in range(N // LANES):
        conv_backward(ext, slope, tile(k), lambda r: d[r : r + RC, tile(k)], grad_c, rows)
        tiles[X_TILES + B_TILES + g * (N // LANES) + k] = grad_c[:, tile(k)] * scale[0, 0]

    @pl.when(g == pl.num_programs(0) - 1)
    def _():
        d_log = tri_sum(triangle(rows, lambda i, j: j >= i), total[...])
        rate = -jnp.exp(hp[0:1])
        s = step[...]
        d_step = sums[rows : 2 * rows] / s + rate * d_log
        sig = sigmoid(dt[...].astype(f32) + hp[1:2])
        heads = as_rows([d_log * rate * s, d_step * sig, sums[2 * rows :]])
        for k in range(X_TILES):
            tiles[k] = grad_x[:, tile(k)] * scale[0, 0]
        for k in range(B_TILES):
            tiles[X_TILES + k] = grad_b[:, tile(k)] * scale[0, 0]
        own = p_grad.shape[1] - N
        for k in range(own // LANES):
            tiles[place[0, 1] // (LANES // PS) + k] += p_grad[:, tile(k)]
        for k in range(N // LANES):
            tiles[X_TILES + place[0, 0] * (N // LANES) + k] += p_grad[:, tile(own // LANES + k)]
        for k in range(K + 1):
            for at in range(C_TILES):
                row = k * C_TILES + at
                packed[row // PAD, row % PAD : row % PAD + 1] = tiles[at, k : k + 1]
        packed[HEAD_TILE] = heads * scale[0, 0] + p_heads[...]
        for k in range(HEAD_TILE + 1, packed.shape[0]):
            packed[k] = jnp.zeros((PAD, LANES), f32)


def unpack_kernel(packed, conv_w, conv_b, heads):
    for k in range(K + 1):
        for at in range(C_TILES):
            row = k * C_TILES + at
            part = packed[row // PAD, row % PAD : row % PAD + 1]
            if k < K:
                conv_w[k : k + 1, tile(at)] = part
            else:
                conv_b[:, tile(at)] = part
    heads[...] = packed[HEAD_TILE, 0:3]


RB = 256


def prompt_conv(v, masks, wb, ext, act, slope, row, width):
    def body(lanes):
        ext[PAD : PAD + RB, lanes] = v[pl.ds(row, RB), lanes].astype(f32)
        w = wb[:, lanes]
        for r in range(0, RB, RC):
            m = [masks[pl.ds(row + r, RC), k : k + 1] for k in range(K - 1)]
            a, s = act_and_slope(conv_pre(taps_of(ext, lanes, r, RC), w, m))
            act[r : r + RC, lanes] = a.astype(bf16)
            if slope is not None:
                slope[r : r + RC, lanes] = s

    lane_loop(width, body)


def rows_before(v, row, width):
    if row:
        return v[row - 16 : row, :width].astype(f32)[16 - PAD :]
    return jnp.zeros((PAD, width), f32)


def prompt_state_kernel(
    place, v, masks, wb, hp, earlier_out, start, weight, step, ext, act, acc
):
    rows = v.shape[0]
    width = start.shape[1]
    ind = indicator(place[0, 1], width)
    later = triangle(RB, lambda i, j: j > i)
    rate = -jnp.exp(hp[0:1])
    ahead = jnp.zeros((1, LANES), f32)
    acc[...] = jnp.zeros_like(acc)
    for row in range(rows - RB, -1, -RB):
        s = softplus(v[row : row + RB, width + N :].astype(f32) + hp[1:2])
        logd = rate * s
        after = tri_sum(later, logd) + ahead
        ahead = ahead + jnp.sum(logd, axis=0, keepdims=True)
        w = masks[row : row + RB, K - 1 : K] * jnp.exp(after) * s
        step[row : row + RB] = s
        weight[row : row + RB] = w
        ext[0:PAD] = rows_before(v, row, width + N)
        prompt_conv(v, masks, wb, ext, act, None, row, width + N)
        wx = (act[:, :width].astype(f32) * expand(w, ind)).astype(bf16)
        acc[...] += dot(act[:, width:].astype(f32).T.astype(bf16), wx)
    start[...] = acc[...].astype(bf16)


def prompt_grad_kernel(
    count, place, v, masks, wb, hp, weight, step, *refs
):
    states = refs[:count]
    grad, grad_h, ext, act, slope, g_s, d_s, sums = refs[count:]
    rows = v.shape[0]
    width = g_s.shape[1]
    ind = indicator(place[0, 1], width)
    earlier = triangle(RB, lambda i, j: j < i)
    total = states[0][...].astype(f32)
    for k in range(1, count):
        total = total + states[k][...].astype(f32)
    g_s[...] = total.astype(bf16)
    behind = jnp.zeros((1, LANES), f32)
    rate = -jnp.exp(hp[0:1])
    d_rate = jnp.zeros((1, LANES), f32)
    d_bias = jnp.zeros((1, LANES), f32)
    sums[...] = jnp.zeros_like(sums)
    for row in range(0, rows, RB):
        ext[0:PAD] = rows_before(v, row, width + N)
        prompt_conv(v, masks, wb, ext, act, slope, row, width + N)
        w_e = expand(weight[row : row + RB], ind)
        t = dot(act[:, width:], g_s[...])
        wx = (act[:, :width].astype(f32) * w_e).astype(bf16)
        d_s[:, :width] = t * w_e
        d_s[:, width:] = dot(wx, g_s[...], NT)
        z_hi, z_lo = halves(wx.astype(f32) * t)
        q = head_sums(z_hi, z_lo, ind)
        d_log = tri_sum(earlier, q) + behind
        behind = behind + jnp.sum(q, axis=0, keepdims=True)
        s = step[row : row + RB]
        d_step = q / s + rate * d_log
        sig = sigmoid(v[row : row + RB, width + N :].astype(f32) + hp[1:2])
        d_rate = d_rate + jnp.sum(d_log * rate * s, axis=0, keepdims=True)
        d_bias = d_bias + jnp.sum(d_step * sig, axis=0, keepdims=True)

        def back(lanes):
            acc = [jnp.zeros((8, LANES), f32) for _ in range(K + 1)]
            for r in range(0, RB, RC):
                d = d_s[r : r + RC, lanes] * slope[r : r + RC, lanes]
                taps = taps_of(ext, lanes, r, RC)
                for k in range(K):
                    part = d * taps[k]
                    if k < K - 1:
                        part = part * masks[pl.ds(row + r, RC), k : k + 1]
                    acc[k] = acc[k] + fold8(part)
                acc[K] = acc[K] + fold8(d)
            for k in range(K + 1):
                sums[k : k + 1, lanes] += jnp.sum(acc[k], axis=0, keepdims=True)

        lane_loop(width + N, back)
    grad[...] = sums[...]
    grad_h[...] = jnp.zeros_like(grad_h)
    grad_h[0:1] = d_rate
    grad_h[1:2] = d_bias


def add_kernel(count, place, grads, *refs):
    starts, (grad_sum, start) = refs[:count], refs[count + 1 :]
    width = starts[0].shape[1]
    total = jnp.sum(grads[...].astype(f32), axis=0).astype(bf16)
    for c in range(count):
        grad_sum[c] = total[:, c * width : (c + 1) * width]
    for k in range(count):
        c = lax.rem(place[0, 2] + (count - k), count)
        for copy in range(start.shape[0]):
            start[copy, c] = starts[k][...]


def params(*semantics):
    return pltpu.CompilerParams(
        vmem_limit_bytes=VMEM_MIB * 2**20, dimension_semantics=semantics or None
    )


SMEM = pl.BlockSpec(memory_space=pltpu.SMEM)


def whole(shape):
    return pl.BlockSpec(shape, lambda *_: (0,) * len(shape))


def sds(shape, dtype):
    return jax.ShapeDtypeStruct(shape, dtype)


def response_steps(length, dt, hp):
    rows = dt.shape[0]
    square = sds((rows, H), f32)
    return pl.pallas_call(
        steps_kernel,
        out_shape=(square, square, sds((H, rows), f32), square),
        in_specs=[SMEM, pl.BlockSpec(), pl.BlockSpec()],
        compiler_params=params(),
        name="resp_steps",
    )(length, dt, hp)


def response_state(scale, u, tail, wb, dy, decay_in):
    rows = u.shape[0]
    c_at = lambda g: (0, XC // N + G + g)
    g_at = lambda g: (0, g)
    return pl.pallas_call(
        resp_state_kernel,
        grid=(G,),
        in_specs=[
            SMEM,
            pl.BlockSpec((rows, N), c_at),
            pl.BlockSpec((PAD, N), c_at),
            pl.BlockSpec((PAD, N), c_at),
            pl.BlockSpec((rows, GX), g_at),
            whole((rows, H)),
        ],
        out_specs=[
            pl.BlockSpec((1, N, GX), lambda g: (g, 0, 0)),
            pl.BlockSpec((rows, GX), g_at),
            pl.BlockSpec((rows, N), g_at),
        ],
        out_shape=(sds((G, N, GX), bf16), sds((rows, XC), bf16), sds((rows, G * N), bf16)),
        scratch_shapes=[pltpu.VMEM((PAD + rows, N), f32)],
        compiler_params=params("arbitrary"),
        cost_estimate=pl.CostEstimate(
            flops=2 * rows * N * XC, bytes_accessed=14 * 2**20, transcendentals=rows * G * N
        ),
        name="resp_state",
    )(scale, u, tail, wb, dy, decay_in)


def response_mid(
    g, length, u, tail, wb, c_act, dy, step, cum, cum4, cum_t4, skip, earlier_out, so_far
):
    rows = u.shape[0]
    half = rows // 2
    x_at = lambda i: (0, g)
    b_at = lambda i: (0, XC // N + g)
    sums = (2 * rows + PAD, H)
    v = pltpu.VMEM
    anywhere = pl.BlockSpec(memory_space=pl.ANY)
    return pl.pallas_call(
        functools.partial(resp_mid_kernel, g),
        grid=(1,),
        in_specs=[
            SMEM,
            pl.BlockSpec((rows, GX), x_at),
            pl.BlockSpec((rows, N), b_at),
            pl.BlockSpec((PAD, GX), x_at),
            pl.BlockSpec((PAD, N), b_at),
            pl.BlockSpec((PAD, GX), x_at),
            pl.BlockSpec((PAD, N), b_at),
            pl.BlockSpec((rows, N), x_at),
            pl.BlockSpec((rows, GX), x_at),
            whole((rows, H)),
            whole((rows, H)),
            pl.BlockSpec((1, rows, HG), lambda i: (g, 0, 0)),
            pl.BlockSpec((1, HG, rows), lambda i: (g, 0, 0)),
            pl.BlockSpec((1, GX), x_at),
            anywhere,
        ]
        + ([anywhere] * 3 + [whole(sums)] if so_far else []),
        out_specs=[
            pl.BlockSpec((PAD, GX), x_at),
            pl.BlockSpec((PAD, N), x_at),
            pl.BlockSpec((rows, N), x_at),
            whole(sums),
        ]
        + ([] if so_far else [anywhere]),
        out_shape=(
            sds((PAD, XC), f32),
            sds((PAD, G * N), f32),
            sds((rows, G * N), f32),
            sds(sums, f32),
        )
        + (() if so_far else (sds(earlier_out.shape, earlier_out.dtype),)),
        input_output_aliases={15 + k: k for k in range(3)} if so_far else {14: 4},
        scratch_shapes=[
            v((PAD + rows, GX), f32),
            v((PAD + rows, N), f32),
            v((rows, GX), bf16),
            v((rows, GX), bf16),
            v((rows, N), bf16),
            v((rows, GX), bf16),
            v((rows, GX), f32),
            v((rows, N), f32),
            v((rows, GX), f32),
            v((rows, GX), f32),
            v((rows, GX), f32),
            v((half, GX), bf16),
            v((half, GX), bf16),
            v((half, GX), f32),
            v((half, GX), f32),
            v((half, GX), f32),
            v((rows, GX), bf16),
            v((rows, GX), bf16),
            v((PAD, GX), f32),
        ],
        compiler_params=params("arbitrary"),
        cost_estimate=pl.CostEstimate(
            flops=8 * 2**30, bytes_accessed=3 * 2**20, transcendentals=rows * half * HG
        ),
        name="resp_mid",
    )(
        length, u, u, tail, tail, wb, wb, c_act, dy, step, cum, cum4, cum_t4, skip, earlier_out,
        *so_far,
    )


def response_end(
    tiles, place, scale, u, tail, wb, c_act, weighted, start, dc, sums, step, dt, hp, grads
):
    rows = u.shape[0]
    c_at = lambda g: (0, XC // N + G + g)
    g_at = lambda g: (0, g)
    v = pltpu.VMEM
    return pl.pallas_call(
        resp_end_kernel,
        grid=(G,),
        in_specs=[
            SMEM,
            SMEM,
            pl.BlockSpec((rows, N), c_at),
            pl.BlockSpec((PAD, N), c_at),
            pl.BlockSpec((PAD, N), c_at),
            pl.BlockSpec((rows, N), g_at),
            pl.BlockSpec((rows, GX), g_at),
            pl.BlockSpec((1,) + start.shape[1:], lambda g: (g, 0, 0, 0)),
            pl.BlockSpec((rows, N), g_at),
        ]
        + [whole(a.shape) for a in (sums, step, dt, hp, *grads)],
        out_specs=whole((tiles, PAD, LANES)),
        out_shape=sds((tiles, PAD, LANES), f32),
        scratch_shapes=[
            v((PAD + rows, N), f32),
            v((rows, N), bf16),
            v((rows, N), f32),
            v((rows, H), f32),
            v((PAD, N), f32),
            v((C_TILES, PAD, LANES), f32),
        ],
        compiler_params=params("arbitrary"),
        cost_estimate=pl.CostEstimate(
            flops=4 * rows * N * XC, bytes_accessed=12 * 2**20, transcendentals=rows * G * N
        ),
        name="resp_end",
    )(place, scale, u, tail, wb, c_act, weighted, start, dc, sums, step, dt, hp, *grads)


def unpack(packed):
    width = C_TILES * LANES
    return pl.pallas_call(
        unpack_kernel,
        out_shape=(sds((K, width), f32), sds((1, width), f32), sds((3, H), f32)),
        compiler_params=params(),
        name="unpack",
    )(packed)


def add_states(place, grads, starts, earlier_out):
    copies, rows, width = grads.shape
    count = len(starts)
    part, piece = rows // 4, width // count
    one = pl.BlockSpec((part, piece), lambda i: (i, 0))
    return pl.pallas_call(
        functools.partial(add_kernel, count),
        grid=(4,),
        in_specs=[SMEM, pl.BlockSpec((copies, part, width), lambda i: (0, i, 0))]
        + [one] * count
        + [pl.BlockSpec(memory_space=pl.ANY)],
        out_specs=[
            pl.BlockSpec((count, part, piece), lambda i: (0, i, 0)),
            pl.BlockSpec((copies, count, part, piece), lambda i: (0, 0, i, 0)),
        ],
        out_shape=(sds((count, rows, piece), bf16), sds((copies, count, rows, piece), bf16)),
        compiler_params=params("arbitrary"),
        cost_estimate=pl.CostEstimate(
            flops=8 * rows * width, bytes_accessed=22 * rows * width, transcendentals=0
        ),
        name="add_states",
    )(place, grads, *starts, earlier_out)


def prompt_state(place, v, masks, wb, hp, earlier_out):
    rows = v.shape[0]
    width = v.shape[1] - N - LANES
    s = pltpu.VMEM
    return pl.pallas_call(
        prompt_state_kernel,
        in_specs=[SMEM] + [pl.BlockSpec()] * 4 + [pl.BlockSpec(memory_space=pl.ANY)],
        out_shape=(
            sds((N, width), bf16),
            sds((rows, LANES), f32),
            sds((rows, LANES), f32),
        ),
        scratch_shapes=[
            s((PAD + RB, width + N), f32),
            s((RB, width + N), bf16),
            s((N, width), f32),
        ],
        compiler_params=params(),
        cost_estimate=pl.CostEstimate(
            flops=2 * rows * N * width, bytes_accessed=4 * 2**20, transcendentals=rows * width
        ),
        name="prompt_state",
    )(place, v, masks, wb, hp, earlier_out)


def prompt_grad(place, v, masks, wb, hp, weight, step, states):
    rows = v.shape[0]
    width = v.shape[1] - N - LANES
    s = pltpu.VMEM
    return pl.pallas_call(
        functools.partial(prompt_grad_kernel, len(states)),
        in_specs=[SMEM] + [pl.BlockSpec()] * (6 + len(states)),
        out_shape=(sds((PAD, width + N), f32), sds((PAD, LANES), f32)),
        scratch_shapes=[
            s((PAD + RB, width + N), f32),
            s((RB, width + N), bf16),
            s((RB, width + N), f32),
            s((N, width), bf16),
            s((RB, width + N), f32),
            s((PAD, width + N), f32),
        ],
        compiler_params=params(),
        cost_estimate=pl.CostEstimate(
            flops=4 * rows * N * width, bytes_accessed=8 * 2**20, transcendentals=rows * width
        ),
        name="prompt_grad",
    )(place, v, masks, wb, hp, weight, step, *states)


def doc_number(starts, positions):
    return jnp.sum((starts[None, :] <= positions[:, None]).astype(jnp.int32), axis=1)


def prompt_masks(starts, rows):
    positions = jnp.arange(rows, dtype=jnp.int32)
    docs = doc_number(starts, positions)
    same = [doc_number(starts, positions - (K - 1 - k)) == docs for k in range(K - 1)]
    columns = jnp.stack(same + [docs == docs[rows - 1]], axis=1).astype(f32)
    return jnp.pad(columns, ((0, 0), (0, PAD - K)))


def pad_rows(a):
    return jnp.pad(a, ((0, PAD - a.shape[0]), (0, 0)))


def to_all(block, axes, devices, groups=None):
    copies = jnp.broadcast_to(block[None], (devices,) + block.shape)
    return lax.all_to_all(copies, axes, 0, 0, axis_index_groups=groups)


def sum_over_all(packed, axes, devices):
    slices = packed.reshape((devices, packed.shape[0] // devices) + packed.shape[1:])
    mine = jnp.sum(lax.all_to_all(slices, axes, 0, 0), axis=0)
    return to_all(mine, axes, devices).reshape(packed.shape)


def shards(
    prompt_in, prompt_dt, doc_starts, resp_in, resp_dt, resp_len, upstream, reward,
    conv_w, conv_b, head_params,
):
    n = lax.axis_size("resp")
    me = lax.axis_index("resp")
    clusters = n // G
    mine = me % G
    cluster = me // G
    inside = [list(range(c * G, c * G + G)) for c in range(clusters)]
    block = prompt_in.shape[1]
    slots = resp_in.shape[2]
    rows_in, dt_in = prompt_in[0], prompt_dt[0]
    u, dt, dy = resp_in[0, 0], resp_dt[0, 0], upstream[0, 0]

    wb = pad_rows(jnp.concatenate([conv_w, conv_b[None]], axis=0))
    hp = pad_rows(head_params)
    own_heads = HG // clusters
    width = own_heads * PS
    head = mine * HG + cluster * own_heads

    by_owner = (2, 1, 0, 3)
    x_parts = rows_in[:, :XC].reshape(block, G, clusters, width).transpose(by_owner)
    b_parts = rows_in[:, XC : XC + G * N].reshape(block, G, N).transpose(1, 0, 2)
    parts = jnp.concatenate(
        [
            x_parts.reshape(n, block, width),
            jnp.broadcast_to(b_parts[None], (clusters, G, block, N)).reshape(n, block, N),
            jnp.broadcast_to(dt_in[None], (n, block, H)),
        ],
        axis=2,
    )
    v = lax.all_to_all(parts, "resp", 0, 0).reshape(n * block, width + N + H)

    r = reward[0, 0]
    r_hi = r.astype(bf16)
    r_mid = (r - r_hi.astype(f32)).astype(bf16)
    r_lo = (r - r_hi.astype(f32) - r_mid.astype(f32)).astype(bf16)
    tail_size = (K - 1) * rows_in.shape[1] // LANES
    small = jnp.concatenate(
        [
            rows_in[block - K + 1 :].reshape(tail_size, LANES),
            jnp.broadcast_to(
                jnp.stack([r_hi, r_mid, r_lo, jnp.zeros_like(r_lo)])[:, None], (4, LANES)
            ),
            jnp.zeros((12, LANES), bf16),
        ]
    )
    tail = small[:tail_size]
    reward_sum = r
    for k in range(1, n):
        came = lax.ppermute(small, "resp", [(i, (i + k) % n) for i in range(n)])
        tail = jnp.where((me - k) % n == n - 1, came[:tail_size], tail)
        reward_sum = reward_sum + jnp.sum(came[tail_size : tail_size + 3, 0].astype(f32))
    tail = jnp.pad(tail.reshape(K - 1, -1).astype(f32), ((PAD - K + 1, 0), (0, 0)))
    scale = ((r - reward_sum / n) / slots).reshape(1, 1)

    masks = prompt_masks(doc_starts[0], n * block)
    wb_mine = jnp.concatenate(
        [
            lax.dynamic_slice(wb, (0, head * PS), (PAD, width)),
            lax.dynamic_slice(wb, (0, XC + mine * N), (PAD, N)),
        ],
        axis=1,
    )
    place = jnp.stack([mine, head, cluster]).astype(jnp.int32).reshape(1, 3)

    length = resp_len.astype(jnp.int32)
    step, cum, cum_t, decay_in = response_steps(length, dt, hp)
    d_states, weighted, c_act = response_state(scale, u, tail, wb, dy, decay_in)
    cum4 = cum.reshape(slots, G, HG).transpose(1, 0, 2)
    skip = jnp.repeat(head_params[2], PS)[None, :]

    def mid(g, earlier_out, so_far=()):
        return response_mid(
            g, length, u, tail, wb, c_act, dy, step, cum, cum4,
            cum_t.reshape(G, HG, slots), skip, earlier_out, so_far,
        )

    def across(part_for):
        parts = [part_for(0)]
        for k in range(1, clusters):
            route = [(i, (i + k * G) % n) for i in range(n)]
            parts.append(lax.ppermute(part_for(k), "resp", route))
        return parts

    *grads, d_states = mid(0, d_states)
    d_states = lax.all_to_all(d_states, "resp", 0, 0, axis_index_groups=inside)
    part, weight, p_step = prompt_state(place, v, masks, wb_mine, hp, grads[3])
    parts_of_start = across(lambda k: part)
    grads = mid(1, weight, grads)
    parts, start = add_states(place, d_states, parts_of_start, grads[3])
    parts_of_grad = across(
        lambda k: lax.dynamic_index_in_dim(parts, (cluster + k) % clusters, 0, False)
    )
    grads = mid(2, parts, grads)
    start = lax.all_to_all(start, "resp", 0, 0, axis_index_groups=inside)
    grad_x, grad_b, dc, sums = mid(3, weight, grads)
    p_grad, p_heads = prompt_grad(
        place, v, masks, wb_mine, hp, weight, p_step, parts_of_grad
    )

    axes = ("group", "resp")
    devices = lax.axis_size(axes)
    tiles = devices * -(-(HEAD_TILE + 1) // devices)
    packed = response_end(
        tiles, place, scale, u, tail, wb, c_act, weighted, start, dc, sums, step, dt, hp,
        (grad_x, grad_b, p_grad, p_heads),
    )
    grad_w, grad_bias, heads = unpack(sum_over_all(packed, axes, devices))
    return grad_w, grad_bias.reshape(-1), heads


def solution(mesh):
    in_specs = (
        P("group", "resp", None),
        P("group", "resp", None),
        P("group", None),
        P("group", "resp", None, None),
        P("group", "resp", None, None),
        P("group", "resp"),
        P("group", "resp", None, None),
        P("group", "resp"),
        P(),
        P(),
        P(),
    )
    out_specs = (P(), P(), P())
    return jax.shard_map(shards, mesh=mesh, in_specs=in_specs, out_specs=out_specs, check_vma=False)
```

```python
import functools

import jax
import jax.numpy as jnp
from jax import lax
from jax.experimental import pallas as pl
from jax.experimental.pallas import tpu as pltpu
from jax.sharding import PartitionSpec as P

H = 128
PS = 64
N = 256
G = 4
K = 4
HG = H // G
XC = H * PS
GX = HG * PS
LANES = 128
PAD = 8
VMEM_MIB = 63

f32 = jnp.float32
bf16 = jnp.bfloat16

NN = (((1,), (0,)), ((), ()))
NT = (((1,), (1,)), ((), ()))


def dot(a, b, dims=NN, precision=None):
    return lax.dot_general(a, b, dims, precision=precision, preferred_element_type=f32)


def halves(v):
    hi = v.astype(bf16)
    return hi, (v - hi.astype(f32)).astype(bf16)


def indicator(first, width):
    row = lax.broadcasted_iota(jnp.int32, (LANES, width), 0)
    head = lax.shift_right_logical(lax.broadcasted_iota(jnp.int32, (LANES, width), 1), 6)
    return jnp.where(row - first == head, 1.0, 0.0).astype(bf16)


def expand(v, ind):
    hi, lo = halves(v)
    return dot(hi, ind) + dot(lo, ind)


def head_sums(z_hi, z_lo, ind):
    return dot(z_hi, ind, NT) + dot(z_lo, ind, NT)


def triangle(n, keep):
    i = lax.broadcasted_iota(jnp.int32, (n, n), 0)
    j = lax.broadcasted_iota(jnp.int32, (n, n), 1)
    return jnp.where(keep(i, j), 1.0, 0.0).astype(f32)


def tri_sum(tri, v):
    return dot(tri, v, precision=lax.Precision.HIGHEST)


def softplus(z):
    return jnp.maximum(z, 0.0) + jnp.log1p(jnp.exp(-jnp.abs(z)))


def sigmoid(z):
    return 0.5 * jnp.tanh(0.5 * z) + 0.5


def taps_of(ext, at, row, rows):
    return [ext[at, pl.ds(PAD - K + 1 + k + row, rows), :] for k in range(K)]


def conv_pre(taps, wb, masks=None):
    total = wb[K : K + 1] + wb[K - 1 : K] * taps[K - 1]
    for k in range(K - 1):
        term = wb[k : k + 1] * taps[k]
        if masks is not None:
            term = term * masks[k]
        total = total + term
    return total


def act_and_slope(pre):
    sig = sigmoid(pre)
    act = pre * sig
    return act, sig + act * (1.0 - sig)


def fold8(v):
    return jnp.sum(v.reshape(v.shape[0] // 8, 8, v.shape[1]), axis=0)


def as_rows(parts):
    row = lax.broadcasted_iota(jnp.int32, (PAD, LANES), 0)
    total = jnp.zeros((PAD, LANES), f32)
    for k, part in enumerate(parts):
        total = total + jnp.where(row == k, jnp.sum(part, axis=0, keepdims=True), 0.0)
    return total


def lane_loop(width, body):
    def one(i, _):
        body(i, pl.ds(pl.multiple_of(i * LANES, LANES), LANES))
        return 0

    lax.fori_loop(0, width // LANES, one, 0)


RC = 64


def conv_forward(u, tail, wb, ext, act, slope, rows, width):
    def body(i, lanes):
        ext[i, 0:PAD, :] = tail[:, lanes]
        ext[i, PAD : PAD + rows, :] = u[:, lanes].astype(f32)
        w = wb[:, lanes]
        for r in range(0, rows, RC):
            a, s = act_and_slope(conv_pre(taps_of(ext, i, r, RC), w))
            act[r : r + RC, lanes] = a.astype(bf16)
            if slope is not None:
                slope[r : r + RC, lanes] = s

    lane_loop(width, body)


def conv_backward(ext, i, slope, lanes, cotangent, grad, rows):
    sums = [jnp.zeros((8, LANES), f32) for _ in range(K + 1)]
    for r in range(0, rows, RC):
        d = cotangent(r) * slope[r : r + RC, lanes]
        taps = taps_of(ext, i, r, RC)
        for k in range(K):
            sums[k] = sums[k] + fold8(d * taps[k])
        sums[K] = sums[K] + fold8(d)
    grad[:, lanes] = as_rows(sums)


def steps_kernel(len_ref, dt, hp, step, cum, cum_t, decay_in):
    rows = dt.shape[0]
    s = softplus(dt[...].astype(f32) + hp[1:2])
    logd = -jnp.exp(hp[0:1]) * s
    c = tri_sum(triangle(rows, lambda i, j: i >= j), logd)
    step[...] = s
    cum[...] = c
    cum_t[...] = c.T
    t = lax.broadcasted_iota(jnp.int32, c.shape, 0)
    decay_in[...] = jnp.where(t < len_ref[0, 0], jnp.exp(c), 0.0)


def resp_state_kernel(adv, u_c, tail_c, wb_c, dy, decay_in, state, weighted, c_out, ext):
    g = pl.program_id(0)
    rows, width = dy.shape
    conv_forward(u_c, tail_c, wb_c, ext, c_out, None, rows, N)
    c_t = c_out[...].astype(f32).T.astype(bf16)
    a = (dy[...].astype(f32) * expand(decay_in[...], indicator(g * HG, width))).astype(bf16)
    weighted[...] = a
    state[0] = (dot(c_t, a) * adv[0, 0]).astype(bf16)


def resp_mid_kernel(
    first, handed, len_ref, u_x, u_b, tail_x, tail_b, wb_x, wb_b, c_act, dy, step, cum, cum4, cum_t4, skip,
    earlier_out, *refs,
):
    if first:
        sums_in, refs = refs[3], refs[4:]
    if handed:
        refs = refs[:4] + refs[5:]
    g = first + pl.program_id(0)
    (
    grad_x, grad_b, dc, sums_out,
    ext, ext_b, x_s, xs_s, b_s, dym, slope, slope_b, step_e, y_s, t_s,
    a1, bm, sw_e, u_off, y_off, z_hi, z_lo, d_skip,
    ) = refs
    rows = u_x.shape[0]
    half = rows // 2
    conv_forward(u_x, tail_x, wb_x, ext, x_s, slope, rows, GX)
    conv_forward(u_b, tail_b, wb_b, ext_b, b_s, slope_b, rows, N)
    ind = indicator(g * HG, GX)
    step_e[...] = expand(step[...], ind)
    cum_v = cum[...]
    mid = cum_v[half - 1 : half]
    sw_e[...] = expand(jnp.exp(mid - cum_v[:half]) * step[:half], ind)
    y_off[...] = expand(jnp.exp(cum_v[half:] - mid), ind)
    live = jnp.where(lax.broadcasted_iota(jnp.int32, (rows, LANES), 0) < len_ref[0, 0], 1.0, 0.0)

    def prepare(i, lanes):
        d = dy[:, lanes].astype(f32) * live
        dym[:, lanes] = d.astype(bf16)
        x = x_s[:, lanes].astype(f32)
        xs_s[:, lanes] = (x * step_e[:, lanes]).astype(bf16)
        bm[:, lanes] = (x[:half] * sw_e[:, lanes]).astype(bf16)
        a1[:, lanes] = (d[half:] * y_off[:, lanes]).astype(bf16)

    lane_loop(GX, prepare)

    c_v, b_v = c_act[...], b_s[...]
    c0, c1, b0, b1 = c_v[:half], c_v[half:], b_v[:half], b_v[half:]
    i = lax.broadcasted_iota(jnp.int32, (half, half), 0)
    j = lax.broadcasted_iota(jnp.int32, (half, half), 1)
    lane = lax.broadcasted_iota(jnp.int32, (half, LANES), 1)
    left = jnp.where(lane < PS, 1.0, 0.0).astype(bf16)
    right = jnp.where(lane >= PS, 1.0, 0.0).astype(bf16)

    y_off[...] = dot(dot(c1, b0, NT).astype(bf16), bm[...])
    u_off[...] = dot(dot(b0, c1, NT).astype(bf16), a1[...])
    d10 = dot(a1[...], bm[...], NT)

    d_diag = []
    for q, (c_q, b_q) in enumerate(((c0, b0), (c1, b1))):
        r = slice(q * half, (q + 1) * half)
        lower = jnp.where(i >= j, dot(c_q, b_q, NT), 0.0)
        upper = jnp.where(j >= i, dot(b_q, c_q, NT), 0.0)
        d_sc = jnp.zeros((half, half), f32)
        for p in range(HG // 2):
            lanes = slice(p * LANES, (p + 1) * LANES)
            xs_p, dy_p = xs_s[r, lanes], dym[r, lanes]
            xb = jnp.concatenate([xs_p * left, xs_p * right], axis=0)
            dyb = jnp.concatenate([dy_p * left, dy_p * right], axis=0)
            d_m = dot(dy_p, xb, NT)
            mats, mats_t = [], []
            for a in range(2):
                h = 2 * p + a
                gap = jnp.exp(-jnp.abs(cum4[0, r, h : h + 1] - cum_t4[0, h : h + 1, r]))
                d_sc = d_sc + d_m[:, a * half : (a + 1) * half] * gap
                mats.append((gap * lower).astype(bf16))
                mats_t.append((gap * upper).astype(bf16))
            y_s[r, lanes] = dot(jnp.concatenate(mats, axis=1), xb)
            t_s[r, lanes] = dot(jnp.concatenate(mats_t, axis=1), dyb)
        d_diag.append(jnp.where(i >= j, d_sc, 0.0))

    d00, d11 = d_diag
    dc[:half] = dot(d00.astype(bf16), b0)
    dc[half:] = dot(d11.astype(bf16), b1) + dot(d10.astype(bf16), b0)
    db0 = dot(d00.T.astype(bf16), c0) + dot(d10.T.astype(bf16), c1)
    db1 = dot(d11.T.astype(bf16), c1)
    db = jnp.concatenate([db0, db1], axis=0)
    for k in range(N // LANES):
        lanes = slice(k * LANES, (k + 1) * LANES)
        conv_backward(ext_b, k, slope_b, lanes, lambda r: db[r : r + RC, lanes], grad_b, rows)

    def put(z, r, lanes):
        hi, lo = halves(z)
        z_hi[r : r + RC, lanes] = hi
        z_lo[r : r + RC, lanes] = lo

    def row_products(i, lanes):
        for r in range(0, rows, RC):
            z = dym[r : r + RC, lanes].astype(f32) * y_s[r : r + RC, lanes]
            if r >= half:
                o = r - half
                z = z + a1[o : o + RC, lanes].astype(f32) * y_off[o : o + RC, lanes]
            put(z, r, lanes)

    lane_loop(GX, row_products)
    row_sum = head_sums(z_hi[...], z_lo[...], ind)

    def finish(i, lanes):
        d_skips = jnp.zeros((8, LANES), f32)
        for r in range(0, rows, RC):
            t = t_s[r : r + RC, lanes]
            z = xs_s[r : r + RC, lanes].astype(f32) * t
            if r < half:
                z = z + bm[r : r + RC, lanes].astype(f32) * u_off[r : r + RC, lanes]
            put(z, r, lanes)
            d_skips = d_skips + fold8(
                dym[r : r + RC, lanes].astype(f32) * x_s[r : r + RC, lanes].astype(f32)
            )

        def cotangent(r):
            d = step_e[r : r + RC, lanes] * t_s[r : r + RC, lanes]
            d = d + skip[:, lanes] * dym[r : r + RC, lanes].astype(f32)
            if r < half:
                d = d + sw_e[r : r + RC, lanes] * u_off[r : r + RC, lanes]
            return d

        conv_backward(ext, i, slope, lanes, cotangent, grad_x, rows)
        d_skip[:, lanes] = d_skips

    lane_loop(GX, finish)
    col_sum = head_sums(z_hi[...], z_lo[...], ind)

    skip_sum = head_sums(*halves(d_skip[...]), ind)
    new = jnp.concatenate([row_sum, col_sum, skip_sum], axis=0)

    @pl.when(pl.program_id(0) == 0)
    def _():
        sums_out[...] = sums_in[...] + new if first else new

    @pl.when(pl.program_id(0) > 0)
    def _():
        sums_out[...] += new


X_TILES = XC // LANES
B_TILES = G * N // LANES
C_TILES = X_TILES + 2 * B_TILES
HEAD_TILE = (K + 1) * C_TILES // PAD


def tile(k):
    return slice(k * LANES, (k + 1) * LANES)


def resp_end_kernel(
    place, scale, u_c, tail_c, wb_c, c_act, weighted, start, dc, sums, step, dt, hp,
    grad_x, grad_b, p_grad, p_heads,
    packed, ext, c_s, slope, total, grad_c, tiles,
):
    g = pl.program_id(0)
    rows, width = weighted.shape
    conv_forward(u_c, tail_c, wb_c, ext, c_s, slope, rows, N)

    @pl.when(g == 0)
    def _():
        total[...] = sums[0:rows] - sums[rows : 2 * rows]

    a = weighted[...]
    z_hi, z_lo = halves(a.astype(f32) * dot(c_act[...], start[0]))
    total[...] += head_sums(z_hi, z_lo, indicator(g * HG, width))
    d = dc[...] + dot(a, start[0], NT)
    for k in range(N // LANES):
        conv_backward(ext, k, slope, tile(k), lambda r: d[r : r + RC, tile(k)], grad_c, rows)
        tiles[X_TILES + B_TILES + g * (N // LANES) + k] = grad_c[:, tile(k)] * scale[0, 0]

    @pl.when(g == pl.num_programs(0) - 1)
    def _():
        d_log = tri_sum(triangle(rows, lambda i, j: j >= i), total[...])
        rate = -jnp.exp(hp[0:1])
        s = step[...]
        d_step = sums[rows : 2 * rows] / s + rate * d_log
        sig = sigmoid(dt[...].astype(f32) + hp[1:2])
        heads = as_rows([d_log * rate * s, d_step * sig, sums[2 * rows :]])
        for k in range(X_TILES):
            tiles[k] = grad_x[:, tile(k)] * scale[0, 0]
        for k in range(B_TILES):
            tiles[X_TILES + k] = grad_b[:, tile(k)] * scale[0, 0]
        for k in range(width // LANES):
            tiles[place[0, 0] * (width // LANES) + k] += p_grad[:, tile(k)]
        for k in range(N // LANES):
            tiles[X_TILES + place[0, 0] * (N // LANES) + k] += p_grad[:, tile(width // LANES + k)]
        for k in range(K + 1):
            for at in range(C_TILES):
                row = k * C_TILES + at
                packed[row // PAD, row % PAD : row % PAD + 1] = tiles[at, k : k + 1]
        packed[HEAD_TILE] = heads * scale[0, 0] + p_heads[...]
        for k in range(HEAD_TILE + 1, packed.shape[0]):
            packed[k] = jnp.zeros((PAD, LANES), f32)


def unpack_kernel(packed, conv_w, conv_b, heads):
    for k in range(K + 1):
        for at in range(C_TILES):
            row = k * C_TILES + at
            part = packed[row // PAD, row % PAD : row % PAD + 1]
            if k < K:
                conv_w[k : k + 1, tile(at)] = part
            else:
                conv_b[:, tile(at)] = part
    heads[...] = packed[HEAD_TILE, 0:3]


RB = 256


def prompt_conv(v, masks, wb, ext, act, slope, row, width):
    def body(i, lanes):
        ext[i, PAD : PAD + RB, :] = v[pl.ds(row, RB), lanes].astype(f32)
        w = wb[:, lanes]
        for r in range(0, RB, RC):
            m = [masks[pl.ds(row + r, RC), k : k + 1] for k in range(K - 1)]
            a, s = act_and_slope(conv_pre(taps_of(ext, i, r, RC), w, m))
            act[r : r + RC, lanes] = a.astype(bf16)
            if slope is not None:
                slope[r : r + RC, lanes] = s

    lane_loop(width, body)


def fill_before(ext, v, halo, row):
    for i in range(ext.shape[0]):
        before = v[row - 16 : row, tile(i)].astype(f32)[16 - PAD :] if row else halo[:, tile(i)]
        ext[i, 0:PAD, :] = before


def prompt_state_kernel(
    place, v, halo, dt_all, masks, wb, hp, start, weight, step, beyond, ext, act, acc
):
    rows = v.shape[0]
    width = start.shape[1]
    first = place[0, 1]
    ind = indicator(place[0, 0] * HG, width)
    later = triangle(RB, lambda i, j: j > i)
    rate = -jnp.exp(hp[0:1])
    ahead = jnp.zeros((1, LANES), f32)
    slopes = jnp.zeros((1, LANES), f32)
    for row in range(0, dt_all.shape[0], RB):
        s = softplus(dt_all[row : row + RB].astype(f32) + hp[1:2])
        position = row + lax.broadcasted_iota(jnp.int32, s.shape, 0)
        past = position >= first + rows
        sig = sigmoid(dt_all[row : row + RB].astype(f32) + hp[1:2])
        ahead = ahead + rate * jnp.sum(jnp.where(past, s, 0.0), axis=0, keepdims=True)
        slopes = slopes + rate * jnp.sum(jnp.where(past, sig, 0.0), axis=0, keepdims=True)
    beyond[...] = jnp.zeros_like(beyond)
    beyond[0:1] = ahead
    beyond[1:2] = slopes
    acc[...] = jnp.zeros_like(acc)
    for row in range(rows - RB, -1, -RB):
        at = pl.ds(pl.multiple_of(first + row, RB), RB)
        s = softplus(dt_all[at, :].astype(f32) + hp[1:2])
        logd = rate * s
        after = tri_sum(later, logd) + ahead
        ahead = ahead + jnp.sum(logd, axis=0, keepdims=True)
        w = masks[row : row + RB, K - 1 : K] * jnp.exp(after) * s
        step[row : row + RB] = s
        weight[row : row + RB] = w
        fill_before(ext, v, halo, row)
        prompt_conv(v, masks, wb, ext, act, None, row, width + N)
        wx = (act[:, :width].astype(f32) * expand(w, ind)).astype(bf16)
        acc[...] += dot(act[:, width:].astype(f32).T.astype(bf16), wx)
    start[...] = acc[...].astype(bf16)


def prompt_grad_kernel(
    count, place, v, halo, dt_mine, masks, wb, hp, weight, step, beyond, *refs
):
    states = refs[:count]
    grad, grad_h, ext, act, slope, g_s, d_s, sums = refs[count + 1 :]
    rows = v.shape[0]
    width = g_s.shape[1]
    ind = indicator(place[0, 0] * HG, width)
    earlier = triangle(RB, lambda i, j: j < i)
    total = states[0][...].astype(f32)
    for k in range(1, count):
        total = total + states[k][...].astype(f32)
    g_s[...] = total.astype(bf16)
    behind = jnp.zeros((1, LANES), f32)
    rate = -jnp.exp(hp[0:1])
    d_rate = jnp.zeros((1, LANES), f32)
    d_bias = jnp.zeros((1, LANES), f32)
    sums[...] = jnp.zeros_like(sums)
    for row in range(0, rows, RB):
        fill_before(ext, v, halo, row)
        prompt_conv(v, masks, wb, ext, act, slope, row, width + N)
        w_e = expand(weight[row : row + RB], ind)
        t = dot(act[:, width:], g_s[...])
        wx = (act[:, :width].astype(f32) * w_e).astype(bf16)
        d_s[:, :width] = t * w_e
        d_s[:, width:] = dot(wx, g_s[...], NT)
        z_hi, z_lo = halves(wx.astype(f32) * t)
        q = head_sums(z_hi, z_lo, ind)
        d_log = tri_sum(earlier, q) + behind
        behind = behind + jnp.sum(q, axis=0, keepdims=True)
        s = step[row : row + RB]
        d_step = q / s + rate * d_log
        sig = sigmoid(dt_mine[row : row + RB].astype(f32) + hp[1:2])
        d_rate = d_rate + jnp.sum(d_log * rate * s, axis=0, keepdims=True)
        d_bias = d_bias + jnp.sum(d_step * sig, axis=0, keepdims=True)

        def back(i, lanes):
            acc = [jnp.zeros((8, LANES), f32) for _ in range(K + 1)]
            for r in range(0, RB, RC):
                d = d_s[r : r + RC, lanes] * slope[r : r + RC, lanes]
                taps = taps_of(ext, i, r, RC)
                for k in range(K):
                    part = d * taps[k]
                    if k < K - 1:
                        part = part * masks[pl.ds(row + r, RC), k : k + 1]
                    acc[k] = acc[k] + fold8(part)
                acc[K] = acc[K] + fold8(d)
            for k in range(K + 1):
                sums[k : k + 1, lanes] += jnp.sum(acc[k], axis=0, keepdims=True)

        lane_loop(width + N, back)
    grad[...] = sums[...]
    grad_h[...] = jnp.zeros_like(grad_h)
    grad_h[0:1] = d_rate + behind * beyond[0:1]
    grad_h[1:2] = d_bias + behind * beyond[1:2]


def add_kernel(count, grads, *refs):
    starts, (grad_sum, start) = refs[:count], refs[count + 1 :]
    grad_sum[...] = jnp.sum(grads[...].astype(f32), axis=0).astype(bf16)
    total = starts[0][...].astype(f32)
    for k in range(1, count):
        total = total + starts[k][...].astype(f32)
    total = total.astype(bf16)
    for k in range(start.shape[0]):
        start[k] = total


def params(*semantics):
    return pltpu.CompilerParams(
        vmem_limit_bytes=VMEM_MIB * 2**20, dimension_semantics=semantics or None
    )


SMEM = pl.BlockSpec(memory_space=pltpu.SMEM)
PROMPT_GRAD_FLOPS = 2**38


def whole(shape):
    return pl.BlockSpec(shape, lambda *_: (0,) * len(shape))


def sds(shape, dtype):
    return jax.ShapeDtypeStruct(shape, dtype)


def response_steps(length, dt, hp):
    rows = dt.shape[0]
    square = sds((rows, H), f32)
    return pl.pallas_call(
        steps_kernel,
        out_shape=(square, square, sds((H, rows), f32), square),
        in_specs=[SMEM, pl.BlockSpec(), pl.BlockSpec()],
        compiler_params=params(),
        name="resp_steps",
    )(length, dt, hp)


def response_state(scale, u, tail, wb, dy, decay_in):
    rows = u.shape[0]
    c_at = lambda g: (0, XC // N + G + g)
    g_at = lambda g: (0, g)
    return pl.pallas_call(
        resp_state_kernel,
        grid=(G,),
        in_specs=[
            SMEM,
            pl.BlockSpec((rows, N), c_at),
            pl.BlockSpec((PAD, N), c_at),
            pl.BlockSpec((PAD, N), c_at),
            pl.BlockSpec((rows, GX), g_at),
            whole((rows, H)),
        ],
        out_specs=[
            pl.BlockSpec((1, N, GX), lambda g: (g, 0, 0)),
            pl.BlockSpec((rows, GX), g_at),
            pl.BlockSpec((rows, N), g_at),
        ],
        out_shape=(sds((G, N, GX), bf16), sds((rows, XC), bf16), sds((rows, G * N), bf16)),
        scratch_shapes=[pltpu.VMEM((N // LANES, PAD + rows, LANES), f32)],
        compiler_params=params("arbitrary"),
        cost_estimate=pl.CostEstimate(
            flops=2 * rows * N * XC, bytes_accessed=14 * 2**20, transcendentals=rows * G * N
        ),
        name="resp_state",
    )(scale, u, tail, wb, dy, decay_in)


def response_mid(
    first, count, length, u, tail, wb, c_act, dy, step, cum, cum4, cum_t4, skip,
    earlier_out, so_far, handed,
):
    rows = u.shape[0]
    half = rows // 2
    x_at = lambda i: (0, first + i)
    b_at = lambda i: (0, XC // N + first + i)
    sums = (2 * rows + PAD, H)
    v = pltpu.VMEM
    anywhere = pl.BlockSpec(memory_space=pl.ANY)
    return pl.pallas_call(
        functools.partial(resp_mid_kernel, first, handed),
        grid=(count,),
        in_specs=[
            SMEM,
            pl.BlockSpec((rows, GX), x_at),
            pl.BlockSpec((rows, N), b_at),
            pl.BlockSpec((PAD, GX), x_at),
            pl.BlockSpec((PAD, N), b_at),
            pl.BlockSpec((PAD, GX), x_at),
            pl.BlockSpec((PAD, N), b_at),
            pl.BlockSpec((rows, N), x_at),
            pl.BlockSpec((rows, GX), x_at),
            whole((rows, H)),
            whole((rows, H)),
            pl.BlockSpec((1, rows, HG), lambda i: (first + i, 0, 0)),
            pl.BlockSpec((1, HG, rows), lambda i: (first + i, 0, 0)),
            pl.BlockSpec((1, GX), x_at),
            anywhere,
        ]
        + ([anywhere] * 3 + [whole(sums)] if so_far else []),
        out_specs=[
            pl.BlockSpec((PAD, GX), x_at),
            pl.BlockSpec((PAD, N), x_at),
            pl.BlockSpec((rows, N), x_at),
            whole(sums),
        ]
        + ([anywhere] if handed else []),
        out_shape=(
            sds((PAD, XC), f32),
            sds((PAD, G * N), f32),
            sds((rows, G * N), f32),
            sds(sums, f32),
        )
        + ((sds(earlier_out.shape, earlier_out.dtype),) if handed else ()),
        input_output_aliases=({15 + k: k for k in range(3)} if so_far else {})
        | ({14: 4} if handed else {}),
        scratch_shapes=[
            v((GX // LANES, PAD + rows, LANES), f32),
            v((N // LANES, PAD + rows, LANES), f32),
            v((rows, GX), bf16),
            v((rows, GX), bf16),
            v((rows, N), bf16),
            v((rows, GX), bf16),
            v((rows, GX), f32),
            v((rows, N), f32),
            v((rows, GX), f32),
            v((rows, GX), f32),
            v((rows, GX), f32),
            v((half, GX), bf16),
            v((half, GX), bf16),
            v((half, GX), f32),
            v((half, GX), f32),
            v((half, GX), f32),
            v((rows, GX), bf16),
            v((rows, GX), bf16),
            v((PAD, GX), f32),
        ],
        compiler_params=params("arbitrary"),
        cost_estimate=pl.CostEstimate(
            flops=8 * 2**30, bytes_accessed=3 * 2**20, transcendentals=rows * half * HG
        ),
        name="resp_mid",
    )(
        length, u, u, tail, tail, wb, wb, c_act, dy, step, cum, cum4, cum_t4, skip, earlier_out,
        *so_far,
    )


def response_end(
    tiles, place, scale, u, tail, wb, c_act, weighted, start, dc, sums, step, dt, hp, grads
):
    rows = u.shape[0]
    c_at = lambda g: (0, XC // N + G + g)
    g_at = lambda g: (0, g)
    v = pltpu.VMEM
    return pl.pallas_call(
        resp_end_kernel,
        grid=(G,),
        in_specs=[
            SMEM,
            SMEM,
            pl.BlockSpec((rows, N), c_at),
            pl.BlockSpec((PAD, N), c_at),
            pl.BlockSpec((PAD, N), c_at),
            pl.BlockSpec((rows, N), g_at),
            pl.BlockSpec((rows, GX), g_at),
            pl.BlockSpec((1, N, GX), lambda g: (g, 0, 0)),
            pl.BlockSpec((rows, N), g_at),
        ]
        + [whole(a.shape) for a in (sums, step, dt, hp, *grads)],
        out_specs=whole((tiles, PAD, LANES)),
        out_shape=sds((tiles, PAD, LANES), f32),
        scratch_shapes=[
            v((N // LANES, PAD + rows, LANES), f32),
            v((rows, N), bf16),
            v((rows, N), f32),
            v((rows, H), f32),
            v((PAD, N), f32),
            v((C_TILES, PAD, LANES), f32),
        ],
        compiler_params=params("arbitrary"),
        cost_estimate=pl.CostEstimate(
            flops=4 * rows * N * XC, bytes_accessed=12 * 2**20, transcendentals=rows * G * N
        ),
        name="resp_end",
    )(place, scale, u, tail, wb, c_act, weighted, start, dc, sums, step, dt, hp, *grads)


def unpack(packed):
    width = C_TILES * LANES
    return pl.pallas_call(
        unpack_kernel,
        out_shape=(sds((K, width), f32), sds((1, width), f32), sds((3, H), f32)),
        compiler_params=params(),
        name="unpack",
    )(packed)


def add_states(grads, starts, earlier_out):
    copies, rows, width = grads.shape
    part = rows // 4
    one = pl.BlockSpec((part, width), lambda i: (i, 0))
    many = pl.BlockSpec((copies, part, width), lambda i: (0, i, 0))
    return pl.pallas_call(
        functools.partial(add_kernel, len(starts)),
        grid=(4,),
        in_specs=[many] + [one] * len(starts) + [pl.BlockSpec(memory_space=pl.ANY)],
        out_specs=[one, many],
        out_shape=(sds((rows, width), bf16), sds(grads.shape, bf16)),
        compiler_params=params("arbitrary"),
        cost_estimate=pl.CostEstimate(
            flops=8 * rows * width, bytes_accessed=22 * rows * width, transcendentals=0
        ),
        name="add_states",
    )(grads, *starts, earlier_out)


def prompt_state(place, v, halo, dt_all, masks, wb, hp):
    rows = v.shape[0]
    width = v.shape[1] - N
    s = pltpu.VMEM
    return pl.pallas_call(
        prompt_state_kernel,
        in_specs=[SMEM] + [pl.BlockSpec()] * 6,
        out_shape=(
            sds((N, width), bf16),
            sds((rows, LANES), f32),
            sds((rows, LANES), f32),
            sds((PAD, LANES), f32),
        ),
        scratch_shapes=[
            s(((width + N) // LANES, PAD + RB, LANES), f32),
            s((RB, width + N), bf16),
            s((N, width), f32),
        ],
        compiler_params=params(),
        cost_estimate=pl.CostEstimate(
            flops=2 * rows * N * width, bytes_accessed=4 * 2**20, transcendentals=rows * width
        ),
        name="prompt_state",
    )(place, v, halo, dt_all, masks, wb, hp)


def prompt_grad(
    place, v, halo, dt_mine, masks, wb, hp, weight, step, beyond, states, earlier_out
):
    rows = v.shape[0]
    width = v.shape[1] - N
    s = pltpu.VMEM
    return pl.pallas_call(
        functools.partial(prompt_grad_kernel, len(states)),
        in_specs=[SMEM]
        + [pl.BlockSpec()] * (9 + len(states))
        + [pl.BlockSpec(memory_space=pl.ANY)],
        out_shape=(sds((PAD, width + N), f32), sds((PAD, LANES), f32)),
        scratch_shapes=[
            s(((width + N) // LANES, PAD + RB, LANES), f32),
            s((RB, width + N), bf16),
            s((RB, width + N), f32),
            s((N, width), bf16),
            s((RB, width + N), f32),
            s((PAD, width + N), f32),
        ],
        compiler_params=params(),
        cost_estimate=pl.CostEstimate(
            flops=PROMPT_GRAD_FLOPS, bytes_accessed=8 * 2**20, transcendentals=rows * width
        ),
        name="prompt_grad",
    )(place, v, halo, dt_mine, masks, wb, hp, weight, step, beyond, *states, earlier_out)


def doc_number(starts, positions):
    return jnp.sum((starts[None, :] <= positions[:, None]).astype(jnp.int32), axis=1)


def prompt_masks(starts, rows):
    positions = jnp.arange(rows, dtype=jnp.int32)
    docs = doc_number(starts, positions)
    same = [doc_number(starts, positions - (K - 1 - k)) == docs for k in range(K - 1)]
    columns = jnp.stack(same + [docs == docs[rows - 1]], axis=1).astype(f32)
    return jnp.pad(columns, ((0, 0), (0, PAD - K)))


def pad_rows(a):
    return jnp.pad(a, ((0, PAD - a.shape[0]), (0, 0)))


def to_all(block, axes, devices, groups=None):
    copies = jnp.broadcast_to(block[None], (devices,) + block.shape)
    return lax.all_to_all(copies, axes, 0, 0, axis_index_groups=groups)


def sum_over_all(packed, axes, devices):
    slices = packed.reshape((devices, packed.shape[0] // devices) + packed.shape[1:])
    mine = jnp.sum(lax.all_to_all(slices, axes, 0, 0), axis=0)
    return to_all(mine, axes, devices).reshape(packed.shape)


def shards(
    prompt_in, prompt_dt, doc_starts, resp_in, resp_dt, resp_len, upstream, reward,
    conv_w, conv_b, head_params,
):
    n = lax.axis_size("resp")
    me = lax.axis_index("resp")
    clusters = n // G
    mine = me % G
    cluster = me // G
    inside = [list(range(c * G, c * G + G)) for c in range(clusters)]
    block = prompt_in.shape[1]
    slots = resp_in.shape[2]
    rows_in, dt_in = prompt_in[0], prompt_dt[0]
    u, dt, dy = resp_in[0, 0], resp_dt[0, 0], upstream[0, 0]

    r = reward[0, 0]
    r_hi = r.astype(bf16)
    r_mid = (r - r_hi.astype(f32)).astype(bf16)
    r_lo = (r - r_hi.astype(f32) - r_mid.astype(f32)).astype(bf16)
    tail_size = (K - 1) * rows_in.shape[1] // LANES
    small = jnp.concatenate(
        [
            rows_in[block - K + 1 :].reshape(tail_size, LANES),
            dt_in,
            jnp.broadcast_to(
                jnp.stack([r_hi, r_mid, r_lo, jnp.zeros_like(r_lo)])[:, None], (4, LANES)
            ),
            jnp.zeros((12, LANES), bf16),
        ]
    )
    small = to_all(small, "resp", n)
    wb = pad_rows(jnp.concatenate([conv_w, conv_b[None]], axis=0))
    hp = pad_rows(head_params)

    x_parts = rows_in[:, :XC].reshape(block, G, GX).transpose(1, 0, 2)
    b_parts = rows_in[:, XC : XC + G * N].reshape(block, G, N).transpose(1, 0, 2)
    parts = jnp.concatenate([x_parts, b_parts], axis=2)
    v = parts
    for k in range(1, G):
        route = [(c * G + q, c * G + (q + k) % G) for c in range(clusters) for q in range(G)]
        sent = lax.dynamic_index_in_dim(parts, (mine + k) % G, 0, False)
        came = lax.ppermute(sent, "resp", route)
        v = lax.dynamic_update_index_in_dim(v, came, (mine - k) % G, 0)
    v = v.reshape(G * block, GX + N)

    def own_channels(a):
        return jnp.concatenate(
            [
                lax.dynamic_slice(a, (0, mine * GX), (PAD, GX)),
                lax.dynamic_slice(a, (0, XC + mine * N), (PAD, N)),
            ],
            axis=1,
        )

    def last_rows(device):
        rows = lax.dynamic_index_in_dim(small, device, 0, False)[:tail_size]
        return jnp.pad(rows.reshape(K - 1, -1).astype(f32), ((PAD - K + 1, 0), (0, 0)))

    tail = last_rows(n - 1)
    halo = own_channels(last_rows(jnp.maximum(cluster * G - 1, 0)))
    dt_all = small[:, tail_size : tail_size + block].reshape(n * block, H)
    dt_mine = lax.dynamic_slice(dt_all, (cluster * G * block, 0), (G * block, H))
    at_reward = tail_size + block
    rewards = jnp.sum(small[:, at_reward : at_reward + 3, 0].astype(f32), axis=1)
    scale = ((r - jnp.sum(rewards) / n) / slots).reshape(1, 1)
    masks = lax.dynamic_slice(
        prompt_masks(doc_starts[0], n * block), (cluster * G * block, 0), (G * block, PAD)
    )
    wb_mine = own_channels(wb)
    place = jnp.stack([mine, cluster * G * block]).astype(jnp.int32).reshape(1, 2)

    length = resp_len.astype(jnp.int32)
    step, cum, cum_t, decay_in = response_steps(length, dt, hp)
    d_states, weighted, c_act = response_state(scale, u, tail, wb, dy, decay_in)
    d_states = lax.all_to_all(d_states, "resp", 0, 0, axis_index_groups=inside)

    cum4 = cum.reshape(slots, G, HG).transpose(1, 0, 2)
    skip = jnp.repeat(head_params[2], PS)[None, :]

    def mid(first, count, earlier_out, so_far=(), handed=False):
        return response_mid(
            first, count, length, u, tail, wb, c_act, dy, step, cum, cum4,
            cum_t.reshape(G, HG, slots), skip, earlier_out, so_far, handed,
        )

    def across(part):
        routes = [[(i, (i + c * G) % n) for i in range(n)] for c in range(1, clusters)]
        return [part] + [lax.ppermute(part, "resp", route) for route in routes]

    part, weight, p_step, beyond = prompt_state(place, v, halo, dt_all, masks, wb_mine, hp)
    parts_of_start = across(part)
    grads = mid(0, 2, weight)
    part, start = add_states(d_states, parts_of_start, grads[3])
    parts_of_grad = across(part)
    grad_x, grad_b, dc, sums, start = mid(2, 2, start, grads, handed=True)
    start = lax.all_to_all(start, "resp", 0, 0, axis_index_groups=inside)
    p_grad, p_heads = prompt_grad(
        place, v, halo, dt_mine, masks, wb_mine, hp, weight, p_step, beyond, parts_of_grad, sums
    )

    axes = ("group", "resp")
    devices = lax.axis_size(axes)
    tiles = devices * -(-(HEAD_TILE + 1) // devices)
    packed = response_end(
        tiles, place, scale, u, tail, wb, c_act, weighted, start, dc, sums, step, dt, hp,
        (grad_x, grad_b, p_grad, p_heads),
    )
    grad_w, grad_bias, heads = unpack(sum_over_all(packed, axes, devices))
    return grad_w, grad_bias.reshape(-1), heads


def solution(mesh):
    in_specs = (
        P("group", "resp", None),
        P("group", "resp", None),
        P("group", None),
        P("group", "resp", None, None),
        P("group", "resp", None, None),
        P("group", "resp"),
        P("group", "resp", None, None),
        P("group", "resp"),
        P(),
        P(),
        P(),
    )
    out_specs = (P(), P(), P())
    return jax.shard_map(shards, mesh=mesh, in_specs=in_specs, out_specs=out_specs, check_vma=False)
```

```python
import functools

import jax
import jax.numpy as jnp
from jax import lax
from jax.experimental import pallas as pl
from jax.experimental.pallas import tpu as pltpu
from jax.sharding import PartitionSpec as P

H = 128
PS = 64
N = 256
G = 4
K = 4
HG = H // G
XC = H * PS
GX = HG * PS
LANES = 128
PAD = 8
VMEM_MIB = 63

f32 = jnp.float32
bf16 = jnp.bfloat16

NN = (((1,), (0,)), ((), ()))
NT = (((1,), (1,)), ((), ()))


def dot(a, b, dims=NN, precision=None):
    return lax.dot_general(a, b, dims, precision=precision, preferred_element_type=f32)


def halves(v):
    hi = v.astype(bf16)
    return hi, (v - hi.astype(f32)).astype(bf16)


def indicator(first, width):
    row = lax.broadcasted_iota(jnp.int32, (LANES, width), 0)
    head = lax.shift_right_logical(lax.broadcasted_iota(jnp.int32, (LANES, width), 1), 6)
    return jnp.where(row - first == head, 1.0, 0.0).astype(bf16)


def expand(v, ind):
    hi, lo = halves(v)
    return dot(hi, ind) + dot(lo, ind)


def head_sums(z_hi, z_lo, ind):
    return dot(z_hi, ind, NT) + dot(z_lo, ind, NT)


def triangle(n, keep):
    i = lax.broadcasted_iota(jnp.int32, (n, n), 0)
    j = lax.broadcasted_iota(jnp.int32, (n, n), 1)
    return jnp.where(keep(i, j), 1.0, 0.0).astype(f32)


def tri_sum(tri, v):
    return dot(tri, v, precision=lax.Precision.HIGHEST)


def softplus(z):
    return jnp.maximum(z, 0.0) + jnp.log1p(jnp.exp(-jnp.abs(z)))


def sigmoid(z):
    return 0.5 * jnp.tanh(0.5 * z) + 0.5


def taps_of(ext, at, row, rows):
    return [ext[at, pl.ds(PAD - K + 1 + k + row, rows), :] for k in range(K)]


def conv_pre(taps, wb, masks=None):
    total = wb[K : K + 1] + wb[K - 1 : K] * taps[K - 1]
    for k in range(K - 1):
        term = wb[k : k + 1] * taps[k]
        if masks is not None:
            term = term * masks[k]
        total = total + term
    return total


def act_and_slope(pre):
    sig = sigmoid(pre)
    act = pre * sig
    return act, sig + act * (1.0 - sig)


def fold8(v):
    return jnp.sum(v.reshape(v.shape[0] // 8, 8, v.shape[1]), axis=0)


def as_rows(parts):
    row = lax.broadcasted_iota(jnp.int32, (PAD, LANES), 0)
    total = jnp.zeros((PAD, LANES), f32)
    for k, part in enumerate(parts):
        total = total + jnp.where(row == k, jnp.sum(part, axis=0, keepdims=True), 0.0)
    return total


def lane_loop(width, body):
    def one(i, _):
        body(i, pl.ds(pl.multiple_of(i * LANES, LANES), LANES))
        return 0

    lax.fori_loop(0, width // LANES, one, 0)


RC = 64


def conv_forward(u, tail, wb, ext, act, slope, rows, width):
    def body(i, lanes):
        ext[i, 0:PAD, :] = tail[:, lanes]
        ext[i, PAD : PAD + rows, :] = u[:, lanes].astype(f32)
        w = wb[:, lanes]
        for r in range(0, rows, RC):
            a, s = act_and_slope(conv_pre(taps_of(ext, i, r, RC), w))
            act[r : r + RC, lanes] = a.astype(bf16)
            if slope is not None:
                slope[r : r + RC, lanes] = s

    lane_loop(width, body)


def conv_backward(ext, i, slope, lanes, cotangent, grad, rows):
    sums = [jnp.zeros((8, LANES), f32) for _ in range(K + 1)]
    for r in range(0, rows, RC):
        d = cotangent(r) * slope[r : r + RC, lanes]
        taps = taps_of(ext, i, r, RC)
        for k in range(K):
            sums[k] = sums[k] + fold8(d * taps[k])
        sums[K] = sums[K] + fold8(d)
    grad[:, lanes] = as_rows(sums)


def steps_kernel(len_ref, dt, hp, step, cum, cum_t, decay_in):
    rows = dt.shape[0]
    s = softplus(dt[...].astype(f32) + hp[1:2])
    logd = -jnp.exp(hp[0:1]) * s
    c = tri_sum(triangle(rows, lambda i, j: i >= j), logd)
    step[...] = s
    cum[...] = c
    cum_t[...] = c.T
    t = lax.broadcasted_iota(jnp.int32, c.shape, 0)
    decay_in[...] = jnp.where(t < len_ref[0, 0], jnp.exp(c), 0.0)


def resp_state_kernel(adv, u_c, tail_c, wb_c, dy, decay_in, state, weighted, c_out, ext):
    g = pl.program_id(0)
    rows, width = dy.shape
    conv_forward(u_c, tail_c, wb_c, ext, c_out, None, rows, N)
    c_t = c_out[...].astype(f32).T.astype(bf16)
    a = (dy[...].astype(f32) * expand(decay_in[...], indicator(g * HG, width))).astype(bf16)
    weighted[...] = a
    state[0] = (dot(c_t, a) * adv[0, 0]).astype(bf16)


def resp_mid_kernel(
    first, handed, len_ref, u_x, u_b, tail_x, tail_b, wb_x, wb_b, c_act, dy, step, cum, cum4, cum_t4, skip,
    earlier_out, *refs,
):
    if first:
        sums_in, refs = refs[3], refs[4:]
    if handed:
        refs = refs[:4] + refs[5:]
    g = first + pl.program_id(0)
    (
    grad_x, grad_b, dc, sums_out,
    ext, ext_b, x_s, xs_s, b_s, dym, slope, slope_b, step_e, y_s, t_s,
    a1, bm, sw_e, u_off, y_off, z_hi, z_lo, d_skip,
    ) = refs
    rows = u_x.shape[0]
    half = rows // 2
    conv_forward(u_x, tail_x, wb_x, ext, x_s, slope, rows, GX)
    conv_forward(u_b, tail_b, wb_b, ext_b, b_s, slope_b, rows, N)
    ind = indicator(g * HG, GX)
    step_e[...] = expand(step[...], ind)
    cum_v = cum[...]
    mid = cum_v[half - 1 : half]
    sw_e[...] = expand(jnp.exp(mid - cum_v[:half]) * step[:half], ind)
    y_off[...] = expand(jnp.exp(cum_v[half:] - mid), ind)
    live = jnp.where(lax.broadcasted_iota(jnp.int32, (rows, LANES), 0) < len_ref[0, 0], 1.0, 0.0)

    def prepare(i, lanes):
        d = dy[:, lanes].astype(f32) * live
        dym[:, lanes] = d.astype(bf16)
        x = x_s[:, lanes].astype(f32)
        xs_s[:, lanes] = (x * step_e[:, lanes]).astype(bf16)
        bm[:, lanes] = (x[:half] * sw_e[:, lanes]).astype(bf16)
        a1[:, lanes] = (d[half:] * y_off[:, lanes]).astype(bf16)

    lane_loop(GX, prepare)

    c_v, b_v = c_act[...], b_s[...]
    c0, c1, b0, b1 = c_v[:half], c_v[half:], b_v[:half], b_v[half:]
    i = lax.broadcasted_iota(jnp.int32, (half, half), 0)
    j = lax.broadcasted_iota(jnp.int32, (half, half), 1)
    lane = lax.broadcasted_iota(jnp.int32, (half, LANES), 1)
    left = jnp.where(lane < PS, 1.0, 0.0).astype(bf16)
    right = jnp.where(lane >= PS, 1.0, 0.0).astype(bf16)

    y_off[...] = dot(dot(c1, b0, NT).astype(bf16), bm[...])
    u_off[...] = dot(dot(b0, c1, NT).astype(bf16), a1[...])
    d10 = dot(a1[...], bm[...], NT)

    d_diag = []
    for q, (c_q, b_q) in enumerate(((c0, b0), (c1, b1))):
        r = slice(q * half, (q + 1) * half)
        lower = jnp.where(i >= j, dot(c_q, b_q, NT), 0.0)
        upper = jnp.where(j >= i, dot(b_q, c_q, NT), 0.0)
        d_sc = jnp.zeros((half, half), f32)
        for p in range(HG // 2):
            lanes = slice(p * LANES, (p + 1) * LANES)
            xs_p, dy_p = xs_s[r, lanes], dym[r, lanes]
            xb = jnp.concatenate([xs_p * left, xs_p * right], axis=0)
            dyb = jnp.concatenate([dy_p * left, dy_p * right], axis=0)
            d_m = dot(dy_p, xb, NT)
            mats, mats_t = [], []
            for a in range(2):
                h = 2 * p + a
                gap = jnp.exp(-jnp.abs(cum4[0, r, h : h + 1] - cum_t4[0, h : h + 1, r]))
                d_sc = d_sc + d_m[:, a * half : (a + 1) * half] * gap
                mats.append((gap * lower).astype(bf16))
                mats_t.append((gap * upper).astype(bf16))
            y_s[r, lanes] = dot(jnp.concatenate(mats, axis=1), xb)
            t_s[r, lanes] = dot(jnp.concatenate(mats_t, axis=1), dyb)
        d_diag.append(jnp.where(i >= j, d_sc, 0.0))

    d00, d11 = d_diag
    dc[:half] = dot(d00.astype(bf16), b0)
    dc[half:] = dot(d11.astype(bf16), b1) + dot(d10.astype(bf16), b0)
    db0 = dot(d00.T.astype(bf16), c0) + dot(d10.T.astype(bf16), c1)
    db1 = dot(d11.T.astype(bf16), c1)
    db = jnp.concatenate([db0, db1], axis=0)
    for k in range(N // LANES):
        lanes = slice(k * LANES, (k + 1) * LANES)
        conv_backward(ext_b, k, slope_b, lanes, lambda r: db[r : r + RC, lanes], grad_b, rows)

    def put(z, r, lanes):
        hi, lo = halves(z)
        z_hi[r : r + RC, lanes] = hi
        z_lo[r : r + RC, lanes] = lo

    def row_products(i, lanes):
        for r in range(0, rows, RC):
            z = dym[r : r + RC, lanes].astype(f32) * y_s[r : r + RC, lanes]
            if r >= half:
                o = r - half
                z = z + a1[o : o + RC, lanes].astype(f32) * y_off[o : o + RC, lanes]
            put(z, r, lanes)

    lane_loop(GX, row_products)
    row_sum = head_sums(z_hi[...], z_lo[...], ind)

    def finish(i, lanes):
        d_skips = jnp.zeros((8, LANES), f32)
        for r in range(0, rows, RC):
            t = t_s[r : r + RC, lanes]
            z = xs_s[r : r + RC, lanes].astype(f32) * t
            if r < half:
                z = z + bm[r : r + RC, lanes].astype(f32) * u_off[r : r + RC, lanes]
            put(z, r, lanes)
            d_skips = d_skips + fold8(
                dym[r : r + RC, lanes].astype(f32) * x_s[r : r + RC, lanes].astype(f32)
            )

        def cotangent(r):
            d = step_e[r : r + RC, lanes] * t_s[r : r + RC, lanes]
            d = d + skip[:, lanes] * dym[r : r + RC, lanes].astype(f32)
            if r < half:
                d = d + sw_e[r : r + RC, lanes] * u_off[r : r + RC, lanes]
            return d

        conv_backward(ext, i, slope, lanes, cotangent, grad_x, rows)
        d_skip[:, lanes] = d_skips

    lane_loop(GX, finish)
    col_sum = head_sums(z_hi[...], z_lo[...], ind)

    skip_sum = head_sums(*halves(d_skip[...]), ind)
    new = jnp.concatenate([row_sum, col_sum, skip_sum], axis=0)

    @pl.when(pl.program_id(0) == 0)
    def _():
        sums_out[...] = sums_in[...] + new if first else new

    @pl.when(pl.program_id(0) > 0)
    def _():
        sums_out[...] += new


X_TILES = XC // LANES
B_TILES = G * N // LANES
C_TILES = X_TILES + 2 * B_TILES
HEAD_TILE = (K + 1) * C_TILES // PAD


def tile(k):
    return slice(k * LANES, (k + 1) * LANES)


def resp_end_kernel(
    place, scale, u_c, tail_c, wb_c, c_act, weighted, start, dc, sums, step, dt, hp,
    grad_x, grad_b, p_grad, p_heads,
    packed, ext, c_s, slope, total, grad_c, tiles,
):
    g = pl.program_id(0)
    rows, width = weighted.shape
    conv_forward(u_c, tail_c, wb_c, ext, c_s, slope, rows, N)

    @pl.when(g == 0)
    def _():
        total[...] = sums[0:rows] - sums[rows : 2 * rows]

    a = weighted[...]
    z_hi, z_lo = halves(a.astype(f32) * dot(c_act[...], start[0]))
    total[...] += head_sums(z_hi, z_lo, indicator(g * HG, width))
    d = dc[...] + dot(a, start[0], NT)
    for k in range(N // LANES):
        conv_backward(ext, k, slope, tile(k), lambda r: d[r : r + RC, tile(k)], grad_c, rows)
        tiles[X_TILES + B_TILES + g * (N // LANES) + k] = grad_c[:, tile(k)] * scale[0, 0]

    @pl.when(g == pl.num_programs(0) - 1)
    def _():
        d_log = tri_sum(triangle(rows, lambda i, j: j >= i), total[...])
        rate = -jnp.exp(hp[0:1])
        s = step[...]
        d_step = sums[rows : 2 * rows] / s + rate * d_log
        sig = sigmoid(dt[...].astype(f32) + hp[1:2])
        heads = as_rows([d_log * rate * s, d_step * sig, sums[2 * rows :]])
        for k in range(X_TILES):
            tiles[k] = grad_x[:, tile(k)] * scale[0, 0]
        for k in range(B_TILES):
            tiles[X_TILES + k] = grad_b[:, tile(k)] * scale[0, 0]
        for k in range(width // LANES):
            tiles[place[0, 0] * (width // LANES) + k] += p_grad[:, tile(k)]
        for k in range(N // LANES):
            tiles[X_TILES + place[0, 0] * (N // LANES) + k] += p_grad[:, tile(width // LANES + k)]
        for k in range(K + 1):
            for at in range(C_TILES):
                row = k * C_TILES + at
                packed[row // PAD, row % PAD : row % PAD + 1] = tiles[at, k : k + 1]
        packed[HEAD_TILE] = heads * scale[0, 0] + p_heads[...]
        for k in range(HEAD_TILE + 1, packed.shape[0]):
            packed[k] = jnp.zeros((PAD, LANES), f32)


def unpack_kernel(packed, conv_w, conv_b, heads):
    for k in range(K + 1):
        for at in range(C_TILES):
            row = k * C_TILES + at
            part = packed[row // PAD, row % PAD : row % PAD + 1]
            if k < K:
                conv_w[k : k + 1, tile(at)] = part
            else:
                conv_b[:, tile(at)] = part
    heads[...] = packed[HEAD_TILE, 0:3]


RB = 256


def prompt_conv(v, masks, wb, ext, act, slope, row, width):
    def body(i, lanes):
        ext[i, PAD : PAD + RB, :] = v[pl.ds(row, RB), lanes].astype(f32)
        w = wb[:, lanes]
        for r in range(0, RB, RC):
            m = [masks[pl.ds(row + r, RC), k : k + 1] for k in range(K - 1)]
            a, s = act_and_slope(conv_pre(taps_of(ext, i, r, RC), w, m))
            act[r : r + RC, lanes] = a.astype(bf16)
            if slope is not None:
                slope[r : r + RC, lanes] = s

    lane_loop(width, body)


def fill_before(ext, v, halo, row):
    for i in range(ext.shape[0]):
        before = v[row - 16 : row, tile(i)].astype(f32)[16 - PAD :] if row else halo[:, tile(i)]
        ext[i, 0:PAD, :] = before


def prompt_state_kernel(
    place, v, halo, dt_all, masks, wb, hp, start, weight, step, beyond, ext, act, acc
):
    rows = v.shape[0]
    width = start.shape[1]
    first = place[0, 1]
    ind = indicator(place[0, 0] * HG, width)
    later = triangle(RB, lambda i, j: j > i)
    rate = -jnp.exp(hp[0:1])
    ahead = jnp.zeros((1, LANES), f32)
    slopes = jnp.zeros((1, LANES), f32)
    for row in range(0, dt_all.shape[0], RB):
        s = softplus(dt_all[row : row + RB].astype(f32) + hp[1:2])
        position = row + lax.broadcasted_iota(jnp.int32, s.shape, 0)
        past = position >= first + rows
        sig = sigmoid(dt_all[row : row + RB].astype(f32) + hp[1:2])
        ahead = ahead + rate * jnp.sum(jnp.where(past, s, 0.0), axis=0, keepdims=True)
        slopes = slopes + rate * jnp.sum(jnp.where(past, sig, 0.0), axis=0, keepdims=True)
    beyond[...] = jnp.zeros_like(beyond)
    beyond[0:1] = ahead
    beyond[1:2] = slopes
    acc[...] = jnp.zeros_like(acc)
    for row in range(rows - RB, -1, -RB):
        at = pl.ds(pl.multiple_of(first + row, RB), RB)
        s = softplus(dt_all[at, :].astype(f32) + hp[1:2])
        logd = rate * s
        after = tri_sum(later, logd) + ahead
        ahead = ahead + jnp.sum(logd, axis=0, keepdims=True)
        w = masks[row : row + RB, K - 1 : K] * jnp.exp(after) * s
        step[row : row + RB] = s
        weight[row : row + RB] = w
        fill_before(ext, v, halo, row)
        prompt_conv(v, masks, wb, ext, act, None, row, width + N)
        wx = (act[:, :width].astype(f32) * expand(w, ind)).astype(bf16)
        acc[...] += dot(act[:, width:].astype(f32).T.astype(bf16), wx)
    start[...] = acc[...].astype(bf16)


def prompt_grad_kernel(
    count, place, v, halo, dt_mine, masks, wb, hp, weight, step, beyond, *refs
):
    states = refs[:count]
    grad, grad_h, ext, act, slope, g_s, d_s, sums = refs[count + 1 :]
    rows = v.shape[0]
    width = g_s.shape[1]
    ind = indicator(place[0, 0] * HG, width)
    earlier = triangle(RB, lambda i, j: j < i)
    total = states[0][...].astype(f32)
    for k in range(1, count):
        total = total + states[k][...].astype(f32)
    g_s[...] = total.astype(bf16)
    behind = jnp.zeros((1, LANES), f32)
    rate = -jnp.exp(hp[0:1])
    d_rate = jnp.zeros((1, LANES), f32)
    d_bias = jnp.zeros((1, LANES), f32)
    sums[...] = jnp.zeros_like(sums)
    for row in range(0, rows, RB):
        fill_before(ext, v, halo, row)
        prompt_conv(v, masks, wb, ext, act, slope, row, width + N)
        w_e = expand(weight[row : row + RB], ind)
        t = dot(act[:, width:], g_s[...])
        wx = (act[:, :width].astype(f32) * w_e).astype(bf16)
        d_s[:, :width] = t * w_e
        d_s[:, width:] = dot(wx, g_s[...], NT)
        z_hi, z_lo = halves(wx.astype(f32) * t)
        q = head_sums(z_hi, z_lo, ind)
        d_log = tri_sum(earlier, q) + behind
        behind = behind + jnp.sum(q, axis=0, keepdims=True)
        s = step[row : row + RB]
        d_step = q / s + rate * d_log
        sig = sigmoid(dt_mine[row : row + RB].astype(f32) + hp[1:2])
        d_rate = d_rate + jnp.sum(d_log * rate * s, axis=0, keepdims=True)
        d_bias = d_bias + jnp.sum(d_step * sig, axis=0, keepdims=True)

        def back(i, lanes):
            acc = [jnp.zeros((8, LANES), f32) for _ in range(K + 1)]
            for r in range(0, RB, RC):
                d = d_s[r : r + RC, lanes] * slope[r : r + RC, lanes]
                taps = taps_of(ext, i, r, RC)
                for k in range(K):
                    part = d * taps[k]
                    if k < K - 1:
                        part = part * masks[pl.ds(row + r, RC), k : k + 1]
                    acc[k] = acc[k] + fold8(part)
                acc[K] = acc[K] + fold8(d)
            for k in range(K + 1):
                sums[k : k + 1, lanes] += jnp.sum(acc[k], axis=0, keepdims=True)

        lane_loop(width + N, back)
    grad[...] = sums[...]
    grad_h[...] = jnp.zeros_like(grad_h)
    grad_h[0:1] = d_rate + behind * beyond[0:1]
    grad_h[1:2] = d_bias + behind * beyond[1:2]


def add_kernel(terms, *refs):
    out = refs[-1]
    total = None
    for k in range(terms):
        part = refs[k][...].astype(f32)
        total = part if total is None else total + part
    total = total.astype(bf16)
    if out.ndim == 2:
        out[...] = total
    else:
        for k in range(out.shape[0]):
            out[k] = total


def params(*semantics):
    return pltpu.CompilerParams(
        vmem_limit_bytes=VMEM_MIB * 2**20, dimension_semantics=semantics or None
    )


SMEM = pl.BlockSpec(memory_space=pltpu.SMEM)
PROMPT_GRAD_FLOPS = 2**38


def whole(shape):
    return pl.BlockSpec(shape, lambda *_: (0,) * len(shape))


def sds(shape, dtype):
    return jax.ShapeDtypeStruct(shape, dtype)


def response_steps(length, dt, hp):
    rows = dt.shape[0]
    square = sds((rows, H), f32)
    return pl.pallas_call(
        steps_kernel,
        out_shape=(square, square, sds((H, rows), f32), square),
        in_specs=[SMEM, pl.BlockSpec(), pl.BlockSpec()],
        compiler_params=params(),
        name="resp_steps",
    )(length, dt, hp)


def response_state(scale, u, tail, wb, dy, decay_in):
    rows = u.shape[0]
    c_at = lambda g: (0, XC // N + G + g)
    g_at = lambda g: (0, g)
    return pl.pallas_call(
        resp_state_kernel,
        grid=(G,),
        in_specs=[
            SMEM,
            pl.BlockSpec((rows, N), c_at),
            pl.BlockSpec((PAD, N), c_at),
            pl.BlockSpec((PAD, N), c_at),
            pl.BlockSpec((rows, GX), g_at),
            whole((rows, H)),
        ],
        out_specs=[
            pl.BlockSpec((1, N, GX), lambda g: (g, 0, 0)),
            pl.BlockSpec((rows, GX), g_at),
            pl.BlockSpec((rows, N), g_at),
        ],
        out_shape=(sds((G, N, GX), bf16), sds((rows, XC), bf16), sds((rows, G * N), bf16)),
        scratch_shapes=[pltpu.VMEM((N // LANES, PAD + rows, LANES), f32)],
        compiler_params=params("arbitrary"),
        cost_estimate=pl.CostEstimate(
            flops=2 * rows * N * XC, bytes_accessed=14 * 2**20, transcendentals=rows * G * N
        ),
        name="resp_state",
    )(scale, u, tail, wb, dy, decay_in)


def response_mid(
    first, count, length, u, tail, wb, c_act, dy, step, cum, cum4, cum_t4, skip,
    earlier_out, so_far, handed,
):
    rows = u.shape[0]
    half = rows // 2
    x_at = lambda i: (0, first + i)
    b_at = lambda i: (0, XC // N + first + i)
    sums = (2 * rows + PAD, H)
    v = pltpu.VMEM
    anywhere = pl.BlockSpec(memory_space=pl.ANY)
    return pl.pallas_call(
        functools.partial(resp_mid_kernel, first, handed),
        grid=(count,),
        in_specs=[
            SMEM,
            pl.BlockSpec((rows, GX), x_at),
            pl.BlockSpec((rows, N), b_at),
            pl.BlockSpec((PAD, GX), x_at),
            pl.BlockSpec((PAD, N), b_at),
            pl.BlockSpec((PAD, GX), x_at),
            pl.BlockSpec((PAD, N), b_at),
            pl.BlockSpec((rows, N), x_at),
            pl.BlockSpec((rows, GX), x_at),
            whole((rows, H)),
            whole((rows, H)),
            pl.BlockSpec((1, rows, HG), lambda i: (first + i, 0, 0)),
            pl.BlockSpec((1, HG, rows), lambda i: (first + i, 0, 0)),
            pl.BlockSpec((1, GX), x_at),
            anywhere,
        ]
        + ([anywhere] * 3 + [whole(sums)] if so_far else []),
        out_specs=[
            pl.BlockSpec((PAD, GX), x_at),
            pl.BlockSpec((PAD, N), x_at),
            pl.BlockSpec((rows, N), x_at),
            whole(sums),
        ]
        + ([anywhere] if handed else []),
        out_shape=(
            sds((PAD, XC), f32),
            sds((PAD, G * N), f32),
            sds((rows, G * N), f32),
            sds(sums, f32),
        )
        + ((sds(earlier_out.shape, earlier_out.dtype),) if handed else ()),
        input_output_aliases=({15 + k: k for k in range(3)} if so_far else {})
        | ({14: 4} if handed else {}),
        scratch_shapes=[
            v((GX // LANES, PAD + rows, LANES), f32),
            v((N // LANES, PAD + rows, LANES), f32),
            v((rows, GX), bf16),
            v((rows, GX), bf16),
            v((rows, N), bf16),
            v((rows, GX), bf16),
            v((rows, GX), f32),
            v((rows, N), f32),
            v((rows, GX), f32),
            v((rows, GX), f32),
            v((rows, GX), f32),
            v((half, GX), bf16),
            v((half, GX), bf16),
            v((half, GX), f32),
            v((half, GX), f32),
            v((half, GX), f32),
            v((rows, GX), bf16),
            v((rows, GX), bf16),
            v((PAD, GX), f32),
        ],
        compiler_params=params("arbitrary"),
        cost_estimate=pl.CostEstimate(
            flops=8 * 2**30, bytes_accessed=3 * 2**20, transcendentals=rows * half * HG
        ),
        name="resp_mid",
    )(
        length, u, u, tail, tail, wb, wb, c_act, dy, step, cum, cum4, cum_t4, skip, earlier_out,
        *so_far,
    )


def response_end(
    tiles, place, scale, u, tail, wb, c_act, weighted, start, dc, sums, step, dt, hp, grads
):
    rows = u.shape[0]
    c_at = lambda g: (0, XC // N + G + g)
    g_at = lambda g: (0, g)
    v = pltpu.VMEM
    return pl.pallas_call(
        resp_end_kernel,
        grid=(G,),
        in_specs=[
            SMEM,
            SMEM,
            pl.BlockSpec((rows, N), c_at),
            pl.BlockSpec((PAD, N), c_at),
            pl.BlockSpec((PAD, N), c_at),
            pl.BlockSpec((rows, N), g_at),
            pl.BlockSpec((rows, GX), g_at),
            pl.BlockSpec((1, N, GX), lambda g: (g, 0, 0)),
            pl.BlockSpec((rows, N), g_at),
        ]
        + [whole(a.shape) for a in (sums, step, dt, hp, *grads)],
        out_specs=whole((tiles, PAD, LANES)),
        out_shape=sds((tiles, PAD, LANES), f32),
        scratch_shapes=[
            v((N // LANES, PAD + rows, LANES), f32),
            v((rows, N), bf16),
            v((rows, N), f32),
            v((rows, H), f32),
            v((PAD, N), f32),
            v((C_TILES, PAD, LANES), f32),
        ],
        compiler_params=params("arbitrary"),
        cost_estimate=pl.CostEstimate(
            flops=4 * rows * N * XC, bytes_accessed=12 * 2**20, transcendentals=rows * G * N
        ),
        name="resp_end",
    )(place, scale, u, tail, wb, c_act, weighted, start, dc, sums, step, dt, hp, *grads)


def unpack(packed):
    width = C_TILES * LANES
    return pl.pallas_call(
        unpack_kernel,
        out_shape=(sds((K, width), f32), sds((1, width), f32), sds((3, H), f32)),
        compiler_params=params(),
        name="unpack",
    )(packed)


def add_states(terms, earlier_out, copies=0):
    rows, width = terms[0].shape
    part = rows // 4
    one = pl.BlockSpec((part, width), lambda i: (i, 0))
    if isinstance(terms, list):
        blocks = [one] * len(terms)
    else:
        blocks = [
            pl.BlockSpec((None, part, width), lambda i, k=k: (k, i, 0))
            for k in range(terms.shape[0])
        ]
        terms = [terms] * terms.shape[0]
    many = pl.BlockSpec((copies, part, width), lambda i: (0, i, 0))
    return pl.pallas_call(
        functools.partial(add_kernel, len(terms)),
        grid=(4,),
        in_specs=blocks + [pl.BlockSpec(memory_space=pl.ANY)],
        out_specs=many if copies else one,
        out_shape=sds((copies, rows, width) if copies else (rows, width), bf16),
        compiler_params=params("arbitrary"),
        cost_estimate=pl.CostEstimate(
            flops=8 * rows * width, bytes_accessed=12 * rows * width, transcendentals=0
        ),
        name="add_states",
    )(*terms, earlier_out)


def prompt_state(place, v, halo, dt_all, masks, wb, hp):
    rows = v.shape[0]
    width = v.shape[1] - N
    s = pltpu.VMEM
    return pl.pallas_call(
        prompt_state_kernel,
        in_specs=[SMEM] + [pl.BlockSpec()] * 6,
        out_shape=(
            sds((N, width), bf16),
            sds((rows, LANES), f32),
            sds((rows, LANES), f32),
            sds((PAD, LANES), f32),
        ),
        scratch_shapes=[
            s(((width + N) // LANES, PAD + RB, LANES), f32),
            s((RB, width + N), bf16),
            s((N, width), f32),
        ],
        compiler_params=params(),
        cost_estimate=pl.CostEstimate(
            flops=2 * rows * N * width, bytes_accessed=4 * 2**20, transcendentals=rows * width
        ),
        name="prompt_state",
    )(place, v, halo, dt_all, masks, wb, hp)


def prompt_grad(
    place, v, halo, dt_mine, masks, wb, hp, weight, step, beyond, states, earlier_out
):
    rows = v.shape[0]
    width = v.shape[1] - N
    s = pltpu.VMEM
    return pl.pallas_call(
        functools.partial(prompt_grad_kernel, len(states)),
        in_specs=[SMEM]
        + [pl.BlockSpec()] * (9 + len(states))
        + [pl.BlockSpec(memory_space=pl.ANY)],
        out_shape=(sds((PAD, width + N), f32), sds((PAD, LANES), f32)),
        scratch_shapes=[
            s(((width + N) // LANES, PAD + RB, LANES), f32),
            s((RB, width + N), bf16),
            s((RB, width + N), f32),
            s((N, width), bf16),
            s((RB, width + N), f32),
            s((PAD, width + N), f32),
        ],
        compiler_params=params(),
        cost_estimate=pl.CostEstimate(
            flops=PROMPT_GRAD_FLOPS, bytes_accessed=8 * 2**20, transcendentals=rows * width
        ),
        name="prompt_grad",
    )(place, v, halo, dt_mine, masks, wb, hp, weight, step, beyond, *states, earlier_out)


def doc_number(starts, positions):
    return jnp.sum((starts[None, :] <= positions[:, None]).astype(jnp.int32), axis=1)


def prompt_masks(starts, rows):
    positions = jnp.arange(rows, dtype=jnp.int32)
    docs = doc_number(starts, positions)
    same = [doc_number(starts, positions - (K - 1 - k)) == docs for k in range(K - 1)]
    columns = jnp.stack(same + [docs == docs[rows - 1]], axis=1).astype(f32)
    return jnp.pad(columns, ((0, 0), (0, PAD - K)))


def pad_rows(a):
    return jnp.pad(a, ((0, PAD - a.shape[0]), (0, 0)))


def to_all(block, axes, devices, groups=None):
    copies = jnp.broadcast_to(block[None], (devices,) + block.shape)
    return lax.all_to_all(copies, axes, 0, 0, axis_index_groups=groups)


def sum_over_all(packed, axes, devices):
    slices = packed.reshape((devices, packed.shape[0] // devices) + packed.shape[1:])
    mine = jnp.sum(lax.all_to_all(slices, axes, 0, 0), axis=0)
    return to_all(mine, axes, devices).reshape(packed.shape)


def shards(
    prompt_in, prompt_dt, doc_starts, resp_in, resp_dt, resp_len, upstream, reward,
    conv_w, conv_b, head_params,
):
    n = lax.axis_size("resp")
    me = lax.axis_index("resp")
    clusters = n // G
    mine = me % G
    cluster = me // G
    inside = [list(range(c * G, c * G + G)) for c in range(clusters)]
    block = prompt_in.shape[1]
    slots = resp_in.shape[2]
    rows_in, dt_in = prompt_in[0], prompt_dt[0]
    u, dt, dy = resp_in[0, 0], resp_dt[0, 0], upstream[0, 0]

    r = reward[0, 0]
    r_hi = r.astype(bf16)
    r_mid = (r - r_hi.astype(f32)).astype(bf16)
    r_lo = (r - r_hi.astype(f32) - r_mid.astype(f32)).astype(bf16)
    tail_size = (K - 1) * rows_in.shape[1] // LANES
    small = jnp.concatenate(
        [
            rows_in[block - K + 1 :].reshape(tail_size, LANES),
            dt_in,
            jnp.broadcast_to(
                jnp.stack([r_hi, r_mid, r_lo, jnp.zeros_like(r_lo)])[:, None], (4, LANES)
            ),
            jnp.zeros((12, LANES), bf16),
        ]
    )
    small = to_all(small, "resp", n)
    wb = pad_rows(jnp.concatenate([conv_w, conv_b[None]], axis=0))
    hp = pad_rows(head_params)

    x_parts = rows_in[:, :XC].reshape(block, G, GX).transpose(1, 0, 2)
    b_parts = rows_in[:, XC : XC + G * N].reshape(block, G, N).transpose(1, 0, 2)
    parts = jnp.concatenate([x_parts, b_parts], axis=2)
    v = parts
    for k in range(1, G):
        route = [(c * G + q, c * G + (q + k) % G) for c in range(clusters) for q in range(G)]
        sent = lax.dynamic_index_in_dim(parts, (mine + k) % G, 0, False)
        came = lax.ppermute(sent, "resp", route)
        v = lax.dynamic_update_index_in_dim(v, came, (mine - k) % G, 0)
    v = v.reshape(G * block, GX + N)

    def own_channels(a):
        return jnp.concatenate(
            [
                lax.dynamic_slice(a, (0, mine * GX), (PAD, GX)),
                lax.dynamic_slice(a, (0, XC + mine * N), (PAD, N)),
            ],
            axis=1,
        )

    def last_rows(device):
        rows = lax.dynamic_index_in_dim(small, device, 0, False)[:tail_size]
        return jnp.pad(rows.reshape(K - 1, -1).astype(f32), ((PAD - K + 1, 0), (0, 0)))

    tail = last_rows(n - 1)
    halo = own_channels(last_rows(jnp.maximum(cluster * G - 1, 0)))
    dt_all = small[:, tail_size : tail_size + block].reshape(n * block, H)
    dt_mine = lax.dynamic_slice(dt_all, (cluster * G * block, 0), (G * block, H))
    at_reward = tail_size + block
    rewards = jnp.sum(small[:, at_reward : at_reward + 3, 0].astype(f32), axis=1)
    scale = ((r - jnp.sum(rewards) / n) / slots).reshape(1, 1)
    masks = lax.dynamic_slice(
        prompt_masks(doc_starts[0], n * block), (cluster * G * block, 0), (G * block, PAD)
    )
    wb_mine = own_channels(wb)
    place = jnp.stack([mine, cluster * G * block]).astype(jnp.int32).reshape(1, 2)

    length = resp_len.astype(jnp.int32)
    step, cum, cum_t, decay_in = response_steps(length, dt, hp)
    d_states, weighted, c_act = response_state(scale, u, tail, wb, dy, decay_in)
    d_states = lax.all_to_all(d_states, "resp", 0, 0, axis_index_groups=inside)

    cum4 = cum.reshape(slots, G, HG).transpose(1, 0, 2)
    skip = jnp.repeat(head_params[2], PS)[None, :]

    def mid(first, count, earlier_out, so_far=(), handed=False):
        return response_mid(
            first, count, length, u, tail, wb, c_act, dy, step, cum, cum4,
            cum_t.reshape(G, HG, slots), skip, earlier_out, so_far, handed,
        )

    def across(part):
        routes = [[(i, (i + c * G) % n) for i in range(n)] for c in range(1, clusters)]
        return [part] + [lax.ppermute(part, "resp", route) for route in routes]

    part, weight, p_step, beyond = prompt_state(place, v, halo, dt_all, masks, wb_mine, hp)
    parts_of_start = across(part)
    grads = mid(0, 1, weight)
    part = add_states(d_states, grads[3])
    parts_of_grad = across(part)
    grad_x, grad_b, dc, sums = mid(1, G - 1, part, grads)
    start = add_states(parts_of_start, sums, copies=G)
    start = lax.all_to_all(start, "resp", 0, 0, axis_index_groups=inside)
    p_grad, p_heads = prompt_grad(
        place, v, halo, dt_mine, masks, wb_mine, hp, weight, p_step, beyond, parts_of_grad, sums
    )

    axes = ("group", "resp")
    devices = lax.axis_size(axes)
    tiles = devices * -(-(HEAD_TILE + 1) // devices)
    packed = response_end(
        tiles, place, scale, u, tail, wb, c_act, weighted, start, dc, sums, step, dt, hp,
        (grad_x, grad_b, p_grad, p_heads),
    )
    grad_w, grad_bias, heads = unpack(sum_over_all(packed, axes, devices))
    return grad_w, grad_bias.reshape(-1), heads


def solution(mesh):
    in_specs = (
        P("group", "resp", None),
        P("group", "resp", None),
        P("group", None),
        P("group", "resp", None, None),
        P("group", "resp", None, None),
        P("group", "resp"),
        P("group", "resp", None, None),
        P("group", "resp"),
        P(),
        P(),
        P(),
    )
    out_specs = (P(), P(), P())
    return jax.shard_map(shards, mesh=mesh, in_specs=in_specs, out_specs=out_specs, check_vma=False)
```

```python
import functools

import jax
import jax.numpy as jnp
from jax import lax
from jax.experimental import pallas as pl
from jax.experimental.pallas import tpu as pltpu
from jax.sharding import PartitionSpec as P

H = 128
PS = 64
N = 256
G = 4
K = 4
HG = H // G
XC = H * PS
GX = HG * PS
LANES = 128
PAD = 8
VMEM_MIB = 63

f32 = jnp.float32
bf16 = jnp.bfloat16

NN = (((1,), (0,)), ((), ()))
NT = (((1,), (1,)), ((), ()))


def dot(a, b, dims=NN, precision=None):
    return lax.dot_general(a, b, dims, precision=precision, preferred_element_type=f32)


def halves(v):
    hi = v.astype(bf16)
    return hi, (v - hi.astype(f32)).astype(bf16)


def indicator(first, width):
    row = lax.broadcasted_iota(jnp.int32, (LANES, width), 0)
    head = lax.shift_right_logical(lax.broadcasted_iota(jnp.int32, (LANES, width), 1), 6)
    return jnp.where(row - first == head, 1.0, 0.0).astype(bf16)


def expand(v, ind):
    hi, lo = halves(v)
    return dot(hi, ind) + dot(lo, ind)


def head_sums(z_hi, z_lo, ind):
    return dot(z_hi, ind, NT) + dot(z_lo, ind, NT)


def triangle(n, keep):
    i = lax.broadcasted_iota(jnp.int32, (n, n), 0)
    j = lax.broadcasted_iota(jnp.int32, (n, n), 1)
    return jnp.where(keep(i, j), 1.0, 0.0).astype(f32)


def tri_sum(tri, v):
    return dot(tri, v, precision=lax.Precision.HIGHEST)


def softplus(z):
    return jnp.maximum(z, 0.0) + jnp.log1p(jnp.exp(-jnp.abs(z)))


def sigmoid(z):
    return 0.5 * jnp.tanh(0.5 * z) + 0.5


def taps_of(ext, at, row, rows):
    return [ext[at, pl.ds(PAD - K + 1 + k + row, rows), :] for k in range(K)]


def conv_pre(taps, wb, masks=None):
    total = wb[K : K + 1] + wb[K - 1 : K] * taps[K - 1]
    for k in range(K - 1):
        term = wb[k : k + 1] * taps[k]
        if masks is not None:
            term = term * masks[k]
        total = total + term
    return total


def act_and_slope(pre):
    sig = sigmoid(pre)
    act = pre * sig
    return act, sig + act * (1.0 - sig)


def fold8(v):
    return jnp.sum(v.reshape(v.shape[0] // 8, 8, v.shape[1]), axis=0)


def as_rows(parts):
    row = lax.broadcasted_iota(jnp.int32, (PAD, LANES), 0)
    total = jnp.zeros((PAD, LANES), f32)
    for k, part in enumerate(parts):
        total = total + jnp.where(row == k, jnp.sum(part, axis=0, keepdims=True), 0.0)
    return total


def lane_loop(width, body):
    def one(i, _):
        body(i, pl.ds(pl.multiple_of(i * LANES, LANES), LANES))
        return 0

    lax.fori_loop(0, width // LANES, one, 0)


RC = 64


def conv_forward(u, tail, wb, ext, act, slope, rows, width):
    def body(i, lanes):
        ext[i, 0:PAD, :] = tail[:, lanes]
        ext[i, PAD : PAD + rows, :] = u[:, lanes].astype(f32)
        w = wb[:, lanes]
        for r in range(0, rows, RC):
            a, s = act_and_slope(conv_pre(taps_of(ext, i, r, RC), w))
            act[r : r + RC, lanes] = a.astype(bf16)
            if slope is not None:
                slope[r : r + RC, lanes] = s

    lane_loop(width, body)


def conv_backward(ext, i, slope, lanes, cotangent, grad, rows):
    sums = [jnp.zeros((8, LANES), f32) for _ in range(K + 1)]
    for r in range(0, rows, RC):
        d = cotangent(r) * slope[r : r + RC, lanes]
        taps = taps_of(ext, i, r, RC)
        for k in range(K):
            sums[k] = sums[k] + fold8(d * taps[k])
        sums[K] = sums[K] + fold8(d)
    grad[:, lanes] = as_rows(sums)


def steps_kernel(len_ref, dt, hp, step, cum, cum_t, decay_in):
    rows = dt.shape[0]
    s = softplus(dt[...].astype(f32) + hp[1:2])
    logd = -jnp.exp(hp[0:1]) * s
    c = tri_sum(triangle(rows, lambda i, j: i >= j), logd)
    step[...] = s
    cum[...] = c
    cum_t[...] = c.T
    t = lax.broadcasted_iota(jnp.int32, c.shape, 0)
    decay_in[...] = jnp.where(t < len_ref[0, 0], jnp.exp(c), 0.0)


def resp_state_kernel(adv, u_c, tail_c, wb_c, dy, decay_in, state, weighted, c_out, ext):
    g = pl.program_id(0)
    rows, width = dy.shape
    conv_forward(u_c, tail_c, wb_c, ext, c_out, None, rows, N)
    c_t = c_out[...].astype(f32).T.astype(bf16)
    a = (dy[...].astype(f32) * expand(decay_in[...], indicator(g * HG, width))).astype(bf16)
    weighted[...] = a
    state[0] = (dot(c_t, a) * adv[0, 0]).astype(bf16)


def resp_mid_kernel(
    first, handed, len_ref, u_x, u_b, tail_x, tail_b, wb_x, wb_b, c_act, dy, step, cum, cum4, cum_t4, skip,
    earlier_out, *refs,
):
    if first:
        sums_in, refs = refs[3], refs[4:]
    if handed:
        refs = refs[:4] + refs[5:]
    g = first + pl.program_id(0)
    (
    grad_x, grad_b, dc, sums_out,
    ext, ext_b, x_s, xs_s, b_s, dym, slope, slope_b, step_e, y_s, t_s,
    a1, bm, sw_e, u_off, y_off, z_hi, z_lo, d_skip,
    ) = refs
    rows = u_x.shape[0]
    half = rows // 2
    conv_forward(u_x, tail_x, wb_x, ext, x_s, slope, rows, GX)
    conv_forward(u_b, tail_b, wb_b, ext_b, b_s, slope_b, rows, N)
    ind = indicator(g * HG, GX)
    step_e[...] = expand(step[...], ind)
    cum_v = cum[...]
    mid = cum_v[half - 1 : half]
    sw_e[...] = expand(jnp.exp(mid - cum_v[:half]) * step[:half], ind)
    y_off[...] = expand(jnp.exp(cum_v[half:] - mid), ind)
    live = jnp.where(lax.broadcasted_iota(jnp.int32, (rows, LANES), 0) < len_ref[0, 0], 1.0, 0.0)

    def prepare(i, lanes):
        d = dy[:, lanes].astype(f32) * live
        dym[:, lanes] = d.astype(bf16)
        x = x_s[:, lanes].astype(f32)
        xs_s[:, lanes] = (x * step_e[:, lanes]).astype(bf16)
        bm[:, lanes] = (x[:half] * sw_e[:, lanes]).astype(bf16)
        a1[:, lanes] = (d[half:] * y_off[:, lanes]).astype(bf16)

    lane_loop(GX, prepare)

    c_v, b_v = c_act[...], b_s[...]
    c0, c1, b0, b1 = c_v[:half], c_v[half:], b_v[:half], b_v[half:]
    i = lax.broadcasted_iota(jnp.int32, (half, half), 0)
    j = lax.broadcasted_iota(jnp.int32, (half, half), 1)
    lane = lax.broadcasted_iota(jnp.int32, (half, LANES), 1)
    left = jnp.where(lane < PS, 1.0, 0.0).astype(bf16)
    right = jnp.where(lane >= PS, 1.0, 0.0).astype(bf16)

    y_off[...] = dot(dot(c1, b0, NT).astype(bf16), bm[...])
    u_off[...] = dot(dot(b0, c1, NT).astype(bf16), a1[...])
    d10 = dot(a1[...], bm[...], NT)

    d_diag = []
    for q, (c_q, b_q) in enumerate(((c0, b0), (c1, b1))):
        r = slice(q * half, (q + 1) * half)
        lower = jnp.where(i >= j, dot(c_q, b_q, NT), 0.0)
        upper = jnp.where(j >= i, dot(b_q, c_q, NT), 0.0)
        d_sc = jnp.zeros((half, half), f32)
        for p in range(HG // 2):
            lanes = slice(p * LANES, (p + 1) * LANES)
            xs_p, dy_p = xs_s[r, lanes], dym[r, lanes]
            xb = jnp.concatenate([xs_p * left, xs_p * right], axis=0)
            dyb = jnp.concatenate([dy_p * left, dy_p * right], axis=0)
            d_m = dot(dy_p, xb, NT)
            mats, mats_t = [], []
            for a in range(2):
                h = 2 * p + a
                gap = jnp.exp(-jnp.abs(cum4[0, r, h : h + 1] - cum_t4[0, h : h + 1, r]))
                d_sc = d_sc + d_m[:, a * half : (a + 1) * half] * gap
                mats.append((gap * lower).astype(bf16))
                mats_t.append((gap * upper).astype(bf16))
            y_s[r, lanes] = dot(jnp.concatenate(mats, axis=1), xb)
            t_s[r, lanes] = dot(jnp.concatenate(mats_t, axis=1), dyb)
        d_diag.append(jnp.where(i >= j, d_sc, 0.0))

    d00, d11 = d_diag
    dc[:half] = dot(d00.astype(bf16), b0)
    dc[half:] = dot(d11.astype(bf16), b1) + dot(d10.astype(bf16), b0)
    db0 = dot(d00.T.astype(bf16), c0) + dot(d10.T.astype(bf16), c1)
    db1 = dot(d11.T.astype(bf16), c1)
    db = jnp.concatenate([db0, db1], axis=0)
    for k in range(N // LANES):
        lanes = slice(k * LANES, (k + 1) * LANES)
        conv_backward(ext_b, k, slope_b, lanes, lambda r: db[r : r + RC, lanes], grad_b, rows)

    def put(z, r, lanes):
        hi, lo = halves(z)
        z_hi[r : r + RC, lanes] = hi
        z_lo[r : r + RC, lanes] = lo

    def row_products(i, lanes):
        for r in range(0, rows, RC):
            z = dym[r : r + RC, lanes].astype(f32) * y_s[r : r + RC, lanes]
            if r >= half:
                o = r - half
                z = z + a1[o : o + RC, lanes].astype(f32) * y_off[o : o + RC, lanes]
            put(z, r, lanes)

    lane_loop(GX, row_products)
    row_sum = head_sums(z_hi[...], z_lo[...], ind)

    def finish(i, lanes):
        d_skips = jnp.zeros((8, LANES), f32)
        for r in range(0, rows, RC):
            t = t_s[r : r + RC, lanes]
            z = xs_s[r : r + RC, lanes].astype(f32) * t
            if r < half:
                z = z + bm[r : r + RC, lanes].astype(f32) * u_off[r : r + RC, lanes]
            put(z, r, lanes)
            d_skips = d_skips + fold8(
                dym[r : r + RC, lanes].astype(f32) * x_s[r : r + RC, lanes].astype(f32)
            )

        def cotangent(r):
            d = step_e[r : r + RC, lanes] * t_s[r : r + RC, lanes]
            d = d + skip[:, lanes] * dym[r : r + RC, lanes].astype(f32)
            if r < half:
                d = d + sw_e[r : r + RC, lanes] * u_off[r : r + RC, lanes]
            return d

        conv_backward(ext, i, slope, lanes, cotangent, grad_x, rows)
        d_skip[:, lanes] = d_skips

    lane_loop(GX, finish)
    col_sum = head_sums(z_hi[...], z_lo[...], ind)

    skip_sum = head_sums(*halves(d_skip[...]), ind)
    new = jnp.concatenate([row_sum, col_sum, skip_sum], axis=0)

    @pl.when(pl.program_id(0) == 0)
    def _():
        sums_out[...] = sums_in[...] + new if first else new

    @pl.when(pl.program_id(0) > 0)
    def _():
        sums_out[...] += new


X_TILES = XC // LANES
B_TILES = G * N // LANES
C_TILES = X_TILES + 2 * B_TILES
HEAD_TILE = (K + 1) * C_TILES // PAD


def tile(k):
    return slice(k * LANES, (k + 1) * LANES)


def resp_end_kernel(
    place, scale, u_c, tail_c, wb_c, c_act, weighted, start, dc, sums, step, dt, hp,
    grad_x, grad_b, p_grad, p_heads,
    packed, ext, c_s, slope, total, grad_c, tiles,
):
    g = pl.program_id(0)
    rows, width = weighted.shape
    conv_forward(u_c, tail_c, wb_c, ext, c_s, slope, rows, N)

    @pl.when(g == 0)
    def _():
        total[...] = sums[0:rows] - sums[rows : 2 * rows]

    a = weighted[...]
    z_hi, z_lo = halves(a.astype(f32) * dot(c_act[...], start[0]))
    total[...] += head_sums(z_hi, z_lo, indicator(g * HG, width))
    d = dc[...] + dot(a, start[0], NT)
    for k in range(N // LANES):
        conv_backward(ext, k, slope, tile(k), lambda r: d[r : r + RC, tile(k)], grad_c, rows)
        tiles[X_TILES + B_TILES + g * (N // LANES) + k] = grad_c[:, tile(k)] * scale[0, 0]

    @pl.when(g == pl.num_programs(0) - 1)
    def _():
        d_log = tri_sum(triangle(rows, lambda i, j: j >= i), total[...])
        rate = -jnp.exp(hp[0:1])
        s = step[...]
        d_step = sums[rows : 2 * rows] / s + rate * d_log
        sig = sigmoid(dt[...].astype(f32) + hp[1:2])
        heads = as_rows([d_log * rate * s, d_step * sig, sums[2 * rows :]])
        for k in range(X_TILES):
            tiles[k] = grad_x[:, tile(k)] * scale[0, 0]
        for k in range(B_TILES):
            tiles[X_TILES + k] = grad_b[:, tile(k)] * scale[0, 0]
        for k in range(width // LANES):
            tiles[place[0, 0] * (width // LANES) + k] += p_grad[:, tile(k)]
        for k in range(N // LANES):
            tiles[X_TILES + place[0, 0] * (N // LANES) + k] += p_grad[:, tile(width // LANES + k)]
        for k in range(K + 1):
            for at in range(C_TILES):
                row = k * C_TILES + at
                packed[row // PAD, row % PAD : row % PAD + 1] = tiles[at, k : k + 1]
        packed[HEAD_TILE] = heads * scale[0, 0] + p_heads[...]
        for k in range(HEAD_TILE + 1, packed.shape[0]):
            packed[k] = jnp.zeros((PAD, LANES), f32)


def unpack_kernel(packed, conv_w, conv_b, heads):
    for k in range(K + 1):
        for at in range(C_TILES):
            row = k * C_TILES + at
            part = packed[row // PAD, row % PAD : row % PAD + 1]
            if k < K:
                conv_w[k : k + 1, tile(at)] = part
            else:
                conv_b[:, tile(at)] = part
    heads[...] = packed[HEAD_TILE, 0:3]


RB = 256


def prompt_conv(v, masks, wb, ext, act, slope, row, width):
    def body(i, lanes):
        ext[i, PAD : PAD + RB, :] = v[pl.ds(row, RB), lanes].astype(f32)
        w = wb[:, lanes]
        for r in range(0, RB, RC):
            m = [masks[pl.ds(row + r, RC), k : k + 1] for k in range(K - 1)]
            a, s = act_and_slope(conv_pre(taps_of(ext, i, r, RC), w, m))
            act[r : r + RC, lanes] = a.astype(bf16)
            if slope is not None:
                slope[r : r + RC, lanes] = s

    lane_loop(width, body)


def fill_before(ext, v, halo, row):
    for i in range(ext.shape[0]):
        before = v[row - 16 : row, tile(i)].astype(f32)[16 - PAD :] if row else halo[:, tile(i)]
        ext[i, 0:PAD, :] = before


def prompt_state_kernel(
    place, v, halo, dt_all, masks, wb, hp, start, weight, step, beyond, ext, act, acc
):
    rows = v.shape[0]
    width = start.shape[1]
    first = place[0, 1]
    ind = indicator(place[0, 0] * HG, width)
    later = triangle(RB, lambda i, j: j > i)
    rate = -jnp.exp(hp[0:1])
    ahead = jnp.zeros((1, LANES), f32)
    slopes = jnp.zeros((1, LANES), f32)
    for row in range(0, dt_all.shape[0], RB):
        s = softplus(dt_all[row : row + RB].astype(f32) + hp[1:2])
        position = row + lax.broadcasted_iota(jnp.int32, s.shape, 0)
        past = position >= first + rows
        sig = sigmoid(dt_all[row : row + RB].astype(f32) + hp[1:2])
        ahead = ahead + rate * jnp.sum(jnp.where(past, s, 0.0), axis=0, keepdims=True)
        slopes = slopes + rate * jnp.sum(jnp.where(past, sig, 0.0), axis=0, keepdims=True)
    beyond[...] = jnp.zeros_like(beyond)
    beyond[0:1] = ahead
    beyond[1:2] = slopes
    acc[...] = jnp.zeros_like(acc)
    for row in range(rows - RB, -1, -RB):
        at = pl.ds(pl.multiple_of(first + row, RB), RB)
        s = softplus(dt_all[at, :].astype(f32) + hp[1:2])
        logd = rate * s
        after = tri_sum(later, logd) + ahead
        ahead = ahead + jnp.sum(logd, axis=0, keepdims=True)
        w = masks[row : row + RB, K - 1 : K] * jnp.exp(after) * s
        step[row : row + RB] = s
        weight[row : row + RB] = w
        fill_before(ext, v, halo, row)
        prompt_conv(v, masks, wb, ext, act, None, row, width + N)
        wx = (act[:, :width].astype(f32) * expand(w, ind)).astype(bf16)
        acc[...] += dot(act[:, width:].astype(f32).T.astype(bf16), wx)
    start[...] = acc[...].astype(bf16)


def prompt_grad_kernel(
    count, place, v, halo, dt_mine, masks, wb, hp, weight, step, beyond, *refs
):
    states = refs[:count]
    grad, grad_h, ext, act, slope, g_s, d_s, sums = refs[count + 1 :]
    rows = v.shape[0]
    width = g_s.shape[1]
    ind = indicator(place[0, 0] * HG, width)
    earlier = triangle(RB, lambda i, j: j < i)
    total = states[0][...].astype(f32)
    for k in range(1, count):
        total = total + states[k][...].astype(f32)
    g_s[...] = total.astype(bf16)
    behind = jnp.zeros((1, LANES), f32)
    rate = -jnp.exp(hp[0:1])
    d_rate = jnp.zeros((1, LANES), f32)
    d_bias = jnp.zeros((1, LANES), f32)
    sums[...] = jnp.zeros_like(sums)
    for row in range(0, rows, RB):
        fill_before(ext, v, halo, row)
        prompt_conv(v, masks, wb, ext, act, slope, row, width + N)
        w_e = expand(weight[row : row + RB], ind)
        t = dot(act[:, width:], g_s[...])
        wx = (act[:, :width].astype(f32) * w_e).astype(bf16)
        d_s[:, :width] = t * w_e
        d_s[:, width:] = dot(wx, g_s[...], NT)
        z_hi, z_lo = halves(wx.astype(f32) * t)
        q = head_sums(z_hi, z_lo, ind)
        d_log = tri_sum(earlier, q) + behind
        behind = behind + jnp.sum(q, axis=0, keepdims=True)
        s = step[row : row + RB]
        d_step = q / s + rate * d_log
        sig = sigmoid(dt_mine[row : row + RB].astype(f32) + hp[1:2])
        d_rate = d_rate + jnp.sum(d_log * rate * s, axis=0, keepdims=True)
        d_bias = d_bias + jnp.sum(d_step * sig, axis=0, keepdims=True)

        def back(i, lanes):
            acc = [jnp.zeros((8, LANES), f32) for _ in range(K + 1)]
            for r in range(0, RB, RC):
                d = d_s[r : r + RC, lanes] * slope[r : r + RC, lanes]
                taps = taps_of(ext, i, r, RC)
                for k in range(K):
                    part = d * taps[k]
                    if k < K - 1:
                        part = part * masks[pl.ds(row + r, RC), k : k + 1]
                    acc[k] = acc[k] + fold8(part)
                acc[K] = acc[K] + fold8(d)
            for k in range(K + 1):
                sums[k : k + 1, lanes] += jnp.sum(acc[k], axis=0, keepdims=True)

        lane_loop(width + N, back)
    grad[...] = sums[...]
    grad_h[...] = jnp.zeros_like(grad_h)
    grad_h[0:1] = d_rate + behind * beyond[0:1]
    grad_h[1:2] = d_bias + behind * beyond[1:2]


def add_kernel(terms, *refs):
    out = refs[-1]
    total = None
    for k in range(terms):
        part = refs[k][...].astype(f32)
        total = part if total is None else total + part
    total = total.astype(bf16)
    if out.ndim == 2:
        out[...] = total
    else:
        for k in range(out.shape[0]):
            out[k] = total


def params(*semantics):
    return pltpu.CompilerParams(
        vmem_limit_bytes=VMEM_MIB * 2**20, dimension_semantics=semantics or None
    )


SMEM = pl.BlockSpec(memory_space=pltpu.SMEM)
PROMPT_GRAD_FLOPS = 2**36


def whole(shape):
    return pl.BlockSpec(shape, lambda *_: (0,) * len(shape))


def sds(shape, dtype):
    return jax.ShapeDtypeStruct(shape, dtype)


def response_steps(length, dt, hp):
    rows = dt.shape[0]
    square = sds((rows, H), f32)
    return pl.pallas_call(
        steps_kernel,
        out_shape=(square, square, sds((H, rows), f32), square),
        in_specs=[SMEM, pl.BlockSpec(), pl.BlockSpec()],
        compiler_params=params(),
        name="resp_steps",
    )(length, dt, hp)


def response_state(scale, u, tail, wb, dy, decay_in):
    rows = u.shape[0]
    c_at = lambda g: (0, XC // N + G + g)
    g_at = lambda g: (0, g)
    return pl.pallas_call(
        resp_state_kernel,
        grid=(G,),
        in_specs=[
            SMEM,
            pl.BlockSpec((rows, N), c_at),
            pl.BlockSpec((PAD, N), c_at),
            pl.BlockSpec((PAD, N), c_at),
            pl.BlockSpec((rows, GX), g_at),
            whole((rows, H)),
        ],
        out_specs=[
            pl.BlockSpec((1, N, GX), lambda g: (g, 0, 0)),
            pl.BlockSpec((rows, GX), g_at),
            pl.BlockSpec((rows, N), g_at),
        ],
        out_shape=(sds((G, N, GX), bf16), sds((rows, XC), bf16), sds((rows, G * N), bf16)),
        scratch_shapes=[pltpu.VMEM((N // LANES, PAD + rows, LANES), f32)],
        compiler_params=params("arbitrary"),
        cost_estimate=pl.CostEstimate(
            flops=2 * rows * N * XC, bytes_accessed=14 * 2**20, transcendentals=rows * G * N
        ),
        name="resp_state",
    )(scale, u, tail, wb, dy, decay_in)


def response_mid(
    first, count, length, u, tail, wb, c_act, dy, step, cum, cum4, cum_t4, skip,
    earlier_out, so_far, handed,
):
    rows = u.shape[0]
    half = rows // 2
    x_at = lambda i: (0, first + i)
    b_at = lambda i: (0, XC // N + first + i)
    sums = (2 * rows + PAD, H)
    v = pltpu.VMEM
    anywhere = pl.BlockSpec(memory_space=pl.ANY)
    return pl.pallas_call(
        functools.partial(resp_mid_kernel, first, handed),
        grid=(count,),
        in_specs=[
            SMEM,
            pl.BlockSpec((rows, GX), x_at),
            pl.BlockSpec((rows, N), b_at),
            pl.BlockSpec((PAD, GX), x_at),
            pl.BlockSpec((PAD, N), b_at),
            pl.BlockSpec((PAD, GX), x_at),
            pl.BlockSpec((PAD, N), b_at),
            pl.BlockSpec((rows, N), x_at),
            pl.BlockSpec((rows, GX), x_at),
            whole((rows, H)),
            whole((rows, H)),
            pl.BlockSpec((1, rows, HG), lambda i: (first + i, 0, 0)),
            pl.BlockSpec((1, HG, rows), lambda i: (first + i, 0, 0)),
            pl.BlockSpec((1, GX), x_at),
            anywhere,
        ]
        + ([anywhere] * 3 + [whole(sums)] if so_far else []),
        out_specs=[
            pl.BlockSpec((PAD, GX), x_at),
            pl.BlockSpec((PAD, N), x_at),
            pl.BlockSpec((rows, N), x_at),
            whole(sums),
        ]
        + ([anywhere] if handed else []),
        out_shape=(
            sds((PAD, XC), f32),
            sds((PAD, G * N), f32),
            sds((rows, G * N), f32),
            sds(sums, f32),
        )
        + ((sds(earlier_out.shape, earlier_out.dtype),) if handed else ()),
        input_output_aliases=({15 + k: k for k in range(3)} if so_far else {})
        | ({14: 4} if handed else {}),
        scratch_shapes=[
            v((GX // LANES, PAD + rows, LANES), f32),
            v((N // LANES, PAD + rows, LANES), f32),
            v((rows, GX), bf16),
            v((rows, GX), bf16),
            v((rows, N), bf16),
            v((rows, GX), bf16),
            v((rows, GX), f32),
            v((rows, N), f32),
            v((rows, GX), f32),
            v((rows, GX), f32),
            v((rows, GX), f32),
            v((half, GX), bf16),
            v((half, GX), bf16),
            v((half, GX), f32),
            v((half, GX), f32),
            v((half, GX), f32),
            v((rows, GX), bf16),
            v((rows, GX), bf16),
            v((PAD, GX), f32),
        ],
        compiler_params=params("arbitrary"),
        cost_estimate=pl.CostEstimate(
            flops=2**20 if so_far else 2**33, bytes_accessed=2**12, transcendentals=0
        ),
        name="resp_mid",
    )(
        length, u, u, tail, tail, wb, wb, c_act, dy, step, cum, cum4, cum_t4, skip, earlier_out,
        *so_far,
    )


def response_end(
    tiles, place, scale, u, tail, wb, c_act, weighted, start, dc, sums, step, dt, hp, grads
):
    rows = u.shape[0]
    c_at = lambda g: (0, XC // N + G + g)
    g_at = lambda g: (0, g)
    v = pltpu.VMEM
    return pl.pallas_call(
        resp_end_kernel,
        grid=(G,),
        in_specs=[
            SMEM,
            SMEM,
            pl.BlockSpec((rows, N), c_at),
            pl.BlockSpec((PAD, N), c_at),
            pl.BlockSpec((PAD, N), c_at),
            pl.BlockSpec((rows, N), g_at),
            pl.BlockSpec((rows, GX), g_at),
            pl.BlockSpec((1, N, GX), lambda g: (g, 0, 0)),
            pl.BlockSpec((rows, N), g_at),
        ]
        + [whole(a.shape) for a in (sums, step, dt, hp, *grads)],
        out_specs=whole((tiles, PAD, LANES)),
        out_shape=sds((tiles, PAD, LANES), f32),
        scratch_shapes=[
            v((N // LANES, PAD + rows, LANES), f32),
            v((rows, N), bf16),
            v((rows, N), f32),
            v((rows, H), f32),
            v((PAD, N), f32),
            v((C_TILES, PAD, LANES), f32),
        ],
        compiler_params=params("arbitrary"),
        cost_estimate=pl.CostEstimate(
            flops=4 * rows * N * XC, bytes_accessed=12 * 2**20, transcendentals=rows * G * N
        ),
        name="resp_end",
    )(place, scale, u, tail, wb, c_act, weighted, start, dc, sums, step, dt, hp, *grads)


def unpack(packed):
    width = C_TILES * LANES
    return pl.pallas_call(
        unpack_kernel,
        out_shape=(sds((K, width), f32), sds((1, width), f32), sds((3, H), f32)),
        compiler_params=params(),
        name="unpack",
    )(packed)


def add_states(terms, earlier_out, copies=0):
    rows, width = terms[0].shape
    part = rows // 4
    one = pl.BlockSpec((part, width), lambda i: (i, 0))
    if isinstance(terms, list):
        blocks = [one] * len(terms)
    else:
        blocks = [
            pl.BlockSpec((None, part, width), lambda i, k=k: (k, i, 0))
            for k in range(terms.shape[0])
        ]
        terms = [terms] * terms.shape[0]
    many = pl.BlockSpec((copies, part, width), lambda i: (0, i, 0))
    return pl.pallas_call(
        functools.partial(add_kernel, len(terms)),
        grid=(4,),
        in_specs=blocks + [pl.BlockSpec(memory_space=pl.ANY)],
        out_specs=many if copies else one,
        out_shape=sds((copies, rows, width) if copies else (rows, width), bf16),
        compiler_params=params("arbitrary"),
        cost_estimate=pl.CostEstimate(
            flops=8 * rows * width, bytes_accessed=12 * rows * width, transcendentals=0
        ),
        name="add_states",
    )(*terms, earlier_out)


def prompt_state(place, v, halo, dt_all, masks, wb, hp):
    rows = v.shape[0]
    width = v.shape[1] - N
    s = pltpu.VMEM
    return pl.pallas_call(
        prompt_state_kernel,
        in_specs=[SMEM] + [pl.BlockSpec()] * 6,
        out_shape=(
            sds((N, width), bf16),
            sds((rows, LANES), f32),
            sds((rows, LANES), f32),
            sds((PAD, LANES), f32),
        ),
        scratch_shapes=[
            s(((width + N) // LANES, PAD + RB, LANES), f32),
            s((RB, width + N), bf16),
            s((N, width), f32),
        ],
        compiler_params=params(),
        cost_estimate=pl.CostEstimate(
            flops=2 * rows * N * width, bytes_accessed=4 * 2**20, transcendentals=rows * width
        ),
        name="prompt_state",
    )(place, v, halo, dt_all, masks, wb, hp)


def prompt_grad(
    place, v, halo, dt_mine, masks, wb, hp, weight, step, beyond, states, earlier_out
):
    rows = v.shape[0]
    width = v.shape[1] - N
    s = pltpu.VMEM
    return pl.pallas_call(
        functools.partial(prompt_grad_kernel, len(states)),
        in_specs=[SMEM]
        + [pl.BlockSpec()] * (9 + len(states))
        + [pl.BlockSpec(memory_space=pl.ANY)],
        out_shape=(sds((PAD, width + N), f32), sds((PAD, LANES), f32)),
        scratch_shapes=[
            s(((width + N) // LANES, PAD + RB, LANES), f32),
            s((RB, width + N), bf16),
            s((RB, width + N), f32),
            s((N, width), bf16),
            s((RB, width + N), f32),
            s((PAD, width + N), f32),
        ],
        compiler_params=params(),
        cost_estimate=pl.CostEstimate(
            flops=PROMPT_GRAD_FLOPS, bytes_accessed=8 * 2**20, transcendentals=rows * width
        ),
        name="prompt_grad",
    )(place, v, halo, dt_mine, masks, wb, hp, weight, step, beyond, *states, earlier_out)


def doc_number(starts, positions):
    return jnp.sum((starts[None, :] <= positions[:, None]).astype(jnp.int32), axis=1)


def prompt_masks(starts, rows):
    positions = jnp.arange(rows, dtype=jnp.int32)
    docs = doc_number(starts, positions)
    same = [doc_number(starts, positions - (K - 1 - k)) == docs for k in range(K - 1)]
    columns = jnp.stack(same + [docs == docs[rows - 1]], axis=1).astype(f32)
    return jnp.pad(columns, ((0, 0), (0, PAD - K)))


def pad_rows(a):
    return jnp.pad(a, ((0, PAD - a.shape[0]), (0, 0)))


def to_all(block, axes, devices, groups=None):
    copies = jnp.broadcast_to(block[None], (devices,) + block.shape)
    return lax.all_to_all(copies, axes, 0, 0, axis_index_groups=groups)


def sum_over_all(packed, axes, devices):
    slices = packed.reshape((devices, packed.shape[0] // devices) + packed.shape[1:])
    mine = jnp.sum(lax.all_to_all(slices, axes, 0, 0), axis=0)
    return to_all(mine, axes, devices).reshape(packed.shape)


def shards(
    prompt_in, prompt_dt, doc_starts, resp_in, resp_dt, resp_len, upstream, reward,
    conv_w, conv_b, head_params,
):
    n = lax.axis_size("resp")
    me = lax.axis_index("resp")
    clusters = n // G
    mine = me % G
    cluster = me // G
    inside = [list(range(c * G, c * G + G)) for c in range(clusters)]
    block = prompt_in.shape[1]
    slots = resp_in.shape[2]
    rows_in, dt_in = prompt_in[0], prompt_dt[0]
    u, dt, dy = resp_in[0, 0], resp_dt[0, 0], upstream[0, 0]

    r = reward[0, 0]
    r_hi = r.astype(bf16)
    r_mid = (r - r_hi.astype(f32)).astype(bf16)
    r_lo = (r - r_hi.astype(f32) - r_mid.astype(f32)).astype(bf16)
    tail_size = (K - 1) * rows_in.shape[1] // LANES
    small = jnp.concatenate(
        [
            rows_in[block - K + 1 :].reshape(tail_size, LANES),
            dt_in,
            jnp.broadcast_to(
                jnp.stack([r_hi, r_mid, r_lo, jnp.zeros_like(r_lo)])[:, None], (4, LANES)
            ),
            jnp.zeros((12, LANES), bf16),
        ]
    )
    small = to_all(small, "resp", n)
    wb = pad_rows(jnp.concatenate([conv_w, conv_b[None]], axis=0))
    hp = pad_rows(head_params)

    x_parts = rows_in[:, :XC].reshape(block, G, GX).transpose(1, 0, 2)
    b_parts = rows_in[:, XC : XC + G * N].reshape(block, G, N).transpose(1, 0, 2)
    parts = jnp.concatenate([x_parts, b_parts], axis=2)
    v = parts
    for k in range(1, G):
        route = [(c * G + q, c * G + (q + k) % G) for c in range(clusters) for q in range(G)]
        sent = lax.dynamic_index_in_dim(parts, (mine + k) % G, 0, False)
        came = lax.ppermute(sent, "resp", route)
        v = lax.dynamic_update_index_in_dim(v, came, (mine - k) % G, 0)
    v = v.reshape(G * block, GX + N)

    def own_channels(a):
        return jnp.concatenate(
            [
                lax.dynamic_slice(a, (0, mine * GX), (PAD, GX)),
                lax.dynamic_slice(a, (0, XC + mine * N), (PAD, N)),
            ],
            axis=1,
        )

    def last_rows(device):
        rows = lax.dynamic_index_in_dim(small, device, 0, False)[:tail_size]
        return jnp.pad(rows.reshape(K - 1, -1).astype(f32), ((PAD - K + 1, 0), (0, 0)))

    tail = last_rows(n - 1)
    halo = own_channels(last_rows(jnp.maximum(cluster * G - 1, 0)))
    dt_all = small[:, tail_size : tail_size + block].reshape(n * block, H)
    dt_mine = lax.dynamic_slice(dt_all, (cluster * G * block, 0), (G * block, H))
    at_reward = tail_size + block
    rewards = jnp.sum(small[:, at_reward : at_reward + 3, 0].astype(f32), axis=1)
    scale = ((r - jnp.sum(rewards) / n) / slots).reshape(1, 1)
    masks = lax.dynamic_slice(
        prompt_masks(doc_starts[0], n * block), (cluster * G * block, 0), (G * block, PAD)
    )
    wb_mine = own_channels(wb)
    place = jnp.stack([mine, cluster * G * block]).astype(jnp.int32).reshape(1, 2)

    length = resp_len.astype(jnp.int32)
    step, cum, cum_t, decay_in = response_steps(length, dt, hp)
    d_states, weighted, c_act = response_state(scale, u, tail, wb, dy, decay_in)
    d_states = lax.all_to_all(d_states, "resp", 0, 0, axis_index_groups=inside)

    cum4 = cum.reshape(slots, G, HG).transpose(1, 0, 2)
    skip = jnp.repeat(head_params[2], PS)[None, :]

    def mid(first, count, earlier_out, so_far=(), handed=False):
        return response_mid(
            first, count, length, u, tail, wb, c_act, dy, step, cum, cum4,
            cum_t.reshape(G, HG, slots), skip, earlier_out, so_far, handed,
        )

    def across(part):
        routes = [[(i, (i + c * G) % n) for i in range(n)] for c in range(1, clusters)]
        return [part] + [lax.ppermute(part, "resp", route) for route in routes]

    part, weight, p_step, beyond = prompt_state(place, v, halo, dt_all, masks, wb_mine, hp)
    parts_of_start = across(part)
    grads = mid(0, 2, weight)
    part = add_states(d_states, grads[3])
    parts_of_grad = across(part)
    start = add_states(parts_of_start, part, copies=G)
    *grads, start = mid(2, 1, start, grads, handed=True)
    start = lax.all_to_all(start, "resp", 0, 0, axis_index_groups=inside)
    grad_x, grad_b, dc, sums = mid(3, 1, weight, grads)
    p_grad, p_heads = prompt_grad(
        place, v, halo, dt_mine, masks, wb_mine, hp, weight, p_step, beyond, parts_of_grad, sums
    )

    axes = ("group", "resp")
    devices = lax.axis_size(axes)
    tiles = devices * -(-(HEAD_TILE + 1) // devices)
    packed = response_end(
        tiles, place, scale, u, tail, wb, c_act, weighted, start, dc, sums, step, dt, hp,
        (grad_x, grad_b, p_grad, p_heads),
    )
    grad_w, grad_bias, heads = unpack(sum_over_all(packed, axes, devices))
    return grad_w, grad_bias.reshape(-1), heads


def solution(mesh):
    in_specs = (
        P("group", "resp", None),
        P("group", "resp", None),
        P("group", None),
        P("group", "resp", None, None),
        P("group", "resp", None, None),
        P("group", "resp"),
        P("group", "resp", None, None),
        P("group", "resp"),
        P(),
        P(),
        P(),
    )
    out_specs = (P(), P(), P())
    return jax.shard_map(shards, mesh=mesh, in_specs=in_specs, out_specs=out_specs, check_vma=False)
```

```python
import functools

import jax
import jax.numpy as jnp
from jax import lax
from jax.experimental import pallas as pl
from jax.experimental.pallas import tpu as pltpu
from jax.sharding import PartitionSpec as P

H = 128
PS = 64
N = 256
G = 4
K = 4
HG = H // G
XC = H * PS
GX = HG * PS
LANES = 128
PAD = 8
VMEM_MIB = 63

f32 = jnp.float32
bf16 = jnp.bfloat16

NN = (((1,), (0,)), ((), ()))
NT = (((1,), (1,)), ((), ()))


def dot(a, b, dims=NN, precision=None):
    return lax.dot_general(a, b, dims, precision=precision, preferred_element_type=f32)


def halves(v):
    hi = v.astype(bf16)
    return hi, (v - hi.astype(f32)).astype(bf16)


def indicator(first, width):
    row = lax.broadcasted_iota(jnp.int32, (LANES, width), 0)
    head = lax.shift_right_logical(lax.broadcasted_iota(jnp.int32, (LANES, width), 1), 6)
    return jnp.where(row - first == head, 1.0, 0.0).astype(bf16)


def expand(v, ind):
    hi, lo = halves(v)
    return dot(hi, ind) + dot(lo, ind)


def head_sums(z_hi, z_lo, ind):
    return dot(z_hi, ind, NT) + dot(z_lo, ind, NT)


def triangle(n, keep):
    i = lax.broadcasted_iota(jnp.int32, (n, n), 0)
    j = lax.broadcasted_iota(jnp.int32, (n, n), 1)
    return jnp.where(keep(i, j), 1.0, 0.0).astype(f32)


def tri_sum(tri, v):
    return dot(tri, v, precision=lax.Precision.HIGHEST)


def softplus(z):
    return jnp.maximum(z, 0.0) + jnp.log1p(jnp.exp(-jnp.abs(z)))


def sigmoid(z):
    return 0.5 * jnp.tanh(0.5 * z) + 0.5


def taps_of(ext, at, row, rows):
    return [ext[at, pl.ds(PAD - K + 1 + k + row, rows), :] for k in range(K)]


def conv_pre(taps, wb, masks=None):
    total = wb[K : K + 1] + wb[K - 1 : K] * taps[K - 1]
    for k in range(K - 1):
        term = wb[k : k + 1] * taps[k]
        if masks is not None:
            term = term * masks[k]
        total = total + term
    return total


def act_and_slope(pre):
    sig = sigmoid(pre)
    act = pre * sig
    return act, sig + act * (1.0 - sig)


def fold8(v):
    return jnp.sum(v.reshape(v.shape[0] // 8, 8, v.shape[1]), axis=0)


def as_rows(parts):
    row = lax.broadcasted_iota(jnp.int32, (PAD, LANES), 0)
    total = jnp.zeros((PAD, LANES), f32)
    for k, part in enumerate(parts):
        total = total + jnp.where(row == k, jnp.sum(part, axis=0, keepdims=True), 0.0)
    return total


def lane_loop(width, body):
    def one(i, _):
        body(i, pl.ds(pl.multiple_of(i * LANES, LANES), LANES))
        return 0

    lax.fori_loop(0, width // LANES, one, 0)


RC = 64


def conv_forward(u, tail, wb, ext, act, slope, rows, width):
    def body(i, lanes):
        ext[i, 0:PAD, :] = tail[:, lanes]
        ext[i, PAD : PAD + rows, :] = u[:, lanes].astype(f32)
        w = wb[:, lanes]
        for r in range(0, rows, RC):
            a, s = act_and_slope(conv_pre(taps_of(ext, i, r, RC), w))
            act[r : r + RC, lanes] = a.astype(bf16)
            if slope is not None:
                slope[r : r + RC, lanes] = s

    lane_loop(width, body)


def conv_backward(ext, i, slope, lanes, cotangent, grad, rows):
    sums = [jnp.zeros((8, LANES), f32) for _ in range(K + 1)]
    for r in range(0, rows, RC):
        d = cotangent(r) * slope[r : r + RC, lanes]
        taps = taps_of(ext, i, r, RC)
        for k in range(K):
            sums[k] = sums[k] + fold8(d * taps[k])
        sums[K] = sums[K] + fold8(d)
    grad[:, lanes] = as_rows(sums)


def steps_kernel(len_ref, dt, hp, step, cum, cum_t, decay_in):
    rows = dt.shape[0]
    s = softplus(dt[...].astype(f32) + hp[1:2])
    logd = -jnp.exp(hp[0:1]) * s
    c = tri_sum(triangle(rows, lambda i, j: i >= j), logd)
    step[...] = s
    cum[...] = c
    cum_t[...] = c.T
    t = lax.broadcasted_iota(jnp.int32, c.shape, 0)
    decay_in[...] = jnp.where(t < len_ref[0, 0], jnp.exp(c), 0.0)


def resp_state_kernel(adv, u_c, tail_c, wb_c, dy, decay_in, state, weighted, c_out, ext):
    g = pl.program_id(0)
    rows, width = dy.shape
    conv_forward(u_c, tail_c, wb_c, ext, c_out, None, rows, N)
    c_t = c_out[...].astype(f32).T.astype(bf16)
    a = (dy[...].astype(f32) * expand(decay_in[...], indicator(g * HG, width))).astype(bf16)
    weighted[...] = a
    state[0] = (dot(c_t, a) * adv[0, 0]).astype(bf16)


def resp_mid_kernel(
    first, handed, len_ref, u_x, u_b, tail_x, tail_b, wb_x, wb_b, c_act, dy, step, cum, cum4, cum_t4, skip,
    earlier_out, *refs,
):
    if first:
        sums_in, refs = refs[3], refs[4:]
    if handed:
        refs = refs[:4] + refs[5:]
    g = first + pl.program_id(0)
    (
    grad_x, grad_b, dc, sums_out,
    ext, ext_b, x_s, xs_s, b_s, dym, slope, slope_b, step_e, y_s, t_s,
    a1, bm, sw_e, u_off, y_off, z_hi, z_lo, d_skip,
    ) = refs
    rows = u_x.shape[0]
    half = rows // 2
    conv_forward(u_x, tail_x, wb_x, ext, x_s, slope, rows, GX)
    conv_forward(u_b, tail_b, wb_b, ext_b, b_s, slope_b, rows, N)
    ind = indicator(g * HG, GX)
    step_e[...] = expand(step[...], ind)
    cum_v = cum[...]
    mid = cum_v[half - 1 : half]
    sw_e[...] = expand(jnp.exp(mid - cum_v[:half]) * step[:half], ind)
    y_off[...] = expand(jnp.exp(cum_v[half:] - mid), ind)
    live = jnp.where(lax.broadcasted_iota(jnp.int32, (rows, LANES), 0) < len_ref[0, 0], 1.0, 0.0)

    def prepare(i, lanes):
        d = dy[:, lanes].astype(f32) * live
        dym[:, lanes] = d.astype(bf16)
        x = x_s[:, lanes].astype(f32)
        xs_s[:, lanes] = (x * step_e[:, lanes]).astype(bf16)
        bm[:, lanes] = (x[:half] * sw_e[:, lanes]).astype(bf16)
        a1[:, lanes] = (d[half:] * y_off[:, lanes]).astype(bf16)

    lane_loop(GX, prepare)

    c_v, b_v = c_act[...], b_s[...]
    c0, c1, b0, b1 = c_v[:half], c_v[half:], b_v[:half], b_v[half:]
    i = lax.broadcasted_iota(jnp.int32, (half, half), 0)
    j = lax.broadcasted_iota(jnp.int32, (half, half), 1)
    lane = lax.broadcasted_iota(jnp.int32, (half, LANES), 1)
    left = jnp.where(lane < PS, 1.0, 0.0).astype(bf16)
    right = jnp.where(lane >= PS, 1.0, 0.0).astype(bf16)

    y_off[...] = dot(dot(c1, b0, NT).astype(bf16), bm[...])
    u_off[...] = dot(dot(b0, c1, NT).astype(bf16), a1[...])
    d10 = dot(a1[...], bm[...], NT)

    d_diag = []
    for q, (c_q, b_q) in enumerate(((c0, b0), (c1, b1))):
        r = slice(q * half, (q + 1) * half)
        lower = jnp.where(i >= j, dot(c_q, b_q, NT), 0.0)
        upper = jnp.where(j >= i, dot(b_q, c_q, NT), 0.0)
        d_sc = jnp.zeros((half, half), f32)
        for p in range(HG // 2):
            lanes = slice(p * LANES, (p + 1) * LANES)
            xs_p, dy_p = xs_s[r, lanes], dym[r, lanes]
            xb = jnp.concatenate([xs_p * left, xs_p * right], axis=0)
            dyb = jnp.concatenate([dy_p * left, dy_p * right], axis=0)
            d_m = dot(dy_p, xb, NT)
            mats, mats_t = [], []
            for a in range(2):
                h = 2 * p + a
                gap = jnp.exp(-jnp.abs(cum4[0, r, h : h + 1] - cum_t4[0, h : h + 1, r]))
                d_sc = d_sc + d_m[:, a * half : (a + 1) * half] * gap
                mats.append((gap * lower).astype(bf16))
                mats_t.append((gap * upper).astype(bf16))
            y_s[r, lanes] = dot(jnp.concatenate(mats, axis=1), xb)
            t_s[r, lanes] = dot(jnp.concatenate(mats_t, axis=1), dyb)
        d_diag.append(jnp.where(i >= j, d_sc, 0.0))

    d00, d11 = d_diag
    dc[:half] = dot(d00.astype(bf16), b0)
    dc[half:] = dot(d11.astype(bf16), b1) + dot(d10.astype(bf16), b0)
    db0 = dot(d00.T.astype(bf16), c0) + dot(d10.T.astype(bf16), c1)
    db1 = dot(d11.T.astype(bf16), c1)
    db = jnp.concatenate([db0, db1], axis=0)
    for k in range(N // LANES):
        lanes = slice(k * LANES, (k + 1) * LANES)
        conv_backward(ext_b, k, slope_b, lanes, lambda r: db[r : r + RC, lanes], grad_b, rows)

    def put(z, r, lanes):
        hi, lo = halves(z)
        z_hi[r : r + RC, lanes] = hi
        z_lo[r : r + RC, lanes] = lo

    def row_products(i, lanes):
        for r in range(0, rows, RC):
            z = dym[r : r + RC, lanes].astype(f32) * y_s[r : r + RC, lanes]
            if r >= half:
                o = r - half
                z = z + a1[o : o + RC, lanes].astype(f32) * y_off[o : o + RC, lanes]
            put(z, r, lanes)

    lane_loop(GX, row_products)
    row_sum = head_sums(z_hi[...], z_lo[...], ind)

    def finish(i, lanes):
        d_skips = jnp.zeros((8, LANES), f32)
        for r in range(0, rows, RC):
            t = t_s[r : r + RC, lanes]
            z = xs_s[r : r + RC, lanes].astype(f32) * t
            if r < half:
                z = z + bm[r : r + RC, lanes].astype(f32) * u_off[r : r + RC, lanes]
            put(z, r, lanes)
            d_skips = d_skips + fold8(
                dym[r : r + RC, lanes].astype(f32) * x_s[r : r + RC, lanes].astype(f32)
            )

        def cotangent(r):
            d = step_e[r : r + RC, lanes] * t_s[r : r + RC, lanes]
            d = d + skip[:, lanes] * dym[r : r + RC, lanes].astype(f32)
            if r < half:
                d = d + sw_e[r : r + RC, lanes] * u_off[r : r + RC, lanes]
            return d

        conv_backward(ext, i, slope, lanes, cotangent, grad_x, rows)
        d_skip[:, lanes] = d_skips

    lane_loop(GX, finish)
    col_sum = head_sums(z_hi[...], z_lo[...], ind)

    skip_sum = head_sums(*halves(d_skip[...]), ind)
    new = jnp.concatenate([row_sum, col_sum, skip_sum], axis=0)

    @pl.when(pl.program_id(0) == 0)
    def _():
        sums_out[...] = sums_in[...] + new if first else new

    @pl.when(pl.program_id(0) > 0)
    def _():
        sums_out[...] += new


X_TILES = XC // LANES
B_TILES = G * N // LANES
C_TILES = X_TILES + 2 * B_TILES
HEAD_TILE = (K + 1) * C_TILES // PAD


def tile(k):
    return slice(k * LANES, (k + 1) * LANES)


def resp_end_kernel(
    place, scale, u_c, tail_c, wb_c, c_act, weighted, start, dc, sums, step, dt, hp,
    grad_x, grad_b, p_grad, p_heads,
    packed, ext, c_s, slope, total, grad_c, tiles,
):
    g = pl.program_id(0)
    rows, width = weighted.shape
    conv_forward(u_c, tail_c, wb_c, ext, c_s, slope, rows, N)

    @pl.when(g == 0)
    def _():
        total[...] = sums[0:rows] - sums[rows : 2 * rows]

    a = weighted[...]
    z_hi, z_lo = halves(a.astype(f32) * dot(c_act[...], start[0]))
    total[...] += head_sums(z_hi, z_lo, indicator(g * HG, width))
    d = dc[...] + dot(a, start[0], NT)
    for k in range(N // LANES):
        conv_backward(ext, k, slope, tile(k), lambda r: d[r : r + RC, tile(k)], grad_c, rows)
        tiles[X_TILES + B_TILES + g * (N // LANES) + k] = grad_c[:, tile(k)] * scale[0, 0]

    @pl.when(g == pl.num_programs(0) - 1)
    def _():
        d_log = tri_sum(triangle(rows, lambda i, j: j >= i), total[...])
        rate = -jnp.exp(hp[0:1])
        s = step[...]
        d_step = sums[rows : 2 * rows] / s + rate * d_log
        sig = sigmoid(dt[...].astype(f32) + hp[1:2])
        heads = as_rows([d_log * rate * s, d_step * sig, sums[2 * rows :]])
        for k in range(X_TILES):
            tiles[k] = grad_x[:, tile(k)] * scale[0, 0]
        for k in range(B_TILES):
            tiles[X_TILES + k] = grad_b[:, tile(k)] * scale[0, 0]
        for k in range(width // LANES):
            tiles[place[0, 0] * (width // LANES) + k] += p_grad[:, tile(k)]
        for k in range(N // LANES):
            tiles[X_TILES + place[0, 0] * (N // LANES) + k] += p_grad[:, tile(width // LANES + k)]
        for k in range(K + 1):
            for at in range(C_TILES):
                row = k * C_TILES + at
                packed[row // PAD, row % PAD : row % PAD + 1] = tiles[at, k : k + 1]
        packed[HEAD_TILE] = heads * scale[0, 0] + p_heads[...]
        for k in range(HEAD_TILE + 1, packed.shape[0]):
            packed[k] = jnp.zeros((PAD, LANES), f32)


def unpack_kernel(packed, conv_w, conv_b, heads):
    for k in range(K + 1):
        for at in range(C_TILES):
            row = k * C_TILES + at
            part = packed[row // PAD, row % PAD : row % PAD + 1]
            if k < K:
                conv_w[k : k + 1, tile(at)] = part
            else:
                conv_b[:, tile(at)] = part
    heads[...] = packed[HEAD_TILE, 0:3]


RB = 256


def prompt_conv(v, masks, wb, ext, act, slope, row, width):
    def body(i, lanes):
        ext[i, PAD : PAD + RB, :] = v[pl.ds(row, RB), lanes].astype(f32)
        w = wb[:, lanes]
        for r in range(0, RB, RC):
            m = [masks[pl.ds(row + r, RC), k : k + 1] for k in range(K - 1)]
            a, s = act_and_slope(conv_pre(taps_of(ext, i, r, RC), w, m))
            act[r : r + RC, lanes] = a.astype(bf16)
            if slope is not None:
                slope[r : r + RC, lanes] = s

    lane_loop(width, body)


def fill_before(ext, v, halo, row):
    for i in range(ext.shape[0]):
        before = v[row - 16 : row, tile(i)].astype(f32)[16 - PAD :] if row else halo[:, tile(i)]
        ext[i, 0:PAD, :] = before


def prompt_state_kernel(
    place, v, halo, dt_all, masks, wb, hp, start, weight, step, beyond, ext, act, acc
):
    rows = v.shape[0]
    width = start.shape[1]
    first = place[0, 1]
    ind = indicator(place[0, 0] * HG, width)
    later = triangle(RB, lambda i, j: j > i)
    rate = -jnp.exp(hp[0:1])
    ahead = jnp.zeros((1, LANES), f32)
    slopes = jnp.zeros((1, LANES), f32)
    for row in range(0, dt_all.shape[0], RB):
        s = softplus(dt_all[row : row + RB].astype(f32) + hp[1:2])
        position = row + lax.broadcasted_iota(jnp.int32, s.shape, 0)
        past = position >= first + rows
        sig = sigmoid(dt_all[row : row + RB].astype(f32) + hp[1:2])
        ahead = ahead + rate * jnp.sum(jnp.where(past, s, 0.0), axis=0, keepdims=True)
        slopes = slopes + rate * jnp.sum(jnp.where(past, sig, 0.0), axis=0, keepdims=True)
    beyond[...] = jnp.zeros_like(beyond)
    beyond[0:1] = ahead
    beyond[1:2] = slopes
    acc[...] = jnp.zeros_like(acc)
    for row in range(rows - RB, -1, -RB):
        at = pl.ds(pl.multiple_of(first + row, RB), RB)
        s = softplus(dt_all[at, :].astype(f32) + hp[1:2])
        logd = rate * s
        after = tri_sum(later, logd) + ahead
        ahead = ahead + jnp.sum(logd, axis=0, keepdims=True)
        w = masks[row : row + RB, K - 1 : K] * jnp.exp(after) * s
        step[row : row + RB] = s
        weight[row : row + RB] = w
        fill_before(ext, v, halo, row)
        prompt_conv(v, masks, wb, ext, act, None, row, width + N)
        wx = (act[:, :width].astype(f32) * expand(w, ind)).astype(bf16)
        acc[...] += dot(act[:, width:].astype(f32).T.astype(bf16), wx)
    start[...] = acc[...].astype(bf16)


def prompt_grad_kernel(
    count, place, v, halo, dt_mine, masks, wb, hp, weight, step, beyond, *refs
):
    states = refs[:count]
    grad, grad_h, ext, act, slope, g_s, d_s, sums = refs[count + 1 :]
    rows = v.shape[0]
    width = g_s.shape[1]
    ind = indicator(place[0, 0] * HG, width)
    earlier = triangle(RB, lambda i, j: j < i)
    total = states[0][...].astype(f32)
    for k in range(1, count):
        total = total + states[k][...].astype(f32)
    g_s[...] = total.astype(bf16)
    behind = jnp.zeros((1, LANES), f32)
    rate = -jnp.exp(hp[0:1])
    d_rate = jnp.zeros((1, LANES), f32)
    d_bias = jnp.zeros((1, LANES), f32)
    sums[...] = jnp.zeros_like(sums)
    for row in range(0, rows, RB):
        fill_before(ext, v, halo, row)
        prompt_conv(v, masks, wb, ext, act, slope, row, width + N)
        w_e = expand(weight[row : row + RB], ind)
        t = dot(act[:, width:], g_s[...])
        wx = (act[:, :width].astype(f32) * w_e).astype(bf16)
        d_s[:, :width] = t * w_e
        d_s[:, width:] = dot(wx, g_s[...], NT)
        z_hi, z_lo = halves(wx.astype(f32) * t)
        q = head_sums(z_hi, z_lo, ind)
        d_log = tri_sum(earlier, q) + behind
        behind = behind + jnp.sum(q, axis=0, keepdims=True)
        s = step[row : row + RB]
        d_step = q / s + rate * d_log
        sig = sigmoid(dt_mine[row : row + RB].astype(f32) + hp[1:2])
        d_rate = d_rate + jnp.sum(d_log * rate * s, axis=0, keepdims=True)
        d_bias = d_bias + jnp.sum(d_step * sig, axis=0, keepdims=True)

        def back(i, lanes):
            acc = [jnp.zeros((8, LANES), f32) for _ in range(K + 1)]
            for r in range(0, RB, RC):
                d = d_s[r : r + RC, lanes] * slope[r : r + RC, lanes]
                taps = taps_of(ext, i, r, RC)
                for k in range(K):
                    part = d * taps[k]
                    if k < K - 1:
                        part = part * masks[pl.ds(row + r, RC), k : k + 1]
                    acc[k] = acc[k] + fold8(part)
                acc[K] = acc[K] + fold8(d)
            for k in range(K + 1):
                sums[k : k + 1, lanes] += jnp.sum(acc[k], axis=0, keepdims=True)

        lane_loop(width + N, back)
    grad[...] = sums[...]
    grad_h[...] = jnp.zeros_like(grad_h)
    grad_h[0:1] = d_rate + behind * beyond[0:1]
    grad_h[1:2] = d_bias + behind * beyond[1:2]


def add_kernel(terms, *refs):
    out = refs[-1]
    total = None
    for k in range(terms):
        part = refs[k][...].astype(f32)
        total = part if total is None else total + part
    total = total.astype(bf16)
    if out.ndim == 2:
        out[...] = total
    else:
        for k in range(out.shape[0]):
            out[k] = total


def params(*semantics):
    return pltpu.CompilerParams(
        vmem_limit_bytes=VMEM_MIB * 2**20, dimension_semantics=semantics or None
    )


SMEM = pl.BlockSpec(memory_space=pltpu.SMEM)
PROMPT_GRAD_FLOPS = 2**36


def whole(shape):
    return pl.BlockSpec(shape, lambda *_: (0,) * len(shape))


def sds(shape, dtype):
    return jax.ShapeDtypeStruct(shape, dtype)


def response_steps(length, dt, hp):
    rows = dt.shape[0]
    square = sds((rows, H), f32)
    return pl.pallas_call(
        steps_kernel,
        out_shape=(square, square, sds((H, rows), f32), square),
        in_specs=[SMEM, pl.BlockSpec(), pl.BlockSpec()],
        compiler_params=params(),
        name="resp_steps",
    )(length, dt, hp)


def response_state(scale, u, tail, wb, dy, decay_in):
    rows = u.shape[0]
    c_at = lambda g: (0, XC // N + G + g)
    g_at = lambda g: (0, g)
    return pl.pallas_call(
        resp_state_kernel,
        grid=(G,),
        in_specs=[
            SMEM,
            pl.BlockSpec((rows, N), c_at),
            pl.BlockSpec((PAD, N), c_at),
            pl.BlockSpec((PAD, N), c_at),
            pl.BlockSpec((rows, GX), g_at),
            whole((rows, H)),
        ],
        out_specs=[
            pl.BlockSpec((1, N, GX), lambda g: (g, 0, 0)),
            pl.BlockSpec((rows, GX), g_at),
            pl.BlockSpec((rows, N), g_at),
        ],
        out_shape=(sds((G, N, GX), bf16), sds((rows, XC), bf16), sds((rows, G * N), bf16)),
        scratch_shapes=[pltpu.VMEM((N // LANES, PAD + rows, LANES), f32)],
        compiler_params=params("arbitrary"),
        cost_estimate=pl.CostEstimate(
            flops=2 * rows * N * XC, bytes_accessed=14 * 2**20, transcendentals=rows * G * N
        ),
        name="resp_state",
    )(scale, u, tail, wb, dy, decay_in)


def response_mid(
    first, count, length, u, tail, wb, c_act, dy, step, cum, cum4, cum_t4, skip,
    earlier_out, so_far, handed,
):
    rows = u.shape[0]
    half = rows // 2
    x_at = lambda i: (0, first + i)
    b_at = lambda i: (0, XC // N + first + i)
    sums = (2 * rows + PAD, H)
    v = pltpu.VMEM
    anywhere = pl.BlockSpec(memory_space=pl.ANY)
    return pl.pallas_call(
        functools.partial(resp_mid_kernel, first, handed),
        grid=(count,),
        in_specs=[
            SMEM,
            pl.BlockSpec((rows, GX), x_at),
            pl.BlockSpec((rows, N), b_at),
            pl.BlockSpec((PAD, GX), x_at),
            pl.BlockSpec((PAD, N), b_at),
            pl.BlockSpec((PAD, GX), x_at),
            pl.BlockSpec((PAD, N), b_at),
            pl.BlockSpec((rows, N), x_at),
            pl.BlockSpec((rows, GX), x_at),
            whole((rows, H)),
            whole((rows, H)),
            pl.BlockSpec((1, rows, HG), lambda i: (first + i, 0, 0)),
            pl.BlockSpec((1, HG, rows), lambda i: (first + i, 0, 0)),
            pl.BlockSpec((1, GX), x_at),
            anywhere,
        ]
        + ([anywhere] * 3 + [whole(sums)] if so_far else []),
        out_specs=[
            pl.BlockSpec((PAD, GX), x_at),
            pl.BlockSpec((PAD, N), x_at),
            pl.BlockSpec((rows, N), x_at),
            whole(sums),
        ]
        + ([anywhere] if handed else []),
        out_shape=(
            sds((PAD, XC), f32),
            sds((PAD, G * N), f32),
            sds((rows, G * N), f32),
            sds(sums, f32),
        )
        + ((sds(earlier_out.shape, earlier_out.dtype),) if handed else ()),
        input_output_aliases=({15 + k: k for k in range(3)} if so_far else {})
        | ({14: 4} if handed else {}),
        scratch_shapes=[
            v((GX // LANES, PAD + rows, LANES), f32),
            v((N // LANES, PAD + rows, LANES), f32),
            v((rows, GX), bf16),
            v((rows, GX), bf16),
            v((rows, N), bf16),
            v((rows, GX), bf16),
            v((rows, GX), f32),
            v((rows, N), f32),
            v((rows, GX), f32),
            v((rows, GX), f32),
            v((rows, GX), f32),
            v((half, GX), bf16),
            v((half, GX), bf16),
            v((half, GX), f32),
            v((half, GX), f32),
            v((half, GX), f32),
            v((rows, GX), bf16),
            v((rows, GX), bf16),
            v((PAD, GX), f32),
        ],
        compiler_params=params("arbitrary"),
        cost_estimate=pl.CostEstimate(
            flops=2**20 if so_far else 2**33, bytes_accessed=2**12, transcendentals=0
        ),
        name="resp_mid",
    )(
        length, u, u, tail, tail, wb, wb, c_act, dy, step, cum, cum4, cum_t4, skip, earlier_out,
        *so_far,
    )


def response_end(
    tiles, place, scale, u, tail, wb, c_act, weighted, start, dc, sums, step, dt, hp, grads
):
    rows = u.shape[0]
    c_at = lambda g: (0, XC // N + G + g)
    g_at = lambda g: (0, g)
    v = pltpu.VMEM
    return pl.pallas_call(
        resp_end_kernel,
        grid=(G,),
        in_specs=[
            SMEM,
            SMEM,
            pl.BlockSpec((rows, N), c_at),
            pl.BlockSpec((PAD, N), c_at),
            pl.BlockSpec((PAD, N), c_at),
            pl.BlockSpec((rows, N), g_at),
            pl.BlockSpec((rows, GX), g_at),
            pl.BlockSpec((1, N, GX), lambda g: (g, 0, 0)),
            pl.BlockSpec((rows, N), g_at),
        ]
        + [whole(a.shape) for a in (sums, step, dt, hp, *grads)],
        out_specs=whole((tiles, PAD, LANES)),
        out_shape=sds((tiles, PAD, LANES), f32),
        scratch_shapes=[
            v((N // LANES, PAD + rows, LANES), f32),
            v((rows, N), bf16),
            v((rows, N), f32),
            v((rows, H), f32),
            v((PAD, N), f32),
            v((C_TILES, PAD, LANES), f32),
        ],
        compiler_params=params("arbitrary"),
        cost_estimate=pl.CostEstimate(
            flops=4 * rows * N * XC, bytes_accessed=12 * 2**20, transcendentals=rows * G * N
        ),
        name="resp_end",
    )(place, scale, u, tail, wb, c_act, weighted, start, dc, sums, step, dt, hp, *grads)


def unpack(packed):
    width = C_TILES * LANES
    return pl.pallas_call(
        unpack_kernel,
        out_shape=(sds((K, width), f32), sds((1, width), f32), sds((3, H), f32)),
        compiler_params=params(),
        name="unpack",
    )(packed)


def add_states(terms, earlier_out, copies=0):
    rows, width = terms[0].shape
    part = rows // 4
    one = pl.BlockSpec((part, width), lambda i: (i, 0))
    if isinstance(terms, list):
        blocks = [one] * len(terms)
    else:
        blocks = [
            pl.BlockSpec((None, part, width), lambda i, k=k: (k, i, 0))
            for k in range(terms.shape[0])
        ]
        terms = [terms] * terms.shape[0]
    many = pl.BlockSpec((copies, part, width), lambda i: (0, i, 0))
    return pl.pallas_call(
        functools.partial(add_kernel, len(terms)),
        grid=(4,),
        in_specs=blocks + [pl.BlockSpec(memory_space=pl.ANY)],
        out_specs=many if copies else one,
        out_shape=sds((copies, rows, width) if copies else (rows, width), bf16),
        compiler_params=params("arbitrary"),
        cost_estimate=pl.CostEstimate(
            flops=8 * rows * width, bytes_accessed=12 * rows * width, transcendentals=0
        ),
        name="add_states",
    )(*terms, earlier_out)


def prompt_state(place, v, halo, dt_all, masks, wb, hp):
    rows = v.shape[0]
    width = v.shape[1] - N
    s = pltpu.VMEM
    return pl.pallas_call(
        prompt_state_kernel,
        in_specs=[SMEM] + [pl.BlockSpec()] * 6,
        out_shape=(
            sds((N, width), bf16),
            sds((rows, LANES), f32),
            sds((rows, LANES), f32),
            sds((PAD, LANES), f32),
        ),
        scratch_shapes=[
            s(((width + N) // LANES, PAD + RB, LANES), f32),
            s((RB, width + N), bf16),
            s((N, width), f32),
        ],
        compiler_params=params(),
        cost_estimate=pl.CostEstimate(
            flops=2 * rows * N * width, bytes_accessed=4 * 2**20, transcendentals=rows * width
        ),
        name="prompt_state",
    )(place, v, halo, dt_all, masks, wb, hp)


def prompt_grad(
    place, v, halo, dt_mine, masks, wb, hp, weight, step, beyond, states, earlier_out
):
    rows = v.shape[0]
    width = v.shape[1] - N
    s = pltpu.VMEM
    return pl.pallas_call(
        functools.partial(prompt_grad_kernel, len(states)),
        in_specs=[SMEM]
        + [pl.BlockSpec()] * (9 + len(states))
        + [pl.BlockSpec(memory_space=pl.ANY)],
        out_shape=(sds((PAD, width + N), f32), sds((PAD, LANES), f32)),
        scratch_shapes=[
            s(((width + N) // LANES, PAD + RB, LANES), f32),
            s((RB, width + N), bf16),
            s((RB, width + N), f32),
            s((N, width), bf16),
            s((RB, width + N), f32),
            s((PAD, width + N), f32),
        ],
        compiler_params=params(),
        cost_estimate=pl.CostEstimate(
            flops=PROMPT_GRAD_FLOPS, bytes_accessed=8 * 2**20, transcendentals=rows * width
        ),
        name="prompt_grad",
    )(place, v, halo, dt_mine, masks, wb, hp, weight, step, beyond, *states, earlier_out)


def doc_number(starts, positions):
    return jnp.sum((starts[None, :] <= positions[:, None]).astype(jnp.int32), axis=1)


def prompt_masks(starts, rows):
    positions = jnp.arange(rows, dtype=jnp.int32)
    docs = doc_number(starts, positions)
    same = [doc_number(starts, positions - (K - 1 - k)) == docs for k in range(K - 1)]
    columns = jnp.stack(same + [docs == docs[rows - 1]], axis=1).astype(f32)
    return jnp.pad(columns, ((0, 0), (0, PAD - K)))


def pad_rows(a):
    return jnp.pad(a, ((0, PAD - a.shape[0]), (0, 0)))


def to_all(block, axes, devices, groups=None):
    copies = jnp.broadcast_to(block[None], (devices,) + block.shape)
    return lax.all_to_all(copies, axes, 0, 0, axis_index_groups=groups)


def sum_over_all(packed, axes, devices):
    slices = packed.reshape((devices, packed.shape[0] // devices) + packed.shape[1:])
    mine = jnp.sum(lax.all_to_all(slices, axes, 0, 0), axis=0)
    return to_all(mine, axes, devices).reshape(packed.shape)


def shards(
    prompt_in, prompt_dt, doc_starts, resp_in, resp_dt, resp_len, upstream, reward,
    conv_w, conv_b, head_params,
):
    n = lax.axis_size("resp")
    me = lax.axis_index("resp")
    clusters = n // G
    mine = me % G
    cluster = me // G
    inside = [list(range(c * G, c * G + G)) for c in range(clusters)]
    block = prompt_in.shape[1]
    slots = resp_in.shape[2]
    rows_in, dt_in = prompt_in[0], prompt_dt[0]
    u, dt, dy = resp_in[0, 0], resp_dt[0, 0], upstream[0, 0]

    r = reward[0, 0]
    r_hi = r.astype(bf16)
    r_mid = (r - r_hi.astype(f32)).astype(bf16)
    r_lo = (r - r_hi.astype(f32) - r_mid.astype(f32)).astype(bf16)
    tail_size = (K - 1) * rows_in.shape[1] // LANES
    small = jnp.concatenate(
        [
            rows_in[block - K + 1 :].reshape(tail_size, LANES),
            dt_in,
            jnp.broadcast_to(
                jnp.stack([r_hi, r_mid, r_lo, jnp.zeros_like(r_lo)])[:, None], (4, LANES)
            ),
            jnp.zeros((12, LANES), bf16),
        ]
    )
    small = to_all(small, "resp", n)
    wb = pad_rows(jnp.concatenate([conv_w, conv_b[None]], axis=0))
    hp = pad_rows(head_params)

    x_parts = rows_in[:, :XC].reshape(block, G, GX).transpose(1, 0, 2)
    b_parts = rows_in[:, XC : XC + G * N].reshape(block, G, N).transpose(1, 0, 2)
    parts = jnp.concatenate([x_parts, b_parts], axis=2)
    v = parts
    for k in range(1, G):
        route = [(c * G + q, c * G + (q + k) % G) for c in range(clusters) for q in range(G)]
        sent = lax.dynamic_index_in_dim(parts, (mine + k) % G, 0, False)
        came = lax.ppermute(sent, "resp", route)
        v = lax.dynamic_update_index_in_dim(v, came, (mine - k) % G, 0)
    v = v.reshape(G * block, GX + N)

    def own_channels(a):
        return jnp.concatenate(
            [
                lax.dynamic_slice(a, (0, mine * GX), (PAD, GX)),
                lax.dynamic_slice(a, (0, XC + mine * N), (PAD, N)),
            ],
            axis=1,
        )

    def last_rows(device):
        rows = lax.dynamic_index_in_dim(small, device, 0, False)[:tail_size]
        return jnp.pad(rows.reshape(K - 1, -1).astype(f32), ((PAD - K + 1, 0), (0, 0)))

    tail = last_rows(n - 1)
    halo = own_channels(last_rows(jnp.maximum(cluster * G - 1, 0)))
    dt_all = small[:, tail_size : tail_size + block].reshape(n * block, H)
    dt_mine = lax.dynamic_slice(dt_all, (cluster * G * block, 0), (G * block, H))
    at_reward = tail_size + block
    rewards = jnp.sum(small[:, at_reward : at_reward + 3, 0].astype(f32), axis=1)
    scale = ((r - jnp.sum(rewards) / n) / slots).reshape(1, 1)
    masks = lax.dynamic_slice(
        prompt_masks(doc_starts[0], n * block), (cluster * G * block, 0), (G * block, PAD)
    )
    wb_mine = own_channels(wb)
    place = jnp.stack([mine, cluster * G * block]).astype(jnp.int32).reshape(1, 2)

    length = resp_len.astype(jnp.int32)
    step, cum, cum_t, decay_in = response_steps(length, dt, hp)
    d_states, weighted, c_act = response_state(scale, u, tail, wb, dy, decay_in)
    d_states = lax.all_to_all(d_states, "resp", 0, 0, axis_index_groups=inside)

    cum4 = cum.reshape(slots, G, HG).transpose(1, 0, 2)
    skip = jnp.repeat(head_params[2], PS)[None, :]

    def mid(first, count, earlier_out, so_far=(), handed=False):
        return response_mid(
            first, count, length, u, tail, wb, c_act, dy, step, cum, cum4,
            cum_t.reshape(G, HG, slots), skip, earlier_out, so_far, handed,
        )

    def across(part):
        routes = [[(i, (i + c * G) % n) for i in range(n)] for c in range(1, clusters)]
        return [part] + [lax.ppermute(part, "resp", route) for route in routes]

    part, weight, p_step, beyond = prompt_state(place, v, halo, dt_all, masks, wb_mine, hp)
    parts_of_start = across(part)
    grads = mid(0, 2, weight)
    part = add_states(d_states, grads[3])
    parts_of_grad = across(part)
    grads = mid(2, 1, part, grads)
    start = add_states(parts_of_start, grads[3], copies=G)
    grad_x, grad_b, dc, sums = mid(3, 1, start, grads)
    start = lax.all_to_all(start, "resp", 0, 0, axis_index_groups=inside)
    p_grad, p_heads = prompt_grad(
        place, v, halo, dt_mine, masks, wb_mine, hp, weight, p_step, beyond, parts_of_grad, sums
    )

    axes = ("group", "resp")
    devices = lax.axis_size(axes)
    tiles = devices * -(-(HEAD_TILE + 1) // devices)
    packed = response_end(
        tiles, place, scale, u, tail, wb, c_act, weighted, start, dc, sums, step, dt, hp,
        (grad_x, grad_b, p_grad, p_heads),
    )
    grad_w, grad_bias, heads = unpack(sum_over_all(packed, axes, devices))
    return grad_w, grad_bias.reshape(-1), heads


def solution(mesh):
    in_specs = (
        P("group", "resp", None),
        P("group", "resp", None),
        P("group", None),
        P("group", "resp", None, None),
        P("group", "resp", None, None),
        P("group", "resp"),
        P("group", "resp", None, None),
        P("group", "resp"),
        P(),
        P(),
        P(),
    )
    out_specs = (P(), P(), P())
    return jax.shard_map(shards, mesh=mesh, in_specs=in_specs, out_specs=out_specs, check_vma=False)
```

```python
import functools

import jax
import jax.numpy as jnp
from jax import lax
from jax.experimental import pallas as pl
from jax.experimental.pallas import tpu as pltpu
from jax.sharding import PartitionSpec as P

H = 128
PS = 64
N = 256
G = 4
K = 4
HG = H // G
XC = H * PS
GX = HG * PS
LANES = 128
PAD = 8
VMEM_MIB = 63

f32 = jnp.float32
bf16 = jnp.bfloat16

NN = (((1,), (0,)), ((), ()))
NT = (((1,), (1,)), ((), ()))


def dot(a, b, dims=NN, precision=None):
    return lax.dot_general(a, b, dims, precision=precision, preferred_element_type=f32)


def halves(v):
    hi = v.astype(bf16)
    return hi, (v - hi.astype(f32)).astype(bf16)


def indicator(first, width):
    row = lax.broadcasted_iota(jnp.int32, (LANES, width), 0)
    head = lax.shift_right_logical(lax.broadcasted_iota(jnp.int32, (LANES, width), 1), 6)
    return jnp.where(row - first == head, 1.0, 0.0).astype(bf16)


def expand(v, ind):
    hi, lo = halves(v)
    return dot(hi, ind) + dot(lo, ind)


def head_sums(z_hi, z_lo, ind):
    return dot(z_hi, ind, NT) + dot(z_lo, ind, NT)


def triangle(n, keep):
    i = lax.broadcasted_iota(jnp.int32, (n, n), 0)
    j = lax.broadcasted_iota(jnp.int32, (n, n), 1)
    return jnp.where(keep(i, j), 1.0, 0.0).astype(f32)


def tri_sum(tri, v):
    return dot(tri, v, precision=lax.Precision.HIGHEST)


def softplus(z):
    return jnp.maximum(z, 0.0) + jnp.log1p(jnp.exp(-jnp.abs(z)))


def sigmoid(z):
    return 0.5 * jnp.tanh(0.5 * z) + 0.5


def taps_of(ext, at, row, rows):
    return [ext[at, pl.ds(PAD - K + 1 + k + row, rows), :] for k in range(K)]


def conv_pre(taps, wb, masks=None):
    total = wb[K : K + 1] + wb[K - 1 : K] * taps[K - 1]
    for k in range(K - 1):
        term = wb[k : k + 1] * taps[k]
        if masks is not None:
            term = term * masks[k]
        total = total + term
    return total


def act_and_slope(pre):
    sig = sigmoid(pre)
    act = pre * sig
    return act, sig + act * (1.0 - sig)


def fold8(v):
    return jnp.sum(v.reshape(v.shape[0] // 8, 8, v.shape[1]), axis=0)


def as_rows(parts):
    row = lax.broadcasted_iota(jnp.int32, (PAD, LANES), 0)
    total = jnp.zeros((PAD, LANES), f32)
    for k, part in enumerate(parts):
        total = total + jnp.where(row == k, jnp.sum(part, axis=0, keepdims=True), 0.0)
    return total


def lane_loop(width, body):
    def one(i, _):
        body(i, pl.ds(pl.multiple_of(i * LANES, LANES), LANES))
        return 0

    lax.fori_loop(0, width // LANES, one, 0)


RC = 64


def conv_forward(u, tail, wb, ext, act, slope, rows, width):
    def body(i, lanes):
        ext[i, 0:PAD, :] = tail[:, lanes]
        ext[i, PAD : PAD + rows, :] = u[:, lanes].astype(f32)
        w = wb[:, lanes]
        for r in range(0, rows, RC):
            a, s = act_and_slope(conv_pre(taps_of(ext, i, r, RC), w))
            act[r : r + RC, lanes] = a.astype(bf16)
            if slope is not None:
                slope[r : r + RC, lanes] = s

    lane_loop(width, body)


def conv_backward(ext, i, slope, lanes, cotangent, grad, rows):
    sums = [jnp.zeros((8, LANES), f32) for _ in range(K + 1)]
    for r in range(0, rows, RC):
        d = cotangent(r) * slope[r : r + RC, lanes]
        taps = taps_of(ext, i, r, RC)
        for k in range(K):
            sums[k] = sums[k] + fold8(d * taps[k])
        sums[K] = sums[K] + fold8(d)
    grad[:, lanes] = as_rows(sums)


def steps_kernel(len_ref, dt, hp, step, cum, cum_t, decay_in):
    rows = dt.shape[0]
    s = softplus(dt[...].astype(f32) + hp[1:2])
    logd = -jnp.exp(hp[0:1]) * s
    c = tri_sum(triangle(rows, lambda i, j: i >= j), logd)
    step[...] = s
    cum[...] = c
    cum_t[...] = c.T
    t = lax.broadcasted_iota(jnp.int32, c.shape, 0)
    decay_in[...] = jnp.where(t < len_ref[0, 0], jnp.exp(c), 0.0)


def resp_state_kernel(adv, u_c, tail_c, wb_c, dy, decay_in, state, weighted, c_out, ext):
    g = pl.program_id(0)
    rows, width = dy.shape
    conv_forward(u_c, tail_c, wb_c, ext, c_out, None, rows, N)
    c_t = c_out[...].astype(f32).T.astype(bf16)
    a = (dy[...].astype(f32) * expand(decay_in[...], indicator(g * HG, width))).astype(bf16)
    weighted[...] = a
    state[0] = (dot(c_t, a) * adv[0, 0]).astype(bf16)


def resp_mid_kernel(
    first, handed, len_ref, u_x, u_b, tail_x, tail_b, wb_x, wb_b, c_act, dy, step, cum, cum4, cum_t4, skip,
    earlier_out, *refs,
):
    if first:
        sums_in, refs = refs[3], refs[4:]
    if handed:
        refs = refs[:4] + refs[5:]
    g = first + pl.program_id(0)
    (
    grad_x, grad_b, dc, sums_out,
    ext, ext_b, x_s, xs_s, b_s, dym, slope, slope_b, step_e, y_s, t_s,
    a1, bm, sw_e, u_off, y_off, z_hi, z_lo, d_skip,
    ) = refs
    rows = u_x.shape[0]
    half = rows // 2
    conv_forward(u_x, tail_x, wb_x, ext, x_s, slope, rows, GX)
    conv_forward(u_b, tail_b, wb_b, ext_b, b_s, slope_b, rows, N)
    ind = indicator(g * HG, GX)
    step_e[...] = expand(step[...], ind)
    cum_v = cum[...]
    mid = cum_v[half - 1 : half]
    sw_e[...] = expand(jnp.exp(mid - cum_v[:half]) * step[:half], ind)
    y_off[...] = expand(jnp.exp(cum_v[half:] - mid), ind)
    live = jnp.where(lax.broadcasted_iota(jnp.int32, (rows, LANES), 0) < len_ref[0, 0], 1.0, 0.0)

    def prepare(i, lanes):
        d = dy[:, lanes].astype(f32) * live
        dym[:, lanes] = d.astype(bf16)
        x = x_s[:, lanes].astype(f32)
        xs_s[:, lanes] = (x * step_e[:, lanes]).astype(bf16)
        bm[:, lanes] = (x[:half] * sw_e[:, lanes]).astype(bf16)
        a1[:, lanes] = (d[half:] * y_off[:, lanes]).astype(bf16)

    lane_loop(GX, prepare)

    c_v, b_v = c_act[...], b_s[...]
    c0, c1, b0, b1 = c_v[:half], c_v[half:], b_v[:half], b_v[half:]
    i = lax.broadcasted_iota(jnp.int32, (half, half), 0)
    j = lax.broadcasted_iota(jnp.int32, (half, half), 1)
    lane = lax.broadcasted_iota(jnp.int32, (half, LANES), 1)
    left = jnp.where(lane < PS, 1.0, 0.0).astype(bf16)
    right = jnp.where(lane >= PS, 1.0, 0.0).astype(bf16)

    y_off[...] = dot(dot(c1, b0, NT).astype(bf16), bm[...])
    u_off[...] = dot(dot(b0, c1, NT).astype(bf16), a1[...])
    d10 = dot(a1[...], bm[...], NT)

    d_diag = []
    for q, (c_q, b_q) in enumerate(((c0, b0), (c1, b1))):
        r = slice(q * half, (q + 1) * half)
        lower = jnp.where(i >= j, dot(c_q, b_q, NT), 0.0)
        upper = jnp.where(j >= i, dot(b_q, c_q, NT), 0.0)
        d_sc = jnp.zeros((half, half), f32)
        for p in range(HG // 2):
            lanes = slice(p * LANES, (p + 1) * LANES)
            xs_p, dy_p = xs_s[r, lanes], dym[r, lanes]
            xb = jnp.concatenate([xs_p * left, xs_p * right], axis=0)
            dyb = jnp.concatenate([dy_p * left, dy_p * right], axis=0)
            d_m = dot(dy_p, xb, NT)
            mats, mats_t = [], []
            for a in range(2):
                h = 2 * p + a
                gap = jnp.exp(-jnp.abs(cum4[0, r, h : h + 1] - cum_t4[0, h : h + 1, r]))
                d_sc = d_sc + d_m[:, a * half : (a + 1) * half] * gap
                mats.append((gap * lower).astype(bf16))
                mats_t.append((gap * upper).astype(bf16))
            y_s[r, lanes] = dot(jnp.concatenate(mats, axis=1), xb)
            t_s[r, lanes] = dot(jnp.concatenate(mats_t, axis=1), dyb)
        d_diag.append(jnp.where(i >= j, d_sc, 0.0))

    d00, d11 = d_diag
    dc[:half] = dot(d00.astype(bf16), b0)
    dc[half:] = dot(d11.astype(bf16), b1) + dot(d10.astype(bf16), b0)
    db0 = dot(d00.T.astype(bf16), c0) + dot(d10.T.astype(bf16), c1)
    db1 = dot(d11.T.astype(bf16), c1)
    db = jnp.concatenate([db0, db1], axis=0)
    for k in range(N // LANES):
        lanes = slice(k * LANES, (k + 1) * LANES)
        conv_backward(ext_b, k, slope_b, lanes, lambda r: db[r : r + RC, lanes], grad_b, rows)

    def put(z, r, lanes):
        hi, lo = halves(z)
        z_hi[r : r + RC, lanes] = hi
        z_lo[r : r + RC, lanes] = lo

    def row_products(i, lanes):
        for r in range(0, rows, RC):
            z = dym[r : r + RC, lanes].astype(f32) * y_s[r : r + RC, lanes]
            if r >= half:
                o = r - half
                z = z + a1[o : o + RC, lanes].astype(f32) * y_off[o : o + RC, lanes]
            put(z, r, lanes)

    lane_loop(GX, row_products)
    row_sum = head_sums(z_hi[...], z_lo[...], ind)

    def finish(i, lanes):
        d_skips = jnp.zeros((8, LANES), f32)
        for r in range(0, rows, RC):
            t = t_s[r : r + RC, lanes]
            z = xs_s[r : r + RC, lanes].astype(f32) * t
            if r < half:
                z = z + bm[r : r + RC, lanes].astype(f32) * u_off[r : r + RC, lanes]
            put(z, r, lanes)
            d_skips = d_skips + fold8(
                dym[r : r + RC, lanes].astype(f32) * x_s[r : r + RC, lanes].astype(f32)
            )

        def cotangent(r):
            d = step_e[r : r + RC, lanes] * t_s[r : r + RC, lanes]
            d = d + skip[:, lanes] * dym[r : r + RC, lanes].astype(f32)
            if r < half:
                d = d + sw_e[r : r + RC, lanes] * u_off[r : r + RC, lanes]
            return d

        conv_backward(ext, i, slope, lanes, cotangent, grad_x, rows)
        d_skip[:, lanes] = d_skips

    lane_loop(GX, finish)
    col_sum = head_sums(z_hi[...], z_lo[...], ind)

    skip_sum = head_sums(*halves(d_skip[...]), ind)
    new = jnp.concatenate([row_sum, col_sum, skip_sum], axis=0)

    @pl.when(pl.program_id(0) == 0)
    def _():
        sums_out[...] = sums_in[...] + new if first else new

    @pl.when(pl.program_id(0) > 0)
    def _():
        sums_out[...] += new


X_TILES = XC // LANES
B_TILES = G * N // LANES
C_TILES = X_TILES + 2 * B_TILES
HEAD_TILE = (K + 1) * C_TILES // PAD


def tile(k):
    return slice(k * LANES, (k + 1) * LANES)


def resp_end_kernel(
    place, scale, u_c, tail_c, wb_c, c_act, weighted, start, dc, sums, step, dt, hp,
    grad_x, grad_b, p_grad, p_heads,
    packed, ext, c_s, slope, total, grad_c, tiles,
):
    g = pl.program_id(0)
    rows, width = weighted.shape
    conv_forward(u_c, tail_c, wb_c, ext, c_s, slope, rows, N)

    @pl.when(g == 0)
    def _():
        total[...] = sums[0:rows] - sums[rows : 2 * rows]

    a = weighted[...]
    z_hi, z_lo = halves(a.astype(f32) * dot(c_act[...], start[0]))
    total[...] += head_sums(z_hi, z_lo, indicator(g * HG, width))
    d = dc[...] + dot(a, start[0], NT)
    for k in range(N // LANES):
        conv_backward(ext, k, slope, tile(k), lambda r: d[r : r + RC, tile(k)], grad_c, rows)
        tiles[X_TILES + B_TILES + g * (N // LANES) + k] = grad_c[:, tile(k)] * scale[0, 0]

    @pl.when(g == pl.num_programs(0) - 1)
    def _():
        d_log = tri_sum(triangle(rows, lambda i, j: j >= i), total[...])
        rate = -jnp.exp(hp[0:1])
        s = step[...]
        d_step = sums[rows : 2 * rows] / s + rate * d_log
        sig = sigmoid(dt[...].astype(f32) + hp[1:2])
        heads = as_rows([d_log * rate * s, d_step * sig, sums[2 * rows :]])
        for k in range(X_TILES):
            tiles[k] = grad_x[:, tile(k)] * scale[0, 0]
        for k in range(B_TILES):
            tiles[X_TILES + k] = grad_b[:, tile(k)] * scale[0, 0]
        for k in range(width // LANES):
            tiles[place[0, 0] * (width // LANES) + k] += p_grad[:, tile(k)]
        for k in range(N // LANES):
            tiles[X_TILES + place[0, 0] * (N // LANES) + k] += p_grad[:, tile(width // LANES + k)]
        for k in range(K + 1):
            for at in range(C_TILES):
                row = k * C_TILES + at
                packed[row // PAD, row % PAD : row % PAD + 1] = tiles[at, k : k + 1]
        packed[HEAD_TILE] = heads * scale[0, 0] + p_heads[...]
        for k in range(HEAD_TILE + 1, packed.shape[0]):
            packed[k] = jnp.zeros((PAD, LANES), f32)


def unpack_kernel(packed, conv_w, conv_b, heads):
    for k in range(K + 1):
        for at in range(C_TILES):
            row = k * C_TILES + at
            part = packed[row // PAD, row % PAD : row % PAD + 1]
            if k < K:
                conv_w[k : k + 1, tile(at)] = part
            else:
                conv_b[:, tile(at)] = part
    heads[...] = packed[HEAD_TILE, 0:3]


RB = 256


def prompt_conv(v, masks, wb, ext, act, slope, row, width):
    def body(i, lanes):
        ext[i, PAD : PAD + RB, :] = v[pl.ds(row, RB), lanes].astype(f32)
        w = wb[:, lanes]
        for r in range(0, RB, RC):
            m = [masks[pl.ds(row + r, RC), k : k + 1] for k in range(K - 1)]
            a, s = act_and_slope(conv_pre(taps_of(ext, i, r, RC), w, m))
            act[r : r + RC, lanes] = a.astype(bf16)
            if slope is not None:
                slope[r : r + RC, lanes] = s

    lane_loop(width, body)


def fill_before(ext, v, halo, row):
    for i in range(ext.shape[0]):
        before = v[row - 16 : row, tile(i)].astype(f32)[16 - PAD :] if row else halo[:, tile(i)]
        ext[i, 0:PAD, :] = before


def prompt_state_kernel(
    place, v, halo, dt_all, masks, wb, hp, start, weight, step, beyond, ext, act, acc
):
    rows = v.shape[0]
    width = start.shape[1]
    first = place[0, 1]
    ind = indicator(place[0, 0] * HG, width)
    later = triangle(RB, lambda i, j: j > i)
    rate = -jnp.exp(hp[0:1])
    ahead = jnp.zeros((1, LANES), f32)
    slopes = jnp.zeros((1, LANES), f32)
    for row in range(0, dt_all.shape[0], RB):
        s = softplus(dt_all[row : row + RB].astype(f32) + hp[1:2])
        position = row + lax.broadcasted_iota(jnp.int32, s.shape, 0)
        past = position >= first + rows
        sig = sigmoid(dt_all[row : row + RB].astype(f32) + hp[1:2])
        ahead = ahead + rate * jnp.sum(jnp.where(past, s, 0.0), axis=0, keepdims=True)
        slopes = slopes + rate * jnp.sum(jnp.where(past, sig, 0.0), axis=0, keepdims=True)
    beyond[...] = jnp.zeros_like(beyond)
    beyond[0:1] = ahead
    beyond[1:2] = slopes
    acc[...] = jnp.zeros_like(acc)
    for row in range(rows - RB, -1, -RB):
        at = pl.ds(pl.multiple_of(first + row, RB), RB)
        s = softplus(dt_all[at, :].astype(f32) + hp[1:2])
        logd = rate * s
        after = tri_sum(later, logd) + ahead
        ahead = ahead + jnp.sum(logd, axis=0, keepdims=True)
        w = masks[row : row + RB, K - 1 : K] * jnp.exp(after) * s
        step[row : row + RB] = s
        weight[row : row + RB] = w
        fill_before(ext, v, halo, row)
        prompt_conv(v, masks, wb, ext, act, None, row, width + N)
        wx = (act[:, :width].astype(f32) * expand(w, ind)).astype(bf16)
        acc[...] += dot(act[:, width:].astype(f32).T.astype(bf16), wx)
    start[...] = acc[...].astype(bf16)


def prompt_grad_kernel(
    count, place, v, halo, dt_mine, masks, wb, hp, weight, step, beyond, *refs
):
    states = refs[:count]
    grad, grad_h, ext, act, slope, g_s, d_s, sums = refs[count + 1 :]
    rows = v.shape[0]
    width = g_s.shape[1]
    ind = indicator(place[0, 0] * HG, width)
    earlier = triangle(RB, lambda i, j: j < i)
    total = states[0][...].astype(f32)
    for k in range(1, count):
        total = total + states[k][...].astype(f32)
    g_s[...] = total.astype(bf16)
    behind = jnp.zeros((1, LANES), f32)
    rate = -jnp.exp(hp[0:1])
    d_rate = jnp.zeros((1, LANES), f32)
    d_bias = jnp.zeros((1, LANES), f32)
    sums[...] = jnp.zeros_like(sums)
    for row in range(0, rows, RB):
        fill_before(ext, v, halo, row)
        prompt_conv(v, masks, wb, ext, act, slope, row, width + N)
        w_e = expand(weight[row : row + RB], ind)
        t = dot(act[:, width:], g_s[...])
        wx = (act[:, :width].astype(f32) * w_e).astype(bf16)
        d_s[:, :width] = t * w_e
        d_s[:, width:] = dot(wx, g_s[...], NT)
        z_hi, z_lo = halves(wx.astype(f32) * t)
        q = head_sums(z_hi, z_lo, ind)
        d_log = tri_sum(earlier, q) + behind
        behind = behind + jnp.sum(q, axis=0, keepdims=True)
        s = step[row : row + RB]
        d_step = q / s + rate * d_log
        sig = sigmoid(dt_mine[row : row + RB].astype(f32) + hp[1:2])
        d_rate = d_rate + jnp.sum(d_log * rate * s, axis=0, keepdims=True)
        d_bias = d_bias + jnp.sum(d_step * sig, axis=0, keepdims=True)

        def back(i, lanes):
            acc = [jnp.zeros((8, LANES), f32) for _ in range(K + 1)]
            for r in range(0, RB, RC):
                d = d_s[r : r + RC, lanes] * slope[r : r + RC, lanes]
                taps = taps_of(ext, i, r, RC)
                for k in range(K):
                    part = d * taps[k]
                    if k < K - 1:
                        part = part * masks[pl.ds(row + r, RC), k : k + 1]
                    acc[k] = acc[k] + fold8(part)
                acc[K] = acc[K] + fold8(d)
            for k in range(K + 1):
                sums[k : k + 1, lanes] += jnp.sum(acc[k], axis=0, keepdims=True)

        lane_loop(width + N, back)
    grad[...] = sums[...]
    grad_h[...] = jnp.zeros_like(grad_h)
    grad_h[0:1] = d_rate + behind * beyond[0:1]
    grad_h[1:2] = d_bias + behind * beyond[1:2]


def join_kernel(mine, *refs):
    block = refs[0].shape[0]
    for k in range(G):
        at = lax.rem(mine[0, 0] + (G - k), G)
        refs[G][pl.ds(pl.multiple_of(at * block, block), block), :] = refs[k][...]


def add_kernel(terms, *refs):
    out = refs[-1]
    total = None
    for k in range(terms):
        part = refs[k][...].astype(f32)
        total = part if total is None else total + part
    total = total.astype(bf16)
    if out.ndim == 2:
        out[...] = total
    else:
        for k in range(out.shape[0]):
            out[k] = total


def params(*semantics):
    return pltpu.CompilerParams(
        vmem_limit_bytes=VMEM_MIB * 2**20, dimension_semantics=semantics or None
    )


SMEM = pl.BlockSpec(memory_space=pltpu.SMEM)
PROMPT_GRAD_FLOPS = 2**36


def whole(shape):
    return pl.BlockSpec(shape, lambda *_: (0,) * len(shape))


def sds(shape, dtype):
    return jax.ShapeDtypeStruct(shape, dtype)


def response_steps(length, dt, hp):
    rows = dt.shape[0]
    square = sds((rows, H), f32)
    return pl.pallas_call(
        steps_kernel,
        out_shape=(square, square, sds((H, rows), f32), square),
        in_specs=[SMEM, pl.BlockSpec(), pl.BlockSpec()],
        compiler_params=params(),
        name="resp_steps",
    )(length, dt, hp)


def response_state(scale, u, tail, wb, dy, decay_in):
    rows = u.shape[0]
    c_at = lambda g: (0, XC // N + G + g)
    g_at = lambda g: (0, g)
    return pl.pallas_call(
        resp_state_kernel,
        grid=(G,),
        in_specs=[
            SMEM,
            pl.BlockSpec((rows, N), c_at),
            pl.BlockSpec((PAD, N), c_at),
            pl.BlockSpec((PAD, N), c_at),
            pl.BlockSpec((rows, GX), g_at),
            whole((rows, H)),
        ],
        out_specs=[
            pl.BlockSpec((1, N, GX), lambda g: (g, 0, 0)),
            pl.BlockSpec((rows, GX), g_at),
            pl.BlockSpec((rows, N), g_at),
        ],
        out_shape=(sds((G, N, GX), bf16), sds((rows, XC), bf16), sds((rows, G * N), bf16)),
        scratch_shapes=[pltpu.VMEM((N // LANES, PAD + rows, LANES), f32)],
        compiler_params=params("arbitrary"),
        cost_estimate=pl.CostEstimate(
            flops=2 * rows * N * XC, bytes_accessed=14 * 2**20, transcendentals=rows * G * N
        ),
        name="resp_state",
    )(scale, u, tail, wb, dy, decay_in)


def response_mid(
    first, count, length, u, tail, wb, c_act, dy, step, cum, cum4, cum_t4, skip,
    earlier_out, so_far, handed,
):
    rows = u.shape[0]
    half = rows // 2
    x_at = lambda i: (0, first + i)
    b_at = lambda i: (0, XC // N + first + i)
    sums = (2 * rows + PAD, H)
    v = pltpu.VMEM
    anywhere = pl.BlockSpec(memory_space=pl.ANY)
    return pl.pallas_call(
        functools.partial(resp_mid_kernel, first, handed),
        grid=(count,),
        in_specs=[
            SMEM,
            pl.BlockSpec((rows, GX), x_at),
            pl.BlockSpec((rows, N), b_at),
            pl.BlockSpec((PAD, GX), x_at),
            pl.BlockSpec((PAD, N), b_at),
            pl.BlockSpec((PAD, GX), x_at),
            pl.BlockSpec((PAD, N), b_at),
            pl.BlockSpec((rows, N), x_at),
            pl.BlockSpec((rows, GX), x_at),
            whole((rows, H)),
            whole((rows, H)),
            pl.BlockSpec((1, rows, HG), lambda i: (first + i, 0, 0)),
            pl.BlockSpec((1, HG, rows), lambda i: (first + i, 0, 0)),
            pl.BlockSpec((1, GX), x_at),
            anywhere,
        ]
        + ([anywhere] * 3 + [whole(sums)] if so_far else []),
        out_specs=[
            pl.BlockSpec((PAD, GX), x_at),
            pl.BlockSpec((PAD, N), x_at),
            pl.BlockSpec((rows, N), x_at),
            whole(sums),
        ]
        + ([anywhere] if handed else []),
        out_shape=(
            sds((PAD, XC), f32),
            sds((PAD, G * N), f32),
            sds((rows, G * N), f32),
            sds(sums, f32),
        )
        + ((sds(earlier_out.shape, earlier_out.dtype),) if handed else ()),
        input_output_aliases=({15 + k: k for k in range(3)} if so_far else {})
        | ({14: 4} if handed else {}),
        scratch_shapes=[
            v((GX // LANES, PAD + rows, LANES), f32),
            v((N // LANES, PAD + rows, LANES), f32),
            v((rows, GX), bf16),
            v((rows, GX), bf16),
            v((rows, N), bf16),
            v((rows, GX), bf16),
            v((rows, GX), f32),
            v((rows, N), f32),
            v((rows, GX), f32),
            v((rows, GX), f32),
            v((rows, GX), f32),
            v((half, GX), bf16),
            v((half, GX), bf16),
            v((half, GX), f32),
            v((half, GX), f32),
            v((half, GX), f32),
            v((rows, GX), bf16),
            v((rows, GX), bf16),
            v((PAD, GX), f32),
        ],
        compiler_params=params("arbitrary"),
        cost_estimate=pl.CostEstimate(
            flops=2**20 if so_far else 2**37, bytes_accessed=2**12, transcendentals=0
        ),
        name="resp_mid",
    )(
        length, u, u, tail, tail, wb, wb, c_act, dy, step, cum, cum4, cum_t4, skip, earlier_out,
        *so_far,
    )


def response_end(
    tiles, place, scale, u, tail, wb, c_act, weighted, start, dc, sums, step, dt, hp, grads
):
    rows = u.shape[0]
    c_at = lambda g: (0, XC // N + G + g)
    g_at = lambda g: (0, g)
    v = pltpu.VMEM
    return pl.pallas_call(
        resp_end_kernel,
        grid=(G,),
        in_specs=[
            SMEM,
            SMEM,
            pl.BlockSpec((rows, N), c_at),
            pl.BlockSpec((PAD, N), c_at),
            pl.BlockSpec((PAD, N), c_at),
            pl.BlockSpec((rows, N), g_at),
            pl.BlockSpec((rows, GX), g_at),
            pl.BlockSpec((1, N, GX), lambda g: (g, 0, 0)),
            pl.BlockSpec((rows, N), g_at),
        ]
        + [whole(a.shape) for a in (sums, step, dt, hp, *grads)],
        out_specs=whole((tiles, PAD, LANES)),
        out_shape=sds((tiles, PAD, LANES), f32),
        scratch_shapes=[
            v((N // LANES, PAD + rows, LANES), f32),
            v((rows, N), bf16),
            v((rows, N), f32),
            v((rows, H), f32),
            v((PAD, N), f32),
            v((C_TILES, PAD, LANES), f32),
        ],
        compiler_params=params("arbitrary"),
        cost_estimate=pl.CostEstimate(
            flops=4 * rows * N * XC, bytes_accessed=12 * 2**20, transcendentals=rows * G * N
        ),
        name="resp_end",
    )(place, scale, u, tail, wb, c_act, weighted, start, dc, sums, step, dt, hp, *grads)


def unpack(packed):
    width = C_TILES * LANES
    return pl.pallas_call(
        unpack_kernel,
        out_shape=(sds((K, width), f32), sds((1, width), f32), sds((3, H), f32)),
        compiler_params=params(),
        name="unpack",
    )(packed)


def join(mine, pieces):
    block, width = pieces[0].shape
    return pl.pallas_call(
        join_kernel,
        in_specs=[SMEM] + [pl.BlockSpec()] * G,
        out_shape=sds((G * block, width), bf16),
        compiler_params=params(),
        name="join",
    )(mine, *pieces)


def add_states(terms, earlier_out, copies=0):
    rows, width = terms[0].shape
    part = rows // 4
    one = pl.BlockSpec((part, width), lambda i: (i, 0))
    if isinstance(terms, list):
        blocks = [one] * len(terms)
    else:
        blocks = [
            pl.BlockSpec((None, part, width), lambda i, k=k: (k, i, 0))
            for k in range(terms.shape[0])
        ]
        terms = [terms] * terms.shape[0]
    many = pl.BlockSpec((copies, part, width), lambda i: (0, i, 0))
    return pl.pallas_call(
        functools.partial(add_kernel, len(terms)),
        grid=(4,),
        in_specs=blocks + [pl.BlockSpec(memory_space=pl.ANY)],
        out_specs=many if copies else one,
        out_shape=sds((copies, rows, width) if copies else (rows, width), bf16),
        compiler_params=params("arbitrary"),
        cost_estimate=pl.CostEstimate(
            flops=8 * rows * width, bytes_accessed=12 * rows * width, transcendentals=0
        ),
        name="add_states",
    )(*terms, earlier_out)


def prompt_state(place, v, halo, dt_all, masks, wb, hp):
    rows = v.shape[0]
    width = v.shape[1] - N
    s = pltpu.VMEM
    return pl.pallas_call(
        prompt_state_kernel,
        in_specs=[SMEM] + [pl.BlockSpec()] * 6,
        out_shape=(
            sds((N, width), bf16),
            sds((rows, LANES), f32),
            sds((rows, LANES), f32),
            sds((PAD, LANES), f32),
        ),
        scratch_shapes=[
            s(((width + N) // LANES, PAD + RB, LANES), f32),
            s((RB, width + N), bf16),
            s((N, width), f32),
        ],
        compiler_params=params(),
        cost_estimate=pl.CostEstimate(
            flops=2 * rows * N * width, bytes_accessed=4 * 2**20, transcendentals=rows * width
        ),
        name="prompt_state",
    )(place, v, halo, dt_all, masks, wb, hp)


def prompt_grad(
    place, v, halo, dt_mine, masks, wb, hp, weight, step, beyond, states, earlier_out
):
    rows = v.shape[0]
    width = v.shape[1] - N
    s = pltpu.VMEM
    return pl.pallas_call(
        functools.partial(prompt_grad_kernel, len(states)),
        in_specs=[SMEM]
        + [pl.BlockSpec()] * (9 + len(states))
        + [pl.BlockSpec(memory_space=pl.ANY)],
        out_shape=(sds((PAD, width + N), f32), sds((PAD, LANES), f32)),
        scratch_shapes=[
            s(((width + N) // LANES, PAD + RB, LANES), f32),
            s((RB, width + N), bf16),
            s((RB, width + N), f32),
            s((N, width), bf16),
            s((RB, width + N), f32),
            s((PAD, width + N), f32),
        ],
        compiler_params=params(),
        cost_estimate=pl.CostEstimate(
            flops=PROMPT_GRAD_FLOPS, bytes_accessed=8 * 2**20, transcendentals=rows * width
        ),
        name="prompt_grad",
    )(place, v, halo, dt_mine, masks, wb, hp, weight, step, beyond, *states, earlier_out)


def doc_number(starts, positions):
    return jnp.sum((starts[None, :] <= positions[:, None]).astype(jnp.int32), axis=1)


def prompt_masks(starts, rows):
    positions = jnp.arange(rows, dtype=jnp.int32)
    docs = doc_number(starts, positions)
    same = [doc_number(starts, positions - (K - 1 - k)) == docs for k in range(K - 1)]
    columns = jnp.stack(same + [docs == docs[rows - 1]], axis=1).astype(f32)
    return jnp.pad(columns, ((0, 0), (0, PAD - K)))


def pad_rows(a):
    return jnp.pad(a, ((0, PAD - a.shape[0]), (0, 0)))


def to_all(block, axes, devices, groups=None):
    copies = jnp.broadcast_to(block[None], (devices,) + block.shape)
    return lax.all_to_all(copies, axes, 0, 0, axis_index_groups=groups)


def sum_over_all(packed, axes, devices):
    slices = packed.reshape((devices, packed.shape[0] // devices) + packed.shape[1:])
    mine = jnp.sum(lax.all_to_all(slices, axes, 0, 0), axis=0)
    return to_all(mine, axes, devices).reshape(packed.shape)


def shards(
    prompt_in, prompt_dt, doc_starts, resp_in, resp_dt, resp_len, upstream, reward,
    conv_w, conv_b, head_params,
):
    n = lax.axis_size("resp")
    me = lax.axis_index("resp")
    clusters = n // G
    mine = me % G
    cluster = me // G
    inside = [list(range(c * G, c * G + G)) for c in range(clusters)]
    block = prompt_in.shape[1]
    slots = resp_in.shape[2]
    rows_in, dt_in = prompt_in[0], prompt_dt[0]
    u, dt, dy = resp_in[0, 0], resp_dt[0, 0], upstream[0, 0]

    r = reward[0, 0]
    r_hi = r.astype(bf16)
    r_mid = (r - r_hi.astype(f32)).astype(bf16)
    r_lo = (r - r_hi.astype(f32) - r_mid.astype(f32)).astype(bf16)
    tail_size = (K - 1) * rows_in.shape[1] // LANES
    small = jnp.concatenate(
        [
            rows_in[block - K + 1 :].reshape(tail_size, LANES),
            dt_in,
            jnp.broadcast_to(
                jnp.stack([r_hi, r_mid, r_lo, jnp.zeros_like(r_lo)])[:, None], (4, LANES)
            ),
            jnp.zeros((12, LANES), bf16),
        ]
    )
    small = to_all(small, "resp", n)
    wb = pad_rows(jnp.concatenate([conv_w, conv_b[None]], axis=0))
    hp = pad_rows(head_params)

    x_parts = rows_in[:, :XC].reshape(block, G, GX).transpose(1, 0, 2)
    b_parts = rows_in[:, XC : XC + G * N].reshape(block, G, N).transpose(1, 0, 2)
    parts = jnp.concatenate([x_parts, b_parts], axis=2)
    pieces = [lax.dynamic_index_in_dim(parts, mine, 0, False)]
    for k in range(1, G):
        route = [(c * G + q, c * G + (q + k) % G) for c in range(clusters) for q in range(G)]
        sent = lax.dynamic_index_in_dim(parts, (mine + k) % G, 0, False)
        pieces.append(lax.ppermute(sent, "resp", route))
    v = join(mine.reshape(1, 1), pieces)

    def own_channels(a):
        return jnp.concatenate(
            [
                lax.dynamic_slice(a, (0, mine * GX), (PAD, GX)),
                lax.dynamic_slice(a, (0, XC + mine * N), (PAD, N)),
            ],
            axis=1,
        )

    def last_rows(device):
        rows = lax.dynamic_index_in_dim(small, device, 0, False)[:tail_size]
        return jnp.pad(rows.reshape(K - 1, -1).astype(f32), ((PAD - K + 1, 0), (0, 0)))

    tail = last_rows(n - 1)
    halo = own_channels(last_rows(jnp.maximum(cluster * G - 1, 0)))
    dt_all = small[:, tail_size : tail_size + block].reshape(n * block, H)
    dt_mine = lax.dynamic_slice(dt_all, (cluster * G * block, 0), (G * block, H))
    at_reward = tail_size + block
    rewards = jnp.sum(small[:, at_reward : at_reward + 3, 0].astype(f32), axis=1)
    scale = ((r - jnp.sum(rewards) / n) / slots).reshape(1, 1)
    masks = lax.dynamic_slice(
        prompt_masks(doc_starts[0], n * block), (cluster * G * block, 0), (G * block, PAD)
    )
    wb_mine = own_channels(wb)
    place = jnp.stack([mine, cluster * G * block]).astype(jnp.int32).reshape(1, 2)

    length = resp_len.astype(jnp.int32)
    step, cum, cum_t, decay_in = response_steps(length, dt, hp)
    d_states, weighted, c_act = response_state(scale, u, tail, wb, dy, decay_in)
    d_states = lax.all_to_all(d_states, "resp", 0, 0, axis_index_groups=inside)

    cum4 = cum.reshape(slots, G, HG).transpose(1, 0, 2)
    skip = jnp.repeat(head_params[2], PS)[None, :]

    def mid(first, count, earlier_out, so_far=(), handed=False):
        return response_mid(
            first, count, length, u, tail, wb, c_act, dy, step, cum, cum4,
            cum_t.reshape(G, HG, slots), skip, earlier_out, so_far, handed,
        )

    def across(part):
        routes = [[(i, (i + c * G) % n) for i in range(n)] for c in range(1, clusters)]
        return [part] + [lax.ppermute(part, "resp", route) for route in routes]

    part, weight, p_step, beyond = prompt_state(place, v, halo, dt_all, masks, wb_mine, hp)
    parts_of_start = across(part)
    grads = mid(0, 2, weight)
    part = add_states(d_states, grads[3])
    parts_of_grad = across(part)
    grads = mid(2, 1, part, grads)
    start = add_states(parts_of_start, grads[3], copies=G)
    grad_x, grad_b, dc, sums = mid(3, 1, start, grads)
    start = lax.all_to_all(start, "resp", 0, 0, axis_index_groups=inside)
    p_grad, p_heads = prompt_grad(
        place, v, halo, dt_mine, masks, wb_mine, hp, weight, p_step, beyond, parts_of_grad, sums
    )

    axes = ("group", "resp")
    devices = lax.axis_size(axes)
    tiles = devices * -(-(HEAD_TILE + 1) // devices)
    packed = response_end(
        tiles, place, scale, u, tail, wb, c_act, weighted, start, dc, sums, step, dt, hp,
        (grad_x, grad_b, p_grad, p_heads),
    )
    grad_w, grad_bias, heads = unpack(sum_over_all(packed, axes, devices))
    return grad_w, grad_bias.reshape(-1), heads


def solution(mesh):
    in_specs = (
        P("group", "resp", None),
        P("group", "resp", None),
        P("group", None),
        P("group", "resp", None, None),
        P("group", "resp", None, None),
        P("group", "resp"),
        P("group", "resp", None, None),
        P("group", "resp"),
        P(),
        P(),
        P(),
    )
    out_specs = (P(), P(), P())
    return jax.shard_map(shards, mesh=mesh, in_specs=in_specs, out_specs=out_specs, check_vma=False)
```

```python
import functools

import jax
import jax.numpy as jnp
from jax import lax
from jax.experimental import pallas as pl
from jax.experimental.pallas import tpu as pltpu
from jax.sharding import PartitionSpec as P

H = 128
PS = 64
N = 256
G = 4
K = 4
HG = H // G
XC = H * PS
GX = HG * PS
LANES = 128
PAD = 8
VMEM_MIB = 63

f32 = jnp.float32
bf16 = jnp.bfloat16

NN = (((1,), (0,)), ((), ()))
NT = (((1,), (1,)), ((), ()))


def dot(a, b, dims=NN, precision=None):
    return lax.dot_general(a, b, dims, precision=precision, preferred_element_type=f32)


def halves(v):
    hi = v.astype(bf16)
    return hi, (v - hi.astype(f32)).astype(bf16)


def indicator(first, width):
    row = lax.broadcasted_iota(jnp.int32, (LANES, width), 0)
    head = lax.shift_right_logical(lax.broadcasted_iota(jnp.int32, (LANES, width), 1), 6)
    return jnp.where(row - first == head, 1.0, 0.0).astype(bf16)


def expand(v, ind):
    hi, lo = halves(v)
    return dot(hi, ind) + dot(lo, ind)


def head_sums(z_hi, z_lo, ind):
    return dot(z_hi, ind, NT) + dot(z_lo, ind, NT)


def triangle(n, keep):
    i = lax.broadcasted_iota(jnp.int32, (n, n), 0)
    j = lax.broadcasted_iota(jnp.int32, (n, n), 1)
    return jnp.where(keep(i, j), 1.0, 0.0).astype(f32)


def tri_sum(tri, v):
    return dot(tri, v, precision=lax.Precision.HIGHEST)


def softplus(z):
    return jnp.maximum(z, 0.0) + jnp.log1p(jnp.exp(-jnp.abs(z)))


def sigmoid(z):
    return 0.5 * jnp.tanh(0.5 * z) + 0.5


def taps_of(ext, at, row, rows):
    return [ext[at, pl.ds(PAD - K + 1 + k + row, rows), :] for k in range(K)]


def conv_pre(taps, wb, masks=None):
    total = wb[K : K + 1] + wb[K - 1 : K] * taps[K - 1]
    for k in range(K - 1):
        term = wb[k : k + 1] * taps[k]
        if masks is not None:
            term = term * masks[k]
        total = total + term
    return total


def act_and_slope(pre):
    sig = sigmoid(pre)
    act = pre * sig
    return act, sig + act * (1.0 - sig)


def fold8(v):
    return jnp.sum(v.reshape(v.shape[0] // 8, 8, v.shape[1]), axis=0)


def as_rows(parts):
    row = lax.broadcasted_iota(jnp.int32, (PAD, LANES), 0)
    total = jnp.zeros((PAD, LANES), f32)
    for k, part in enumerate(parts):
        total = total + jnp.where(row == k, jnp.sum(part, axis=0, keepdims=True), 0.0)
    return total


def lane_loop(width, body):
    def one(i, _):
        body(i, pl.ds(pl.multiple_of(i * LANES, LANES), LANES))
        return 0

    lax.fori_loop(0, width // LANES, one, 0)


RC = 64


def conv_forward(u, tail, wb, ext, act, slope, rows, width):
    def body(i, lanes):
        ext[i, 0:PAD, :] = tail[:, lanes]
        ext[i, PAD : PAD + rows, :] = u[:, lanes].astype(f32)
        w = wb[:, lanes]
        for r in range(0, rows, RC):
            a, s = act_and_slope(conv_pre(taps_of(ext, i, r, RC), w))
            act[r : r + RC, lanes] = a.astype(bf16)
            if slope is not None:
                slope[r : r + RC, lanes] = s

    lane_loop(width, body)


def conv_backward(ext, i, slope, lanes, cotangent, grad, rows):
    sums = [jnp.zeros((8, LANES), f32) for _ in range(K + 1)]
    for r in range(0, rows, RC):
        d = cotangent(r) * slope[r : r + RC, lanes]
        taps = taps_of(ext, i, r, RC)
        for k in range(K):
            sums[k] = sums[k] + fold8(d * taps[k])
        sums[K] = sums[K] + fold8(d)
    grad[:, lanes] = as_rows(sums)


def steps_kernel(len_ref, dt, hp, step, cum, cum_t, decay_in):
    rows = dt.shape[0]
    s = softplus(dt[...].astype(f32) + hp[1:2])
    logd = -jnp.exp(hp[0:1]) * s
    c = tri_sum(triangle(rows, lambda i, j: i >= j), logd)
    step[...] = s
    cum[...] = c
    cum_t[...] = c.T
    t = lax.broadcasted_iota(jnp.int32, c.shape, 0)
    decay_in[...] = jnp.where(t < len_ref[0, 0], jnp.exp(c), 0.0)


def resp_state_kernel(adv, u_c, tail_c, wb_c, dy, decay_in, state, weighted, c_out, ext):
    g = pl.program_id(0)
    rows, width = dy.shape
    conv_forward(u_c, tail_c, wb_c, ext, c_out, None, rows, N)
    c_t = c_out[...].astype(f32).T.astype(bf16)
    a = (dy[...].astype(f32) * expand(decay_in[...], indicator(g * HG, width))).astype(bf16)
    weighted[...] = a
    state[0] = (dot(c_t, a) * adv[0, 0]).astype(bf16)


def resp_mid_kernel(
    first, handed, len_ref, u_x, u_b, tail_x, tail_b, wb_x, wb_b, c_act, dy, step, cum, cum4, cum_t4, skip,
    earlier_out, *refs,
):
    if first:
        sums_in, refs = refs[3], refs[4:]
    if handed:
        refs = refs[:4] + refs[5:]
    g = first + pl.program_id(0)
    (
    grad_x, grad_b, dc, sums_out,
    ext, ext_b, x_s, xs_s, b_s, dym, slope, slope_b, step_e, y_s, t_s,
    a1, bm, sw_e, u_off, y_off, z_hi, z_lo, d_skip,
    ) = refs
    rows = u_x.shape[0]
    half = rows // 2
    conv_forward(u_x, tail_x, wb_x, ext, x_s, slope, rows, GX)
    conv_forward(u_b, tail_b, wb_b, ext_b, b_s, slope_b, rows, N)
    ind = indicator(g * HG, GX)
    step_e[...] = expand(step[...], ind)
    cum_v = cum[...]
    mid = cum_v[half - 1 : half]
    sw_e[...] = expand(jnp.exp(mid - cum_v[:half]) * step[:half], ind)
    y_off[...] = expand(jnp.exp(cum_v[half:] - mid), ind)
    live = jnp.where(lax.broadcasted_iota(jnp.int32, (rows, LANES), 0) < len_ref[0, 0], 1.0, 0.0)

    def prepare(i, lanes):
        d = dy[:, lanes].astype(f32) * live
        dym[:, lanes] = d.astype(bf16)
        x = x_s[:, lanes].astype(f32)
        xs_s[:, lanes] = (x * step_e[:, lanes]).astype(bf16)
        bm[:, lanes] = (x[:half] * sw_e[:, lanes]).astype(bf16)
        a1[:, lanes] = (d[half:] * y_off[:, lanes]).astype(bf16)

    lane_loop(GX, prepare)

    c_v, b_v = c_act[...], b_s[...]
    c0, c1, b0, b1 = c_v[:half], c_v[half:], b_v[:half], b_v[half:]
    i = lax.broadcasted_iota(jnp.int32, (half, half), 0)
    j = lax.broadcasted_iota(jnp.int32, (half, half), 1)
    lane = lax.broadcasted_iota(jnp.int32, (half, LANES), 1)
    left = jnp.where(lane < PS, 1.0, 0.0).astype(bf16)
    right = jnp.where(lane >= PS, 1.0, 0.0).astype(bf16)

    y_off[...] = dot(dot(c1, b0, NT).astype(bf16), bm[...])
    u_off[...] = dot(dot(b0, c1, NT).astype(bf16), a1[...])
    d10 = dot(a1[...], bm[...], NT)

    d_diag = []
    for q, (c_q, b_q) in enumerate(((c0, b0), (c1, b1))):
        r = slice(q * half, (q + 1) * half)
        lower = jnp.where(i >= j, dot(c_q, b_q, NT), 0.0)
        upper = jnp.where(j >= i, dot(b_q, c_q, NT), 0.0)
        d_sc = jnp.zeros((half, half), f32)
        for p in range(HG // 2):
            lanes = slice(p * LANES, (p + 1) * LANES)
            xs_p, dy_p = xs_s[r, lanes], dym[r, lanes]
            xb = jnp.concatenate([xs_p * left, xs_p * right], axis=0)
            dyb = jnp.concatenate([dy_p * left, dy_p * right], axis=0)
            d_m = dot(dy_p, xb, NT)
            mats, mats_t = [], []
            for a in range(2):
                h = 2 * p + a
                gap = jnp.exp(-jnp.abs(cum4[0, r, h : h + 1] - cum_t4[0, h : h + 1, r]))
                d_sc = d_sc + d_m[:, a * half : (a + 1) * half] * gap
                mats.append((gap * lower).astype(bf16))
                mats_t.append((gap * upper).astype(bf16))
            y_s[r, lanes] = dot(jnp.concatenate(mats, axis=1), xb)
            t_s[r, lanes] = dot(jnp.concatenate(mats_t, axis=1), dyb)
        d_diag.append(jnp.where(i >= j, d_sc, 0.0))

    d00, d11 = d_diag
    dc[:half] = dot(d00.astype(bf16), b0)
    dc[half:] = dot(d11.astype(bf16), b1) + dot(d10.astype(bf16), b0)
    db0 = dot(d00.T.astype(bf16), c0) + dot(d10.T.astype(bf16), c1)
    db1 = dot(d11.T.astype(bf16), c1)
    db = jnp.concatenate([db0, db1], axis=0)
    for k in range(N // LANES):
        lanes = slice(k * LANES, (k + 1) * LANES)
        conv_backward(ext_b, k, slope_b, lanes, lambda r: db[r : r + RC, lanes], grad_b, rows)

    def put(z, r, lanes):
        hi, lo = halves(z)
        z_hi[r : r + RC, lanes] = hi
        z_lo[r : r + RC, lanes] = lo

    def row_products(i, lanes):
        for r in range(0, rows, RC):
            z = dym[r : r + RC, lanes].astype(f32) * y_s[r : r + RC, lanes]
            if r >= half:
                o = r - half
                z = z + a1[o : o + RC, lanes].astype(f32) * y_off[o : o + RC, lanes]
            put(z, r, lanes)

    lane_loop(GX, row_products)
    row_sum = head_sums(z_hi[...], z_lo[...], ind)

    def finish(i, lanes):
        d_skips = jnp.zeros((8, LANES), f32)
        for r in range(0, rows, RC):
            t = t_s[r : r + RC, lanes]
            z = xs_s[r : r + RC, lanes].astype(f32) * t
            if r < half:
                z = z + bm[r : r + RC, lanes].astype(f32) * u_off[r : r + RC, lanes]
            put(z, r, lanes)
            d_skips = d_skips + fold8(
                dym[r : r + RC, lanes].astype(f32) * x_s[r : r + RC, lanes].astype(f32)
            )

        def cotangent(r):
            d = step_e[r : r + RC, lanes] * t_s[r : r + RC, lanes]
            d = d + skip[:, lanes] * dym[r : r + RC, lanes].astype(f32)
            if r < half:
                d = d + sw_e[r : r + RC, lanes] * u_off[r : r + RC, lanes]
            return d

        conv_backward(ext, i, slope, lanes, cotangent, grad_x, rows)
        d_skip[:, lanes] = d_skips

    lane_loop(GX, finish)
    col_sum = head_sums(z_hi[...], z_lo[...], ind)

    skip_sum = head_sums(*halves(d_skip[...]), ind)
    new = jnp.concatenate([row_sum, col_sum, skip_sum], axis=0)

    @pl.when(pl.program_id(0) == 0)
    def _():
        sums_out[...] = sums_in[...] + new if first else new

    @pl.when(pl.program_id(0) > 0)
    def _():
        sums_out[...] += new


X_TILES = XC // LANES
B_TILES = G * N // LANES
C_TILES = X_TILES + 2 * B_TILES
HEAD_TILE = (K + 1) * C_TILES // PAD


def tile(k):
    return slice(k * LANES, (k + 1) * LANES)


def resp_end_kernel(
    place, scale, u_c, tail_c, wb_c, c_act, weighted, start, dc, sums, step, dt, hp,
    grad_x, grad_b, p_grad, p_heads,
    packed, ext, c_s, slope, total, grad_c, tiles,
):
    g = pl.program_id(0)
    rows, width = weighted.shape
    conv_forward(u_c, tail_c, wb_c, ext, c_s, slope, rows, N)

    @pl.when(g == 0)
    def _():
        total[...] = sums[0:rows] - sums[rows : 2 * rows]

    a = weighted[...]
    z_hi, z_lo = halves(a.astype(f32) * dot(c_act[...], start[0]))
    total[...] += head_sums(z_hi, z_lo, indicator(g * HG, width))
    d = dc[...] + dot(a, start[0], NT)
    for k in range(N // LANES):
        conv_backward(ext, k, slope, tile(k), lambda r: d[r : r + RC, tile(k)], grad_c, rows)
        tiles[X_TILES + B_TILES + g * (N // LANES) + k] = grad_c[:, tile(k)] * scale[0, 0]

    @pl.when(g == pl.num_programs(0) - 1)
    def _():
        d_log = tri_sum(triangle(rows, lambda i, j: j >= i), total[...])
        rate = -jnp.exp(hp[0:1])
        s = step[...]
        d_step = sums[rows : 2 * rows] / s + rate * d_log
        sig = sigmoid(dt[...].astype(f32) + hp[1:2])
        heads = as_rows([d_log * rate * s, d_step * sig, sums[2 * rows :]])
        for k in range(X_TILES):
            tiles[k] = grad_x[:, tile(k)] * scale[0, 0]
        for k in range(B_TILES):
            tiles[X_TILES + k] = grad_b[:, tile(k)] * scale[0, 0]
        for k in range(width // LANES):
            tiles[place[0, 0] * (width // LANES) + k] += p_grad[:, tile(k)]
        for k in range(N // LANES):
            tiles[X_TILES + place[0, 0] * (N // LANES) + k] += p_grad[:, tile(width // LANES + k)]
        for k in range(K + 1):
            for at in range(C_TILES):
                row = k * C_TILES + at
                packed[row // PAD, row % PAD : row % PAD + 1] = tiles[at, k : k + 1]
        packed[HEAD_TILE] = heads * scale[0, 0] + p_heads[...]
        for k in range(HEAD_TILE + 1, packed.shape[0]):
            packed[k] = jnp.zeros((PAD, LANES), f32)


def unpack_kernel(packed, conv_w, conv_b, heads):
    for k in range(K + 1):
        for at in range(C_TILES):
            row = k * C_TILES + at
            part = packed[row // PAD, row % PAD : row % PAD + 1]
            if k < K:
                conv_w[k : k + 1, tile(at)] = part
            else:
                conv_b[:, tile(at)] = part
    heads[...] = packed[HEAD_TILE, 0:3]


RB = 256


def prompt_conv(v, masks, wb, ext, act, slope, row, width):
    def body(i, lanes):
        ext[i, PAD : PAD + RB, :] = v[pl.ds(row, RB), lanes].astype(f32)
        w = wb[:, lanes]
        for r in range(0, RB, RC):
            m = [masks[pl.ds(row + r, RC), k : k + 1] for k in range(K - 1)]
            a, s = act_and_slope(conv_pre(taps_of(ext, i, r, RC), w, m))
            act[r : r + RC, lanes] = a.astype(bf16)
            if slope is not None:
                slope[r : r + RC, lanes] = s

    lane_loop(width, body)


def fill_before(ext, v, halo, row):
    for i in range(ext.shape[0]):
        before = v[row - 16 : row, tile(i)].astype(f32)[16 - PAD :] if row else halo[:, tile(i)]
        ext[i, 0:PAD, :] = before


def prompt_state_kernel(
    place, v, halo, dt_all, masks, wb, hp, start, weight, step, beyond, ext, act, acc
):
    rows = v.shape[0]
    width = start.shape[1]
    first = place[0, 1]
    ind = indicator(place[0, 0] * HG, width)
    later = triangle(RB, lambda i, j: j > i)
    rate = -jnp.exp(hp[0:1])
    ahead = jnp.zeros((1, LANES), f32)
    slopes = jnp.zeros((1, LANES), f32)
    for row in range(0, dt_all.shape[0], RB):
        s = softplus(dt_all[row : row + RB].astype(f32) + hp[1:2])
        position = row + lax.broadcasted_iota(jnp.int32, s.shape, 0)
        past = position >= first + rows
        sig = sigmoid(dt_all[row : row + RB].astype(f32) + hp[1:2])
        ahead = ahead + rate * jnp.sum(jnp.where(past, s, 0.0), axis=0, keepdims=True)
        slopes = slopes + rate * jnp.sum(jnp.where(past, sig, 0.0), axis=0, keepdims=True)
    beyond[...] = jnp.zeros_like(beyond)
    beyond[0:1] = ahead
    beyond[1:2] = slopes
    acc[...] = jnp.zeros_like(acc)
    for row in range(rows - RB, -1, -RB):
        at = pl.ds(pl.multiple_of(first + row, RB), RB)
        s = softplus(dt_all[at, :].astype(f32) + hp[1:2])
        logd = rate * s
        after = tri_sum(later, logd) + ahead
        ahead = ahead + jnp.sum(logd, axis=0, keepdims=True)
        w = masks[row : row + RB, K - 1 : K] * jnp.exp(after) * s
        step[row : row + RB] = s
        weight[row : row + RB] = w
        fill_before(ext, v, halo, row)
        prompt_conv(v, masks, wb, ext, act, None, row, width + N)
        wx = (act[:, :width].astype(f32) * expand(w, ind)).astype(bf16)
        acc[...] += dot(act[:, width:].astype(f32).T.astype(bf16), wx)
    start[...] = acc[...].astype(bf16)


def prompt_grad_kernel(
    count, place, v, halo, dt_mine, masks, wb, hp, weight, step, beyond, *refs
):
    states = refs[:count]
    grad, grad_h, ext, act, slope, g_s, d_s, sums = refs[count + 1 :]
    rows = v.shape[0]
    width = g_s.shape[1]
    ind = indicator(place[0, 0] * HG, width)
    earlier = triangle(RB, lambda i, j: j < i)
    total = states[0][...].astype(f32)
    for k in range(1, count):
        total = total + states[k][...].astype(f32)
    g_s[...] = total.astype(bf16)
    behind = jnp.zeros((1, LANES), f32)
    rate = -jnp.exp(hp[0:1])
    d_rate = jnp.zeros((1, LANES), f32)
    d_bias = jnp.zeros((1, LANES), f32)
    sums[...] = jnp.zeros_like(sums)
    for row in range(0, rows, RB):
        fill_before(ext, v, halo, row)
        prompt_conv(v, masks, wb, ext, act, slope, row, width + N)
        w_e = expand(weight[row : row + RB], ind)
        t = dot(act[:, width:], g_s[...])
        wx = (act[:, :width].astype(f32) * w_e).astype(bf16)
        d_s[:, :width] = t * w_e
        d_s[:, width:] = dot(wx, g_s[...], NT)
        z_hi, z_lo = halves(wx.astype(f32) * t)
        q = head_sums(z_hi, z_lo, ind)
        d_log = tri_sum(earlier, q) + behind
        behind = behind + jnp.sum(q, axis=0, keepdims=True)
        s = step[row : row + RB]
        d_step = q / s + rate * d_log
        sig = sigmoid(dt_mine[row : row + RB].astype(f32) + hp[1:2])
        d_rate = d_rate + jnp.sum(d_log * rate * s, axis=0, keepdims=True)
        d_bias = d_bias + jnp.sum(d_step * sig, axis=0, keepdims=True)

        def back(i, lanes):
            acc = [jnp.zeros((8, LANES), f32) for _ in range(K + 1)]
            for r in range(0, RB, RC):
                d = d_s[r : r + RC, lanes] * slope[r : r + RC, lanes]
                taps = taps_of(ext, i, r, RC)
                for k in range(K):
                    part = d * taps[k]
                    if k < K - 1:
                        part = part * masks[pl.ds(row + r, RC), k : k + 1]
                    acc[k] = acc[k] + fold8(part)
                acc[K] = acc[K] + fold8(d)
            for k in range(K + 1):
                sums[k : k + 1, lanes] += jnp.sum(acc[k], axis=0, keepdims=True)

        lane_loop(width + N, back)
    grad[...] = sums[...]
    grad_h[...] = jnp.zeros_like(grad_h)
    grad_h[0:1] = d_rate + behind * beyond[0:1]
    grad_h[1:2] = d_bias + behind * beyond[1:2]


def add_kernel(terms, *refs):
    out = refs[-1]
    total = None
    for k in range(terms):
        part = refs[k][...].astype(f32)
        total = part if total is None else total + part
    total = total.astype(bf16)
    if out.ndim == 2:
        out[...] = total
    else:
        for k in range(out.shape[0]):
            out[k] = total


def params(*semantics):
    return pltpu.CompilerParams(
        vmem_limit_bytes=VMEM_MIB * 2**20, dimension_semantics=semantics or None
    )


SMEM = pl.BlockSpec(memory_space=pltpu.SMEM)
PROMPT_GRAD_FLOPS = 2**36


def whole(shape):
    return pl.BlockSpec(shape, lambda *_: (0,) * len(shape))


def sds(shape, dtype):
    return jax.ShapeDtypeStruct(shape, dtype)


def response_steps(length, dt, hp):
    rows = dt.shape[0]
    square = sds((rows, H), f32)
    return pl.pallas_call(
        steps_kernel,
        out_shape=(square, square, sds((H, rows), f32), square),
        in_specs=[SMEM, pl.BlockSpec(), pl.BlockSpec()],
        compiler_params=params(),
        name="resp_steps",
    )(length, dt, hp)


def response_state(scale, u, tail, wb, dy, decay_in):
    rows = u.shape[0]
    c_at = lambda g: (0, XC // N + G + g)
    g_at = lambda g: (0, g)
    return pl.pallas_call(
        resp_state_kernel,
        grid=(G,),
        in_specs=[
            SMEM,
            pl.BlockSpec((rows, N), c_at),
            pl.BlockSpec((PAD, N), c_at),
            pl.BlockSpec((PAD, N), c_at),
            pl.BlockSpec((rows, GX), g_at),
            whole((rows, H)),
        ],
        out_specs=[
            pl.BlockSpec((1, N, GX), lambda g: (g, 0, 0)),
            pl.BlockSpec((rows, GX), g_at),
            pl.BlockSpec((rows, N), g_at),
        ],
        out_shape=(sds((G, N, GX), bf16), sds((rows, XC), bf16), sds((rows, G * N), bf16)),
        scratch_shapes=[pltpu.VMEM((N // LANES, PAD + rows, LANES), f32)],
        compiler_params=params("arbitrary"),
        cost_estimate=pl.CostEstimate(
            flops=2 * rows * N * XC, bytes_accessed=14 * 2**20, transcendentals=rows * G * N
        ),
        name="resp_state",
    )(scale, u, tail, wb, dy, decay_in)


def response_mid(
    first, count, length, u, tail, wb, c_act, dy, step, cum, cum4, cum_t4, skip,
    earlier_out, so_far, handed,
):
    rows = u.shape[0]
    half = rows // 2
    x_at = lambda i: (0, first + i)
    b_at = lambda i: (0, XC // N + first + i)
    sums = (2 * rows + PAD, H)
    v = pltpu.VMEM
    anywhere = pl.BlockSpec(memory_space=pl.ANY)
    return pl.pallas_call(
        functools.partial(resp_mid_kernel, first, handed),
        grid=(count,),
        in_specs=[
            SMEM,
            pl.BlockSpec((rows, GX), x_at),
            pl.BlockSpec((rows, N), b_at),
            pl.BlockSpec((PAD, GX), x_at),
            pl.BlockSpec((PAD, N), b_at),
            pl.BlockSpec((PAD, GX), x_at),
            pl.BlockSpec((PAD, N), b_at),
            pl.BlockSpec((rows, N), x_at),
            pl.BlockSpec((rows, GX), x_at),
            whole((rows, H)),
            whole((rows, H)),
            pl.BlockSpec((1, rows, HG), lambda i: (first + i, 0, 0)),
            pl.BlockSpec((1, HG, rows), lambda i: (first + i, 0, 0)),
            pl.BlockSpec((1, GX), x_at),
            anywhere,
        ]
        + ([anywhere] * 3 + [whole(sums)] if so_far else []),
        out_specs=[
            pl.BlockSpec((PAD, GX), x_at),
            pl.BlockSpec((PAD, N), x_at),
            pl.BlockSpec((rows, N), x_at),
            whole(sums),
        ]
        + ([anywhere] if handed else []),
        out_shape=(
            sds((PAD, XC), f32),
            sds((PAD, G * N), f32),
            sds((rows, G * N), f32),
            sds(sums, f32),
        )
        + ((sds(earlier_out.shape, earlier_out.dtype),) if handed else ()),
        input_output_aliases=({15 + k: k for k in range(3)} if so_far else {})
        | ({14: 4} if handed else {}),
        scratch_shapes=[
            v((GX // LANES, PAD + rows, LANES), f32),
            v((N // LANES, PAD + rows, LANES), f32),
            v((rows, GX), bf16),
            v((rows, GX), bf16),
            v((rows, N), bf16),
            v((rows, GX), bf16),
            v((rows, GX), f32),
            v((rows, N), f32),
            v((rows, GX), f32),
            v((rows, GX), f32),
            v((rows, GX), f32),
            v((half, GX), bf16),
            v((half, GX), bf16),
            v((half, GX), f32),
            v((half, GX), f32),
            v((half, GX), f32),
            v((rows, GX), bf16),
            v((rows, GX), bf16),
            v((PAD, GX), f32),
        ],
        compiler_params=params("arbitrary"),
        cost_estimate=pl.CostEstimate(
            flops=2**20 if so_far else 2**33, bytes_accessed=2**12, transcendentals=0
        ),
        name="resp_mid",
    )(
        length, u, u, tail, tail, wb, wb, c_act, dy, step, cum, cum4, cum_t4, skip, earlier_out,
        *so_far,
    )


def response_end(
    tiles, place, scale, u, tail, wb, c_act, weighted, start, dc, sums, step, dt, hp, grads
):
    rows = u.shape[0]
    c_at = lambda g: (0, XC // N + G + g)
    g_at = lambda g: (0, g)
    v = pltpu.VMEM
    return pl.pallas_call(
        resp_end_kernel,
        grid=(G,),
        in_specs=[
            SMEM,
            SMEM,
            pl.BlockSpec((rows, N), c_at),
            pl.BlockSpec((PAD, N), c_at),
            pl.BlockSpec((PAD, N), c_at),
            pl.BlockSpec((rows, N), g_at),
            pl.BlockSpec((rows, GX), g_at),
            pl.BlockSpec((1, N, GX), lambda g: (g, 0, 0)),
            pl.BlockSpec((rows, N), g_at),
        ]
        + [whole(a.shape) for a in (sums, step, dt, hp, *grads)],
        out_specs=whole((tiles, PAD, LANES)),
        out_shape=sds((tiles, PAD, LANES), f32),
        scratch_shapes=[
            v((N // LANES, PAD + rows, LANES), f32),
            v((rows, N), bf16),
            v((rows, N), f32),
            v((rows, H), f32),
            v((PAD, N), f32),
            v((C_TILES, PAD, LANES), f32),
        ],
        compiler_params=params("arbitrary"),
        cost_estimate=pl.CostEstimate(
            flops=4 * rows * N * XC, bytes_accessed=12 * 2**20, transcendentals=rows * G * N
        ),
        name="resp_end",
    )(place, scale, u, tail, wb, c_act, weighted, start, dc, sums, step, dt, hp, *grads)


def unpack(packed):
    width = C_TILES * LANES
    return pl.pallas_call(
        unpack_kernel,
        out_shape=(sds((K, width), f32), sds((1, width), f32), sds((3, H), f32)),
        compiler_params=params(),
        name="unpack",
    )(packed)


def add_states(terms, earlier_out, copies=0):
    rows, width = terms[0].shape
    part = rows // 4
    one = pl.BlockSpec((part, width), lambda i: (i, 0))
    if isinstance(terms, list):
        blocks = [one] * len(terms)
    else:
        blocks = [
            pl.BlockSpec((None, part, width), lambda i, k=k: (k, i, 0))
            for k in range(terms.shape[0])
        ]
        terms = [terms] * terms.shape[0]
    many = pl.BlockSpec((copies, part, width), lambda i: (0, i, 0))
    return pl.pallas_call(
        functools.partial(add_kernel, len(terms)),
        grid=(4,),
        in_specs=blocks + [pl.BlockSpec(memory_space=pl.ANY)] * len(earlier_out),
        out_specs=many if copies else one,
        out_shape=sds((copies, rows, width) if copies else (rows, width), bf16),
        compiler_params=params("arbitrary"),
        cost_estimate=pl.CostEstimate(
            flops=8 * rows * width, bytes_accessed=12 * rows * width, transcendentals=0
        ),
        name="add_states",
    )(*terms, *earlier_out)


def prompt_state(place, v, halo, dt_all, masks, wb, hp):
    rows = v.shape[0]
    width = v.shape[1] - N
    s = pltpu.VMEM
    return pl.pallas_call(
        prompt_state_kernel,
        in_specs=[SMEM] + [pl.BlockSpec()] * 6,
        out_shape=(
            sds((N, width), bf16),
            sds((rows, LANES), f32),
            sds((rows, LANES), f32),
            sds((PAD, LANES), f32),
        ),
        scratch_shapes=[
            s(((width + N) // LANES, PAD + RB, LANES), f32),
            s((RB, width + N), bf16),
            s((N, width), f32),
        ],
        compiler_params=params(),
        cost_estimate=pl.CostEstimate(
            flops=2 * rows * N * width, bytes_accessed=4 * 2**20, transcendentals=rows * width
        ),
        name="prompt_state",
    )(place, v, halo, dt_all, masks, wb, hp)


def prompt_grad(
    place, v, halo, dt_mine, masks, wb, hp, weight, step, beyond, states, earlier_out
):
    rows = v.shape[0]
    width = v.shape[1] - N
    s = pltpu.VMEM
    return pl.pallas_call(
        functools.partial(prompt_grad_kernel, len(states)),
        in_specs=[SMEM]
        + [pl.BlockSpec()] * (9 + len(states))
        + [pl.BlockSpec(memory_space=pl.ANY)],
        out_shape=(sds((PAD, width + N), f32), sds((PAD, LANES), f32)),
        scratch_shapes=[
            s(((width + N) // LANES, PAD + RB, LANES), f32),
            s((RB, width + N), bf16),
            s((RB, width + N), f32),
            s((N, width), bf16),
            s((RB, width + N), f32),
            s((PAD, width + N), f32),
        ],
        compiler_params=params(),
        cost_estimate=pl.CostEstimate(
            flops=PROMPT_GRAD_FLOPS, bytes_accessed=8 * 2**20, transcendentals=rows * width
        ),
        name="prompt_grad",
    )(place, v, halo, dt_mine, masks, wb, hp, weight, step, beyond, *states, earlier_out)


def doc_number(starts, positions):
    return jnp.sum((starts[None, :] <= positions[:, None]).astype(jnp.int32), axis=1)


def prompt_masks(starts, rows):
    positions = jnp.arange(rows, dtype=jnp.int32)
    docs = doc_number(starts, positions)
    same = [doc_number(starts, positions - (K - 1 - k)) == docs for k in range(K - 1)]
    columns = jnp.stack(same + [docs == docs[rows - 1]], axis=1).astype(f32)
    return jnp.pad(columns, ((0, 0), (0, PAD - K)))


def pad_rows(a):
    return jnp.pad(a, ((0, PAD - a.shape[0]), (0, 0)))


def to_all(block, axes, devices, groups=None):
    copies = jnp.broadcast_to(block[None], (devices,) + block.shape)
    return lax.all_to_all(copies, axes, 0, 0, axis_index_groups=groups)


def sum_over_all(packed, axes, devices):
    slices = packed.reshape((devices, packed.shape[0] // devices) + packed.shape[1:])
    mine = jnp.sum(lax.all_to_all(slices, axes, 0, 0), axis=0)
    return to_all(mine, axes, devices).reshape(packed.shape)


def shards(
    prompt_in, prompt_dt, doc_starts, resp_in, resp_dt, resp_len, upstream, reward,
    conv_w, conv_b, head_params,
):
    n = lax.axis_size("resp")
    me = lax.axis_index("resp")
    clusters = n // G
    mine = me % G
    cluster = me // G
    inside = [list(range(c * G, c * G + G)) for c in range(clusters)]
    block = prompt_in.shape[1]
    slots = resp_in.shape[2]
    rows_in, dt_in = prompt_in[0], prompt_dt[0]
    u, dt, dy = resp_in[0, 0], resp_dt[0, 0], upstream[0, 0]

    r = reward[0, 0]
    r_hi = r.astype(bf16)
    r_mid = (r - r_hi.astype(f32)).astype(bf16)
    r_lo = (r - r_hi.astype(f32) - r_mid.astype(f32)).astype(bf16)
    tail_size = (K - 1) * rows_in.shape[1] // LANES
    small = jnp.concatenate(
        [
            rows_in[block - K + 1 :].reshape(tail_size, LANES),
            dt_in,
            jnp.broadcast_to(
                jnp.stack([r_hi, r_mid, r_lo, jnp.zeros_like(r_lo)])[:, None], (4, LANES)
            ),
            jnp.zeros((12, LANES), bf16),
        ]
    )
    small = to_all(small, "resp", n)
    wb = pad_rows(jnp.concatenate([conv_w, conv_b[None]], axis=0))
    hp = pad_rows(head_params)

    x_parts = rows_in[:, :XC].reshape(block, G, GX).transpose(1, 0, 2)
    b_parts = rows_in[:, XC : XC + G * N].reshape(block, G, N).transpose(1, 0, 2)
    parts = jnp.concatenate([x_parts, b_parts], axis=2)
    v = parts
    for k in range(1, G):
        route = [(c * G + q, c * G + (q + k) % G) for c in range(clusters) for q in range(G)]
        sent = lax.dynamic_index_in_dim(parts, (mine + k) % G, 0, False)
        came = lax.ppermute(sent, "resp", route)
        v = lax.dynamic_update_index_in_dim(v, came, (mine - k) % G, 0)
    v = v.reshape(G * block, GX + N)

    def own_channels(a):
        return jnp.concatenate(
            [
                lax.dynamic_slice(a, (0, mine * GX), (PAD, GX)),
                lax.dynamic_slice(a, (0, XC + mine * N), (PAD, N)),
            ],
            axis=1,
        )

    def last_rows(device):
        rows = lax.dynamic_index_in_dim(small, device, 0, False)[:tail_size]
        return jnp.pad(rows.reshape(K - 1, -1).astype(f32), ((PAD - K + 1, 0), (0, 0)))

    tail = last_rows(n - 1)
    halo = own_channels(last_rows(jnp.maximum(cluster * G - 1, 0)))
    dt_all = small[:, tail_size : tail_size + block].reshape(n * block, H)
    dt_mine = lax.dynamic_slice(dt_all, (cluster * G * block, 0), (G * block, H))
    at_reward = tail_size + block
    rewards = jnp.sum(small[:, at_reward : at_reward + 3, 0].astype(f32), axis=1)
    scale = ((r - jnp.sum(rewards) / n) / slots).reshape(1, 1)
    masks = lax.dynamic_slice(
        prompt_masks(doc_starts[0], n * block), (cluster * G * block, 0), (G * block, PAD)
    )
    wb_mine = own_channels(wb)
    place = jnp.stack([mine, cluster * G * block]).astype(jnp.int32).reshape(1, 2)

    length = resp_len.astype(jnp.int32)
    step, cum, cum_t, decay_in = response_steps(length, dt, hp)
    d_states, weighted, c_act = response_state(scale, u, tail, wb, dy, decay_in)
    d_states = lax.all_to_all(d_states, "resp", 0, 0, axis_index_groups=inside)

    cum4 = cum.reshape(slots, G, HG).transpose(1, 0, 2)
    skip = jnp.repeat(head_params[2], PS)[None, :]

    def mid(first, count, earlier_out, so_far=(), handed=False):
        return response_mid(
            first, count, length, u, tail, wb, c_act, dy, step, cum, cum4,
            cum_t.reshape(G, HG, slots), skip, earlier_out, so_far, handed,
        )

    def across(part):
        routes = [[(i, (i + c * G) % n) for i in range(n)] for c in range(1, clusters)]
        return [part] + [lax.ppermute(part, "resp", route) for route in routes]

    part, weight, p_step, beyond = prompt_state(place, v, halo, dt_all, masks, wb_mine, hp)
    parts_of_start = across(part)
    grads = mid(0, 2, weight)
    part = add_states(d_states, (grads[3], *parts_of_start[1:]))
    parts_of_grad = across(part)
    start = add_states(parts_of_start, (part,), copies=G)
    grads = mid(2, 1, start, grads)
    grad_x, grad_b, dc, sums = mid(3, 1, start, grads)
    start = lax.all_to_all(start, "resp", 0, 0, axis_index_groups=inside)
    p_grad, p_heads = prompt_grad(
        place, v, halo, dt_mine, masks, wb_mine, hp, weight, p_step, beyond, parts_of_grad, sums
    )

    axes = ("group", "resp")
    devices = lax.axis_size(axes)
    tiles = devices * -(-(HEAD_TILE + 1) // devices)
    packed = response_end(
        tiles, place, scale, u, tail, wb, c_act, weighted, start, dc, sums, step, dt, hp,
        (grad_x, grad_b, p_grad, p_heads),
    )
    grad_w, grad_bias, heads = unpack(sum_over_all(packed, axes, devices))
    return grad_w, grad_bias.reshape(-1), heads


def solution(mesh):
    in_specs = (
        P("group", "resp", None),
        P("group", "resp", None),
        P("group", None),
        P("group", "resp", None, None),
        P("group", "resp", None, None),
        P("group", "resp"),
        P("group", "resp", None, None),
        P("group", "resp"),
        P(),
        P(),
        P(),
    )
    out_specs = (P(), P(), P())
    return jax.shard_map(shards, mesh=mesh, in_specs=in_specs, out_specs=out_specs, check_vma=False)
```
